32 devices in a mesh: grp: 4 (over x, core), seq: 8 (over z, y).
Axes of the slice: x: 2, y: 2, z: 4, core: 2. Of those that a mesh axis runs over, the one named last changes fastest.
Arguments:
- fields: bfloat16 [4096, 192], P(('grp', 'seq')), may hold values from -6 to 6
- patch_weight: bfloat16 [192, 1024], P(None, ('grp', 'seq')), may hold values from -3 to 3
- variable_embed: bfloat16 [48, 1024], P(None, ('grp', 'seq')), may hold values from -6 to 6
- query_vector: bfloat16 [1024], P(('grp', 'seq')), may hold values from -6 to 6
- key_weight: bfloat16 [1024, 1024], P(('grp', 'seq')), may hold values from -0.1875 to 0.1875
- value_weight: bfloat16 [1024, 1024], P(('grp', 'seq')), may hold values from -0.1875 to 0.1875
- merge_weight: bfloat16 [1024, 1024], P(('grp', 'seq')), may hold values from -0.75 to 0.75
- merge_bias: bfloat16 [1024], P(('grp', 'seq')), may hold values from -3 to 3
- position_table: bfloat16 [1024, 1024], P('seq', 'grp'), may hold values from -3 to 3
- lead_weight: bfloat16 [1024], P(('grp', 'seq')), may hold values from -6 to 6
- lead_bias: bfloat16 [1024], P(('grp', 'seq')), may hold values from -3 to 3
- first_gain: bfloat16 [1024], P(('grp', 'seq')), may hold values from 0.25 to 1.75
- first_shift: bfloat16 [1024], P(('grp', 'seq')), may hold values from -3 to 3
- joint_weight: bfloat16 [1024, 3072], P(('grp', 'seq')), may hold values from -0.1875 to 0.1875
- joint_bias: bfloat16 [2, 1024], P(None, ('grp', 'seq')), may hold values from -3 to 3
- output_weight: bfloat16 [1024, 1024], P(('grp', 'seq')), may hold values from -6 to 6
- output_bias: bfloat16 [1024], P(('grp', 'seq')), may hold values from -8 to 8
- second_gain: bfloat16 [1024], P(('grp', 'seq')), may hold values from 0.25 to 1.75
- second_shift: bfloat16 [1024], P(('grp', 'seq')), may hold values from -3 to 3
- expand_weight: bfloat16 [1024, 4096], P(('grp', 'seq')), may hold values from -0.1875 to 0.1875
- expand_bias: bfloat16 [4096], P(('grp', 'seq')), may hold values from -3 to 3
- reduce_weight: bfloat16 [4096, 1024], P(('grp', 'seq')), may hold values from -0.09375 to 0.09375
- reduce_bias: bfloat16 [1024], P(('grp', 'seq')), may hold values from -12 to 12
- segment_ids: int32 [4096], P(('grp', 'seq')), may hold values from 0 to 3, as said below
- live_rows: int32 [4096], P(('grp', 'seq')), may hold values from 0 to 1
- lead_steps: int32 [4, 4], P('grp'), may hold values from 1 to 28
- cotangent: bfloat16 [4096, 1024], P(('grp', 'seq')), may hold values from -6 to 6
Outputs:
- activations: float32 [4096, 1024], P(('grp', 'seq'))
- field_grad: float32 [4096, 192], P(('grp', 'seq'))
- grad_patch_weight: float32 [192, 1024], P(None, ('grp', 'seq'))
- grad_variable_embed: float32 [48, 1024], P(None, ('grp', 'seq'))
- grad_query_vector: float32 [1024], P(('grp', 'seq'))
- grad_key_weight: float32 [1024, 1024], P(('grp', 'seq'))
- grad_value_weight: float32 [1024, 1024], P(('grp', 'seq'))
- grad_merge_weight: float32 [1024, 1024], P(('grp', 'seq'))
- grad_merge_bias: float32 [1024], P(('grp', 'seq'))
- grad_position_table: float32 [1024, 1024], P('seq', 'grp')
- grad_lead_weight: float32 [1024], P(('grp', 'seq'))
- grad_lead_bias: float32 [1024], P(('grp', 'seq'))
- grad_first_gain: float32 [1024], P(('grp', 'seq'))
- grad_first_shift: float32 [1024], P(('grp', 'seq'))
- grad_joint_weight: float32 [1024, 3072], P(('grp', 'seq'))
- grad_joint_bias: float32 [2, 1024], P(None, ('grp', 'seq'))
- grad_output_weight: float32 [1024, 1024], P(('grp', 'seq'))
- grad_output_bias: float32 [1024], P(('grp', 'seq'))
- grad_second_gain: float32 [1024], P(('grp', 'seq'))
- grad_second_shift: float32 [1024], P(('grp', 'seq'))
- grad_expand_weight: float32 [1024, 4096], P(('grp', 'seq'))
- grad_expand_bias: float32 [4096], P(('grp', 'seq'))
- grad_reduce_weight: float32 [4096, 1024], P(('grp', 'seq'))
- grad_reduce_bias: float32 [1024], P(('grp', 'seq'))
The draws below stay inside these ranges and needn't reach their ends.
Inputs may be any that keep to these rules, and one draw needn't show every extreme that they name: `segment_ids`: ids are compared only within a group of 1024 rows; in every group each id that occurs has rows with live_rows equal to 1.
All inputs are finite; a program needn't handle non-finite values.
Results may differ from the reference program's by a relative error of at most 0.023.
Values may be sent and summed in bfloat16 or wider, within the bound.
A program may use at most 384 MiB of HBM per device.

```python
import math
import jax
import jax.numpy as jnp
from jax import lax

D = 1024
HEADS = 16
FF = 4096
VARS = 48
PIX = 4
SEGS = 4
ROWS_DEV = 128
HDIM = 64
VP = 192
GROUP_ROWS = 1024
TOKENS = 4096
N_GRP = 4


def block_layout(key):
    block_rows = ROWS_DEV // 2
    block_count = GROUP_ROWS // block_rows
    group_count = TOKENS // GROUP_ROWS
    kind_key = jax.random.fold_in(key, 11)
    label_key = jax.random.fold_in(key, 12)
    offset = jax.random.randint(kind_key, (), 0, 2)
    mixed_kind = (jnp.arange(group_count) + offset) % 2
    labels = jax.random.randint(label_key, (group_count, block_count), 0, SEGS)
    block_index = jnp.arange(block_count)[None, :]
    labels = jnp.where((block_index == 1) | (block_index == 2), SEGS - 1, labels)
    labels = jnp.where(block_index == block_count - 1, labels[:, :1], labels)
    labels = labels * mixed_kind[:, None]
    return (labels, mixed_kind, block_rows, block_count)


def draw_segment_ids(key, part):
    labels, mixed_kind, block_rows, block_count = block_layout(key)
    return jnp.repeat(labels, block_rows, axis=1).reshape(TOKENS).astype(jnp.int32)


def draw_live_rows(key, part):
    labels, mixed_kind, block_rows, block_count = block_layout(key)
    block_index = jnp.arange(block_count)[None, :]
    padded_block = (mixed_kind[:, None] == 1) & (labels == SEGS - 1) & (block_index >= 2)
    row_index = jnp.arange(block_rows)
    padded = padded_block[:, :, None] & (row_index[None, None, :] >= block_rows // 2)
    return (1 - padded.astype(jnp.int32)).reshape(TOKENS)


def place_ends(entries, key, smallest, top_value):
    longest = entries.shape.index(max(entries.shape))
    spots = []
    for shift in (0, 1):
        where = [jax.random.randint(jax.random.fold_in(key, axis), (), 0, length) for axis, length in enumerate(entries.shape)]
        where[longest] = (where[longest] + shift) % entries.shape[longest]
        spots.append(tuple(where))
    return entries.at[spots[0]].set(smallest).at[spots[1]].set(top_value)


def steps_of(rng, dims, shards, low, top_value):
    gain, own = 1.0, jax.random.fold_in(rng, 6)
    for dim, shards_of in shards:
        heights = jnp.exp(jax.random.uniform(jax.random.fold_in(own, dim), (shards_of,), jnp.float32, low / len(shards), top_value / len(shards)))
        gain = gain * jnp.repeat(heights, dims[dim] // shards_of).reshape([-1 if axis == dim else 1 for axis in range(len(dims))])
    return gain


def bell_draw(own_key, dims, width, reach, split=(), dtype=jnp.bfloat16):
    loudness = steps_of(own_key, dims, split, -0.22, 0.18) if split else 1.0
    values = jax.random.normal(own_key, dims, jnp.float32) * width * loudness
    return jnp.minimum(jnp.maximum(values, -reach), reach).astype(dtype)


def setup_inputs(seed: int = 0) -> dict:
    keys = jax.random.split(jax.random.key(seed), 28)
    return {
        "fields": bell_draw(keys[0], (TOKENS, VP), 1.0, 6.0, ((0, 32),)),
        "patch_weight": bell_draw(keys[1], (VP, D), PIX ** -0.5, 3.0, ((1, 32),)),
        "variable_embed": bell_draw(keys[2], (VARS, D), 1.0, 6.0, ((1, 32),)),
        "query_vector": bell_draw(keys[3], (D,), 1.0, 6.0, ((0, 32),)),
        "key_weight": bell_draw(keys[4], (D, D), D ** -0.5, 0.1875, ((0, 32),)),
        "value_weight": bell_draw(keys[5], (D, D), D ** -0.5, 0.1875, ((0, 32),)),
        "merge_weight": bell_draw(keys[6], (D, D), (D // 16) ** -0.5, 0.75, ((0, 32),)),
        "merge_bias": bell_draw(keys[7], (D,), 0.5, 3.0, ((0, 32),)),
        "position_table": bell_draw(keys[8], (GROUP_ROWS, D), 0.5, 3.0, ((0, 8), (1, 4))),
        "lead_weight": bell_draw(keys[9], (D,), 1.0, 6.0, ((0, 32),)),
        "lead_bias": bell_draw(keys[10], (D,), 0.5, 3.0, ((0, 32),)),
        "first_gain": jnp.clip(1.0 + 0.15 * jax.random.normal(keys[11], (D,), jnp.float32), 0.25, 1.75).astype(jnp.bfloat16),
        "first_shift": bell_draw(keys[12], (D,), 0.5, 3.0, ((0, 32),)),
        "joint_weight": bell_draw(keys[13], (D, 3 * D), D ** -0.5, 0.1875, ((0, 32),)),
        "joint_bias": bell_draw(keys[14], (2, D), 0.5, 3.0, ((1, 32),)),
        "output_weight": bell_draw(keys[15], (D, D), 1 ** -0.5, 6.0, ((0, 32),)),
        "output_bias": bell_draw(keys[16], (D,), 1.5, 8.0, ((0, 32),)),
        "second_gain": jnp.clip(1.0 + 0.15 * jax.random.normal(keys[17], (D,), jnp.float32), 0.25, 1.75).astype(jnp.bfloat16),
        "second_shift": bell_draw(keys[18], (D,), 0.5, 3.0, ((0, 32),)),
        "expand_weight": bell_draw(keys[19], (D, FF), D ** -0.5, 0.1875, ((0, 32),)),
        "expand_bias": bell_draw(keys[20], (FF,), 0.5, 3.0, ((0, 32),)),
        "reduce_weight": bell_draw(keys[21], (FF, D), FF ** -0.5, 0.09375, ((0, 32),)),
        "reduce_bias": bell_draw(keys[22], (D,), 2.0, 12.0, ((0, 32),)),
        "segment_ids": draw_segment_ids(jax.random.fold_in(keys[27], 71), 0),
        "live_rows": draw_live_rows(jax.random.fold_in(keys[27], 71), 0),
        "lead_steps": place_ends(jax.random.randint(keys[25], (N_GRP, SEGS), 1, 29), jax.random.fold_in(keys[25], 1), 1, 28).astype(jnp.int32),
        "cotangent": bell_draw(keys[26], (TOKENS, D), 1.0, 6.0, ((0, 32),)),
    }


@jax.custom_vjp
def low(v):
    return lax.optimization_barrier(v.astype(jnp.bfloat16)).astype(jnp.float32)

@jax.custom_vjp
def low_back(v):
    return v

def low_keep(v):
    return (low(v), None)

def low_pass(kept, grad):
    return (grad,)

def back_keep(v):
    return (v, None)

def back_low(kept, grad):
    return (low(grad),)
low.defvjp(low_keep, low_pass)
low_back.defvjp(back_keep, back_low)
HIGHEST = lax.Precision.HIGHEST
EPSILON = 1e-05
SCALE = 0.125
LEAD_UNIT = 0.06
MASKED = -1e+30

def layer_norm(inputs, scale_row, shift_row):
    center = inputs - lax.optimization_barrier(jnp.mean(inputs, axis=-1, keepdims=True))
    spread = lax.optimization_barrier(jnp.mean(center * center, axis=-1, keepdims=True))
    return center * lax.rsqrt(spread + EPSILON) * scale_row + shift_row

def aggregate_rows(pieces, patch_weight, variable_embed, probe_low, value_weight):
    row_count = pieces.shape[0]
    tokens = jnp.einsum('rvp,vpd->rvd', pieces.reshape(row_count, VARS, PIX), patch_weight.reshape(VARS, PIX, D), precision=HIGHEST) + variable_embed[None]
    tokens = low(low_back(tokens))
    scores = low_back(jnp.einsum('rvd,dh->rvh', tokens, probe_low, precision=HIGHEST))
    chosen = low(jax.nn.softmax(scores, axis=1))
    mixture = low(low_back(jnp.einsum('rvh,rvd->rhd', chosen, tokens, precision=HIGHEST)))
    head_rows = jnp.einsum('rhd,dhc->rhc', mixture, value_weight.reshape(D, HEADS, HDIM), precision=HIGHEST)
    return low(low_back(head_rows.reshape(row_count, D)))

def attend_rows(query_rows, query_segs, keys_all, values_all, segs_all, live_all):
    row_count = query_rows.shape[0]
    query_heads = query_rows.reshape(row_count, HEADS, HDIM)
    key_heads = keys_all.reshape(-1, HEADS, HDIM)
    value_heads = values_all.reshape(-1, HEADS, HDIM)
    scores = low_back(jnp.einsum('qhc,khc->hqk', query_heads, key_heads, precision=HIGHEST) * SCALE)
    allowed = (query_segs[:, None] == segs_all[None, :]) & (live_all[None, :] == 1)
    scores = jnp.where(allowed[None], scores, MASKED)
    weights = low(jax.nn.softmax(scores, axis=-1))
    mixed_rows = jnp.einsum('hqk,khc->qhc', weights, value_heads, precision=HIGHEST)
    return mixed_rows.reshape(row_count, D)

def group_forward(params, pieces, segs, live, steps):
    patch_weight, variable_embed, query_vector, key_weight, value_weight, merge_weight, merge_bias, position_table, lead_weight, lead_bias, first_gain, first_shift, joint_weight, joint_bias, output_weight, output_bias, second_gain, second_shift, expand_weight, expand_bias, reduce_weight, reduce_bias = params
    probe_full = jnp.einsum('dhc,hc->dh', key_weight.reshape(D, HEADS, HDIM), query_vector.reshape(HEADS, HDIM), precision=HIGHEST) * SCALE
    probe_low = low(probe_full)
    row_block = math.gcd(GROUP_ROWS, 256)
    aggregate_step = jax.checkpoint(lambda pieces_block: aggregate_rows(pieces_block, patch_weight, variable_embed, probe_low, value_weight))
    head_rows = lax.map(aggregate_step, pieces.reshape(GROUP_ROWS // row_block, row_block, VP)).reshape(GROUP_ROWS, D)
    merged = low_back(jnp.dot(head_rows, merge_weight, precision=HIGHEST) + merge_bias)
    picked = jnp.where(segs[:, None] == jnp.arange(SEGS)[None, :], steps[None, :], 0)
    lead_rows = LEAD_UNIT * lax.optimization_barrier(jnp.sum(picked, axis=1)).astype(jnp.float32)
    start_rows = merged + position_table + lead_rows[:, None] * lead_weight + lead_bias
    normed = low(layer_norm(start_rows, first_gain, first_shift))
    joint_rows = jnp.dot(normed, joint_weight, precision=HIGHEST)
    queries = low(low_back(joint_rows[:, :D] + joint_bias[0]))
    key_rows = low(low_back(joint_rows[:, D:2 * D]))
    values = low(low_back(joint_rows[:, 2 * D:] + joint_bias[1]))
    attend_step = jax.checkpoint(lambda pair_item: attend_rows(pair_item[0], pair_item[1], key_rows, values, segs, live))
    attended = lax.map(attend_step, (queries.reshape(-1, row_block, D), segs.reshape(-1, row_block))).reshape(GROUP_ROWS, D)
    attended = low(low_back(attended))
    middle = start_rows + low_back(jnp.dot(attended, output_weight, precision=HIGHEST) + output_bias)
    second = low(layer_norm(middle, second_gain, second_shift))
    hidden = low_back(jnp.dot(second, expand_weight, precision=HIGHEST) + expand_bias)
    active = low(jax.nn.gelu(hidden, approximate=True))
    return middle + jnp.dot(active, reduce_weight, precision=HIGHEST) + reduce_bias

def forward(fields, params, segment_ids, live_rows, lead_steps):
    group_step = jax.checkpoint(lambda group_item: group_forward(params, group_item[0], group_item[1], group_item[2], group_item[3]))
    outputs = lax.map(group_step, (fields.reshape(N_GRP, GROUP_ROWS, VP), segment_ids.reshape(N_GRP, GROUP_ROWS), live_rows.reshape(N_GRP, GROUP_ROWS), lead_steps))
    return outputs.reshape(TOKENS, D)

def reference(fields, patch_weight, variable_embed, query_vector, key_weight, value_weight, merge_weight, merge_bias, position_table, lead_weight, lead_bias, first_gain, first_shift, joint_weight, joint_bias, output_weight, output_bias, second_gain, second_shift, expand_weight, expand_bias, reduce_weight, reduce_bias, segment_ids, live_rows, lead_steps, cotangent):
    params = tuple((weight.astype(jnp.float32) for weight in (patch_weight, variable_embed, query_vector, key_weight, value_weight, merge_weight, merge_bias, position_table, lead_weight, lead_bias, first_gain, first_shift, joint_weight, joint_bias, output_weight, output_bias, second_gain, second_shift, expand_weight, expand_bias, reduce_weight, reduce_bias)))

    def whole(field_values, weight_values):
        return forward(field_values, weight_values, segment_ids, live_rows, lead_steps)
    activations, pullback = jax.vjp(whole, fields.astype(jnp.float32), params)
    field_grad, weight_grads = pullback(cotangent.astype(jnp.float32))
    return (activations, field_grad, weight_grads[0], weight_grads[1], weight_grads[2], weight_grads[3], weight_grads[4], weight_grads[5], weight_grads[6], weight_grads[7], weight_grads[8], weight_grads[9], weight_grads[10], weight_grads[11], weight_grads[12], weight_grads[13], weight_grads[14], weight_grads[15], weight_grads[16], weight_grads[17], weight_grads[18], weight_grads[19], weight_grads[20], weight_grads[21])
```

```python
import functools

import jax
import jax.numpy as jnp
from jax import lax
from jax.experimental import pallas as pl
from jax.experimental.pallas import tpu as pltpu
from jax.sharding import PartitionSpec as P

D = 1024
HEADS = 16
FF = 4096
VARS = 48
PIX = 4
HDIM = 64
VP = 192
KP = 256

EPSILON = 1e-05
SCALE = 0.125
LEAD_UNIT = 0.06
MASKED = -1e30

MESH = pl.DeviceIdType.MESH
ROWS = ("grp", "seq")
F32 = jnp.float32
BF16 = jnp.bfloat16


def f32(x):
    return x.astype(F32)


def low(x):
    return x.astype(BF16)


def dot(a, b, ca, cb):
    return lax.dot_general(a, b, (((ca,), (cb,)), ((), ())), preferred_element_type=F32)


def low_sums(x):
    return dot(jnp.ones((8, x.shape[0]), BF16), x, 1, 0)[0]


def exchange_kernel(axis, count, modes, *refs):
    n = len(modes)
    ins, outs = refs[:n], refs[n : 2 * n]
    send, recv, own = refs[2 * n :]
    me = lax.axis_index(axis)
    other = lax.axis_index("seq" if axis == "grp" else "grp")

    def device(index):
        return (index, other) if axis == "grp" else (other, index)

    barrier = pltpu.get_barrier_semaphore()
    for step in range(1, count):
        pl.semaphore_signal(
            barrier, inc=1, device_id=device(lax.rem(me + step, count)), device_id_type=MESH
        )
    pl.semaphore_wait(barrier, count - 1)
    copies = []
    for step in range(1, count):
        peer = lax.rem(me + step, count)
        for k in range(n):
            copy = pltpu.make_async_remote_copy(
                src_ref=ins[k] if modes[k] == "all" else ins[k].at[peer],
                dst_ref=outs[k].at[me],
                send_sem=send.at[k, step - 1],
                recv_sem=recv.at[k, step - 1],
                device_id=device(peer),
                device_id_type=MESH,
            )
            copy.start()
            copies.append(copy)
    for k in range(n):
        copy = pltpu.make_async_copy(
            ins[k] if modes[k] == "all" else ins[k].at[me], outs[k].at[me], own.at[k]
        )
        copy.start()
        copies.append(copy)
    for copy in copies:
        copy.wait()


def exchange(axis, count, ident, parts):
    arrays = [a for a, _ in parts]
    modes = tuple(m for _, m in parts)
    if ident is None:
        return [
            lax.all_gather(a, axis, axis=0, tiled=False)
            if m == "all"
            else lax.all_to_all(a, axis, 0, 0, tiled=False)
            for a, m in parts
        ]
    shapes = [
        jax.ShapeDtypeStruct(((count,) + a.shape) if m == "all" else a.shape, a.dtype)
        for a, m in parts
    ]
    n = len(parts)
    return pl.pallas_call(
        functools.partial(exchange_kernel, axis, count, modes),
        out_shape=shapes,
        in_specs=[pl.BlockSpec(memory_space=pl.ANY)] * n,
        out_specs=[pl.BlockSpec(memory_space=pl.ANY)] * n,
        scratch_shapes=[
            pltpu.SemaphoreType.DMA((n, count - 1)),
            pltpu.SemaphoreType.DMA((n, count - 1)),
            pltpu.SemaphoreType.DMA((n,)),
        ],
        compiler_params=pltpu.CompilerParams(collective_id=ident, has_side_effects=True),
    )(*arrays)


def norm_parts(x):
    center = x - jnp.mean(x, axis=-1, keepdims=True)
    spread = jnp.mean(center * center, axis=-1, keepdims=True)
    inverse = lax.rsqrt(spread + EPSILON)
    return center * inverse, inverse


def norm_back(hat, inverse, gain, grad):
    f = grad * gain
    return inverse * (
        f
        - jnp.mean(f, axis=-1, keepdims=True)
        - hat * jnp.mean(f * hat, axis=-1, keepdims=True)
    )


def pack(pieces):
    flat = jnp.concatenate([f32(p).reshape(-1) for p in pieces])
    short = -flat.shape[0] % 1024
    return jnp.pad(flat, (0, short)).reshape(-1, 128)


def unpack(table, sizes):
    flat = table.reshape(table.shape[:-2] + (-1,))
    out, at = [], 0
    for size in sizes:
        out.append(flat[..., at : at + size])
        at += size
    return out


def softmax_parts(q, k, allowed):
    scores = jnp.einsum("hqc,hkc->hqk", q, k, preferred_element_type=F32) * SCALE
    masked = jnp.where(allowed[None], scores, MASKED)
    top = jnp.max(masked, axis=-1, keepdims=True)
    terms = jnp.where(allowed[None], jnp.exp(masked - top), 0.0)
    total = jnp.sum(terms, axis=-1, keepdims=True)
    return terms * (1.0 / total)


def attend(q, k, v, allowed):
    weights = softmax_parts(q, k, allowed)
    return jnp.einsum("hqk,hkc->hqc", low(weights), v, preferred_element_type=F32)


def attend_back(q, k, v, allowed, grad, attended):
    weights = softmax_parts(q, k, allowed)
    offset = jnp.sum(f32(grad) * attended, axis=-1)
    pushed = jnp.einsum("hqc,hkc->hqk", grad, v, preferred_element_type=F32)
    slopes = low(weights * (pushed - offset[..., None])) * BF16(SCALE)
    grad_q = jnp.einsum("hqk,hkc->hqc", slopes, k, preferred_element_type=F32)
    grad_k = jnp.einsum("hqk,hqc->hkc", slopes, q, preferred_element_type=F32)
    grad_v = jnp.einsum("hqk,hqc->hkc", low(weights), grad, preferred_element_type=F32)
    return grad_q, grad_k, grad_v


def heads_first(x):
    return x.transpose(1, 0, 2)


def heads_last(x):
    return x.transpose(1, 0, 2)


def allowed_pairs(query_codes, key_codes):
    return ((query_codes[:, None] >> 1) == (key_codes[None, :] >> 1)) & (
        (key_codes[None, :] & 1) == 1
    )


def shards(
    G,
    S,
    fields,
    patch_weight,
    variable_embed,
    query_vector,
    key_weight,
    value_weight,
    merge_weight,
    merge_bias,
    position_table,
    lead_weight,
    lead_bias,
    first_gain,
    first_shift,
    joint_weight,
    joint_bias,
    output_weight,
    output_bias,
    second_gain,
    second_shift,
    expand_weight,
    expand_bias,
    reduce_weight,
    reduce_bias,
    segment_ids,
    live_rows,
    lead_steps,
    cotangent,
):
    R = fields.shape[0]
    dn = value_weight.shape[0]
    fn = reduce_weight.shape[0]
    RG = G * R
    HL = HEADS // G
    CL = HL * HDIM
    FL = FF // G
    pairs = G * HL
    direct = pairs % S == 0 and HL % max(pairs // S, 1) == 0 and dn % 16 == 0 and R % 16 == 0
    idents = iter(range(1, 100))

    def swap(axis, *parts):
        return exchange(axis, G if axis == "grp" else S, next(idents) if direct else None, parts)

    def gather_rows(w):
        return lax.all_gather(w, "seq", axis=0, tiled=True)

    merge_s = gather_rows(merge_weight)
    output_s = gather_rows(output_weight)

    table = jnp.concatenate(
        [patch_weight, variable_embed, jnp.zeros((KP - VP - VARS, dn), BF16)], axis=0
    )
    value_part = low(dot(value_weight, table, 0, 1)).reshape(G, CL, KP)
    key_part = low(dot(key_weight, table, 0, 1)).reshape(G, CL, KP)
    both = jnp.concatenate([value_part, key_part], axis=1)
    codes_own = segment_ids * 2 + live_rows
    vectors_own = [
        query_vector,
        merge_bias,
        lead_weight,
        lead_bias,
        first_gain,
        first_shift,
        output_bias,
        second_gain,
        second_shift,
        reduce_bias,
    ]
    small_own = pack([codes_own] + vectors_own)
    widen = (jnp.arange(VP)[:, None] == jnp.arange(KP)[None, :]).astype(BF16)
    column = jnp.arange(KP)
    field_own = low(dot(fields, widen, 1, 0) + ((column >= VP) & (column < VP + VARS)))
    joint_own = joint_weight.reshape(dn, 3, G, CL).transpose(2, 0, 1, 3).reshape(G, dn, 3 * CL)
    expand_own = expand_weight.reshape(dn, G, FL).transpose(1, 0, 2)
    both, joint_in, expand_in, field_in, position_in, small_in, cot_in = swap(
        "grp",
        (both, "each"),
        (joint_own, "each"),
        (expand_own, "each"),
        (field_own, "all"),
        (position_table, "all"),
        (small_own, "all"),
        (cotangent, "all"),
    )
    joint_s = (
        lax.all_gather(joint_in, "seq", axis=0, tiled=False)
        .transpose(1, 0, 2, 3)
        .reshape(D, 3 * CL)
    )
    expand_s = (
        lax.all_gather(expand_in, "seq", axis=0, tiled=False).transpose(1, 0, 2, 3).reshape(D, FL)
    )
    reduce_s = gather_rows(reduce_weight)
    field_rows = field_in.reshape(RG, KP)
    field_wide = dot(field_rows, (column[:, None] == column[None, :]).astype(BF16), 1, 0)
    cot_rows = cot_in.reshape(RG, D)
    position_rows = position_in.transpose(1, 0, 2).reshape(R, D)
    both = low(jnp.sum(f32(both), axis=0)).reshape(2, S, dn, KP).transpose(1, 0, 2, 3)
    small_rows = small_in.shape[0] * small_in.shape[1]
    slim = pack([joint_bias, expand_bias])
    both, small_all, slim_all = swap(
        "seq",
        (both.reshape(S, 2 * dn, KP), "each"),
        (small_in.reshape(small_rows, 128), "all"),
        (slim, "all"),
    )
    both = jnp.sum(f32(both), axis=0).reshape(2, dn, KP)
    value_own, key_own = both[0], both[1]
    probe_part = jnp.sum(key_own * f32(query_vector)[:, None], axis=0) * SCALE
    value_table, probe_parts = swap(
        "seq",
        (low(value_own), "all"),
        (jnp.broadcast_to(probe_part[None], (8, KP)), "all"),
    )
    value_table = value_table.reshape(CL, KP)
    probe_table = jnp.sum(probe_parts[:, 0].reshape(HL, S // HL, KP), axis=1)

    small_all = small_all.reshape(S, G, -1, 128)
    pieces = unpack(small_all, [R] + [dn] * len(vectors_own))
    codes = pieces[0].astype(jnp.int32)
    (
        full_query,
        full_merge_bias,
        full_lead,
        full_lead_bias,
        full_first_gain,
        full_first_shift,
        full_output_bias,
        full_second_gain,
        full_second_shift,
        full_reduce_bias,
    ) = [p.transpose(1, 0, 2).reshape(D) for p in pieces[1:]]
    joint_shift, expand_shift = unpack(slim_all, [2 * dn, fn])
    joint_shift = joint_shift.reshape(S, 2, dn).transpose(1, 0, 2).reshape(2, CL)
    expand_shift = expand_shift.reshape(FL)

    picked = jnp.where(
        segment_ids[:, None] == jnp.arange(lead_steps.shape[1])[None, :], lead_steps, 0
    )
    lead_rows = LEAD_UNIT * jnp.sum(picked, axis=1).astype(F32)

    owner = jnp.concatenate(
        [jnp.arange(VP) // PIX, jnp.arange(VARS), jnp.full((KP - VP - VARS,), VARS)]
    )
    select = (owner[:, None] == jnp.arange(VARS)[None, :]).astype(BF16)
    maps = probe_table[:, :, None] * f32(select)[None]
    maps_high = low(maps)
    maps_low = low(maps - f32(maps_high))
    scores = jnp.einsum("rk,hkv->hrv", field_rows, maps_high, preferred_element_type=F32)
    scores = scores + jnp.einsum("rk,hkv->hrv", field_rows, maps_low, preferred_element_type=F32)
    chosen = jax.nn.softmax(scores, axis=-1)
    spread = jnp.einsum("hrv,kv->hrk", low(chosen), select, preferred_element_type=F32)
    mixed = low(spread * field_wide[None])
    value_heads = value_table.reshape(HL, HDIM, KP)
    head_low = low(
        jnp.einsum("hrk,hck->rhc", mixed, value_heads, preferred_element_type=F32).reshape(RG, CL)
    )
    merged = low(dot(head_low, merge_s, 1, 0)).reshape(G, R, D)
    (merged,) = swap("grp", (merged, "each"))
    start = (
        jnp.sum(f32(merged), axis=0)
        + full_merge_bias
        + f32(position_rows)
        + lead_rows[:, None] * full_lead
        + full_lead_bias
    )
    start_hat, start_inv = norm_parts(start)
    (normed,) = swap("grp", (low(start_hat * full_first_gain + full_first_shift), "all"))
    normed = normed.reshape(RG, D)
    joint = dot(normed, joint_s, 1, 0)
    shift = jnp.concatenate([joint_shift[0], jnp.zeros((CL,), F32), joint_shift[1]])
    joint = low(joint + shift)

    if direct:
        per = pairs // S
        split = HL // per
        width = per * HDIM

        def to_pairs(x, kinds):
            x = x.reshape(G, R, kinds, split, width).transpose(0, 3, 1, 2, 4)
            (x,) = swap("seq", (x.reshape(S, R, kinds * width), "each"))
            return x.reshape(S * R, kinds, per, HDIM)

        def from_pairs(x, kinds):
            (x,) = swap("seq", (x.reshape(S, R, kinds * width), "each"))
            return (
                x.reshape(G, split, R, kinds, width)
                .transpose(0, 2, 3, 1, 4)
                .reshape(RG, kinds * CL)
            )

        mine = lax.axis_index("seq") // split
        pair_codes = lax.dynamic_index_in_dim(codes, mine, axis=1, keepdims=False).reshape(S * R)
        allowed = allowed_pairs(pair_codes, pair_codes)
        qkv = to_pairs(joint, 3)
        q, k, v = [heads_first(qkv[:, i]) for i in range(3)]
        attended = attend(q, k, v, allowed)
        attended_low = from_pairs(heads_last(low(attended)), 1)
    else:
        heads = joint.reshape(G, R, 3, HL, HDIM).transpose(0, 2, 3, 1, 4)
        everyone = lax.all_gather(heads[:, 1:], "seq", axis=3, tiled=True)
        all_codes = codes.transpose(1, 0, 2).reshape(G, S * R)
        my_codes = lax.dynamic_index_in_dim(codes, lax.axis_index("seq"), 0, keepdims=False)

        def forward_group(item):
            q, kv, query_codes, key_codes = item
            return attend(q, kv[0], kv[1], allowed_pairs(query_codes, key_codes))

        attended = lax.map(forward_group, (heads[:, 0], everyone, my_codes, all_codes))
        attended_low = low(attended).transpose(0, 2, 1, 3).reshape(RG, CL)

    branch = low(dot(attended_low, output_s, 1, 0)).reshape(G, R, D)
    (branch,) = swap("grp", (branch, "each"))
    middle = start + jnp.sum(f32(branch), axis=0) + full_output_bias
    middle_hat, middle_inv = norm_parts(middle)
    (second,) = swap("grp", (low(middle_hat * full_second_gain + full_second_shift), "all"))
    second = second.reshape(RG, D)
    hidden = dot(second, expand_s, 1, 0) + expand_shift
    inner = 0.7978845608028654 * (hidden + 0.044715 * hidden * hidden * hidden)
    bend = jnp.tanh(inner)
    active = low(0.5 * hidden * (1.0 + bend))
    slope = 0.5 * (1.0 + bend) + 0.5 * hidden * (1.0 - bend * bend) * 0.7978845608028654 * (
        1.0 + 3.0 * 0.044715 * hidden * hidden
    )
    reduced = low(dot(active, reduce_s, 1, 0)).reshape(G, R, D)

    grad_active = dot(cot_rows, reduce_s, 1, 1)
    grad_hidden = low(grad_active * slope)
    grad_second = low(dot(grad_hidden, expand_s, 1, 1)).reshape(G, R, D)
    grad_second, reduced = swap("grp", (grad_second, "each"), (reduced, "each"))
    activations = middle + jnp.sum(f32(reduced), axis=0) + full_reduce_bias
    grad_second = jnp.sum(f32(grad_second), axis=0)
    grad_top = f32(cotangent)
    grad_middle = grad_top + norm_back(middle_hat, middle_inv, full_second_gain, grad_second)
    grad_branch = low(grad_middle)

    def scatter_rows(w):
        return lax.psum_scatter(w, "seq", scatter_dimension=0, tiled=True)

    def scatter_mixed(w):
        cols = w.shape[1]
        w = w.reshape(G, S, dn, cols).transpose(1, 0, 2, 3).reshape(S, G * dn * cols // 1024, 1024)
        w = lax.psum_scatter(w, "seq", scatter_dimension=0, tiled=False)
        return w.reshape(G, dn, cols)

    grad_reduce_weight = f32(scatter_rows(low(dot(active, cot_rows, 0, 0))))
    grad_expand_mixed = scatter_mixed(low(dot(second, grad_hidden, 0, 0)))
    grad_expand_bias = low_sums(grad_hidden)

    (grad_branch_rows,) = swap("grp", (grad_branch, "all"))
    grad_branch_rows = grad_branch_rows.reshape(RG, D)
    grad_attended = low(dot(grad_branch_rows, output_s, 1, 1))
    grad_output_weight = f32(scatter_rows(low(dot(attended_low, grad_branch_rows, 0, 0))))
    if direct:
        pushed = heads_first(to_pairs(grad_attended, 1)[:, 0])
        grad_q, grad_k, grad_v = attend_back(q, k, v, allowed, pushed, attended)
        grads = [heads_last(low(x)) for x in (grad_q, grad_k, grad_v)]
        grad_joint = from_pairs(jnp.stack(grads, axis=1), 3)
    else:
        grad_heads = grad_attended.reshape(G, R, HL, HDIM).transpose(0, 2, 1, 3)

        def backward_group(item):
            q, kv, query_codes, key_codes, grad, done = item
            grad_q, grad_k, grad_v = attend_back(
                q, kv[0], kv[1], allowed_pairs(query_codes, key_codes), grad, done
            )
            return grad_q, jnp.stack([grad_k, grad_v], axis=0)

        grad_q, grad_kv = lax.map(
            backward_group,
            (heads[:, 0], everyone, my_codes, all_codes, grad_heads, attended),
        )
        grad_kv = lax.psum_scatter(grad_kv, "seq", scatter_dimension=3, tiled=True)
        grad_joint = low(jnp.concatenate([grad_q[:, None], grad_kv], axis=1))
        grad_joint = grad_joint.transpose(0, 3, 1, 2, 4).reshape(RG, 3 * CL)
    grad_normed = low(dot(grad_joint, joint_s, 1, 1)).reshape(G, R, D)
    (grad_normed,) = swap("grp", (grad_normed, "each"))
    grad_normed = jnp.sum(f32(grad_normed), axis=0)
    grad_joint_mixed = scatter_mixed(low(dot(normed, grad_joint, 0, 0)))
    joint_sums = low_sums(grad_joint)
    grad_start = grad_middle + norm_back(start_hat, start_inv, full_first_gain, grad_normed)
    grad_merged = low(grad_start)

    grad_merged_rows, grad_joint_in, grad_expand_in = swap(
        "grp", (grad_merged, "all"), (grad_joint_mixed, "each"), (grad_expand_mixed, "each")
    )
    grad_joint_weight = f32(
        grad_joint_in.reshape(G, dn, 3, CL).transpose(1, 2, 0, 3).reshape(dn, 3 * D)
    )
    grad_expand_weight = f32(grad_expand_in.transpose(1, 0, 2).reshape(dn, FF))
    grad_merged_rows = grad_merged_rows.reshape(RG, D)
    grad_head = low(dot(grad_merged_rows, merge_s, 1, 1))
    grad_merge_weight = f32(scatter_rows(low(dot(head_low, grad_merged_rows, 0, 0))))
    grad_heads_low = grad_head.reshape(RG, HL, HDIM)
    value_back = jnp.einsum(
        "rhc,hck->hrk", grad_heads_low, value_heads, preferred_element_type=F32
    )
    weighed = value_back * field_wide[None]
    weighed_high = low(weighed)
    weighed_low = low(weighed - f32(weighed_high))
    grad_chosen = jnp.einsum("hrk,kv->hrv", weighed_high, select, preferred_element_type=F32)
    grad_chosen = grad_chosen + jnp.einsum(
        "hrk,kv->hrv", weighed_low, select, preferred_element_type=F32
    )
    grad_scores = low(
        chosen * (grad_chosen - jnp.sum(chosen * grad_chosen, axis=-1, keepdims=True))
    )
    score_spread = jnp.einsum("hrv,kv->hrk", grad_scores, select, preferred_element_type=F32)
    field_part = jnp.sum(spread * value_back + score_spread * probe_table[:, None, :], axis=0)
    field_part = field_part.reshape(G, R, KP)
    score_sums = jnp.sum(score_spread * field_wide[None], axis=1)
    head_sums = jnp.einsum(
        "rhc,hrk->hck", grad_heads_low, mixed, preferred_element_type=F32
    ).reshape(S, dn, KP)

    column_sums = jnp.stack(
        [
            low_sums(grad_merged),
            jnp.sum(lead_rows[:, None] * grad_start, axis=0),
            jnp.sum(grad_start, axis=0),
            jnp.sum(grad_normed * start_hat, axis=0),
            jnp.sum(grad_normed, axis=0),
            low_sums(grad_branch),
            jnp.sum(grad_second * middle_hat, axis=0),
            jnp.sum(grad_second, axis=0),
            jnp.sum(grad_top, axis=0),
        ]
    )
    kinds = column_sums.shape[0]
    column_sums = jnp.pad(column_sums, ((0, -kinds % 16), (0, 0)))
    column_sums = column_sums.reshape(-1, G, CL).transpose(1, 0, 2)
    position_blocks = grad_merged.reshape(R, G, CL).transpose(1, 0, 2)
    column_sums, position_blocks, field_part = swap(
        "grp", (column_sums, "each"), (position_blocks, "each"), (field_part, "each")
    )
    grad_position_table = jnp.sum(f32(position_blocks), axis=0)
    field_grad = jnp.sum(field_part, axis=0)[:, :VP]
    column_sums = jnp.sum(column_sums, axis=0)
    team_sums = jnp.concatenate(
        [
            column_sums[:kinds].reshape(kinds, S, dn).transpose(1, 0, 2).reshape(S, kinds * dn),
            joint_sums[:CL].reshape(S, dn),
            joint_sums[2 * CL :].reshape(S, dn),
            grad_expand_bias.reshape(S, fn),
        ],
        axis=1,
    )
    wide = team_sums.shape[1]
    team_sums = jnp.pad(team_sums, ((0, 0), (0, -wide % 1024))).reshape(S, -1, 128)
    score_sums = jnp.pad(score_sums, ((0, -HL % 8), (0, 0)))
    team_sums, head_sums, score_sums = swap(
        "seq", (team_sums, "each"), (low(head_sums), "each"), (score_sums, "all")
    )
    team_sums = jnp.sum(team_sums, axis=0).reshape(-1)[:wide]
    own_sums = team_sums[: kinds * dn].reshape(kinds, dn)
    grad_joint_bias = team_sums[kinds * dn : (kinds + 2) * dn].reshape(2, dn)
    grad_expand_bias = team_sums[(kinds + 2) * dn :]
    (
        grad_merge_bias,
        grad_lead_weight,
        grad_lead_bias,
        grad_first_gain,
        grad_first_shift,
        grad_output_bias,
        grad_second_gain,
        grad_second_shift,
        grad_reduce_bias,
    ) = [own_sums[i] for i in range(kinds)]
    head_sums = jnp.sum(f32(head_sums), axis=0)
    score_sums = jnp.sum(score_sums, axis=0)
    my_head = lax.axis_index("seq") * dn // HDIM
    my_scores = lax.dynamic_index_in_dim(score_sums, my_head, axis=0, keepdims=False)
    grad_query_vector = jnp.sum(key_own * my_scores[None], axis=1) * SCALE
    (head_all,) = swap("seq", (low(head_sums), "all"))
    head_all, score_all = swap(
        "grp", (head_all.reshape(S * dn, KP), "all"), (score_sums, "all")
    )
    head_all = head_all.reshape(D, KP)
    score_all = score_all[:, :HL].reshape(HEADS, KP)
    grad_value_weight = dot(table, head_all, 0, 1)
    probe_own = low(
        jnp.sum((f32(key_weight) * full_query).reshape(dn, HEADS, HDIM), axis=-1) * SCALE
    )
    grad_table = dot(head_all, value_weight, 0, 1)
    grad_table = grad_table + jnp.einsum("hk,dh->kd", score_all, f32(probe_own))
    grad_probe = jnp.einsum("kd,hk->dh", f32(table), score_all)
    grad_key_weight = (
        grad_probe[:, :, None] * full_query.reshape(HEADS, HDIM)[None] * SCALE
    ).reshape(dn, D)
    grad_patch_weight = grad_table[:VP]
    grad_variable_embed = grad_table[VP : VP + VARS]
    return (
        activations,
        field_grad,
        grad_patch_weight,
        grad_variable_embed,
        grad_query_vector,
        grad_key_weight,
        grad_value_weight,
        grad_merge_weight,
        grad_merge_bias,
        grad_position_table,
        grad_lead_weight,
        grad_lead_bias,
        grad_first_gain,
        grad_first_shift,
        grad_joint_weight,
        grad_joint_bias,
        grad_output_weight,
        grad_output_bias,
        grad_second_gain,
        grad_second_shift,
        grad_expand_weight,
        grad_expand_bias,
        grad_reduce_weight,
        grad_reduce_bias,
    )


def solution(mesh):
    by_row = P(ROWS, None)
    by_column = P(None, ROWS)
    vector = P(ROWS)
    in_specs = (
        by_row,
        by_column,
        by_column,
        vector,
        by_row,
        by_row,
        by_row,
        vector,
        P("seq", "grp"),
        vector,
        vector,
        vector,
        vector,
        by_row,
        by_column,
        by_row,
        vector,
        vector,
        vector,
        by_row,
        vector,
        by_row,
        vector,
        vector,
        vector,
        P("grp", None),
        by_row,
    )
    out_specs = (
        by_row,
        by_row,
        by_column,
        by_column,
        vector,
        by_row,
        by_row,
        by_row,
        vector,
        P("seq", "grp"),
        vector,
        vector,
        vector,
        vector,
        by_row,
        by_column,
        by_row,
        vector,
        vector,
        vector,
        by_row,
        vector,
        by_row,
        vector,
    )
    body = functools.partial(shards, mesh.shape["grp"], mesh.shape["seq"])
    return jax.shard_map(body, mesh=mesh, in_specs=in_specs, out_specs=out_specs, check_vma=False)
```

```python
import types

import jax
import jax.numpy as jnp
from jax import lax
from jax.experimental import pallas as pl
from jax.experimental.pallas import tpu as pltpu
from jax.sharding import PartitionSpec as P

D = 1024
HEADS = 16
FF = 4096
VARS = 48
PIX = 4
HDIM = 64
VP = 192
KP = 256

EPSILON = 1e-05
SCALE = 0.125
LEAD_UNIT = 0.06
MASKED = -1e30

MESH = pl.DeviceIdType.MESH
ROWS = ("grp", "seq")
F32 = jnp.float32
BF16 = jnp.bfloat16


def f32(x):
    return x.astype(F32)


def low(x):
    return x.astype(BF16)


def dot(a, b, ca, cb):
    return lax.dot_general(a, b, (((ca,), (cb,)), ((), ())), preferred_element_type=F32)


def low_sums(x):
    return dot(jnp.ones((8, x.shape[0]), BF16), x, 1, 0)[0]


def exchange(axis, parts):
    return [
        lax.all_gather(a, axis, axis=0, tiled=False)
        if mode == "all"
        else lax.all_to_all(a, axis, 0, 0, tiled=False)
        for a, mode in parts
    ]


def norm_parts(x):
    center = x - jnp.mean(x, axis=-1, keepdims=True)
    spread = jnp.mean(center * center, axis=-1, keepdims=True)
    inverse = lax.rsqrt(spread + EPSILON)
    return center * inverse, inverse


def norm_back(hat, inverse, gain, grad):
    f = grad * gain
    return inverse * (
        f
        - jnp.mean(f, axis=-1, keepdims=True)
        - hat * jnp.mean(f * hat, axis=-1, keepdims=True)
    )


def pack(pieces):
    flat = jnp.concatenate([f32(p).reshape(-1) for p in pieces])
    short = -flat.shape[0] % 1024
    return jnp.pad(flat, (0, short)).reshape(-1, 128)


def unpack(table, sizes):
    flat = table.reshape(table.shape[:-2] + (-1,))
    out, at = [], 0
    for size in sizes:
        out.append(flat[..., at : at + size])
        at += size
    return out


def softmax_parts(q, k, allowed):
    scores = jnp.einsum("hqc,hkc->hqk", q, k, preferred_element_type=F32) * SCALE
    masked = jnp.where(allowed[None], scores, MASKED)
    top = jnp.max(masked, axis=-1, keepdims=True)
    terms = jnp.where(allowed[None], jnp.exp(masked - top), 0.0)
    total = jnp.sum(terms, axis=-1, keepdims=True)
    return terms * (1.0 / total)


def attend(q, k, v, allowed):
    weights = softmax_parts(q, k, allowed)
    return jnp.einsum("hqk,hkc->hqc", low(weights), v, preferred_element_type=F32)


def attend_back(q, k, v, allowed, grad, attended):
    weights = softmax_parts(q, k, allowed)
    offset = jnp.sum(f32(grad) * attended, axis=-1)
    pushed = jnp.einsum("hqc,hkc->hqk", grad, v, preferred_element_type=F32)
    slopes = low(weights * (pushed - offset[..., None])) * BF16(SCALE)
    grad_q = jnp.einsum("hqk,hkc->hqc", slopes, k, preferred_element_type=F32)
    grad_k = jnp.einsum("hqk,hqc->hkc", slopes, q, preferred_element_type=F32)
    grad_v = jnp.einsum("hqk,hqc->hkc", low(weights), grad, preferred_element_type=F32)
    return grad_q, grad_k, grad_v


def heads_first(x):
    return x.transpose(1, 0, 2)


def heads_last(x):
    return x.transpose(1, 0, 2)


def allowed_pairs(query_codes, key_codes):
    return ((query_codes[:, None] >> 1) == (key_codes[None, :] >> 1)) & (
        (key_codes[None, :] & 1) == 1
    )


def shards(
    G,
    S,
    fields,
    patch_weight,
    variable_embed,
    query_vector,
    key_weight,
    value_weight,
    merge_weight,
    merge_bias,
    position_table,
    lead_weight,
    lead_bias,
    first_gain,
    first_shift,
    joint_weight,
    joint_bias,
    output_weight,
    output_bias,
    second_gain,
    second_shift,
    expand_weight,
    expand_bias,
    reduce_weight,
    reduce_bias,
    segment_ids,
    live_rows,
    lead_steps,
    cotangent,
):
    R = fields.shape[0]
    dn = value_weight.shape[0]
    fn = reduce_weight.shape[0]
    RG = G * R
    HL = HEADS // G
    CL = HL * HDIM
    FL = FF // G
    pairs = G * HL
    direct = pairs % S == 0 and HL % max(pairs // S, 1) == 0

    def swap(axis, *parts):
        return exchange(axis, parts)

    def gather_rows(w):
        return lax.all_gather(w, "seq", axis=0, tiled=True)

    merge_s = gather_rows(merge_weight)
    output_s = gather_rows(output_weight)

    table = jnp.concatenate(
        [patch_weight, variable_embed, jnp.zeros((KP - VP - VARS, dn), BF16)], axis=0
    )
    value_part = low(dot(value_weight, table, 0, 1)).reshape(G, CL, KP)
    key_part = low(dot(key_weight, table, 0, 1)).reshape(G, CL, KP)
    both = jnp.concatenate([value_part, key_part], axis=1)
    codes_own = segment_ids * 2 + live_rows
    vectors_own = [
        query_vector,
        merge_bias,
        lead_weight,
        lead_bias,
        first_gain,
        first_shift,
        output_bias,
        second_gain,
        second_shift,
        reduce_bias,
    ]
    small_own = pack([codes_own] + vectors_own)
    widen = (jnp.arange(VP)[:, None] == jnp.arange(KP)[None, :]).astype(BF16)
    column = jnp.arange(KP)
    field_own = low(dot(fields, widen, 1, 0) + ((column >= VP) & (column < VP + VARS)))
    joint_own = joint_weight.reshape(dn, 3, G, CL).transpose(2, 0, 1, 3).reshape(G, dn, 3 * CL)
    expand_own = expand_weight.reshape(dn, G, FL).transpose(1, 0, 2)
    both, joint_in, expand_in, field_in, position_in, small_in, cot_in = swap(
        "grp",
        (both, "each"),
        (joint_own, "each"),
        (expand_own, "each"),
        (field_own, "all"),
        (position_table, "all"),
        (small_own, "all"),
        (cotangent, "all"),
    )
    joint_s = (
        lax.all_gather(joint_in, "seq", axis=0, tiled=False)
        .transpose(1, 0, 2, 3)
        .reshape(D, 3 * CL)
    )
    expand_s = (
        lax.all_gather(expand_in, "seq", axis=0, tiled=False).transpose(1, 0, 2, 3).reshape(D, FL)
    )
    reduce_s = gather_rows(reduce_weight)
    field_rows = field_in.reshape(RG, KP)
    field_wide = dot(field_rows, (column[:, None] == column[None, :]).astype(BF16), 1, 0)
    cot_rows = cot_in.reshape(RG, D)
    position_rows = position_in.transpose(1, 0, 2).reshape(R, D)
    both = low(jnp.sum(f32(both), axis=0)).reshape(2, S, dn, KP).transpose(1, 0, 2, 3)
    small_rows = small_in.shape[0] * small_in.shape[1]
    slim = pack([joint_bias, expand_bias])
    both, small_all, slim_all = swap(
        "seq",
        (both.reshape(S, 2 * dn, KP), "each"),
        (small_in.reshape(small_rows, 128), "all"),
        (slim, "all"),
    )
    both = jnp.sum(f32(both), axis=0).reshape(2, dn, KP)
    value_own, key_own = both[0], both[1]
    probe_part = jnp.sum(key_own * f32(query_vector)[:, None], axis=0) * SCALE
    value_table, probe_parts = swap(
        "seq",
        (low(value_own), "all"),
        (jnp.broadcast_to(probe_part[None], (8, KP)), "all"),
    )
    value_table = value_table.reshape(CL, KP)
    probe_table = jnp.sum(probe_parts[:, 0].reshape(HL, S // HL, KP), axis=1)

    small_all = small_all.reshape(S, G, -1, 128)
    pieces = unpack(small_all, [R] + [dn] * len(vectors_own))
    codes = pieces[0].astype(jnp.int32)
    (
        full_query,
        full_merge_bias,
        full_lead,
        full_lead_bias,
        full_first_gain,
        full_first_shift,
        full_output_bias,
        full_second_gain,
        full_second_shift,
        full_reduce_bias,
    ) = [p.transpose(1, 0, 2).reshape(D) for p in pieces[1:]]
    joint_shift, expand_shift = unpack(slim_all, [2 * dn, fn])
    joint_shift = joint_shift.reshape(S, 2, dn).transpose(1, 0, 2).reshape(2, CL)
    expand_shift = expand_shift.reshape(FL)

    picked = jnp.where(
        segment_ids[:, None] == jnp.arange(lead_steps.shape[1])[None, :], lead_steps, 0
    )
    lead_rows = LEAD_UNIT * jnp.sum(picked, axis=1).astype(F32)

    owner = jnp.concatenate(
        [jnp.arange(VP) // PIX, jnp.arange(VARS), jnp.full((KP - VP - VARS,), VARS)]
    )
    select = (owner[:, None] == jnp.arange(VARS)[None, :]).astype(BF16)
    maps = probe_table[:, :, None] * f32(select)[None]
    maps_high = low(maps)
    maps_low = low(maps - f32(maps_high))
    scores = jnp.einsum("rk,hkv->hrv", field_rows, maps_high, preferred_element_type=F32)
    scores = scores + jnp.einsum("rk,hkv->hrv", field_rows, maps_low, preferred_element_type=F32)
    chosen = jax.nn.softmax(scores, axis=-1)
    spread = jnp.einsum("hrv,kv->hrk", low(chosen), select, preferred_element_type=F32)
    mixed = low(spread * field_wide[None])
    value_heads = value_table.reshape(HL, HDIM, KP)
    head_low = low(
        jnp.einsum("hrk,hck->rhc", mixed, value_heads, preferred_element_type=F32).reshape(RG, CL)
    )
    merged = low(dot(head_low, merge_s, 1, 0)).reshape(G, R, D)
    (merged,) = swap("grp", (merged, "each"))
    start = (
        jnp.sum(f32(merged), axis=0)
        + full_merge_bias
        + f32(position_rows)
        + lead_rows[:, None] * full_lead
        + full_lead_bias
    )
    start_hat, start_inv = norm_parts(start)
    (normed,) = swap("grp", (low(start_hat * full_first_gain + full_first_shift), "all"))
    normed = normed.reshape(RG, D)
    joint = dot(normed, joint_s, 1, 0)
    shift = jnp.concatenate([joint_shift[0], jnp.zeros((CL,), F32), joint_shift[1]])
    joint = low(joint + shift)

    if direct:
        per = pairs // S
        split = HL // per
        width = per * HDIM

        def to_pairs(x, kinds):
            x = x.reshape(G, R, kinds, split, width).transpose(0, 3, 1, 2, 4)
            (x,) = swap("seq", (x.reshape(S, R, kinds * width), "each"))
            return x.reshape(S * R, kinds, per, HDIM)

        def from_pairs(x, kinds):
            (x,) = swap("seq", (x.reshape(S, R, kinds * width), "each"))
            return (
                x.reshape(G, split, R, kinds, width)
                .transpose(0, 2, 3, 1, 4)
                .reshape(RG, kinds * CL)
            )

        mine = lax.axis_index("seq") // split
        pair_codes = lax.dynamic_index_in_dim(codes, mine, axis=1, keepdims=False).reshape(S * R)
        allowed = allowed_pairs(pair_codes, pair_codes)
        qkv = to_pairs(joint, 3)
        q, k, v = [heads_first(qkv[:, i]) for i in range(3)]
        attended = attend(q, k, v, allowed)
        attended_low = from_pairs(heads_last(low(attended)), 1)
    else:
        heads = joint.reshape(G, R, 3, HL, HDIM).transpose(0, 2, 3, 1, 4)
        everyone = lax.all_gather(heads[:, 1:], "seq", axis=3, tiled=True)
        all_codes = codes.transpose(1, 0, 2).reshape(G, S * R)
        my_codes = lax.dynamic_index_in_dim(codes, lax.axis_index("seq"), 0, keepdims=False)

        def forward_group(item):
            q, kv, query_codes, key_codes = item
            return attend(q, kv[0], kv[1], allowed_pairs(query_codes, key_codes))

        attended = lax.map(forward_group, (heads[:, 0], everyone, my_codes, all_codes))
        attended_low = low(attended).transpose(0, 2, 1, 3).reshape(RG, CL)

    branch = low(dot(attended_low, output_s, 1, 0)).reshape(G, R, D)
    (branch,) = swap("grp", (branch, "each"))
    middle = start + jnp.sum(f32(branch), axis=0) + full_output_bias
    middle_hat, middle_inv = norm_parts(middle)
    (second,) = swap("grp", (low(middle_hat * full_second_gain + full_second_shift), "all"))
    second = second.reshape(RG, D)
    hidden = dot(second, expand_s, 1, 0) + expand_shift
    inner = 0.7978845608028654 * (hidden + 0.044715 * hidden * hidden * hidden)
    bend = jnp.tanh(inner)
    active = low(0.5 * hidden * (1.0 + bend))
    slope = 0.5 * (1.0 + bend) + 0.5 * hidden * (1.0 - bend * bend) * 0.7978845608028654 * (
        1.0 + 3.0 * 0.044715 * hidden * hidden
    )
    reduced = low(dot(active, reduce_s, 1, 0)).reshape(G, R, D)

    grad_active = dot(cot_rows, reduce_s, 1, 1)
    grad_hidden = low(grad_active * slope)
    grad_second = low(dot(grad_hidden, expand_s, 1, 1)).reshape(G, R, D)
    grad_second, reduced = swap("grp", (grad_second, "each"), (reduced, "each"))
    activations = middle + jnp.sum(f32(reduced), axis=0) + full_reduce_bias
    grad_second = jnp.sum(f32(grad_second), axis=0)
    grad_top = f32(cotangent)
    grad_middle = grad_top + norm_back(middle_hat, middle_inv, full_second_gain, grad_second)
    grad_branch = low(grad_middle)

    def scatter_rows(w):
        return lax.psum_scatter(w, "seq", scatter_dimension=0, tiled=True)

    def scatter_mixed(w):
        cols = w.shape[1]
        w = w.reshape(G, S, dn, cols).transpose(1, 0, 2, 3).reshape(S, G * dn * cols // 1024, 1024)
        w = lax.psum_scatter(w, "seq", scatter_dimension=0, tiled=False)
        return w.reshape(G, dn, cols)

    grad_reduce_weight = f32(scatter_rows(low(dot(active, cot_rows, 0, 0))))
    grad_expand_mixed = scatter_mixed(low(dot(second, grad_hidden, 0, 0)))
    grad_expand_bias = low_sums(grad_hidden)

    (grad_branch_rows,) = swap("grp", (grad_branch, "all"))
    grad_branch_rows = grad_branch_rows.reshape(RG, D)
    grad_attended = low(dot(grad_branch_rows, output_s, 1, 1))
    grad_output_weight = f32(scatter_rows(low(dot(attended_low, grad_branch_rows, 0, 0))))
    if direct:
        pushed = heads_first(to_pairs(grad_attended, 1)[:, 0])
        grad_q, grad_k, grad_v = attend_back(q, k, v, allowed, pushed, attended)
        grads = [heads_last(low(x)) for x in (grad_q, grad_k, grad_v)]
        grad_joint = from_pairs(jnp.stack(grads, axis=1), 3)
    else:
        grad_heads = grad_attended.reshape(G, R, HL, HDIM).transpose(0, 2, 1, 3)

        def backward_group(item):
            q, kv, query_codes, key_codes, grad, done = item
            grad_q, grad_k, grad_v = attend_back(
                q, kv[0], kv[1], allowed_pairs(query_codes, key_codes), grad, done
            )
            return grad_q, jnp.stack([grad_k, grad_v], axis=0)

        grad_q, grad_kv = lax.map(
            backward_group,
            (heads[:, 0], everyone, my_codes, all_codes, grad_heads, attended),
        )
        grad_kv = lax.psum_scatter(grad_kv, "seq", scatter_dimension=3, tiled=True)
        grad_joint = low(jnp.concatenate([grad_q[:, None], grad_kv], axis=1))
        grad_joint = grad_joint.transpose(0, 3, 1, 2, 4).reshape(RG, 3 * CL)
    grad_normed = low(dot(grad_joint, joint_s, 1, 1)).reshape(G, R, D)
    (grad_normed,) = swap("grp", (grad_normed, "each"))
    grad_normed = jnp.sum(f32(grad_normed), axis=0)
    grad_joint_mixed = scatter_mixed(low(dot(normed, grad_joint, 0, 0)))
    joint_sums = low_sums(grad_joint)
    grad_start = grad_middle + norm_back(start_hat, start_inv, full_first_gain, grad_normed)
    grad_merged = low(grad_start)

    grad_merged_rows, grad_joint_in, grad_expand_in = swap(
        "grp", (grad_merged, "all"), (grad_joint_mixed, "each"), (grad_expand_mixed, "each")
    )
    grad_joint_weight = f32(
        grad_joint_in.reshape(G, dn, 3, CL).transpose(1, 2, 0, 3).reshape(dn, 3 * D)
    )
    grad_expand_weight = f32(grad_expand_in.transpose(1, 0, 2).reshape(dn, FF))
    grad_merged_rows = grad_merged_rows.reshape(RG, D)
    grad_head = low(dot(grad_merged_rows, merge_s, 1, 1))
    grad_merge_weight = f32(scatter_rows(low(dot(head_low, grad_merged_rows, 0, 0))))
    grad_heads_low = grad_head.reshape(RG, HL, HDIM)
    value_back = jnp.einsum(
        "rhc,hck->hrk", grad_heads_low, value_heads, preferred_element_type=F32
    )
    weighed = value_back * field_wide[None]
    weighed_high = low(weighed)
    weighed_low = low(weighed - f32(weighed_high))
    grad_chosen = jnp.einsum("hrk,kv->hrv", weighed_high, select, preferred_element_type=F32)
    grad_chosen = grad_chosen + jnp.einsum(
        "hrk,kv->hrv", weighed_low, select, preferred_element_type=F32
    )
    grad_scores = low(
        chosen * (grad_chosen - jnp.sum(chosen * grad_chosen, axis=-1, keepdims=True))
    )
    score_spread = jnp.einsum("hrv,kv->hrk", grad_scores, select, preferred_element_type=F32)
    field_part = jnp.sum(spread * value_back + score_spread * probe_table[:, None, :], axis=0)
    field_part = field_part.reshape(G, R, KP)
    score_sums = jnp.sum(score_spread * field_wide[None], axis=1)
    head_sums = jnp.einsum(
        "rhc,hrk->hck", grad_heads_low, mixed, preferred_element_type=F32
    ).reshape(S, dn, KP)

    column_sums = jnp.stack(
        [
            low_sums(grad_merged),
            jnp.sum(lead_rows[:, None] * grad_start, axis=0),
            jnp.sum(grad_start, axis=0),
            jnp.sum(grad_normed * start_hat, axis=0),
            jnp.sum(grad_normed, axis=0),
            low_sums(grad_branch),
            jnp.sum(grad_second * middle_hat, axis=0),
            jnp.sum(grad_second, axis=0),
            jnp.sum(grad_top, axis=0),
        ]
    )
    kinds = column_sums.shape[0]
    column_sums = jnp.pad(column_sums, ((0, -kinds % 16), (0, 0)))
    column_sums = column_sums.reshape(-1, G, CL).transpose(1, 0, 2)
    position_blocks = grad_merged.reshape(R, G, CL).transpose(1, 0, 2)
    column_sums, position_blocks, field_part = swap(
        "grp", (column_sums, "each"), (position_blocks, "each"), (field_part, "each")
    )
    grad_position_table = jnp.sum(f32(position_blocks), axis=0)
    field_grad = jnp.sum(field_part, axis=0)[:, :VP]
    column_sums = jnp.sum(column_sums, axis=0)
    team_sums = jnp.concatenate(
        [
            column_sums[:kinds].reshape(kinds, S, dn).transpose(1, 0, 2).reshape(S, kinds * dn),
            joint_sums[:CL].reshape(S, dn),
            joint_sums[2 * CL :].reshape(S, dn),
            grad_expand_bias.reshape(S, fn),
        ],
        axis=1,
    )
    wide = team_sums.shape[1]
    team_sums = jnp.pad(team_sums, ((0, 0), (0, -wide % 1024))).reshape(S, -1, 128)
    score_sums = jnp.pad(score_sums, ((0, -HL % 8), (0, 0)))
    team_sums, head_sums, score_sums = swap(
        "seq", (team_sums, "each"), (low(head_sums), "each"), (score_sums, "all")
    )
    team_sums = jnp.sum(team_sums, axis=0).reshape(-1)[:wide]
    own_sums = team_sums[: kinds * dn].reshape(kinds, dn)
    grad_joint_bias = team_sums[kinds * dn : (kinds + 2) * dn].reshape(2, dn)
    grad_expand_bias = team_sums[(kinds + 2) * dn :]
    (
        grad_merge_bias,
        grad_lead_weight,
        grad_lead_bias,
        grad_first_gain,
        grad_first_shift,
        grad_output_bias,
        grad_second_gain,
        grad_second_shift,
        grad_reduce_bias,
    ) = [own_sums[i] for i in range(kinds)]
    head_sums = jnp.sum(f32(head_sums), axis=0)
    score_sums = jnp.sum(score_sums, axis=0)
    my_head = lax.axis_index("seq") * dn // HDIM
    my_scores = lax.dynamic_index_in_dim(score_sums, my_head, axis=0, keepdims=False)
    grad_query_vector = jnp.sum(key_own * my_scores[None], axis=1) * SCALE
    (head_all,) = swap("seq", (low(head_sums), "all"))
    head_all, score_all = swap(
        "grp", (head_all.reshape(S * dn, KP), "all"), (score_sums, "all")
    )
    head_all = head_all.reshape(D, KP)
    score_all = score_all[:, :HL].reshape(HEADS, KP)
    grad_value_weight = dot(table, head_all, 0, 1)
    probe_own = low(
        jnp.sum((f32(key_weight) * full_query).reshape(dn, HEADS, HDIM), axis=-1) * SCALE
    )
    grad_table = dot(head_all, value_weight, 0, 1)
    grad_table = grad_table + jnp.einsum("hk,dh->kd", score_all, f32(probe_own))
    grad_probe = jnp.einsum("kd,hk->dh", f32(table), score_all)
    grad_key_weight = (
        grad_probe[:, :, None] * full_query.reshape(HEADS, HDIM)[None] * SCALE
    ).reshape(dn, D)
    grad_patch_weight = grad_table[:VP]
    grad_variable_embed = grad_table[VP : VP + VARS]
    return (
        activations,
        field_grad,
        grad_patch_weight,
        grad_variable_embed,
        grad_query_vector,
        grad_key_weight,
        grad_value_weight,
        grad_merge_weight,
        grad_merge_bias,
        grad_position_table,
        grad_lead_weight,
        grad_lead_bias,
        grad_first_gain,
        grad_first_shift,
        grad_joint_weight,
        grad_joint_bias,
        grad_output_weight,
        grad_output_bias,
        grad_second_gain,
        grad_second_shift,
        grad_expand_weight,
        grad_expand_bias,
        grad_reduce_weight,
        grad_reduce_bias,
    )


TEAM = 4
LINE = 8
ROW = 128
TALL = TEAM * ROW
GROUP = LINE * ROW
WD = D // (TEAM * LINE)
QC = D // TEAM
TEAM_HEADS = HEADS // TEAM
VECTORS = 12
QUERY, MERGE_BIAS, LEAD_WEIGHT, LEAD_BIAS, FIRST_GAIN, FIRST_SHIFT = range(6)
OUTPUT_BIAS, SECOND_GAIN, SECOND_SHIFT, REDUCE_BIAS = range(6, 10)
SUM_ROWS = 24

INPUTS = dict(
    fields=pltpu.VMEM,
    patch=pltpu.VMEM,
    embed=pltpu.VMEM,
    key_w=pltpu.VMEM,
    value_w=pltpu.VMEM,
    pack=pltpu.VMEM,
    steps=pltpu.SMEM,
    cot=pltpu.VMEM,
    position=pl.ANY,
    joint_w=pl.ANY,
    expand_w=pl.ANY,
    merge_w=pl.ANY,
    output_w=pl.ANY,
    reduce_w=pl.ANY,
)

OUTPUTS = dict(
    activations=((ROW, D), F32),
    field_grad=((VP, ROW), F32),
    g_patch=((WD, VP), F32),
    g_embed=((WD, VARS), F32),
    g_key=((WD, D), F32),
    g_value=((WD, D), F32),
    g_merge=((WD, D), F32),
    g_position=((ROW, QC), F32),
    g_joint=((WD, 3 * D), F32),
    g_output=((WD, D), F32),
    g_expand=((WD, FF), F32),
    g_reduce=((ROW, D), F32),
    small=((32, 128), F32),
)

SCRATCH = dict(
    head_all=((TEAM, LINE, WD, KP), BF16),
    score_all=((TEAM, 8, KP), F32),
    score_rows=((16, KP), F32),
    key_own=((WD, KP), F32),
    sums=((SUM_ROWS, QC), F32),
    pe=((WD, KP), BF16),
    field_all=((TEAM, ROW, KP), BF16),
    pos=((ROW, D), BF16),
    cot_all=((TEAM, ROW, D), BF16),
    pack_all=((LINE, TEAM, 32, 128), BF16),
    vecs=((16, D), F32),
    shift_e=((8, D), F32),
    seg_q=((16, GROUP), BF16),
    seg_k=((16, GROUP), BF16),
    merge_s=((LINE, WD, D), BF16),
    output_s=((LINE, WD, D), BF16),
    reduce_s=((LINE, ROW, D), BF16),
    joint_s=((TEAM, LINE, WD, 3 * QC), BF16),
    expand_s=((TEAM, LINE, WD, D), BF16),
    e2_send=((2, LINE, WD, KP), BF16),
    e2_recv=((LINE, 2, WD, KP), BF16),
    pv=((LINE, WD, KP), BF16),
    at=((LINE, 8, KP), F32),
    probe=((8, KP), F32),
    select=((KP, 128), BF16),
    select_t=((128, KP), BF16),
    chosen=((TEAM_HEADS, TALL, 128), F32),
    mixed=((TEAM_HEADS, TALL, KP), BF16),
    head_low=((TALL, QC), BF16),
    start=((ROW, D), F32),
    start_hat=((ROW, D), F32),
    start_inv=((ROW, 128), F32),
    middle=((ROW, D), F32),
    middle_hat=((ROW, D), F32),
    middle_inv=((ROW, 128), F32),
    grad_mid=((ROW, D), F32),
    normed_all=((TEAM, ROW, D), BF16),
    second_all=((TEAM, ROW, D), BF16),
    gb_all=((TEAM, ROW, D), BF16),
    gm_all=((TEAM, ROW, D), BF16),
    pair_send=((LINE, 3, ROW, 128), BF16),
    qkv=((3, GROUP, 128), BF16),
    p_low=((2, GROUP, GROUP), BF16),
    att_f=((GROUP, 128), F32),
    att_low=((GROUP, 128), BF16),
    att_all=((TEAM, ROW, QC), BF16),
    g_send=((TEAM, 2, ROW, 128), BF16),
    go=((GROUP, 128), BF16),
    dk=((GROUP, 128), F32),
    dv=((GROUP, 128), F32),
    d_all=((TEAM, 3, ROW, QC), BF16),
    active_all=((TEAM, ROW, D), BF16),
    gh_all=((TEAM, ROW, D), BF16),
    own_a=((ROW, D), F32),
    own_b=((ROW, D), F32),
    far_a=((ROW, D), F32),
    far_b=((ROW, D), F32),
    gw_merge=((LINE, WD, D), BF16),
    gw_output=((LINE, WD, D), BF16),
    gw_reduce=((LINE, ROW, D), BF16),
    gw_joint=((TEAM, LINE, WD, 3 * QC), BF16),
    gw_expand=((TEAM, LINE, WD, D), BF16),
    yr_merge=((4, WD, D), BF16),
    yr_output=((4, WD, D), BF16),
    yr_reduce=((4, ROW, D), BF16),
    yr_joint=((4, TEAM, WD, 3 * QC), BF16),
    yr_expand=((4, TEAM, WD, D), BF16),
    zr_merge=((3, WD, D), BF16),
    za_merge=((2, WD, D), BF16),
    zr_output=((3, WD, D), BF16),
    za_output=((2, WD, D), BF16),
    zr_reduce=((3, ROW, D), BF16),
    za_reduce=((2, ROW, D), BF16),
    zr_joint=((3, TEAM, WD, 3 * QC), BF16),
    za_joint=((2, TEAM, WD, 3 * QC), BF16),
    zr_expand=((3, TEAM, WD, D), BF16),
    za_expand=((2, TEAM, WD, D), BF16),
    xs_joint=((TEAM, WD, 3 * QC), BF16),
    xs_expand=((TEAM, WD, D), BF16),
    xr_joint=((TEAM, WD, 3 * QC), BF16),
    xr_expand=((TEAM, WD, D), BF16),
    csum=((16, D), F32),
    crecv=((TEAM, 16, QC), F32),
    tsum=((LINE, SUM_ROWS, QC), F32),
    f_own=((TEAM, ROW, KP), F32),
    f_recv=((3, ROW, KP), F32),
    t_send=((LINE, WD, KP), BF16),
    t_recv=((LINE, WD, KP), BF16),
    q_all=((LINE, 8, KP), F32),
)

TEAM_SUMS = dict(
    both=(2 * QC, KP),
    merge=(ROW, D),
    branch=(ROW, D),
    second=(ROW, D),
    reduced=(ROW, D),
    normed=(ROW, D),
)


def team_sum_buffers(shape):
    near = ((2,) + shape, BF16)
    one = (shape, BF16)
    return (near, near, one, one)


SEMAPHORES = 304


def nn(a, b):
    return dot(a, b, 1, 0)


def nt(a, b):
    return dot(a, b, 1, 1)


def tn(a, b):
    return dot(a, b, 0, 0)


def lanes(at, size):
    return pl.ds(pl.multiple_of(at, 128), size)


def rows(at, size):
    return pl.ds(pl.multiple_of(at, size), size)


def fused_kernel(*refs):
    n_in, n_out = len(INPUTS), len(OUTPUTS)
    results = types.SimpleNamespace(**dict(zip(OUTPUTS, refs[n_in : n_in + n_out])))
    names = list(INPUTS) + list(SCRATCH) + list(OUTPUTS)
    rest = refs[:n_in] + refs[n_in + n_out :]
    ref = types.SimpleNamespace(**dict(zip(names, rest)))
    rest = rest[len(names) :]
    send, recv = rest[-2:]
    sums = dict(zip(TEAM_SUMS, [rest[4 * i : 4 * i + 4] for i in range(len(TEAM_SUMS))]))
    sums = types.SimpleNamespace(**sums)
    g = lax.axis_index("grp")
    s = lax.axis_index("seq")
    sib = g + 1 - 2 * lax.rem(g, 2)
    far = lax.rem(g + 2, TEAM)
    diag = lax.rem(sib + 2, TEAM)
    z = s // 2
    y = s - 2 * z
    beside = s + 1 - 2 * y
    mine = lax.rem(3 * z, TEAM)
    is_middle = (z == 1) | (z == 2)
    is_end = (z == 0) | (z == 3)
    partner = s + 2 - 4 * lax.rem(z, 2)
    facing = lax.rem(s + 6 - 4 * z + LINE, LINE)
    near_places = [4 * (z // 2) + y + 2 * i for i in range(2)]
    far_places = [4 * (1 - z // 2) + y + 2 * i for i in range(2)]

    def to_team(j):
        return (j, s)

    def to_line(j):
        return (g, j)

    used = [0]
    begun = []

    def reserve(count):
        at = used[0]
        used[0] += count
        assert used[0] <= SEMAPHORES
        return at

    def remote(src, dst, device, at):
        return pltpu.make_async_remote_copy(
            src_ref=src,
            dst_ref=dst,
            send_sem=send.at[at],
            recv_sem=recv.at[at],
            device_id=device,
            device_id_type=MESH,
        )

    def push(src, dst, device):
        copy = remote(src, dst, device, reserve(1))
        copy.start()
        begun.append(copy)
        return copy

    barrier = pltpu.get_barrier_semaphore()
    for step in range(1, TEAM):
        pl.semaphore_signal(
            barrier, inc=1, device_id=to_team(lax.rem(g + step, TEAM)), device_id_type=MESH
        )
    for step in range(1, LINE):
        pl.semaphore_signal(
            barrier, inc=1, device_id=to_line(lax.rem(s + step, LINE)), device_id_type=MESH
        )

    def spread(buf):
        half = buf.shape[1] // 2
        across = []
        for h in range(2):
            part = buf.at[g, pl.ds(h * half, half)]
            across.append(push(part, part, to_team(far)))
        return push(buf.at[g], buf.at[g], to_team(sib)), across

    def spread_on(buf, across):
        half = buf.shape[1] // 2
        handed = []
        for h in range(2):
            across[h].wait_recv()
            part = buf.at[far, pl.ds(h * half, half)]
            handed.append(push(part, part, to_team(sib)))
        return handed

    def wait_all(copies):
        for copy in copies:
            copy.wait_recv()

    class TeamSum:
        def __init__(self, buffers):
            self.ps, self.r, self.t, self.x = buffers
            self.near_copies = [None, None]

        def near(self, slot, value=None):
            if value is not None:
                self.ps[slot] = low(value)
            self.near_copies[slot] = push(self.ps.at[slot], self.r.at[slot], to_team(sib))

        def across(self, value):
            self.near_copies[1].wait_recv()
            half = self.t.shape[0] // 2
            self.far_copies = []
            for h in range(2):
                part = pl.ds(h * half, half)
                self.t[part] = low(value(part) + f32(self.r[1, part]))
                self.far_copies.append(push(self.t.at[part], self.x.at[part], to_team(far)))

        def total(self, own):
            self.near_copies[0].wait_recv()
            wait_all(self.far_copies)
            return own + f32(self.r[0]) + f32(self.x[...])

    deposits = []

    def deposit(src, dst):
        copy = pltpu.make_async_copy(src, dst, recv.at[reserve(1)])
        copy.start()
        deposits.append(copy)

    def share_line(src, dst):
        return [push(src, dst, to_line(lax.rem(s + step, LINE))) for step in range(1, LINE)]

    def mean(x):
        return jnp.sum(x, axis=-1, keepdims=True) * (1.0 / D)

    class Gather:
        def __init__(self, slot):
            self.slot = slot
            self.at = reserve(9)

        def send(self, place, device, i, shard=None):
            part = self.slot(place)
            remote(part if shard is None else shard, part, device, self.at + i).start()

        def come(self, i):
            part = self.slot(s)
            remote(part, part, to_line(beside), self.at + i).wait_recv()

        def stage1(self, shard=None):
            self.send(s, to_line(partner), 0, shard)
            self.send(s, to_line(beside), 1, shard)

        def stage2(self):
            self.come(0)

            @pl.when(is_middle)
            def _():
                for i in range(2):
                    self.send(near_places[i], to_line(facing), 2 + i)

            self.send(partner, to_line(beside), 4)

        def stage3(self):
            @pl.when(is_middle)
            def _():
                for i in range(2):
                    self.come(2 + i)
                    self.send(far_places[i], to_line(partner), 5 + i)
                    self.send(far_places[i], to_line(beside), 7 + i)

        def stage4(self):
            @pl.when(is_end)
            def _():
                for i in range(2):
                    self.come(5 + i)
                    self.send(far_places[i], to_line(beside), 7 + i)

        def finish(self):
            for i in (1, 4, 7, 8):
                self.come(i)

        def sent(self):
            part = self.slot(s)

            def gone(i):
                remote(part, part, to_line(beside), self.at + i).wait_send()

            for i in (0, 1, 4, 7, 8):
                gone(i)

            @pl.when(is_middle)
            def _():
                for i in (2, 3, 5, 6):
                    gone(i)

    pe = ref.pe
    pe[:, 0:VP] = ref.patch[...]
    pe[:, VP : VP + VARS] = ref.embed[...]
    pe[:, VP + VARS :] = jnp.zeros((WD, KP - VP - VARS), BF16)
    field_all, cot_all, pack_all = ref.field_all, ref.cot_all, ref.pack_all
    field_all[g, :, 0:VP] = ref.fields[...].T
    lane = lax.broadcasted_iota(jnp.int32, (ROW, KP - VP), 1)
    field_all[g, :, VP:] = (lane < VARS).astype(BF16)
    cot_all[g] = ref.cot[...]
    pack_all[s, g] = ref.pack[...]
    pl.semaphore_wait(barrier, TEAM - 1 + LINE - 1)

    both = TeamSum(sums.both)

    def table_product(weight, j):
        return tn(weight[:, lanes(j * QC, QC)], pe[...])

    for slot, j in ((1, diag), (0, sib)):
        both.ps[slot, 0:QC] = low(table_product(ref.value_w, j))
        both.ps[slot, QC:] = low(table_product(ref.key_w, j))
        both.near(slot)
    field_copies = spread(field_all)
    far_parts = [table_product(ref.value_w, far), table_product(ref.key_w, far)]
    both.across(lambda part: far_parts[0] if part.start == 0 else far_parts[1])
    own_parts = [table_product(ref.value_w, g), table_product(ref.key_w, g)]
    pack_copies = [
        push(pack_all.at[s, g], pack_all.at[s, g], to_team(j)) for j in (far, diag, sib)
    ]

    def whole(buf):
        return lambda i: buf.at[i]

    def inner(buf):
        return lambda i: buf.at[:, i]

    gather_merge = Gather(whole(ref.merge_s))
    gather_output = Gather(whole(ref.output_s))
    gather_reduce = Gather(whole(ref.reduce_s))
    gather_joint = Gather(inner(ref.joint_s))
    gather_expand = Gather(inner(ref.expand_s))
    local = []

    def keep(src, dst):
        copy = pltpu.make_async_copy(src, dst, recv.at[reserve(1)])
        copy.start()
        local.append(copy)

    keep(ref.merge_w, ref.merge_s.at[s])
    keep(ref.output_w, ref.output_s.at[s])
    keep(ref.reduce_w, ref.reduce_s.at[s])
    gather_merge.stage1(ref.merge_w)
    gather_output.stage1(ref.output_w)
    gather_reduce.stage1(ref.reduce_w)

    joint_copies, expand_copies = [], []
    for j in (far, diag, sib):
        for kind in range(3):
            joint_copies.append(
                push(
                    ref.joint_w.at[:, lanes(kind * D + j * QC, QC)],
                    ref.joint_s.at[g, s, :, pl.ds(kind * QC, QC)],
                    to_team(j),
                )
            )
    for kind in range(3):
        keep(
            ref.joint_w.at[:, lanes(kind * D + g * QC, QC)],
            ref.joint_s.at[g, s, :, pl.ds(kind * QC, QC)],
        )
    for j in (far, diag, sib):
        expand_copies.append(
            push(ref.expand_w.at[:, lanes(j * D, D)], ref.expand_s.at[g, s], to_team(j))
        )
    keep(ref.expand_w.at[:, lanes(g * D, D)], ref.expand_s.at[g, s])
    keep(ref.position, ref.pos.at[:, lanes(g * QC, QC)])
    position_copies = [
        push(ref.position, ref.pos.at[:, lanes(g * QC, QC)], to_team(j))
        for j in (far, diag, sib)
    ]

    both.near_copies[0].wait_recv()
    wait_all(both.far_copies)
    for part in range(2):
        block = pl.ds(part * QC, QC)
        total = own_parts[part] + f32(both.r[0, block]) + f32(both.x[block])
        ref.e2_send[part] = low(total).reshape(LINE, WD, KP)
    e2_send, e2_recv = ref.e2_send, ref.e2_recv
    e2_copies = []
    for step in range(1, LINE):
        to = lax.rem(s + step, LINE)
        e2_copies.append(push(e2_send.at[:, to], e2_recv.at[s], to_line(to)))
    e2_recv[s] = e2_send[:, s]
    for copy in local:
        copy.wait()
    gather_merge.stage2()
    gather_output.stage2()
    wait_all(joint_copies)
    gather_joint.stage1()

    wait_all(e2_copies)
    table_own = jnp.sum(f32(e2_recv[...]), axis=0)
    key_own = table_own[1]
    ref.key_own[...] = key_own
    query = f32(pack_all[s, g])[0:1, 0:WD]
    key_high = low(key_own)
    key_rest = low(key_own - f32(key_high))
    query_rows = low(jnp.broadcast_to(query, (16, WD)))
    probe_part = (nn(query_rows, key_high) + nn(query_rows, key_rest)) * SCALE
    pv, at = ref.pv, ref.at
    pv[s] = low(table_own[0])
    at[s] = probe_part[0:8]
    pv_copies = share_line(pv.at[s], pv.at[s])
    at_copies = share_line(at.at[s], at.at[s])
    gather_merge.stage3()
    gather_output.stage3()
    wait_all(pv_copies)
    wait_all(at_copies)
    gather_joint.stage2()
    wait_all(pack_copies)
    pack_line = share_line(pack_all.at[s], pack_all.at[s])
    gather_merge.stage4()
    gather_reduce.stage2()

    probe = ref.probe
    for h in range(TEAM_HEADS):
        probe[h : h + 1] = at[2 * h, 0:1] + at[2 * h + 1, 0:1]
    probe[TEAM_HEADS:] = jnp.zeros((8 - TEAM_HEADS, KP), F32)

    def owner_of(k):
        return jnp.where(k < VP, k // PIX, jnp.where(k < VP + VARS, k - VP, VARS + 64))

    select, select_t = ref.select, ref.select_t
    select[...] = (
        owner_of(lax.broadcasted_iota(jnp.int32, (KP, 128), 0))
        == lax.broadcasted_iota(jnp.int32, (KP, 128), 1)
    ).astype(BF16)
    select_t[...] = (
        owner_of(lax.broadcasted_iota(jnp.int32, (128, KP), 1))
        == lax.broadcasted_iota(jnp.int32, (128, KP), 0)
    ).astype(BF16)
    valid = lax.broadcasted_iota(jnp.int32, (1, 128), 1) < VARS
    head_of_lane = lax.broadcasted_iota(jnp.int32, (1, QC), 1) // HDIM

    field_handed = spread_on(field_all, field_copies[1])
    field_copies[0].wait_recv()
    wait_all(field_handed)

    def tall(buf):
        return buf[...].reshape(TALL, -1)

    def split_dot(x, b):
        high = low(x)
        return nn(high, b) + nn(low(x - f32(high)), b)

    chosen, mixed, head_low = ref.chosen, ref.mixed, ref.head_low

    def choose(h):
        field = f32(tall(field_all))
        scores = split_dot(field * probe[h : h + 1], select[...])
        scores = jnp.where(valid, scores, MASKED)
        terms = jnp.exp(scores - jnp.max(scores, axis=-1, keepdims=True))
        weights = terms * (1.0 / jnp.sum(terms, axis=-1, keepdims=True))
        chosen[h] = weights
        mix = low(nn(low(weights), select_t[...]) * field)
        mixed[h] = mix
        table_value = pv[2 * h : 2 * h + 2].reshape(HDIM, KP)
        head_low[:, h * HDIM : (h + 1) * HDIM] = low(nt(mix, table_value))

    for h in range(TEAM_HEADS):
        choose(h)
        if h == 1:
            gather_joint.stage3()
            wait_all(expand_copies)
            gather_expand.stage1()

    merge_s, output_s = ref.merge_s, ref.output_s
    gather_output.stage4()
    gather_merge.finish()
    merge = TeamSum(sums.merge)

    def row_weight(buf):
        return buf[...].reshape(-1, D)

    def two(buf, i, j):
        return jnp.concatenate([buf[i], buf[j]], axis=0)

    def merge_part(j):
        return nn(head_low[rows(j * ROW, ROW)], row_weight(merge_s))

    merge.near(1, merge_part(diag))
    merge.near(0, merge_part(sib))
    ref.far_a[...] = merge_part(far)
    merge.across(lambda part: ref.far_a[part])
    ref.own_a[...] = merge_part(g)

    wait_all(pack_line)
    vecs, shift_e = ref.vecs, ref.shift_e
    place = (
        (lax.broadcasted_iota(jnp.int32, (128, QC), 1) % WD)
        == lax.broadcasted_iota(jnp.int32, (128, QC), 0)
    ).astype(BF16)
    lane_piece = lax.broadcasted_iota(jnp.int32, (LINE, 1, QC), 2) // WD
    piece = lax.broadcasted_iota(jnp.int32, (LINE, 1, QC), 0)
    for j in range(TEAM):
        spreadout = nn(pack_all[:, j, 0:16, :].reshape(LINE * 16, 128), place)
        spreadout = jnp.where(lane_piece == piece, spreadout.reshape(LINE, 16, QC), 0.0)
        vecs[:, j * QC : (j + 1) * QC] = jnp.sum(spreadout, axis=0)

    def vector(i):
        return vecs[i : i + 1, :]

    joint_shift = vecs[10:12, lanes(g * QC, QC)]
    seg_q, seg_k = ref.seg_q, ref.seg_k
    sub = lax.broadcasted_iota(jnp.int32, (16, 128), 0).astype(F32)
    for j in range(LINE):
        part = f32(pack_all[j, g])
        shift_e[:, j * 128 : (j + 1) * 128] = jnp.broadcast_to(part[16:17], (8, 128))
        part = f32(pack_all[j, mine])
        same = jnp.where(sub == part[17:18], 1.0, 0.0)
        seg_q[:, j * 128 : (j + 1) * 128] = low(same)
        seg_k[:, j * 128 : (j + 1) * 128] = low(same * part[18:19])
    own_seg = f32(ref.pack[...])[17:18]
    steps = ref.steps
    lead_lanes = jnp.zeros((1, 128), F32)
    for i in range(steps.shape[1]):
        lead_lanes = jnp.where(own_seg == i, LEAD_UNIT * steps[0, i].astype(F32), lead_lanes)
    lead = jnp.broadcast_to(lead_lanes, (ROW, 128)).T[:, 0:1]
    wait_all(position_copies)

    start_ref = ref.start
    start_ref[...] = (
        merge.total(ref.own_a[...])
        + vector(MERGE_BIAS)
        + f32(ref.pos[...])
        + lead * vector(LEAD_WEIGHT)
        + vector(LEAD_BIAS)
    )

    def norm(x, hat_ref, inv_ref, gain, shift):
        center = x - mean(x)
        inverse = lax.rsqrt(mean(center * center) + EPSILON)
        hat = center * inverse
        hat_ref[...] = hat
        inv_ref[...] = jnp.broadcast_to(inverse, (ROW, 128))
        return low(hat * gain + shift)

    def norm_back_ref(grad, hat_ref, inv_ref, gain):
        f = grad * gain
        hat = hat_ref[...]
        return inv_ref[:, 0:1] * (f - mean(f) - hat * mean(f * hat))

    normed_all = ref.normed_all
    normed_all[g] = norm(
        start_ref[...],
        ref.start_hat,
        ref.start_inv,
        vector(FIRST_GAIN),
        vector(FIRST_SHIFT),
    )
    normed_copies = spread(normed_all)
    joint_s, pair_send, qkv = ref.joint_s, ref.pair_send, ref.qkv
    gather_joint.stage4()
    gather_reduce.stage3()
    gather_expand.stage2()
    gather_joint.finish()
    e6 = reserve(LINE)

    def pair_place(j, t):
        return 2 * lax.rem(3 * j, TEAM) + t

    def to_pair(src, dst, base, j, t):
        there = pair_place(j, t)
        index = base + lax.rem(there - s + LINE, LINE)

        @pl.when(there != s)
        def _():
            remote(src, dst, to_line(there), index).start()

        @pl.when(there == s)
        def _():
            pltpu.make_async_copy(src, dst, recv.at[index]).start()

    def pairs_done(src, dst, base):
        pltpu.make_async_copy(src, dst, recv.at[base]).wait()
        for step in range(1, LINE):
            copy = remote(src, dst, to_line(lax.rem(s + step, LINE)), base + step)
            copy.wait_recv()
            copy.wait_send()

    line_rows = rows(s * ROW, ROW)

    def joint_rows(i, j):
        block = two(normed_all, i, j)
        for kind in range(3):
            weight = joint_s[:, :, :, kind * QC : (kind + 1) * QC].reshape(D, QC)
            part = nn(block, weight)
            if kind != 1:
                part = part + joint_shift[kind // 2 : kind // 2 + 1]
            part = low(part)
            for n, group in enumerate((i, j)):
                for t in range(2):
                    pair_send[2 * group + t, kind] = part[
                        n * ROW : (n + 1) * ROW, t * 128 : (t + 1) * 128
                    ]
        for group in (i, j):
            for t in range(2):
                to_pair(pair_send.at[2 * group + t], qkv.at[:, line_rows, :], e6, group, t)

    normed_copies[0].wait_recv()
    joint_rows(g, sib)
    normed_handed = spread_on(normed_all, normed_copies[1])
    wait_all(normed_handed)
    joint_rows(far, diag)
    pairs_done(pair_send.at[0], qkv.at[:, line_rows, :], e6)
    gather_reduce.stage4()
    gather_expand.stage3()
    cot_copies = spread(cot_all)

    half_of_lane = lax.broadcasted_iota(jnp.int32, (1, 128), 1) // HDIM
    p_low, att_f, att_low, att_all = ref.p_low, ref.att_f, ref.att_low, ref.att_all
    e7 = reserve(LINE)
    pair_lanes = lanes(y * 128, 128)

    def attend_rows(b, carry):
        here = rows(b * 256, 256)
        queries = f32(qkv[0, here, :]) * SCALE
        keys, values = qkv[1], qkv[2]
        allowed = tn(seg_q[:, lanes(b * 256, 256)], seg_k[...]) > 0.5
        outs = []
        for t in range(2):
            scores = nt(low(jnp.where(half_of_lane == t, queries, 0.0)), keys)
            scores = jnp.where(allowed, scores, MASKED)
            terms = jnp.exp(scores - jnp.max(scores, axis=-1, keepdims=True))
            weights = low(terms * (1.0 / jnp.sum(terms, axis=-1, keepdims=True)))
            p_low[t, here, :] = weights
            outs.append(nn(weights, values))
        out = jnp.where(half_of_lane == 0, outs[0], outs[1])
        att_f[here] = out
        att_low[here] = low(out)
        for t in range(2):
            there = 2 * b + t
            index = e7 + lax.rem(there - s + LINE, LINE)
            src = att_low.at[rows(there * ROW, ROW)]
            dst = att_all.at[mine, :, pair_lanes]

            @pl.when(there != s)
            def _():
                remote(src, dst, to_line(there), index).start()

            @pl.when(there == s)
            def _():
                pltpu.make_async_copy(src, dst, recv.at[index]).start()

        return carry

    lax.fori_loop(0, GROUP // 256, attend_rows, 0)
    gather_output.finish()
    pairs_done(att_low.at[pl.ds(0, ROW)], att_all.at[mine, :, pair_lanes], e7)

    gather_expand.stage4()
    branch = TeamSum(sums.branch)

    def branch_part(j):
        return nn(att_all[j], row_weight(output_s))

    branch.near(1, branch_part(diag))
    branch.near(0, branch_part(sib))
    ref.far_a[...] = branch_part(far)
    branch.across(lambda part: ref.far_a[part])
    ref.own_a[...] = branch_part(g)
    cot_handed = spread_on(cot_all, cot_copies[1])
    middle_ref = ref.middle
    middle_ref[...] = branch.total(ref.own_a[...]) + start_ref[...] + vector(OUTPUT_BIAS)

    second_all = ref.second_all
    second_all[g] = norm(
        middle_ref[...],
        ref.middle_hat,
        ref.middle_inv,
        vector(SECOND_GAIN),
        vector(SECOND_SHIFT),
    )
    second_copies = spread(second_all)
    gather_expand.finish()
    gather_reduce.finish()
    cot_copies[0].wait_recv()
    wait_all(cot_handed)
    expand_s, reduce_s = ref.expand_s, ref.reduce_s
    active_all, gh_all = ref.active_all, ref.gh_all
    root = 0.7978845608028654

    def feed(j, k, acc_a, acc_b):
        def tile(i, carry):
            here = lanes(i * 256, 256)
            up = expand_s[:, :, :, here].reshape(D, 256)
            down = reduce_s[pl.ds(2 * i, 2)].reshape(256, D)
            hidden = nn(two(second_all, j, k), up) + shift_e[0:1, here]
            square = hidden * hidden
            bend = jnp.tanh(root * hidden * (1.0 + 0.044715 * square))
            active = low(0.5 * hidden * (1.0 + bend))
            slope = 0.5 * (1.0 + bend) + (0.5 * root) * hidden * (1.0 - bend * bend) * (
                1.0 + (3.0 * 0.044715) * square
            )
            grad = low(nt(two(cot_all, j, k), down) * slope)
            for n, block in enumerate((j, k)):
                active_all[block, :, here] = active[n * ROW : (n + 1) * ROW]
                gh_all[block, :, here] = grad[n * ROW : (n + 1) * ROW]
            for part, acc in ((nt(grad, up), acc_a), (nn(active, down), acc_b)):
                for n in range(2):
                    rows_of = part[n * ROW : (n + 1) * ROW]

                    @pl.when(i == 0)
                    def _():
                        acc[n][...] = rows_of

                    @pl.when(i > 0)
                    def _():
                        acc[n][...] += rows_of

            return carry

        lax.fori_loop(0, FF // TEAM // 256, tile, 0)

    second = TeamSum(sums.second)
    reduced = TeamSum(sums.reduced)
    own_a, own_b, far_a, far_b = ref.own_a, ref.own_b, ref.far_a, ref.far_b
    spare_a, spare_b = ref.grad_mid, ref.activations
    second_copies[0].wait_recv()
    feed(g, sib, (own_a, spare_a), (own_b, spare_b))
    second.near(0, spare_a[...])
    reduced.ps[0] = low(spare_b[...])
    second_handed = spread_on(second_all, second_copies[1])
    wait_all(second_handed)
    feed(far, diag, (far_a, spare_a), (far_b, spare_b))
    second.near(1, spare_a[...])
    reduced.ps[1] = low(spare_b[...])
    second.across(lambda part: far_a[part])
    reduced.near(0)
    reduced.near(1)

    class LineSum:
        def __init__(self, gw, yr, zr, za):
            self.gw, self.yr, self.zr, self.za = gw, yr, zr, za
            self.slot = whole(gw) if len(gw.shape) == 3 else inner(gw)
            self.at = reserve(6)

        def send(self, src, dst, device, i):
            remote(src, dst, device, self.at + i).start()

        def come(self, i):
            part = self.zr.at[0]
            remote(part, part, to_line(beside), self.at + i).wait_recv()

        def along_y(self):
            self.y_copies = [
                push(self.slot(2 * i + 1 - y), self.yr.at[i], to_line(beside)) for i in range(4)
            ]

        def sum_y(self):
            wait_all(self.y_copies)

            def add(i, carry):
                block = self.slot(2 * i + y)
                block[...] = low(f32(block[...]) + f32(self.yr[i]))
                return carry

            lax.fori_loop(0, 4, add, 0)

        def stage1(self):
            @pl.when(is_end)
            def _():
                for i, place in enumerate(far_places + [partner]):
                    self.send(self.slot(place), self.zr.at[i], to_line(partner), i)

        def stage2(self):
            @pl.when(is_middle)
            def _():
                for i, place in enumerate(far_places):
                    self.come(i)
                    block = self.slot(place)
                    block[...] = low(f32(block[...]) + f32(self.zr[i]))
                    self.send(block, self.za.at[i], to_line(facing), 3 + i)

        def stage3(self):
            @pl.when(is_middle)
            def _():
                for i in range(2):
                    self.come(3 + i)
                block = self.slot(partner)
                block[...] = low(f32(block[...]) + f32(self.za[1 - lax.rem(z, 2)]))
                self.send(block, self.zr.at[0], to_line(partner), 5)

        def total(self, out):
            own = f32(self.slot(s)[...])

            @pl.when(is_middle)
            def _():
                self.come(2)
                total = own + f32(self.zr[2]) + f32(self.za[lax.rem(z, 2)])
                out[...] = total.astype(out.dtype)

            @pl.when(is_end)
            def _():
                self.come(5)
                out[...] = (own + f32(self.zr[0])).astype(out.dtype)

        def sent(self):
            part = self.zr.at[0]

            def gone(i):
                remote(part, part, to_line(beside), self.at + i).wait_send()

            @pl.when(is_middle)
            def _():
                for i in (3, 4, 5):
                    gone(i)

            @pl.when(is_end)
            def _():
                for i in range(3):
                    gone(i)

    reduce_sum = LineSum(ref.gw_reduce, ref.yr_reduce, ref.zr_reduce, ref.za_reduce)
    expand_sum = LineSum(ref.gw_expand, ref.yr_expand, ref.zr_expand, ref.za_expand)
    output_sum = LineSum(ref.gw_output, ref.yr_output, ref.zr_output, ref.za_output)
    joint_sum = LineSum(ref.gw_joint, ref.yr_joint, ref.zr_joint, ref.za_joint)
    merge_sum = LineSum(ref.gw_merge, ref.yr_merge, ref.zr_merge, ref.za_merge)

    gw_reduce = ref.gw_reduce

    def reduce_block(j):
        lhs = active_all[:, :, lanes(j * ROW, ROW)].reshape(TALL, ROW)
        gw_reduce[j] = low(tn(lhs, tall(cot_all)))

    def reduce_beside(i, carry):
        reduce_block(2 * i + 1 - y)
        return carry

    def reduce_here(i, carry):
        reduce_block(2 * i + y)
        return carry

    lax.fori_loop(0, 4, reduce_beside, 0)
    reduce_sum.along_y()

    csum = ref.csum

    def note(i, value):
        csum[i : i + 1] = jnp.sum(value, axis=0, keepdims=True)

    grad_second = second.total(own_a[...])
    grad_mid = ref.grad_mid
    note(6, grad_second * ref.middle_hat[...])
    note(7, grad_second)
    grad_top = f32(ref.cot[...])
    note(8, grad_top)
    grad_mid[...] = grad_top + norm_back_ref(
        grad_second, ref.middle_hat, ref.middle_inv, vector(SECOND_GAIN)
    )
    gb_all = ref.gb_all
    gb_all[g] = low(grad_mid[...])
    gb_copies = spread(gb_all)
    note(5, f32(gb_all[g]))
    lax.fori_loop(0, 4, reduce_here, 0)
    gw_expand = ref.gw_expand

    def expand_block(i, carry):
        lhs = second_all[:, :, lanes(i * QC, QC)].reshape(TALL, QC)
        gw_expand[i] = low(tn(lhs, tall(gh_all))).reshape(LINE, WD, D)
        return carry

    e12 = reserve(LINE)
    g_send, go = ref.g_send, ref.go

    def attended_back(i, j):
        part = low(nt(two(gb_all, i, j), row_weight(output_s)))
        for n, group in enumerate((i, j)):
            for t in range(2):
                g_send[group, t] = part[n * ROW : (n + 1) * ROW, t * 128 : (t + 1) * 128]
                to_pair(g_send.at[group, t], go.at[line_rows, :], e12, group, t)

    gb_copies[0].wait_recv()
    attended_back(g, sib)
    lax.fori_loop(0, 2, expand_block, 0)
    gb_handed = spread_on(gb_all, gb_copies[1])
    wait_all(gb_handed)
    attended_back(far, diag)
    reduced.across(lambda part: far_b[part])
    lax.fori_loop(2, 4, expand_block, 0)
    gw_output = ref.gw_output
    gw_output[...] = low(tn(tall(att_all), tall(gb_all))).reshape(LINE, WD, D)
    reduce_sum.sum_y()
    expand_sum.along_y()
    reduce_sum.stage1()
    pairs_done(g_send.at[0, 0], go.at[line_rows, :], e12)

    dk, dv, d_all = ref.dk, ref.dv, ref.d_all
    dk[...] = jnp.zeros_like(dk)
    dv[...] = jnp.zeros_like(dv)
    e13 = reserve(LINE)

    def attend_back_rows(b, carry):
        here = rows(b * 256, 256)
        queries = qkv[0, here, :]
        keys, values = qkv[1], qkv[2]
        grad = go[here]
        products = f32(grad) * att_f[here]
        outs = []
        for t in range(2):
            mine_lanes = half_of_lane == t
            offset = jnp.sum(jnp.where(mine_lanes, products, 0.0), axis=-1, keepdims=True)
            grad_t = low(jnp.where(mine_lanes, f32(grad), 0.0))
            query_t = low(jnp.where(mine_lanes, f32(queries), 0.0))
            weights = p_low[t, here, :]
            slopes = low(low(f32(weights) * (nt(grad_t, values) - offset)) * SCALE)
            outs.append(nn(slopes, keys))
            dk[...] += tn(slopes, query_t)
            dv[...] += tn(weights, grad_t)
        grad_queries = low(jnp.where(half_of_lane == 0, outs[0], outs[1]))
        pair_send[pl.ds(2 * b, 2), 0] = grad_queries.reshape(2, ROW, 128)
        for t in range(2):
            there = 2 * b + t
            index = e13 + lax.rem(there - s + LINE, LINE)
            src = pair_send.at[there, 0]
            dst = d_all.at[mine, 0, :, pair_lanes]

            @pl.when(there != s)
            def _():
                remote(src, dst, to_line(there), index).start()

            @pl.when(there == s)
            def _():
                pltpu.make_async_copy(src, dst, recv.at[index]).start()

        return carry

    lax.fori_loop(0, GROUP // 256, attend_back_rows, 0)
    pair_send[:, 1] = low(dk[...]).reshape(LINE, ROW, 128)
    pair_send[:, 2] = low(dv[...]).reshape(LINE, ROW, 128)
    d_copies = []
    d_dst = d_all.at[mine, pl.ds(1, 2), :, pair_lanes]
    for step in range(1, LINE):
        there = lax.rem(s + step, LINE)
        d_copies.append(push(pair_send.at[there, pl.ds(1, 2)], d_dst, to_line(there)))
    d_here = pltpu.make_async_copy(
        pair_send.at[s, pl.ds(1, 2)], d_dst, recv.at[reserve(1)]
    )
    d_here.start()
    d_here.wait()
    wait_all(d_copies)
    pairs_done(pair_send.at[0, 0], d_all.at[mine, 0, :, pair_lanes], e13)
    output_sum.along_y()
    reduce_sum.stage2()

    normed = TeamSum(sums.normed)

    def joint_back(j):
        total = None
        for kind in range(3):
            weight = joint_s[:, :, :, kind * QC : (kind + 1) * QC].reshape(D, QC)
            part = nt(d_all[j, kind], weight)
            total = part if total is None else total + part
        return total

    normed.near(1, joint_back(diag))
    normed.near(0, joint_back(sib))
    far_a[...] = joint_back(far)
    normed.across(lambda part: far_a[part])
    own_a[...] = joint_back(g)
    gw_joint = ref.gw_joint
    tsum = ref.tsum
    for kind in range(3):
        block = d_all[:, kind].reshape(TALL, QC)
        for i in range(TEAM):
            lhs = normed_all[:, :, i * QC : (i + 1) * QC].reshape(TALL, QC)
            part = low(tn(lhs, block)).reshape(LINE, WD, QC)
            gw_joint[i, :, :, kind * QC : (kind + 1) * QC] = part
        if kind != 1:
            row = 16 + kind // 2
            tsum[s, row : row + 1] = jnp.sum(f32(block), axis=0, keepdims=True)
    joint_sum.along_y()
    expand_sum.sum_y()
    expand_sum.stage1()
    hidden_sums = jnp.sum(f32(tall(gh_all)), axis=0, keepdims=True)
    for i in range(4):
        tsum[s, 18 + i : 19 + i] = hidden_sums[:, i * QC : (i + 1) * QC]
    tsum[s, 22:24] = jnp.zeros((2, QC), F32)

    grad_normed = normed.total(own_a[...])
    note(3, grad_normed * ref.start_hat[...])
    note(4, grad_normed)
    grad_start = grad_mid[...] + norm_back_ref(
        grad_normed, ref.start_hat, ref.start_inv, vector(FIRST_GAIN)
    )
    gm_all = ref.gm_all
    gm_all[g] = low(grad_start)
    gm_copies = spread(gm_all)
    note(0, f32(gm_all[g]))
    note(1, lead * grad_start)
    note(2, grad_start)
    csum[9:16] = jnp.zeros((7, D), F32)
    crecv = ref.crecv
    crecv[g] = csum[:, lanes(g * QC, QC)]
    c_copies = [
        push(csum.at[:, lanes(j * QC, QC)], crecv.at[g], to_team(j)) for j in (far, diag, sib)
    ]
    ref.activations[...] = (
        reduced.total(own_b[...]) + middle_ref[...] + vector(REDUCE_BIAS)
    )
    deposit(ref.activations, results.activations)
    output_sum.sum_y()
    output_sum.stage1()
    reduce_sum.stage3()
    gm_handed = spread_on(gm_all, gm_copies[1])
    gm_copies[0].wait_recv()
    wait_all(gm_handed)

    gw_merge = ref.gw_merge
    f_own = ref.f_own
    t_send = ref.t_send
    q_all = ref.q_all
    grad_heads = low(nt(tall(gm_all), row_weight(merge_s)))
    head_grad = ref.att_all
    head_grad[...] = grad_heads.reshape(TEAM, ROW, QC)
    q_all[s] = jnp.zeros((8, KP), F32)

    def choose_back(h):
        field = f32(tall(field_all))
        grad_h = low(jnp.where(head_of_lane == h, f32(tall(head_grad)), 0.0))
        value_back = nn(grad_h, pv[...].reshape(QC, KP))
        grad_chosen = split_dot(value_back * field, select[...])
        weights = chosen[h]
        shifted = grad_chosen - jnp.sum(weights * grad_chosen, axis=-1, keepdims=True)
        score_spread = nn(low(weights * shifted), select_t[...])
        field_part = nn(low(weights), select_t[...]) * value_back + score_spread * probe[h : h + 1]
        field_part = field_part.reshape(TEAM, ROW, KP)
        if h == 0:
            f_own[...] = field_part
        else:
            f_own[...] += field_part
        q_all[s, h : h + 1] = jnp.sum(score_spread * field, axis=0, keepdims=True)

    for h in range(TEAM_HEADS):
        choose_back(h)
        if h == 0:
            expand_sum.stage2()
        if h == 2:
            joint_sum.sum_y()
            joint_sum.stage1()
    for h in range(TEAM_HEADS):
        pair = tall(head_grad)[:, (h // 2) * 128 : (h // 2 + 1) * 128]
        part = tn(pair, mixed[h])
        at_row = (h % 2) * HDIM
        t_send[2 * h : 2 * h + 2] = low(part[at_row : at_row + HDIM]).reshape(2, WD, KP)

    t_recv = ref.t_recv
    t_copies = []
    for step in range(1, LINE):
        there = lax.rem(s + step, LINE)
        t_copies.append(push(t_send.at[there], t_recv.at[s], to_line(there)))
    t_recv[s] = t_send[s]
    q_copies = share_line(q_all.at[s], q_all.at[s])
    gw_merge[...] = low(tn(head_low[...], tall(gm_all))).reshape(LINE, WD, D)
    merge_sum.along_y()
    f_recv = ref.f_recv
    f_copies = []
    for step in range(1, TEAM):
        j = lax.rem(g + step, TEAM)
        f_copies.append(push(f_own.at[j], f_recv.at[step - 1], to_team(j)))
    output_sum.stage2()
    wait_all(c_copies)
    tsum[s, 0:16] = jnp.sum(crecv[...], axis=0)
    s_copies = share_line(tsum.at[s], tsum.at[s])
    position = jnp.zeros((ROW, QC), F32)
    for j in range(TEAM):
        position += f32(gm_all[j, :, lanes(g * QC, QC)])
    ref.g_position[...] = position
    deposit(ref.g_position, results.g_position)

    wait_all(t_copies)
    head_all, score_all = ref.head_all, ref.score_all
    head_all[g, s] = low(jnp.sum(f32(t_recv[...]), axis=0))
    h_copies = share_line(head_all.at[g, s], head_all.at[g, s])
    wait_all(q_copies)
    score_all[g] = jnp.sum(q_all[...], axis=0)
    score_copies = [push(score_all.at[g], score_all.at[g], to_team(j)) for j in (far, diag, sib)]
    merge_sum.sum_y()
    merge_sum.stage1()
    expand_sum.stage3()
    output_sum.stage3()
    joint_sum.stage2()
    merge_sum.stage2()

    xs_joint, xs_expand = ref.xs_joint, ref.xs_expand
    xr_joint, xr_expand = ref.xr_joint, ref.xr_expand
    expand_sum.total(xs_expand)
    x_copies = []
    for j in (far, diag, sib):
        x_copies.append(push(xs_expand.at[j], xr_expand.at[g], to_team(j)))
    xr_expand[g] = xs_expand[g]
    joint_sum.stage3()
    merge_sum.stage3()
    joint_sum.total(xs_joint)
    for j in (far, diag, sib):
        x_copies.append(push(xs_joint.at[j], xr_joint.at[g], to_team(j)))
    xr_joint[g] = xs_joint[g]
    wait_all(h_copies)
    h_spread = spread(head_all)
    reduce_sum.total(ref.g_reduce)
    deposit(ref.g_reduce, results.g_reduce)
    output_sum.total(ref.g_output)
    deposit(ref.g_output, results.g_output)
    wait_all(f_copies)
    ref.field_grad[...] = (f_own[g] + f_recv[0] + f_recv[1] + f_recv[2]).T[0:VP]
    deposit(ref.field_grad, results.field_grad)
    wait_all(s_copies)
    ref.sums[...] = jnp.sum(tsum[...], axis=0)
    h_handed = spread_on(head_all, h_spread[1])
    merge_sum.total(ref.g_merge)
    deposit(ref.g_merge, results.g_merge)
    wait_all(x_copies)
    for j in range(TEAM):
        ref.g_expand[:, j * D : (j + 1) * D] = f32(xr_expand[j])
        for kind in range(3):
            at_lane = kind * D + j * QC
            ref.g_joint[:, at_lane : at_lane + QC] = f32(
                xr_joint[j, :, kind * QC : (kind + 1) * QC]
            )
    deposit(ref.g_expand, results.g_expand)
    deposit(ref.g_joint, results.g_joint)
    wait_all(score_copies)
    score_rows = ref.score_rows
    for j in range(TEAM):
        score_rows[TEAM_HEADS * j : TEAM_HEADS * (j + 1)] = score_all[j, 0:TEAM_HEADS]

    def exact(a, b, ca, cb):
        return lax.dot_general(
            a,
            b,
            (((ca,), (cb,)), ((), ())),
            precision=lax.Precision.HIGHEST,
            preferred_element_type=F32,
        )

    scores = score_rows[...]
    query_row = vector(QUERY)
    head_of = lax.broadcasted_iota(jnp.int32, (16, D), 1) // HDIM
    head_rows = (head_of == lax.broadcasted_iota(jnp.int32, (16, D), 0)).astype(F32)
    probe_own = f32(
        low(exact(f32(ref.key_w[...]) * query_row, head_rows, 1, 1) * SCALE)
    )
    grad_probe = exact(f32(pe[...]), scores, 1, 1)
    ref.g_key[...] = exact(grad_probe, head_rows, 1, 0) * (query_row * SCALE)
    deposit(ref.g_key, results.g_key)
    small = ref.small
    picks = (
        lax.broadcasted_iota(jnp.int32, (QC, 128), 0)
        == lax.broadcasted_iota(jnp.int32, (QC, 128), 1) + s * WD
    ) & (lax.broadcasted_iota(jnp.int32, (QC, 128), 1) < WD)
    small[0:SUM_ROWS] = exact(ref.sums[...], picks.astype(F32), 1, 0)
    hidden_row = jnp.zeros((1, QC), F32)
    score_row = jnp.zeros((1, KP), F32)
    own_scores = score_all[g]
    for i in range(4):
        hidden_row = jnp.where(s // 2 == i, ref.sums[18 + i : 19 + i], hidden_row)
        score_row = jnp.where(s // 2 == i, own_scores[i : i + 1], score_row)
    hidden_row = jnp.where(s % 2 == 0, hidden_row[:, 0:128], hidden_row[:, 128:256])
    query_grad = exact(jnp.broadcast_to(score_row, (8, KP)), ref.key_own[...], 1, 1) * SCALE
    small[24:32] = jnp.zeros((8, 128), F32)
    small[24:25] = hidden_row
    small[25:26, 0:WD] = query_grad[0:1]
    deposit(small, results.small)
    h_spread[0].wait_recv()
    wait_all(h_handed)
    heads = head_all[...].reshape(D, KP)
    ref.g_value[...] = nt(pe[...], heads)
    deposit(ref.g_value, results.g_value)
    grad_table = nn(ref.value_w[...], heads) + exact(probe_own, scores, 1, 0)
    ref.g_patch[...] = grad_table[:, 0:VP]
    ref.g_embed[...] = grad_table[:, VP : VP + VARS]
    deposit(ref.g_patch, results.g_patch)
    deposit(ref.g_embed, results.g_embed)
    for copy in begun:
        copy.wait_send()
    for gather in (gather_merge, gather_output, gather_reduce, gather_joint, gather_expand):
        gather.sent()
    for line_sum in (reduce_sum, expand_sum, output_sum, joint_sum, merge_sum):
        line_sum.sent()
    for copy in deposits:
        copy.wait()


def fused(operands):
    scratch = list(SCRATCH.values()) + list(OUTPUTS.values())
    for shape in TEAM_SUMS.values():
        scratch += team_sum_buffers(shape)
    return pl.pallas_call(
        fused_kernel,
        out_shape=[jax.ShapeDtypeStruct(*shape) for shape in OUTPUTS.values()],
        in_specs=[pl.BlockSpec(memory_space=space) for space in INPUTS.values()],
        out_specs=[pl.BlockSpec(memory_space=pl.ANY)] * len(OUTPUTS),
        scratch_shapes=[pltpu.VMEM(*shape) for shape in scratch]
        + [pltpu.SemaphoreType.DMA((SEMAPHORES,))] * 2,
        compiler_params=pltpu.CompilerParams(
            collective_id=1, has_side_effects=True, vmem_limit_bytes=64 << 20
        ),
    )(*operands)


def hand_out_kernel(*refs):
    n = (len(refs) - 2) // 3
    arrays, results, held = refs[:n], refs[n : 2 * n], refs[2 * n : 3 * n]
    came, left = refs[3 * n :]
    fetches = [pltpu.make_async_copy(arrays[i], held[i], came.at[i]) for i in range(n)]
    for copy in fetches:
        copy.start()
    stores = [pltpu.make_async_copy(held[i], results[i], left.at[i]) for i in range(n)]
    for i in range(n):
        fetches[i].wait()
        stores[i].start()
    for copy in stores:
        copy.wait()


def hand_out(arrays):
    n = len(arrays)
    return pl.pallas_call(
        hand_out_kernel,
        out_shape=[jax.ShapeDtypeStruct(a.shape, a.dtype) for a in arrays],
        in_specs=[pl.BlockSpec(memory_space=pl.ANY)] * n,
        out_specs=[pl.BlockSpec(memory_space=pl.ANY)] * n,
        scratch_shapes=[pltpu.VMEM(a.shape, a.dtype) for a in arrays]
        + [pltpu.SemaphoreType.DMA((n,))] * 2,
        compiler_params=pltpu.CompilerParams(vmem_limit_bytes=64 << 20),
    )(*arrays)


def shards_fused(
    fields,
    patch_weight,
    variable_embed,
    query_vector,
    key_weight,
    value_weight,
    merge_weight,
    merge_bias,
    position_table,
    lead_weight,
    lead_bias,
    first_gain,
    first_shift,
    joint_weight,
    joint_bias,
    output_weight,
    output_bias,
    second_gain,
    second_shift,
    expand_weight,
    expand_bias,
    reduce_weight,
    reduce_bias,
    segment_ids,
    live_rows,
    lead_steps,
    cotangent,
):
    vectors = jnp.stack(
        [
            query_vector,
            merge_bias,
            lead_weight,
            lead_bias,
            first_gain,
            first_shift,
            output_bias,
            second_gain,
            second_shift,
            reduce_bias,
            joint_bias[0],
            joint_bias[1],
        ]
    )
    wide = jnp.stack([expand_bias, low(segment_ids), low(live_rows)])
    pack = jnp.concatenate(
        [
            jnp.pad(vectors, ((0, 16 - VECTORS), (0, 128 - WD))),
            jnp.pad(wide, ((0, 13), (0, 0))),
        ]
    )
    *whole, small = fused(
        (
            fields.T,
            patch_weight.T,
            variable_embed.T,
            key_weight,
            value_weight,
            pack,
            lead_steps,
            cotangent,
            position_table,
            joint_weight,
            expand_weight,
            merge_weight,
            output_weight,
            reduce_weight,
        )
    )
    (
        activations,
        field_grad,
        g_patch,
        g_embed,
        g_key,
        g_value,
        g_merge,
        g_position,
        g_joint,
        g_output,
        g_expand,
        g_reduce,
    ) = hand_out(whole)
    own = small[:, :WD]
    return (
        activations,
        field_grad.T,
        g_patch.T,
        g_embed.T,
        own[25],
        g_key,
        g_value,
        g_merge,
        own[0],
        g_position,
        own[1],
        own[2],
        own[3],
        own[4],
        g_joint,
        own[16:18],
        g_output,
        own[5],
        own[6],
        own[7],
        g_expand,
        small[24],
        g_reduce,
        own[8],
    )


def solution(mesh):
    by_row = P(ROWS, None)
    by_column = P(None, ROWS)
    vector = P(ROWS)
    in_specs = (
        by_row,
        by_column,
        by_column,
        vector,
        by_row,
        by_row,
        by_row,
        vector,
        P("seq", "grp"),
        vector,
        vector,
        vector,
        vector,
        by_row,
        by_column,
        by_row,
        vector,
        vector,
        vector,
        by_row,
        vector,
        by_row,
        vector,
        vector,
        vector,
        P("grp", None),
        by_row,
    )
    out_specs = (
        by_row,
        by_row,
        by_column,
        by_column,
        vector,
        by_row,
        by_row,
        by_row,
        vector,
        P("seq", "grp"),
        vector,
        vector,
        vector,
        vector,
        by_row,
        by_column,
        by_row,
        vector,
        vector,
        vector,
        by_row,
        vector,
        by_row,
        vector,
    )
    G, S = mesh.shape["grp"], mesh.shape["seq"]

    def body(*args):
        rows_here, weight_rows = args[0].shape[0], args[5].shape[0]
        if (G, S, rows_here, weight_rows) == (TEAM, LINE, ROW, WD):
            return shards_fused(*args)
        return shards(G, S, *args)

    return jax.shard_map(body, mesh=mesh, in_specs=in_specs, out_specs=out_specs, check_vma=False)
```

```python
import types

import jax
import jax.numpy as jnp
from jax import lax
from jax.experimental import pallas as pl
from jax.experimental.pallas import tpu as pltpu
from jax.sharding import PartitionSpec as P

D = 1024
HEADS = 16
FF = 4096
VARS = 48
PIX = 4
HDIM = 64
VP = 192
KP = 256

EPSILON = 1e-05
SCALE = 0.125
LEAD_UNIT = 0.06
MASKED = -1e30

MESH = pl.DeviceIdType.MESH
ROWS = ("grp", "seq")
F32 = jnp.float32
BF16 = jnp.bfloat16


def f32(x):
    return x.astype(F32)


def low(x):
    return x.astype(BF16)


def dot(a, b, ca, cb):
    return lax.dot_general(a, b, (((ca,), (cb,)), ((), ())), preferred_element_type=F32)


def low_sums(x):
    return dot(jnp.ones((8, x.shape[0]), BF16), x, 1, 0)[0]


def exchange(axis, parts):
    return [
        lax.all_gather(a, axis, axis=0, tiled=False)
        if mode == "all"
        else lax.all_to_all(a, axis, 0, 0, tiled=False)
        for a, mode in parts
    ]


def norm_parts(x):
    center = x - jnp.mean(x, axis=-1, keepdims=True)
    spread = jnp.mean(center * center, axis=-1, keepdims=True)
    inverse = lax.rsqrt(spread + EPSILON)
    return center * inverse, inverse


def norm_back(hat, inverse, gain, grad):
    f = grad * gain
    return inverse * (
        f
        - jnp.mean(f, axis=-1, keepdims=True)
        - hat * jnp.mean(f * hat, axis=-1, keepdims=True)
    )


def pack(pieces):
    flat = jnp.concatenate([f32(p).reshape(-1) for p in pieces])
    short = -flat.shape[0] % 1024
    return jnp.pad(flat, (0, short)).reshape(-1, 128)


def unpack(table, sizes):
    flat = table.reshape(table.shape[:-2] + (-1,))
    out, at = [], 0
    for size in sizes:
        out.append(flat[..., at : at + size])
        at += size
    return out


def softmax_parts(q, k, allowed):
    scores = jnp.einsum("hqc,hkc->hqk", q, k, preferred_element_type=F32) * SCALE
    masked = jnp.where(allowed[None], scores, MASKED)
    top = jnp.max(masked, axis=-1, keepdims=True)
    terms = jnp.where(allowed[None], jnp.exp(masked - top), 0.0)
    total = jnp.sum(terms, axis=-1, keepdims=True)
    return terms * (1.0 / total)


def attend(q, k, v, allowed):
    weights = softmax_parts(q, k, allowed)
    return jnp.einsum("hqk,hkc->hqc", low(weights), v, preferred_element_type=F32)


def attend_back(q, k, v, allowed, grad, attended):
    weights = softmax_parts(q, k, allowed)
    offset = jnp.sum(f32(grad) * attended, axis=-1)
    pushed = jnp.einsum("hqc,hkc->hqk", grad, v, preferred_element_type=F32)
    slopes = low(weights * (pushed - offset[..., None])) * BF16(SCALE)
    grad_q = jnp.einsum("hqk,hkc->hqc", slopes, k, preferred_element_type=F32)
    grad_k = jnp.einsum("hqk,hqc->hkc", slopes, q, preferred_element_type=F32)
    grad_v = jnp.einsum("hqk,hqc->hkc", low(weights), grad, preferred_element_type=F32)
    return grad_q, grad_k, grad_v


def heads_first(x):
    return x.transpose(1, 0, 2)


def heads_last(x):
    return x.transpose(1, 0, 2)


def allowed_pairs(query_codes, key_codes):
    return ((query_codes[:, None] >> 1) == (key_codes[None, :] >> 1)) & (
        (key_codes[None, :] & 1) == 1
    )


def shards(
    G,
    S,
    fields,
    patch_weight,
    variable_embed,
    query_vector,
    key_weight,
    value_weight,
    merge_weight,
    merge_bias,
    position_table,
    lead_weight,
    lead_bias,
    first_gain,
    first_shift,
    joint_weight,
    joint_bias,
    output_weight,
    output_bias,
    second_gain,
    second_shift,
    expand_weight,
    expand_bias,
    reduce_weight,
    reduce_bias,
    segment_ids,
    live_rows,
    lead_steps,
    cotangent,
):
    R = fields.shape[0]
    dn = value_weight.shape[0]
    fn = reduce_weight.shape[0]
    RG = G * R
    HL = HEADS // G
    CL = HL * HDIM
    FL = FF // G
    pairs = G * HL
    direct = pairs % S == 0 and HL % max(pairs // S, 1) == 0

    def swap(axis, *parts):
        return exchange(axis, parts)

    def gather_rows(w):
        return lax.all_gather(w, "seq", axis=0, tiled=True)

    merge_s = gather_rows(merge_weight)
    output_s = gather_rows(output_weight)

    table = jnp.concatenate(
        [patch_weight, variable_embed, jnp.zeros((KP - VP - VARS, dn), BF16)], axis=0
    )
    value_part = low(dot(value_weight, table, 0, 1)).reshape(G, CL, KP)
    key_part = low(dot(key_weight, table, 0, 1)).reshape(G, CL, KP)
    both = jnp.concatenate([value_part, key_part], axis=1)
    codes_own = segment_ids * 2 + live_rows
    vectors_own = [
        query_vector,
        merge_bias,
        lead_weight,
        lead_bias,
        first_gain,
        first_shift,
        output_bias,
        second_gain,
        second_shift,
        reduce_bias,
    ]
    small_own = pack([codes_own] + vectors_own)
    widen = (jnp.arange(VP)[:, None] == jnp.arange(KP)[None, :]).astype(BF16)
    column = jnp.arange(KP)
    field_own = low(dot(fields, widen, 1, 0) + ((column >= VP) & (column < VP + VARS)))
    joint_own = joint_weight.reshape(dn, 3, G, CL).transpose(2, 0, 1, 3).reshape(G, dn, 3 * CL)
    expand_own = expand_weight.reshape(dn, G, FL).transpose(1, 0, 2)
    both, joint_in, expand_in, field_in, position_in, small_in, cot_in = swap(
        "grp",
        (both, "each"),
        (joint_own, "each"),
        (expand_own, "each"),
        (field_own, "all"),
        (position_table, "all"),
        (small_own, "all"),
        (cotangent, "all"),
    )
    joint_s = (
        lax.all_gather(joint_in, "seq", axis=0, tiled=False)
        .transpose(1, 0, 2, 3)
        .reshape(D, 3 * CL)
    )
    expand_s = (
        lax.all_gather(expand_in, "seq", axis=0, tiled=False).transpose(1, 0, 2, 3).reshape(D, FL)
    )
    reduce_s = gather_rows(reduce_weight)
    field_rows = field_in.reshape(RG, KP)
    field_wide = dot(field_rows, (column[:, None] == column[None, :]).astype(BF16), 1, 0)
    cot_rows = cot_in.reshape(RG, D)
    position_rows = position_in.transpose(1, 0, 2).reshape(R, D)
    both = low(jnp.sum(f32(both), axis=0)).reshape(2, S, dn, KP).transpose(1, 0, 2, 3)
    small_rows = small_in.shape[0] * small_in.shape[1]
    slim = pack([joint_bias, expand_bias])
    both, small_all, slim_all = swap(
        "seq",
        (both.reshape(S, 2 * dn, KP), "each"),
        (small_in.reshape(small_rows, 128), "all"),
        (slim, "all"),
    )
    both = jnp.sum(f32(both), axis=0).reshape(2, dn, KP)
    value_own, key_own = both[0], both[1]
    probe_part = jnp.sum(key_own * f32(query_vector)[:, None], axis=0) * SCALE
    value_table, probe_parts = swap(
        "seq",
        (low(value_own), "all"),
        (jnp.broadcast_to(probe_part[None], (8, KP)), "all"),
    )
    value_table = value_table.reshape(CL, KP)
    probe_table = jnp.sum(probe_parts[:, 0].reshape(HL, S // HL, KP), axis=1)

    small_all = small_all.reshape(S, G, -1, 128)
    pieces = unpack(small_all, [R] + [dn] * len(vectors_own))
    codes = pieces[0].astype(jnp.int32)
    (
        full_query,
        full_merge_bias,
        full_lead,
        full_lead_bias,
        full_first_gain,
        full_first_shift,
        full_output_bias,
        full_second_gain,
        full_second_shift,
        full_reduce_bias,
    ) = [p.transpose(1, 0, 2).reshape(D) for p in pieces[1:]]
    joint_shift, expand_shift = unpack(slim_all, [2 * dn, fn])
    joint_shift = joint_shift.reshape(S, 2, dn).transpose(1, 0, 2).reshape(2, CL)
    expand_shift = expand_shift.reshape(FL)

    picked = jnp.where(
        segment_ids[:, None] == jnp.arange(lead_steps.shape[1])[None, :], lead_steps, 0
    )
    lead_rows = LEAD_UNIT * jnp.sum(picked, axis=1).astype(F32)

    owner = jnp.concatenate(
        [jnp.arange(VP) // PIX, jnp.arange(VARS), jnp.full((KP - VP - VARS,), VARS)]
    )
    select = (owner[:, None] == jnp.arange(VARS)[None, :]).astype(BF16)
    maps = probe_table[:, :, None] * f32(select)[None]
    maps_high = low(maps)
    maps_low = low(maps - f32(maps_high))
    scores = jnp.einsum("rk,hkv->hrv", field_rows, maps_high, preferred_element_type=F32)
    scores = scores + jnp.einsum("rk,hkv->hrv", field_rows, maps_low, preferred_element_type=F32)
    chosen = jax.nn.softmax(scores, axis=-1)
    spread = jnp.einsum("hrv,kv->hrk", low(chosen), select, preferred_element_type=F32)
    mixed = low(spread * field_wide[None])
    value_heads = value_table.reshape(HL, HDIM, KP)
    head_low = low(
        jnp.einsum("hrk,hck->rhc", mixed, value_heads, preferred_element_type=F32).reshape(RG, CL)
    )
    merged = low(dot(head_low, merge_s, 1, 0)).reshape(G, R, D)
    (merged,) = swap("grp", (merged, "each"))
    start = (
        jnp.sum(f32(merged), axis=0)
        + full_merge_bias
        + f32(position_rows)
        + lead_rows[:, None] * full_lead
        + full_lead_bias
    )
    start_hat, start_inv = norm_parts(start)
    (normed,) = swap("grp", (low(start_hat * full_first_gain + full_first_shift), "all"))
    normed = normed.reshape(RG, D)
    joint = dot(normed, joint_s, 1, 0)
    shift = jnp.concatenate([joint_shift[0], jnp.zeros((CL,), F32), joint_shift[1]])
    joint = low(joint + shift)

    if direct:
        per = pairs // S
        split = HL // per
        width = per * HDIM

        def to_pairs(x, kinds):
            x = x.reshape(G, R, kinds, split, width).transpose(0, 3, 1, 2, 4)
            (x,) = swap("seq", (x.reshape(S, R, kinds * width), "each"))
            return x.reshape(S * R, kinds, per, HDIM)

        def from_pairs(x, kinds):
            (x,) = swap("seq", (x.reshape(S, R, kinds * width), "each"))
            return (
                x.reshape(G, split, R, kinds, width)
                .transpose(0, 2, 3, 1, 4)
                .reshape(RG, kinds * CL)
            )

        mine = lax.axis_index("seq") // split
        pair_codes = lax.dynamic_index_in_dim(codes, mine, axis=1, keepdims=False).reshape(S * R)
        allowed = allowed_pairs(pair_codes, pair_codes)
        qkv = to_pairs(joint, 3)
        q, k, v = [heads_first(qkv[:, i]) for i in range(3)]
        attended = attend(q, k, v, allowed)
        attended_low = from_pairs(heads_last(low(attended)), 1)
    else:
        heads = joint.reshape(G, R, 3, HL, HDIM).transpose(0, 2, 3, 1, 4)
        everyone = lax.all_gather(heads[:, 1:], "seq", axis=3, tiled=True)
        all_codes = codes.transpose(1, 0, 2).reshape(G, S * R)
        my_codes = lax.dynamic_index_in_dim(codes, lax.axis_index("seq"), 0, keepdims=False)

        def forward_group(item):
            q, kv, query_codes, key_codes = item
            return attend(q, kv[0], kv[1], allowed_pairs(query_codes, key_codes))

        attended = lax.map(forward_group, (heads[:, 0], everyone, my_codes, all_codes))
        attended_low = low(attended).transpose(0, 2, 1, 3).reshape(RG, CL)

    branch = low(dot(attended_low, output_s, 1, 0)).reshape(G, R, D)
    (branch,) = swap("grp", (branch, "each"))
    middle = start + jnp.sum(f32(branch), axis=0) + full_output_bias
    middle_hat, middle_inv = norm_parts(middle)
    (second,) = swap("grp", (low(middle_hat * full_second_gain + full_second_shift), "all"))
    second = second.reshape(RG, D)
    hidden = dot(second, expand_s, 1, 0) + expand_shift
    inner = 0.7978845608028654 * (hidden + 0.044715 * hidden * hidden * hidden)
    bend = jnp.tanh(inner)
    active = low(0.5 * hidden * (1.0 + bend))
    slope = 0.5 * (1.0 + bend) + 0.5 * hidden * (1.0 - bend * bend) * 0.7978845608028654 * (
        1.0 + 3.0 * 0.044715 * hidden * hidden
    )
    reduced = low(dot(active, reduce_s, 1, 0)).reshape(G, R, D)

    grad_active = dot(cot_rows, reduce_s, 1, 1)
    grad_hidden = low(grad_active * slope)
    grad_second = low(dot(grad_hidden, expand_s, 1, 1)).reshape(G, R, D)
    grad_second, reduced = swap("grp", (grad_second, "each"), (reduced, "each"))
    activations = middle + jnp.sum(f32(reduced), axis=0) + full_reduce_bias
    grad_second = jnp.sum(f32(grad_second), axis=0)
    grad_top = f32(cotangent)
    grad_middle = grad_top + norm_back(middle_hat, middle_inv, full_second_gain, grad_second)
    grad_branch = low(grad_middle)

    def scatter_rows(w):
        return lax.psum_scatter(w, "seq", scatter_dimension=0, tiled=True)

    def scatter_mixed(w):
        cols = w.shape[1]
        w = w.reshape(G, S, dn, cols).transpose(1, 0, 2, 3).reshape(S, G * dn * cols // 1024, 1024)
        w = lax.psum_scatter(w, "seq", scatter_dimension=0, tiled=False)
        return w.reshape(G, dn, cols)

    grad_reduce_weight = f32(scatter_rows(low(dot(active, cot_rows, 0, 0))))
    grad_expand_mixed = scatter_mixed(low(dot(second, grad_hidden, 0, 0)))
    grad_expand_bias = low_sums(grad_hidden)

    (grad_branch_rows,) = swap("grp", (grad_branch, "all"))
    grad_branch_rows = grad_branch_rows.reshape(RG, D)
    grad_attended = low(dot(grad_branch_rows, output_s, 1, 1))
    grad_output_weight = f32(scatter_rows(low(dot(attended_low, grad_branch_rows, 0, 0))))
    if direct:
        pushed = heads_first(to_pairs(grad_attended, 1)[:, 0])
        grad_q, grad_k, grad_v = attend_back(q, k, v, allowed, pushed, attended)
        grads = [heads_last(low(x)) for x in (grad_q, grad_k, grad_v)]
        grad_joint = from_pairs(jnp.stack(grads, axis=1), 3)
    else:
        grad_heads = grad_attended.reshape(G, R, HL, HDIM).transpose(0, 2, 1, 3)

        def backward_group(item):
            q, kv, query_codes, key_codes, grad, done = item
            grad_q, grad_k, grad_v = attend_back(
                q, kv[0], kv[1], allowed_pairs(query_codes, key_codes), grad, done
            )
            return grad_q, jnp.stack([grad_k, grad_v], axis=0)

        grad_q, grad_kv = lax.map(
            backward_group,
            (heads[:, 0], everyone, my_codes, all_codes, grad_heads, attended),
        )
        grad_kv = lax.psum_scatter(grad_kv, "seq", scatter_dimension=3, tiled=True)
        grad_joint = low(jnp.concatenate([grad_q[:, None], grad_kv], axis=1))
        grad_joint = grad_joint.transpose(0, 3, 1, 2, 4).reshape(RG, 3 * CL)
    grad_normed = low(dot(grad_joint, joint_s, 1, 1)).reshape(G, R, D)
    (grad_normed,) = swap("grp", (grad_normed, "each"))
    grad_normed = jnp.sum(f32(grad_normed), axis=0)
    grad_joint_mixed = scatter_mixed(low(dot(normed, grad_joint, 0, 0)))
    joint_sums = low_sums(grad_joint)
    grad_start = grad_middle + norm_back(start_hat, start_inv, full_first_gain, grad_normed)
    grad_merged = low(grad_start)

    grad_merged_rows, grad_joint_in, grad_expand_in = swap(
        "grp", (grad_merged, "all"), (grad_joint_mixed, "each"), (grad_expand_mixed, "each")
    )
    grad_joint_weight = f32(
        grad_joint_in.reshape(G, dn, 3, CL).transpose(1, 2, 0, 3).reshape(dn, 3 * D)
    )
    grad_expand_weight = f32(grad_expand_in.transpose(1, 0, 2).reshape(dn, FF))
    grad_merged_rows = grad_merged_rows.reshape(RG, D)
    grad_head = low(dot(grad_merged_rows, merge_s, 1, 1))
    grad_merge_weight = f32(scatter_rows(low(dot(head_low, grad_merged_rows, 0, 0))))
    grad_heads_low = grad_head.reshape(RG, HL, HDIM)
    value_back = jnp.einsum(
        "rhc,hck->hrk", grad_heads_low, value_heads, preferred_element_type=F32
    )
    weighed = value_back * field_wide[None]
    weighed_high = low(weighed)
    weighed_low = low(weighed - f32(weighed_high))
    grad_chosen = jnp.einsum("hrk,kv->hrv", weighed_high, select, preferred_element_type=F32)
    grad_chosen = grad_chosen + jnp.einsum(
        "hrk,kv->hrv", weighed_low, select, preferred_element_type=F32
    )
    grad_scores = low(
        chosen * (grad_chosen - jnp.sum(chosen * grad_chosen, axis=-1, keepdims=True))
    )
    score_spread = jnp.einsum("hrv,kv->hrk", grad_scores, select, preferred_element_type=F32)
    field_part = jnp.sum(spread * value_back + score_spread * probe_table[:, None, :], axis=0)
    field_part = field_part.reshape(G, R, KP)
    score_sums = jnp.sum(score_spread * field_wide[None], axis=1)
    head_sums = jnp.einsum(
        "rhc,hrk->hck", grad_heads_low, mixed, preferred_element_type=F32
    ).reshape(S, dn, KP)

    column_sums = jnp.stack(
        [
            low_sums(grad_merged),
            jnp.sum(lead_rows[:, None] * grad_start, axis=0),
            jnp.sum(grad_start, axis=0),
            jnp.sum(grad_normed * start_hat, axis=0),
            jnp.sum(grad_normed, axis=0),
            low_sums(grad_branch),
            jnp.sum(grad_second * middle_hat, axis=0),
            jnp.sum(grad_second, axis=0),
            jnp.sum(grad_top, axis=0),
        ]
    )
    kinds = column_sums.shape[0]
    column_sums = jnp.pad(column_sums, ((0, -kinds % 16), (0, 0)))
    column_sums = column_sums.reshape(-1, G, CL).transpose(1, 0, 2)
    position_blocks = grad_merged.reshape(R, G, CL).transpose(1, 0, 2)
    column_sums, position_blocks, field_part = swap(
        "grp", (column_sums, "each"), (position_blocks, "each"), (field_part, "each")
    )
    grad_position_table = jnp.sum(f32(position_blocks), axis=0)
    field_grad = jnp.sum(field_part, axis=0)[:, :VP]
    column_sums = jnp.sum(column_sums, axis=0)
    team_sums = jnp.concatenate(
        [
            column_sums[:kinds].reshape(kinds, S, dn).transpose(1, 0, 2).reshape(S, kinds * dn),
            joint_sums[:CL].reshape(S, dn),
            joint_sums[2 * CL :].reshape(S, dn),
            grad_expand_bias.reshape(S, fn),
        ],
        axis=1,
    )
    wide = team_sums.shape[1]
    team_sums = jnp.pad(team_sums, ((0, 0), (0, -wide % 1024))).reshape(S, -1, 128)
    score_sums = jnp.pad(score_sums, ((0, -HL % 8), (0, 0)))
    team_sums, head_sums, score_sums = swap(
        "seq", (team_sums, "each"), (low(head_sums), "each"), (score_sums, "all")
    )
    team_sums = jnp.sum(team_sums, axis=0).reshape(-1)[:wide]
    own_sums = team_sums[: kinds * dn].reshape(kinds, dn)
    grad_joint_bias = team_sums[kinds * dn : (kinds + 2) * dn].reshape(2, dn)
    grad_expand_bias = team_sums[(kinds + 2) * dn :]
    (
        grad_merge_bias,
        grad_lead_weight,
        grad_lead_bias,
        grad_first_gain,
        grad_first_shift,
        grad_output_bias,
        grad_second_gain,
        grad_second_shift,
        grad_reduce_bias,
    ) = [own_sums[i] for i in range(kinds)]
    head_sums = jnp.sum(f32(head_sums), axis=0)
    score_sums = jnp.sum(score_sums, axis=0)
    my_head = lax.axis_index("seq") * dn // HDIM
    my_scores = lax.dynamic_index_in_dim(score_sums, my_head, axis=0, keepdims=False)
    grad_query_vector = jnp.sum(key_own * my_scores[None], axis=1) * SCALE
    (head_all,) = swap("seq", (low(head_sums), "all"))
    head_all, score_all = swap(
        "grp", (head_all.reshape(S * dn, KP), "all"), (score_sums, "all")
    )
    head_all = head_all.reshape(D, KP)
    score_all = score_all[:, :HL].reshape(HEADS, KP)
    grad_value_weight = dot(table, head_all, 0, 1)
    probe_own = low(
        jnp.sum((f32(key_weight) * full_query).reshape(dn, HEADS, HDIM), axis=-1) * SCALE
    )
    grad_table = dot(head_all, value_weight, 0, 1)
    grad_table = grad_table + jnp.einsum("hk,dh->kd", score_all, f32(probe_own))
    grad_probe = jnp.einsum("kd,hk->dh", f32(table), score_all)
    grad_key_weight = (
        grad_probe[:, :, None] * full_query.reshape(HEADS, HDIM)[None] * SCALE
    ).reshape(dn, D)
    grad_patch_weight = grad_table[:VP]
    grad_variable_embed = grad_table[VP : VP + VARS]
    return (
        activations,
        field_grad,
        grad_patch_weight,
        grad_variable_embed,
        grad_query_vector,
        grad_key_weight,
        grad_value_weight,
        grad_merge_weight,
        grad_merge_bias,
        grad_position_table,
        grad_lead_weight,
        grad_lead_bias,
        grad_first_gain,
        grad_first_shift,
        grad_joint_weight,
        grad_joint_bias,
        grad_output_weight,
        grad_output_bias,
        grad_second_gain,
        grad_second_shift,
        grad_expand_weight,
        grad_expand_bias,
        grad_reduce_weight,
        grad_reduce_bias,
    )


TEAM = 4
LINE = 8
ROW = 128
TALL = TEAM * ROW
GROUP = LINE * ROW
WD = D // (TEAM * LINE)
QC = D // TEAM
TEAM_HEADS = HEADS // TEAM
PACKED = 4
VECTORS = 12
QUERY, MERGE_BIAS, LEAD_WEIGHT, LEAD_BIAS, FIRST_GAIN, FIRST_SHIFT = range(6)
OUTPUT_BIAS, SECOND_GAIN, SECOND_SHIFT, REDUCE_BIAS = range(6, 10)
SUM_ROWS = 24

INPUTS = dict(
    fields=pltpu.VMEM,
    patch=pltpu.VMEM,
    embed=pltpu.VMEM,
    key_w=pltpu.VMEM,
    value_w=pltpu.VMEM,
    pack=pltpu.VMEM,
    joint_b=pltpu.VMEM,
    segments=pltpu.VMEM,
    live=pltpu.VMEM,
    steps=pltpu.SMEM,
    cot=pl.ANY,
    position=pl.ANY,
    joint_w=pl.ANY,
    expand_w=pl.ANY,
    merge_w=pl.ANY,
    output_w=pl.ANY,
    reduce_w=pl.ANY,
)

OUTPUTS = dict(
    activations=((ROW, D), F32),
    field_grad=((VP, ROW), F32),
    g_patch=((WD, VP), F32),
    g_embed=((WD, VARS), F32),
    g_key=((WD, D), F32),
    g_value=((WD, D), F32),
    g_merge=((WD, D), F32),
    g_position=((ROW, QC), F32),
    g_joint=((WD, 3 * D), F32),
    g_output=((WD, D), F32),
    g_expand=((WD, FF), F32),
    g_reduce=((ROW, D), F32),
    small=((32, 128), F32),
)

SCRATCH = dict(
    head_all=((TEAM, LINE, WD, KP), BF16),
    score_all=((TEAM, 8, KP), F32),
    score_rows=((16, KP), F32),
    key_own=((WD, KP), F32),
    sums=((SUM_ROWS, QC), F32),
    pe=((WD, KP), BF16),
    field_all=((TEAM, ROW, KP), BF16),
    pos=((ROW, D), BF16),
    cot_all=((TEAM, ROW, D), BF16),
    pack_rows=((16, 128), F32),
    pack_all=((LINE, TEAM, 16, 128), BF16),
    vecs=((16, D), F32),
    shift_e=((8, D), F32),
    seg_q=((16, GROUP), BF16),
    seg_k=((16, GROUP), BF16),
    merge_s=((LINE, WD, D), BF16),
    output_s=((LINE, WD, D), BF16),
    reduce_s=((LINE, ROW, D), BF16),
    joint_s=((TEAM, LINE, WD, 3 * QC), BF16),
    expand_s=((TEAM, LINE, WD, D), BF16),
    e2_send=((2, LINE, WD, KP), BF16),
    e2_recv=((LINE, 2, WD, KP), BF16),
    pv=((LINE, WD, KP), BF16),
    at=((LINE, 8, KP), F32),
    probe=((8, KP), F32),
    select=((KP, 128), BF16),
    select_t=((128, KP), BF16),
    chosen=((TEAM_HEADS, TALL, 128), F32),
    head_low=((TALL, QC), BF16),
    start=((ROW, D), F32),
    start_hat=((ROW, D), F32),
    start_inv=((ROW, 128), F32),
    middle=((ROW, D), F32),
    middle_hat=((ROW, D), F32),
    middle_inv=((ROW, 128), F32),
    grad_mid=((ROW, D), F32),
    normed_all=((TEAM, ROW, D), BF16),
    second_all=((TEAM, ROW, D), BF16),
    gb_all=((TEAM, ROW, D), BF16),
    gm_all=((TEAM, ROW, D), BF16),
    pair_send=((LINE, 3, ROW, 128), BF16),
    qkv=((3, GROUP, 128), BF16),
    p_low=((2, GROUP, GROUP), BF16),
    att_f=((GROUP, 128), F32),
    att_low=((GROUP, 128), BF16),
    att_all=((TEAM, ROW, QC), BF16),
    g_send=((TEAM, 2, ROW, 128), BF16),
    go=((GROUP, 128), BF16),
    dq=((GROUP, 128), F32),
    d_all=((TEAM, 3, ROW, QC), BF16),
    active_all=((TEAM, ROW, D), BF16),
    gh_all=((TEAM, ROW, D), BF16),
    own_a=((ROW, D), F32),
    own_b=((ROW, D), F32),
    far_a=((ROW, D), F32),
    far_b=((ROW, D), F32),
    far_d=((ROW, D), F32),
    gw_merge=((LINE, WD, D), BF16),
    gw_output=((LINE, WD, D), BF16),
    gw_reduce=((LINE, ROW, D), BF16),
    gw_joint=((TEAM, LINE, WD, 3 * QC), BF16),
    gw_expand=((TEAM, LINE, WD, D), BF16),
    yr_merge=((4, WD, D), BF16),
    yr_output=((4, WD, D), BF16),
    yr_reduce=((4, ROW // 2, D), BF16),
    yr_half=((1, ROW // 2, D), BF16),
    zr_half=((6, ROW // 2, D), BF16),
    za_half=((4, ROW // 2, D), BF16),
    yr_joint=((4, TEAM, WD, 3 * QC), BF16),
    yr_expand=((4, TEAM, WD, D), BF16),
    zr_merge=((3, WD, D), BF16),
    za_merge=((2, WD, D), BF16),
    zr_output=((3, WD, D), BF16),
    za_output=((2, WD, D), BF16),
    zr_reduce=((3, ROW // 2, D), BF16),
    za_reduce=((2, ROW // 2, D), BF16),
    zr_joint=((3, TEAM, WD, 3 * QC), BF16),
    za_joint=((2, TEAM, WD, 3 * QC), BF16),
    zr_expand=((3, TEAM, WD, D), BF16),
    za_expand=((2, TEAM, WD, D), BF16),
    xs_joint=((TEAM, WD, 3 * QC), BF16),
    xs_expand=((TEAM, WD, D), BF16),
    xr_joint=((TEAM, WD, 3 * QC), BF16),
    xr_expand=((TEAM, WD, D), BF16),
    csum=((16, D), F32),
    crecv=((TEAM, 16, QC), F32),
    tsum=((LINE, SUM_ROWS, QC), F32),
    f_own=((TEAM, ROW, KP), F32),
    f_recv=((3, ROW, KP), F32),
    t_send=((LINE, WD, KP), BF16),
    t_recv=((LINE, WD, KP), BF16),
    q_all=((LINE, 8, KP), F32),
)

TEAM_SUMS = dict(
    both=(2 * QC, KP),
    merge=(ROW, D),
    branch=(ROW, D),
    second=(ROW, D),
    reduced=(ROW, D),
    normed=(ROW, D),
)


def team_sum_buffers(shape):
    near = ((2,) + shape, BF16)
    one = (shape, BF16)
    return (near, near, one, one)


SEMAPHORES = 252


def nn(a, b):
    return dot(a, b, 1, 0)


def nt(a, b):
    return dot(a, b, 1, 1)


def tn(a, b):
    return dot(a, b, 0, 0)


def lanes(at, size):
    return pl.ds(pl.multiple_of(at, 128), size)


def rows(at, size):
    return pl.ds(pl.multiple_of(at, size), size)


def fused_kernel(*refs):
    n_in, n_out = len(INPUTS), len(OUTPUTS)
    results = types.SimpleNamespace(**dict(zip(OUTPUTS, refs[n_in : n_in + n_out])))
    names = list(INPUTS) + list(SCRATCH) + list(OUTPUTS)
    rest = refs[:n_in] + refs[n_in + n_out :]
    ref = types.SimpleNamespace(**dict(zip(names, rest)))
    rest = rest[len(names) :]
    send, recv = rest[-2:]
    sums = dict(zip(TEAM_SUMS, [rest[4 * i : 4 * i + 4] for i in range(len(TEAM_SUMS))]))
    sums = types.SimpleNamespace(**sums)
    g = lax.axis_index("grp")
    s = lax.axis_index("seq")
    sib = g + 1 - 2 * lax.rem(g, 2)
    far = lax.rem(g + 2, TEAM)
    diag = lax.rem(sib + 2, TEAM)
    z = s // 2
    y = s - 2 * z
    beside = s + 1 - 2 * y
    mine = lax.rem(3 * z, TEAM)
    is_middle = (z == 1) | (z == 2)
    is_end = (z == 0) | (z == 3)
    partner = s + 2 - 4 * lax.rem(z, 2)
    facing = lax.rem(s + 6 - 4 * z + LINE, LINE)
    near_places = [4 * (z // 2) + y + 2 * i for i in range(2)]
    far_places = [4 * (1 - z // 2) + y + 2 * i for i in range(2)]

    def to_team(j):
        return (j, s)

    def to_line(j):
        return (g, j)

    used = [0]
    begun = []

    def reserve(count):
        at = used[0]
        used[0] += count
        assert used[0] <= SEMAPHORES
        return at

    def remote(src, dst, device, at):
        return pltpu.make_async_remote_copy(
            src_ref=src,
            dst_ref=dst,
            send_sem=send.at[at],
            recv_sem=recv.at[at],
            device_id=device,
            device_id_type=MESH,
        )

    def push(src, dst, device):
        copy = remote(src, dst, device, reserve(1))
        copy.start()
        begun.append(copy)
        return copy

    barrier = pltpu.get_barrier_semaphore()
    for step in range(1, TEAM):
        pl.semaphore_signal(
            barrier, inc=1, device_id=to_team(lax.rem(g + step, TEAM)), device_id_type=MESH
        )
    for step in range(1, LINE):
        pl.semaphore_signal(
            barrier, inc=1, device_id=to_line(lax.rem(s + step, LINE)), device_id_type=MESH
        )

    class Together:
        def __init__(self, bulk, waits_itself=False):
            self.bulk, self.at = bulk, reserve(1)
            if not waits_itself:
                begun_together.append(self)

        def push(self, src, dst, device):
            remote(src, dst, device, self.at).start()

        def wait_recv(self):
            remote(self.bulk, self.bulk, to_line(beside), self.at).wait_recv()

        def wait_send(self):
            remote(self.bulk, self.bulk, to_line(beside), self.at).wait_send()

    begun_together = []

    def spread(buf):
        half = buf.shape[1] // 2
        across = []
        for h in range(2):
            part = buf.at[g, pl.ds(h * half, half)]
            across.append(push(part, part, to_team(far)))
        return push(buf.at[g], buf.at[g], to_team(sib)), across

    def spread_on(buf, across):
        half = buf.shape[1] // 2
        handed = Together(buf.at[far])
        for h in range(2):
            across[h].wait_recv()
            part = buf.at[far, pl.ds(h * half, half)]
            handed.push(part, part, to_team(sib))
        return [handed]

    def wait_all(copies):
        for copy in copies:
            copy.wait_recv()

    class TeamSum:
        def __init__(self, buffers):
            self.ps, self.r, self.t, self.x = buffers
            self.near_copies = [None, None]

        def near(self, slot, value=None):
            if value is not None:
                self.ps[slot] = low(value)
            self.near_copies[slot] = push(self.ps.at[slot], self.r.at[slot], to_team(sib))

        def across(self, value):
            self.near_copies[1].wait_recv()
            half = self.t.shape[0] // 2
            self.far_copies = [Together(self.x)]
            for h in range(2):
                part = pl.ds(h * half, half)
                self.t[part] = low(value(part) + f32(self.r[1, part]))
                self.far_copies[0].push(self.t.at[part], self.x.at[part], to_team(far))

        def total(self, own):
            self.near_copies[0].wait_recv()
            wait_all(self.far_copies)
            return own + f32(self.r[0]) + f32(self.x[...])

    deposits = []

    def deposit(src, dst):
        copy = pltpu.make_async_copy(src, dst, recv.at[reserve(1)])
        copy.start()
        deposits.append(copy)

    def to_whole_line(src, dst, bulk):
        group = Together(bulk)
        for step in range(1, LINE):
            place = lax.rem(s + step, LINE)
            group.push(src(place), dst, to_line(place))
        return [group]

    def share_line(buf):
        return to_whole_line(lambda place: buf.at[s], buf.at[s], buf.at[pl.ds(0, LINE - 1)])

    def to_whole_team(src, dst, bulk):
        group = Together(bulk)
        for j in (far, diag, sib):
            group.push(src(j), dst, to_team(j))
        return [group]

    def mean(x):
        return jnp.sum(x, axis=-1, keepdims=True) * (1.0 / D)

    class Gather:
        def __init__(self, slot):
            self.slot = slot
            self.at = reserve(9)

        def send(self, place, device, i, shard=None):
            part = self.slot(place)
            remote(part if shard is None else shard, part, device, self.at + i).start()

        def come(self, i):
            part = self.slot(s)
            remote(part, part, to_line(beside), self.at + i).wait_recv()

        def stage1(self, shard=None):
            self.send(s, to_line(partner), 0, shard)
            self.send(s, to_line(beside), 1, shard)

        def stage2(self, hold=False):
            self.come(0)

            @pl.when(is_middle)
            def _():
                for i in range(2):
                    self.send(near_places[i], to_line(facing), 2 + i)

            if not hold:
                self.hand_on()

        def hand_on(self):
            self.send(partner, to_line(beside), 4)

        def stage3(self):
            @pl.when(is_middle)
            def _():
                for i in range(2):
                    self.come(2 + i)
                    self.send(far_places[i], to_line(partner), 5 + i)
                    self.send(far_places[i], to_line(beside), 7 + i)

        def stage4(self):
            @pl.when(is_end)
            def _():
                for i in range(2):
                    self.come(5 + i)
                    self.send(far_places[i], to_line(beside), 7 + i)

        def finish(self):
            for i in (1, 4, 7, 8):
                self.come(i)

        def sent(self):
            part = self.slot(s)

            def gone(i):
                remote(part, part, to_line(beside), self.at + i).wait_send()

            for i in (0, 1, 4, 7, 8):
                gone(i)

            @pl.when(is_middle)
            def _():
                for i in (2, 3, 5, 6):
                    gone(i)

    class PairExchange:
        def __init__(self, bulk):
            self.group, self.own = Together(bulk, waits_itself=True), reserve(1)

        def send(self, src, dst, there):
            @pl.when(there != s)
            def _():
                self.group.push(src, dst, to_line(there))

            @pl.when(there == s)
            def _():
                pltpu.make_async_copy(src, dst, recv.at[self.own]).start()

        def wait(self, src, dst):
            pltpu.make_async_copy(src, dst, recv.at[self.own]).wait()
            self.group.wait_recv()
            self.group.wait_send()

    pe = ref.pe
    pe[:, 0:VP] = ref.patch[...]
    pe[:, VP : VP + VARS] = ref.embed[...]
    pe[:, VP + VARS :] = jnp.zeros((WD, KP - VP - VARS), BF16)
    field_all, cot_all, pack_all = ref.field_all, ref.cot_all, ref.pack_all
    field_all[g, :, 0:VP] = ref.fields[...].T
    lane = lax.broadcasted_iota(jnp.int32, (ROW, KP - VP), 1)
    field_all[g, :, VP:] = (lane < VARS).astype(BF16)
    pack_rows = ref.pack_rows
    pack_rows[...] = f32(ref.pack[...])
    for i in range(2):
        pack_rows[2:3, 64 + i * WD : 64 + (i + 1) * WD] = f32(ref.joint_b[...])[i : i + 1]
    pack_rows[4:5] = ref.segments[...].astype(F32)
    pack_rows[5:6] = ref.live[...].astype(F32)
    pack_all[s, g] = low(pack_rows[...])
    pl.semaphore_wait(barrier, TEAM - 1 + LINE - 1)

    both = TeamSum(sums.both)

    def table_product(weight, j):
        return tn(weight[:, lanes(j * QC, QC)], pe[...])

    for slot, j in ((1, diag), (0, sib)):
        both.ps[slot, 0:QC] = low(table_product(ref.value_w, j))
        both.ps[slot, QC:] = low(table_product(ref.key_w, j))
        both.near(slot)
    field_copies = spread(field_all)
    far_parts = [table_product(ref.value_w, far), table_product(ref.key_w, far)]
    both.across(lambda part: far_parts[0] if part.start == 0 else far_parts[1])
    own_parts = [table_product(ref.value_w, g), table_product(ref.key_w, g)]
    pack_here = pack_all.at[s, g]
    pack_copies = to_whole_team(lambda j: pack_here, pack_here, pack_all.at[0, pl.ds(0, 3)])

    def whole(buf):
        return lambda i: buf.at[i]

    def inner(buf):
        return lambda i: buf.at[:, i]

    def some_rows(buf, at, size):
        return lambda i: buf.at[i, pl.ds(at, size)]

    def some_lanes(buf, at, size):
        return lambda i: buf.at[:, i, :, pl.ds(at, size)]

    half_rows, half_lanes = ROW // 2, D // 2
    gather_merge = Gather(whole(ref.merge_s))
    gather_output = Gather(whole(ref.output_s))
    gather_reduce = [Gather(some_rows(ref.reduce_s, i * half_rows, half_rows)) for i in range(2)]
    gather_joint = [Gather(some_lanes(ref.joint_s, i * QC, QC)) for i in range(3)]
    gather_expand = [Gather(some_lanes(ref.expand_s, i * half_lanes, half_lanes)) for i in range(2)]
    local = []

    def keep(src, dst):
        copy = pltpu.make_async_copy(src, dst, recv.at[reserve(1)])
        copy.start()
        local.append(copy)

    keep(ref.merge_w, ref.merge_s.at[s])
    keep(ref.output_w, ref.output_s.at[s])
    keep(ref.reduce_w, ref.reduce_s.at[s])
    keep(ref.cot, cot_all.at[g])
    gather_merge.stage1(ref.merge_w)
    for i in range(2):
        gather_reduce[i].stage1(ref.reduce_w.at[pl.ds(i * half_rows, half_rows)])

    joint_copies = [Together(ref.joint_s.at[pl.ds(0, 3), 0])]
    for j in (far, diag, sib):
        for kind in range(3):
            joint_copies[0].push(
                ref.joint_w.at[:, lanes(kind * D + j * QC, QC)],
                ref.joint_s.at[g, s, :, pl.ds(kind * QC, QC)],
                to_team(j),
            )
    for kind in range(3):
        keep(
            ref.joint_w.at[:, lanes(kind * D + g * QC, QC)],
            ref.joint_s.at[g, s, :, pl.ds(kind * QC, QC)],
        )
    expand_copies = to_whole_team(
        lambda j: ref.expand_w.at[:, lanes(j * D, D)],
        ref.expand_s.at[g, s],
        ref.expand_s.at[pl.ds(0, 3), 0],
    )
    keep(ref.expand_w.at[:, lanes(g * D, D)], ref.expand_s.at[g, s])
    keep(ref.position, ref.pos.at[:, lanes(g * QC, QC)])
    position_copies = to_whole_team(
        lambda j: ref.position, ref.pos.at[:, lanes(g * QC, QC)], ref.pos.at[:, pl.ds(0, 3 * QC)]
    )

    for copy in local:
        copy.wait()
    gather_merge.stage2()

    both.near_copies[0].wait_recv()
    wait_all(both.far_copies)
    for part in range(2):
        block = pl.ds(part * QC, QC)
        total = own_parts[part] + f32(both.r[0, block]) + f32(both.x[block])
        ref.e2_send[part] = low(total).reshape(LINE, WD, KP)
    e2_send, e2_recv = ref.e2_send, ref.e2_recv
    e2_copies = to_whole_line(
        lambda place: e2_send.at[:, place], e2_recv.at[s], e2_recv.at[pl.ds(0, LINE - 1)]
    )
    e2_recv[s] = e2_send[:, s]
    wait_all(joint_copies)
    for gather in gather_joint:
        gather.stage1()
    gather_merge.stage3()

    wait_all(e2_copies)
    table_own = jnp.sum(f32(e2_recv[...]), axis=0)
    key_own = table_own[1]
    ref.key_own[...] = key_own
    query = f32(pack_all[s, g])[0:1, 0:WD]
    key_high = low(key_own)
    key_rest = low(key_own - f32(key_high))
    query_rows = low(jnp.broadcast_to(query, (16, WD)))
    probe_part = (nn(query_rows, key_high) + nn(query_rows, key_rest)) * SCALE
    pv, at = ref.pv, ref.at
    pv[s] = low(table_own[0])
    at[s] = probe_part[0:8]
    pv_copies = share_line(pv)
    at_copies = to_whole_line(
        lambda place: at.at[s, pl.ds(0, 1)],
        at.at[s, pl.ds(0, 1)],
        at.at[pl.ds(0, LINE - 1), pl.ds(0, 1)],
    )
    for gather in gather_joint:
        gather.stage2()
    wait_all(pv_copies)
    wait_all(at_copies)
    gather_merge.stage4()
    wait_all(pack_copies)
    pack_line = share_line(pack_all)
    wait_all(expand_copies)
    for gather in gather_expand:
        gather.stage1()

    probe = ref.probe
    for h in range(TEAM_HEADS):
        probe[h : h + 1] = at[2 * h, 0:1] + at[2 * h + 1, 0:1]
    probe[TEAM_HEADS:] = jnp.zeros((8 - TEAM_HEADS, KP), F32)

    def owner_of(k):
        return jnp.where(k < VP, k // PIX, jnp.where(k < VP + VARS, k - VP, VARS + 64))

    select, select_t = ref.select, ref.select_t
    select[...] = (
        owner_of(lax.broadcasted_iota(jnp.int32, (KP, 128), 0))
        == lax.broadcasted_iota(jnp.int32, (KP, 128), 1)
    ).astype(BF16)
    select_t[...] = (
        owner_of(lax.broadcasted_iota(jnp.int32, (128, KP), 1))
        == lax.broadcasted_iota(jnp.int32, (128, KP), 0)
    ).astype(BF16)
    valid = lax.broadcasted_iota(jnp.int32, (1, 128), 1) < VARS
    head_of_lane = lax.broadcasted_iota(jnp.int32, (1, QC), 1) // HDIM

    field_handed = spread_on(field_all, field_copies[1])
    field_copies[0].wait_recv()
    wait_all(field_handed)

    def tall(buf):
        return buf[...].reshape(TALL, -1)

    def split_dot(x, b):
        high = low(x)
        return nn(high, b) + nn(low(x - f32(high)), b)

    chosen, head_low = ref.chosen, ref.head_low

    def choose(h):
        field = f32(tall(field_all))
        scores = split_dot(field * probe[h : h + 1], select[...])
        scores = jnp.where(valid, scores, MASKED)
        terms = jnp.exp(scores - jnp.max(scores, axis=-1, keepdims=True))
        weights = terms * (1.0 / jnp.sum(terms, axis=-1, keepdims=True))
        chosen[h] = weights
        mix = low(nn(low(weights), select_t[...]) * field)
        table_value = pv[2 * h : 2 * h + 2].reshape(HDIM, KP)
        head_low[:, h * HDIM : (h + 1) * HDIM] = low(nt(mix, table_value))

    for h in range(TEAM_HEADS):
        choose(h)

    merge_s, output_s = ref.merge_s, ref.output_s
    gather_merge.finish()
    merge = TeamSum(sums.merge)

    def row_weight(buf):
        return buf[...].reshape(-1, D)

    def two(buf, i, j):
        return jnp.concatenate([buf[i], buf[j]], axis=0)

    def merge_part(j):
        return nn(head_low[rows(j * ROW, ROW)], row_weight(merge_s))

    merge.near(1, merge_part(diag))
    ref.far_a[...] = merge_part(far)
    merge.across(lambda part: ref.far_a[part])
    merge.near(0, merge_part(sib))
    ref.own_a[...] = merge_part(g)

    wait_all(pack_line)
    vecs, shift_e = ref.vecs, ref.shift_e
    lane_piece = lax.broadcasted_iota(jnp.int32, (LINE, 1, QC), 2) // WD
    piece = lax.broadcasted_iota(jnp.int32, (LINE, 1, QC), 0)
    for q in range(PACKED):
        place = (
            lax.broadcasted_iota(jnp.int32, (128, QC), 1) % WD + q * WD
            == lax.broadcasted_iota(jnp.int32, (128, QC), 0)
        ).astype(BF16)
        for j in range(TEAM):
            spreadout = nn(pack_all[:, j].reshape(LINE * 16, 128), place)
            spreadout = jnp.where(lane_piece == piece, spreadout.reshape(LINE, 16, QC), 0.0)
            spreadout = jnp.sum(spreadout, axis=0)
            vecs[4 * q : 4 * q + 4, j * QC : (j + 1) * QC] = spreadout[0:4]

    def vector(i):
        at_row = 4 * (i % PACKED) + i // PACKED
        return vecs[at_row : at_row + 1, :]

    joint_shift = [
        vecs[4 * (i % PACKED) + i // PACKED, lanes(g * QC, QC)].reshape(1, QC) for i in (10, 11)
    ]
    seg_q, seg_k = ref.seg_q, ref.seg_k
    sub = lax.broadcasted_iota(jnp.int32, (16, 128), 0).astype(F32)
    for j in range(LINE):
        part = f32(pack_all[j, g])
        shift_e[:, j * 128 : (j + 1) * 128] = jnp.broadcast_to(part[3:4], (8, 128))
        part = f32(pack_all[j, mine])
        same = jnp.where(sub == part[4:5], 1.0, 0.0)
        seg_q[:, j * 128 : (j + 1) * 128] = low(same)
        seg_k[:, j * 128 : (j + 1) * 128] = low(same * part[5:6])
    own_seg = ref.segments[...].astype(F32)
    steps = ref.steps
    lead_lanes = jnp.zeros((1, 128), F32)
    for i in range(steps.shape[1]):
        lead_lanes = jnp.where(own_seg == i, LEAD_UNIT * steps[0, i].astype(F32), lead_lanes)
    lead = jnp.broadcast_to(lead_lanes, (ROW, 128)).T[:, 0:1]
    wait_all(position_copies)
    for gather in gather_joint:
        gather.stage3()
    gather_output.stage1(ref.output_w)
    for gather in gather_reduce:
        gather.stage2(hold=True)

    start_ref = ref.start
    start_ref[...] = (
        merge.total(ref.own_a[...])
        + vector(MERGE_BIAS)
        + f32(ref.pos[...])
        + lead * vector(LEAD_WEIGHT)
        + vector(LEAD_BIAS)
    )

    def norm(x, hat_ref, inv_ref, gain, shift):
        center = x - mean(x)
        inverse = lax.rsqrt(mean(center * center) + EPSILON)
        hat = center * inverse
        hat_ref[...] = hat
        inv_ref[...] = jnp.broadcast_to(inverse, (ROW, 128))
        return low(hat * gain + shift)

    def norm_back_ref(grad, hat_ref, inv_ref, gain):
        f = grad * gain
        hat = hat_ref[...]
        return inv_ref[:, 0:1] * (f - mean(f) - hat * mean(f * hat))

    normed_all = ref.normed_all
    normed_all[g] = norm(
        start_ref[...],
        ref.start_hat,
        ref.start_inv,
        vector(FIRST_GAIN),
        vector(FIRST_SHIFT),
    )
    normed_copies = spread(normed_all)
    joint_s, pair_send, qkv = ref.joint_s, ref.pair_send, ref.qkv
    for gather in gather_joint:
        gather.stage4()
    e6 = [PairExchange(qkv.at[kind, pl.ds(0, 7 * ROW), :]) for kind in range(3)]

    def pair_place(j, t):
        return 2 * lax.rem(3 * j, TEAM) + t

    line_rows = rows(s * ROW, ROW)

    def joint_rows(i, j):
        block = two(normed_all, i, j)
        for kind in range(3):
            if i is g:
                gather_joint[kind].finish()
            weight = joint_s[:, :, :, kind * QC : (kind + 1) * QC].reshape(D, QC)
            part = nn(block, weight)
            if kind != 1:
                part = part + joint_shift[kind // 2]
            part = low(part)
            for n, group in enumerate((i, j)):
                for t in range(2):
                    place = pair_place(group, t)
                    pair_send[place, kind] = part[n * ROW : (n + 1) * ROW, t * 128 : (t + 1) * 128]
                    e6[kind].send(pair_send.at[place, kind], qkv.at[kind, line_rows, :], place)

    normed_copies[0].wait_recv()
    joint_rows(g, sib)
    normed_handed = spread_on(normed_all, normed_copies[1])
    wait_all(normed_handed)
    joint_rows(far, diag)
    gather_output.stage2()
    gather_expand[0].stage2()
    for gather in gather_reduce:
        gather.hand_on()
        gather.stage3()
    for kind in range(3):
        e6[kind].wait(pair_send.at[0, kind], qkv.at[kind, line_rows, :])
    gather_output.stage3()
    gather_expand[1].stage2()
    cot_copies = spread(cot_all)

    half_of_lane = lax.broadcasted_iota(jnp.int32, (1, 128), 1) // HDIM
    p_low, att_f, att_low, att_all = ref.p_low, ref.att_f, ref.att_low, ref.att_all
    e7 = PairExchange(att_low.at[pl.ds(0, 7 * ROW)])
    pair_lanes = lanes(y * 128, 128)

    def attend_rows(b, carry):
        here = rows(b * 256, 256)
        queries = f32(qkv[0, here, :]) * SCALE
        keys, values = qkv[1], qkv[2]
        allowed = tn(seg_q[:, lanes(b * 256, 256)], seg_k[...]) > 0.5
        outs = []
        for t in range(2):
            scores = nt(low(jnp.where(half_of_lane == t, queries, 0.0)), keys)
            scores = jnp.where(allowed, scores, MASKED)
            terms = jnp.exp(scores - jnp.max(scores, axis=-1, keepdims=True))
            weights = low(terms * (1.0 / jnp.sum(terms, axis=-1, keepdims=True)))
            p_low[t, here, :] = weights
            outs.append(nn(weights, values))
        out = jnp.where(half_of_lane == 0, outs[0], outs[1])
        att_f[here] = out
        att_low[here] = low(out)
        for t in range(2):
            there = 2 * b + t
            e7.send(att_low.at[rows(there * ROW, ROW)], att_all.at[mine, :, pair_lanes], there)

        return carry

    lax.fori_loop(0, GROUP // 256, attend_rows, 0, unroll=2)
    gather_output.stage4()
    for gather in gather_reduce:
        gather.stage4()
    for gather in gather_expand:
        gather.stage3()
    gather_output.finish()
    e7.wait(att_low.at[pl.ds(0, ROW)], att_all.at[mine, :, pair_lanes])

    branch = TeamSum(sums.branch)

    def branch_part(j):
        return nn(att_all[j], row_weight(output_s))

    branch.near(1, branch_part(diag))
    ref.far_a[...] = branch_part(far)
    branch.across(lambda part: ref.far_a[part])
    branch.near(0, branch_part(sib))
    ref.own_a[...] = branch_part(g)
    cot_handed = spread_on(cot_all, cot_copies[1])
    gather_expand[0].stage4()
    middle_ref = ref.middle
    middle_ref[...] = branch.total(ref.own_a[...]) + start_ref[...] + vector(OUTPUT_BIAS)

    second_all = ref.second_all
    second_all[g] = norm(
        middle_ref[...],
        ref.middle_hat,
        ref.middle_inv,
        vector(SECOND_GAIN),
        vector(SECOND_SHIFT),
    )
    second_copies = spread(second_all)
    for gather in [gather_expand[0]] + gather_reduce:
        gather.finish()
    cot_copies[0].wait_recv()
    wait_all(cot_handed)
    expand_s, reduce_s = ref.expand_s, ref.reduce_s
    active_all, gh_all = ref.active_all, ref.gh_all
    root = 0.7978845608028654

    def feed(j, k, acc_a, acc_b, half):
        def tile(i, carry):
            here = lanes(i * 256, 256)
            up = expand_s[:, :, :, here].reshape(D, 256)
            down = reduce_s[pl.ds(2 * i, 2)].reshape(256, D)
            hidden = nn(two(second_all, j, k), up) + shift_e[0:1, here]
            square = hidden * hidden
            bend = jnp.tanh(root * hidden * (1.0 + 0.044715 * square))
            active = low(0.5 * hidden * (1.0 + bend))
            slope = 0.5 * (1.0 + bend) + (0.5 * root) * hidden * (1.0 - bend * bend) * (
                1.0 + (3.0 * 0.044715) * square
            )
            grad = low(nt(two(cot_all, j, k), down) * slope)
            for n, block in enumerate((j, k)):
                active_all[block, :, here] = active[n * ROW : (n + 1) * ROW]
                gh_all[block, :, here] = grad[n * ROW : (n + 1) * ROW]
            for part, acc in ((nt(grad, up), acc_a), (nn(active, down), acc_b)):
                for n in range(2):
                    rows_of = part[n * ROW : (n + 1) * ROW]

                    @pl.when(i == 0)
                    def _():
                        acc[n][...] = rows_of

                    @pl.when(i > 0)
                    def _():
                        acc[n][...] += rows_of

            return carry

        lax.fori_loop(2 * half, 2 * half + 2, tile, 0, unroll=True)

    second = TeamSum(sums.second)
    reduced = TeamSum(sums.reduced)
    own_a, own_b, far_a, far_b = ref.own_a, ref.own_b, ref.far_a, ref.far_b
    spare_a, spare_b = ref.grad_mid, ref.activations
    far_c, far_d = ref.g_reduce, ref.far_d
    near_blocks = (g, sib, (own_a, spare_a), (own_b, spare_b))
    far_blocks = (far, diag, (far_a, far_c), (far_b, far_d))
    second_copies[0].wait_recv()
    feed(*near_blocks, 0)
    second_handed = spread_on(second_all, second_copies[1])
    gather_expand[1].stage4()
    wait_all(second_handed)
    feed(*far_blocks, 0)
    gather_expand[1].finish()
    feed(*near_blocks, 1)
    second.near(0, spare_a[...])
    reduced.ps[0] = low(spare_b[...])
    feed(*far_blocks, 1)
    second.near(1, far_c[...])
    reduced.ps[1] = low(far_d[...])
    second.across(lambda part: far_a[part])
    reduced.near(0)
    reduced.near(1)

    class LineSum:
        def __init__(self, four, slot, yr, zr, za):
            self.four = four
            self.slot, self.yr, self.zr, self.za = slot, yr, zr, za
            self.at = reserve(6)

        def send(self, src, dst, device, i):
            remote(src, dst, device, self.at + i).start()

        def come(self, i):
            part = self.zr(0)
            remote(part, part, to_line(beside), self.at + i).wait_recv()

        def along_y(self):
            self.y_copies = Together(self.four)
            for i in range(4):
                self.y_copies.push(self.slot(2 * i + 1 - y), self.yr(i), to_line(beside))

        def add(self, place, came):
            block = self.slot(place)
            block[...] = low(f32(block[...]) + f32(came[...]))
            return block

        def sum_y(self):
            self.y_copies.wait_recv()

            def add(i, carry):
                self.add(2 * i + y, self.yr(i))
                return carry

            lax.fori_loop(0, 4, add, 0)

        def stage1(self):
            @pl.when(is_end)
            def _():
                for i, place in enumerate(far_places + [partner]):
                    self.send(self.slot(place), self.zr(i), to_line(partner), i)

        def stage2(self):
            @pl.when(is_middle)
            def _():
                for i, place in enumerate(far_places):
                    self.come(i)
                    block = self.add(place, self.zr(i))
                    self.send(block, self.za(i), to_line(facing), 3 + i)

        def stage3(self):
            @pl.when(is_middle)
            def _():
                for i in range(2):
                    self.come(3 + i)
                block = self.add(partner, self.za(1 - lax.rem(z, 2)))
                self.send(block, self.zr(0), to_line(partner), 5)

        def total(self, out):
            own = f32(self.slot(s)[...])

            @pl.when(is_middle)
            def _():
                self.come(2)
                total = own + f32(self.zr(2)[...]) + f32(self.za(lax.rem(z, 2))[...])
                out[...] = total.astype(out.dtype)

            @pl.when(is_end)
            def _():
                self.come(5)
                out[...] = (own + f32(self.zr(0)[...])).astype(out.dtype)

        def sent(self):
            part = self.zr(0)

            def gone(i):
                remote(part, part, to_line(beside), self.at + i).wait_send()

            @pl.when(is_middle)
            def _():
                for i in (3, 4, 5):
                    gone(i)

            @pl.when(is_end)
            def _():
                for i in range(3):
                    gone(i)

    class LineSumZ:
        def __init__(self, slot, zr, za, yr):
            self.slot, self.zr, self.za, self.yr = slot, zr, za, yr
            self.at = reserve(13)

        def both_y(self, place):
            return [place - y, place - y + 1]

        def send(self, src, dst, device, i):
            remote(src, dst, device, self.at + i).start()

        def come(self, i):
            part = self.zr(0)
            remote(part, part, to_line(beside), self.at + i).wait_recv()

        def add(self, place, came):
            block = self.slot(place)
            block[...] = low(f32(block[...]) + f32(came[...]))
            return block

        def stage1(self):
            @pl.when(is_end)
            def _():
                for i, place in enumerate(
                    self.both_y(far_places[0]) + self.both_y(far_places[1]) + self.both_y(partner)
                ):
                    self.send(self.slot(place), self.zr(i), to_line(partner), i)

        def stage2(self):
            @pl.when(is_middle)
            def _():
                for i, place in enumerate(self.both_y(far_places[0]) + self.both_y(far_places[1])):
                    self.come(i)
                    block = self.add(place, self.zr(i))
                    self.send(block, self.za(i), to_line(facing), 6 + i)

        def stage3(self):
            @pl.when(is_middle)
            def _():
                for i in range(4):
                    self.come(6 + i)
                for i, place in enumerate(self.both_y(partner)):
                    block = self.add(place, self.za(2 * (1 - lax.rem(z, 2)) + i))
                    self.send(block, self.zr(i), to_line(partner), 10 + i)
                for i, place in enumerate(self.both_y(s)):
                    self.come(4 + i)
                    self.add(place, self.zr(4 + i))
                    self.add(place, self.za(2 * lax.rem(z, 2) + i))

        def along_y(self):
            @pl.when(is_end)
            def _():
                for i, place in enumerate(self.both_y(s)):
                    self.come(10 + i)
                    self.add(place, self.zr(i))

            self.send(self.slot(beside), self.yr(0), to_line(beside), 12)

        def total(self, out):
            self.come(12)
            out[...] = f32(self.slot(s)[...]) + f32(self.yr(0)[...])

        def sent(self):
            part = self.zr(0)

            def gone(i):
                remote(part, part, to_line(beside), self.at + i).wait_send()

            gone(12)

            @pl.when(is_middle)
            def _():
                for i in (6, 7, 8, 9, 10, 11):
                    gone(i)

            @pl.when(is_end)
            def _():
                for i in range(6):
                    gone(i)

    def line_sum_of(gw, others, at=None, size=None):
        four = others[0]
        if at is None:
            return LineSum(four, whole(gw), *[whole(buf) for buf in others])
        if len(gw.shape) == 3:
            return LineSum(four, some_rows(gw, at, size), *[whole(buf) for buf in others])

        def part(buf):
            return lambda i: buf.at[i, :, :, pl.ds(at, size)]

        four = four.at[:, :, :, pl.ds(at, size)]
        return LineSum(four, some_lanes(gw, at, size), *[part(buf) for buf in others])

    output_sum = line_sum_of(ref.gw_output, [ref.yr_output, ref.zr_output, ref.za_output])
    merge_sum = line_sum_of(ref.gw_merge, [ref.yr_merge, ref.zr_merge, ref.za_merge])
    reduce_y = line_sum_of(
        ref.gw_reduce, [ref.yr_reduce, ref.zr_reduce, ref.za_reduce], 0, half_rows
    )
    reduce_z = LineSumZ(
        some_rows(ref.gw_reduce, half_rows, half_rows),
        whole(ref.zr_half),
        whole(ref.za_half),
        whole(ref.yr_half),
    )
    reduce_sums = [reduce_y, reduce_z]
    expand_sums = [
        line_sum_of(
            ref.gw_expand,
            [ref.yr_expand, ref.zr_expand, ref.za_expand],
            i * half_lanes,
            half_lanes,
        )
        for i in range(2)
    ]
    joint_sums = [
        line_sum_of(ref.gw_joint, [ref.yr_joint, ref.zr_joint, ref.za_joint], i * QC, QC)
        for i in range(3)
    ]

    gw_reduce = ref.gw_reduce

    def reduce_block(j):
        lhs = active_all[:, :, lanes(j * ROW, ROW)].reshape(TALL, ROW)
        gw_reduce[j] = low(tn(lhs, tall(cot_all)))

    def reduce_beside(i, carry):
        reduce_block(2 * i + 1 - y)
        return carry

    def reduce_here(i, carry):
        reduce_block(2 * i + y)
        return carry

    lax.fori_loop(0, 4, reduce_beside, 0)
    reduce_y.along_y()
    lax.fori_loop(0, 4, reduce_here, 0)
    reduce_z.stage1()

    csum = ref.csum

    def note(i, value):
        csum[i : i + 1] = jnp.sum(value, axis=0, keepdims=True)

    grad_second = second.total(own_a[...])
    grad_mid = ref.grad_mid
    note(6, grad_second * ref.middle_hat[...])
    note(7, grad_second)
    grad_top = f32(cot_all[g])
    note(8, grad_top)
    grad_mid[...] = grad_top + norm_back_ref(
        grad_second, ref.middle_hat, ref.middle_inv, vector(SECOND_GAIN)
    )
    gb_all = ref.gb_all
    gb_all[g] = low(grad_mid[...])
    gb_copies = spread(gb_all)
    note(5, f32(gb_all[g]))
    gw_expand = ref.gw_expand

    def expand_block(i, carry):
        lhs = second_all[:, :, lanes(i * QC, QC)].reshape(TALL, QC)
        gw_expand[i] = low(tn(lhs, tall(gh_all))).reshape(LINE, WD, D)
        return carry

    g_send, go = ref.g_send, ref.go
    e12 = PairExchange(go.at[pl.ds(0, 7 * ROW)])

    def attended_back(i, j):
        part = low(nt(two(gb_all, i, j), row_weight(output_s)))
        for n, group in enumerate((i, j)):
            for t in range(2):
                g_send[group, t] = part[n * ROW : (n + 1) * ROW, t * 128 : (t + 1) * 128]
                e12.send(g_send.at[group, t], go.at[line_rows, :], pair_place(group, t))

    gb_copies[0].wait_recv()
    attended_back(g, sib)
    lax.fori_loop(0, 2, expand_block, 0)
    gb_handed = spread_on(gb_all, gb_copies[1])
    wait_all(gb_handed)
    attended_back(far, diag)
    reduced.across(lambda part: far_b[part])
    lax.fori_loop(2, 4, expand_block, 0)
    expand_sums[0].along_y()
    gw_output = ref.gw_output
    gw_output[...] = low(tn(tall(att_all), tall(gb_all))).reshape(LINE, WD, D)
    e12.wait(g_send.at[0, 0], go.at[line_rows, :])
    output_sum.along_y()
    reduce_y.sum_y()
    reduce_y.stage1()

    dq, d_all = ref.dq, ref.d_all
    dq[...] = jnp.zeros_like(dq)
    e13 = PairExchange(qkv.at[pl.ds(0, 2), pl.ds(0, 7 * ROW), :])
    products = f32(go[...]) * att_f[...]
    offsets = [
        jnp.sum(jnp.where(half_of_lane == t, products, 0.0), axis=-1, keepdims=True)
        for t in range(2)
    ]
    att_f[...] = jnp.where(half_of_lane == 0, offsets[0], offsets[1])
    pair_d = d_all.at[mine, pl.ds(1, 2), :, pair_lanes]

    def attend_back_keys(b, carry):
        here = rows(b * 256, 256)
        keys, values = qkv[1, here, :], qkv[2, here, :]
        queries, grad = f32(qkv[0]), f32(go[...])
        outs, grad_keys, grad_values = [], 0.0, 0.0
        for t in range(2):
            grad_t = low(jnp.where(half_of_lane == t, grad, 0.0))
            query_t = low(jnp.where(half_of_lane == t, queries, 0.0))
            weights = p_low[t, :, lanes(b * 256, 256)]
            offset = att_f[:, t * HDIM : t * HDIM + 1]
            slopes = low(low(f32(weights) * (nt(grad_t, values) - offset)) * SCALE)
            outs.append(nn(slopes, keys))
            grad_keys += tn(slopes, query_t)
            grad_values += tn(weights, grad_t)
        dq[...] += jnp.where(half_of_lane == 0, outs[0], outs[1])
        pair_send[pl.ds(2 * b, 2), 1] = low(grad_keys).reshape(2, ROW, 128)
        pair_send[pl.ds(2 * b, 2), 2] = low(grad_values).reshape(2, ROW, 128)
        for t in range(2):
            there = 2 * b + t
            e13.send(pair_send.at[there, pl.ds(1, 2)], pair_d, there)

        return carry

    lax.fori_loop(0, 2, attend_back_keys, 0, unroll=True)
    lax.fori_loop(2, GROUP // 256, attend_back_keys, 0, unroll=True)
    pair_send[:, 0] = low(dq[...]).reshape(LINE, ROW, 128)
    d_dst = d_all.at[mine, 0, :, pair_lanes]
    d_copies = to_whole_line(
        lambda place: pair_send.at[place, 0], d_dst, att_low.at[pl.ds(0, 7 * ROW)]
    )
    d_here = pltpu.make_async_copy(pair_send.at[s, 0], d_dst, recv.at[reserve(1)])
    d_here.start()
    d_here.wait()
    wait_all(d_copies)
    e13.wait(pair_send.at[0, pl.ds(1, 2)], pair_d)
    normed = TeamSum(sums.normed)

    def joint_back(j):
        total = None
        for kind in range(3):
            weight = joint_s[:, :, :, kind * QC : (kind + 1) * QC].reshape(D, QC)
            part = nt(d_all[j, kind], weight)
            total = part if total is None else total + part
        return total

    normed.near(1, joint_back(diag))
    far_a[...] = joint_back(far)
    normed.across(lambda part: far_a[part])
    expand_sums[1].along_y()
    expand_sums[0].sum_y()
    expand_sums[0].stage1()
    reduce_z.stage2()
    normed.near(0, joint_back(sib))
    own_a[...] = joint_back(g)
    gw_joint = ref.gw_joint
    tsum = ref.tsum
    for kind in range(3):
        block = d_all[:, kind].reshape(TALL, QC)
        for i in range(TEAM):
            lhs = normed_all[:, :, i * QC : (i + 1) * QC].reshape(TALL, QC)
            part = low(tn(lhs, block)).reshape(LINE, WD, QC)
            gw_joint[i, :, :, kind * QC : (kind + 1) * QC] = part
        if kind != 1:
            row = 16 + kind // 2
            tsum[s, row : row + 1] = jnp.sum(f32(block), axis=0, keepdims=True)
    for part in joint_sums:
        part.along_y()
    hidden_sums = jnp.sum(f32(tall(gh_all)), axis=0, keepdims=True)
    for i in range(4):
        tsum[s, 18 + i : 19 + i] = hidden_sums[:, i * QC : (i + 1) * QC]
    tsum[s, 22:24] = jnp.zeros((2, QC), F32)

    grad_normed = normed.total(own_a[...])
    note(3, grad_normed * ref.start_hat[...])
    note(4, grad_normed)
    grad_start = grad_mid[...] + norm_back_ref(
        grad_normed, ref.start_hat, ref.start_inv, vector(FIRST_GAIN)
    )
    gm_all = ref.gm_all
    gm_all[g] = low(grad_start)
    gm_copies = spread(gm_all)
    note(0, f32(gm_all[g]))
    note(1, lead * grad_start)
    note(2, grad_start)
    csum[9:16] = jnp.zeros((7, D), F32)
    crecv = ref.crecv
    crecv[g] = csum[:, lanes(g * QC, QC)]
    c_copies = to_whole_team(
        lambda j: csum.at[:, lanes(j * QC, QC)], crecv.at[g], crecv.at[pl.ds(0, 3)]
    )
    ref.activations[...] = (
        reduced.total(own_b[...]) + middle_ref[...] + vector(REDUCE_BIAS)
    )
    deposit(ref.activations, results.activations)
    reduce_y.stage2()
    expand_sums[1].sum_y()
    expand_sums[1].stage1()
    gm_handed = spread_on(gm_all, gm_copies[1])
    gm_copies[0].wait_recv()
    wait_all(gm_handed)

    gw_merge = ref.gw_merge
    f_own = ref.f_own
    t_send = ref.t_send
    q_all = ref.q_all
    grad_heads = low(nt(tall(gm_all), row_weight(merge_s)))
    head_grad = ref.att_all
    head_grad[...] = grad_heads.reshape(TEAM, ROW, QC)
    q_all[s] = jnp.zeros((8, KP), F32)

    def choose_back(h):
        field = f32(tall(field_all))
        grad_h = low(jnp.where(head_of_lane == h, f32(tall(head_grad)), 0.0))
        value_back = nn(grad_h, pv[...].reshape(QC, KP))
        grad_chosen = split_dot(value_back * field, select[...])
        weights = chosen[h]
        shifted = grad_chosen - jnp.sum(weights * grad_chosen, axis=-1, keepdims=True)
        score_spread = nn(low(weights * shifted), select_t[...])
        spread_weights = nn(low(weights), select_t[...])
        pair = tall(head_grad)[:, (h // 2) * 128 : (h // 2 + 1) * 128]
        part = tn(pair, low(spread_weights * field))
        at_row = (h % 2) * HDIM
        t_send[2 * h : 2 * h + 2] = low(part[at_row : at_row + HDIM]).reshape(2, WD, KP)
        field_part = spread_weights * value_back + score_spread * probe[h : h + 1]
        field_part = field_part.reshape(TEAM, ROW, KP)
        if h == 0:
            f_own[...] = field_part
        else:
            f_own[...] += field_part
        q_all[s, h : h + 1] = jnp.sum(score_spread * field, axis=0, keepdims=True)

    for h in range(TEAM_HEADS):
        choose_back(h)
        if h == 0:
            reduce_z.stage3()
            expand_sums[0].stage2()
        if h == 2:
            joint_sums[0].sum_y()
            joint_sums[0].stage1()
            reduce_y.stage3()
    t_recv = ref.t_recv
    t_copies = to_whole_line(
        lambda place: t_send.at[place], t_recv.at[s], t_recv.at[pl.ds(0, LINE - 1)]
    )
    t_recv[s] = t_send[s]
    gw_merge[...] = low(tn(head_low[...], tall(gm_all))).reshape(LINE, WD, D)
    merge_sum.along_y()
    joint_sums[1].sum_y()
    joint_sums[1].stage1()
    expand_sums[1].stage2()
    reduce_z.along_y()
    expand_sums[0].stage3()
    output_sum.sum_y()
    output_sum.stage1()
    f_recv = ref.f_recv
    f_copies = Together(f_recv)
    for step in range(1, TEAM):
        j = lax.rem(g + step, TEAM)
        f_copies.push(f_own.at[j], f_recv.at[step - 1], to_team(j))
    position = jnp.zeros((ROW, QC), F32)
    for j in range(TEAM):
        position += f32(gm_all[j, :, lanes(g * QC, QC)])
    ref.g_position[...] = position
    deposit(ref.g_position, results.g_position)
    wait_all(c_copies)
    tsum[s, 0:16] = jnp.sum(crecv[...], axis=0)

    joint_sums[0].stage2()
    joint_sums[2].sum_y()
    joint_sums[2].stage1()
    wait_all(t_copies)
    head_all, score_all = ref.head_all, ref.score_all
    head_all[g, s] = low(jnp.sum(f32(t_recv[...]), axis=0))
    h_here = head_all.at[g, s]
    h_copies = to_whole_line(lambda place: h_here, h_here, head_all.at[0, pl.ds(0, LINE - 1)])
    joint_sums[1].stage2()
    expand_sums[1].stage3()
    joint_sums[0].stage3()
    merge_sum.sum_y()
    merge_sum.stage1()
    joint_sums[2].stage2()
    output_sum.stage2()
    joint_sums[1].stage3()
    wait_all(h_copies)
    h_spread = spread(head_all)
    q_copies = share_line(q_all)
    s_copies = share_line(tsum)
    merge_sum.stage2()
    joint_sums[2].stage3()
    output_sum.stage3()
    wait_all(q_copies)
    score_all[g] = jnp.sum(q_all[...], axis=0)
    score_here = score_all.at[g]
    score_copies = to_whole_team(lambda j: score_here, score_here, score_all.at[pl.ds(0, 3)])

    xs_joint, xs_expand = ref.xs_joint, ref.xs_expand
    xr_joint, xr_expand = ref.xr_joint, ref.xr_expand
    x_copies = []

    def to_owners(line_sum, xs, xr, at, size):
        here = pl.ds(at, size)
        line_sum.total(xs.at[:, :, here])
        x_copies.extend(
            to_whole_team(
                lambda j: xs.at[j, :, here], xr.at[g, :, here], xr.at[pl.ds(0, 3), :, here]
            )
        )
        xr[g, :, here] = xs[g, :, here]

    for i in range(2):
        to_owners(expand_sums[i], xs_expand, xr_expand, i * half_lanes, half_lanes)
    h_handed = spread_on(head_all, h_spread[1])
    merge_sum.stage3()
    for i in range(3):
        to_owners(joint_sums[i], xs_joint, xr_joint, i * QC, QC)
    for i in range(2):
        reduce_sums[i].total(ref.g_reduce.at[pl.ds(i * half_rows, half_rows)])
    deposit(ref.g_reduce, results.g_reduce)
    output_sum.total(ref.g_output)
    deposit(ref.g_output, results.g_output)
    f_copies.wait_recv()
    ref.field_grad[...] = (f_own[g] + f_recv[0] + f_recv[1] + f_recv[2]).T[0:VP]
    deposit(ref.field_grad, results.field_grad)
    wait_all(s_copies)
    ref.sums[...] = jnp.sum(tsum[...], axis=0)
    merge_sum.total(ref.g_merge)
    deposit(ref.g_merge, results.g_merge)
    wait_all(x_copies)
    for j in range(TEAM):
        ref.g_expand[:, j * D : (j + 1) * D] = f32(xr_expand[j])
        for kind in range(3):
            at_lane = kind * D + j * QC
            ref.g_joint[:, at_lane : at_lane + QC] = f32(
                xr_joint[j, :, kind * QC : (kind + 1) * QC]
            )
    deposit(ref.g_expand, results.g_expand)
    deposit(ref.g_joint, results.g_joint)
    wait_all(score_copies)
    score_rows = ref.score_rows
    for j in range(TEAM):
        score_rows[TEAM_HEADS * j : TEAM_HEADS * (j + 1)] = score_all[j, 0:TEAM_HEADS]

    def exact(a, b, ca, cb):
        return lax.dot_general(
            a,
            b,
            (((ca,), (cb,)), ((), ())),
            precision=lax.Precision.HIGHEST,
            preferred_element_type=F32,
        )

    scores = score_rows[...]
    query_row = vector(QUERY)
    head_of = lax.broadcasted_iota(jnp.int32, (16, D), 1) // HDIM
    head_rows = (head_of == lax.broadcasted_iota(jnp.int32, (16, D), 0)).astype(F32)
    probe_own = f32(
        low(exact(f32(ref.key_w[...]) * query_row, head_rows, 1, 1) * SCALE)
    )
    grad_probe = exact(f32(pe[...]), scores, 1, 1)
    ref.g_key[...] = exact(grad_probe, head_rows, 1, 0) * (query_row * SCALE)
    deposit(ref.g_key, results.g_key)
    small = ref.small
    picks = (
        lax.broadcasted_iota(jnp.int32, (QC, 128), 0)
        == lax.broadcasted_iota(jnp.int32, (QC, 128), 1) + s * WD
    ) & (lax.broadcasted_iota(jnp.int32, (QC, 128), 1) < WD)
    small[0:SUM_ROWS] = exact(ref.sums[...], picks.astype(F32), 1, 0)
    hidden_row = jnp.zeros((1, QC), F32)
    score_row = jnp.zeros((1, KP), F32)
    own_scores = score_all[g]
    for i in range(4):
        hidden_row = jnp.where(s // 2 == i, ref.sums[18 + i : 19 + i], hidden_row)
        score_row = jnp.where(s // 2 == i, own_scores[i : i + 1], score_row)
    hidden_row = jnp.where(s % 2 == 0, hidden_row[:, 0:128], hidden_row[:, 128:256])
    query_grad = exact(jnp.broadcast_to(score_row, (8, KP)), ref.key_own[...], 1, 1) * SCALE
    small[24:32] = jnp.zeros((8, 128), F32)
    small[24:25] = hidden_row
    small[25:26, 0:WD] = query_grad[0:1]
    deposit(small, results.small)
    h_spread[0].wait_recv()
    wait_all(h_handed)
    heads = head_all[...].reshape(D, KP)
    ref.g_value[...] = nt(pe[...], heads)
    deposit(ref.g_value, results.g_value)
    grad_table = nn(ref.value_w[...], heads) + exact(probe_own, scores, 1, 0)
    ref.g_patch[...] = grad_table[:, 0:VP]
    ref.g_embed[...] = grad_table[:, VP : VP + VARS]
    deposit(ref.g_patch, results.g_patch)
    deposit(ref.g_embed, results.g_embed)
    for copy in begun + begun_together:
        copy.wait_send()
    for gather in [gather_merge, gather_output] + gather_reduce + gather_joint + gather_expand:
        gather.sent()
    for line_sum in [output_sum, merge_sum] + reduce_sums + joint_sums + expand_sums:
        line_sum.sent()
    for copy in deposits:
        copy.wait()


def fused(operands):
    scratch = list(SCRATCH.values()) + list(OUTPUTS.values())
    for shape in TEAM_SUMS.values():
        scratch += team_sum_buffers(shape)
    return pl.pallas_call(
        fused_kernel,
        out_shape=[jax.ShapeDtypeStruct(*shape) for shape in OUTPUTS.values()],
        in_specs=[pl.BlockSpec(memory_space=space) for space in INPUTS.values()],
        out_specs=[pl.BlockSpec(memory_space=pl.ANY)] * len(OUTPUTS),
        scratch_shapes=[pltpu.VMEM(*shape) for shape in scratch]
        + [pltpu.SemaphoreType.DMA((SEMAPHORES,))] * 2,
        compiler_params=pltpu.CompilerParams(
            collective_id=1, has_side_effects=True, vmem_limit_bytes=64 << 20
        ),
    )(*operands)


VECTOR_ROWS = (25, 0, 1, 2, 3, 4, 5, 6, 7, 8)


def hand_out_kernel(*refs):
    n, m = len(OUTPUTS), len(VECTOR_ROWS)
    arrays = refs[:n]
    results = refs[n : 2 * n - 1]
    vectors = refs[2 * n - 1 : 2 * n - 1 + m]
    joint, hidden = refs[2 * n - 1 + m : 2 * n + 1 + m]
    held = refs[2 * n + 1 + m : 3 * n + 1 + m]
    narrow, came, left = refs[3 * n + 1 + m :]
    fetches = [pltpu.make_async_copy(arrays[i], held[i], came.at[i]) for i in range(n)]
    for copy in fetches:
        copy.start()
    small = held[n - 1]
    fetches[n - 1].wait()
    narrow[...] = small[:, 0:WD]
    stores = [
        pltpu.make_async_copy(narrow.at[row], vectors[i], left.at[n + i])
        for i, row in enumerate(VECTOR_ROWS)
    ]
    stores.append(pltpu.make_async_copy(narrow.at[pl.ds(16, 2)], joint, left.at[n + m]))
    stores.append(pltpu.make_async_copy(small.at[24], hidden, left.at[n + m + 1]))
    for copy in stores:
        copy.start()
    for i in range(n - 1):
        fetches[i].wait()
        copy = pltpu.make_async_copy(held[i], results[i], left.at[i])
        copy.start()
        stores.append(copy)
    for copy in stores:
        copy.wait()


def hand_out(arrays):
    n, m = len(arrays), len(VECTOR_ROWS)
    shapes = [jax.ShapeDtypeStruct(a.shape, a.dtype) for a in arrays[:-1]]
    shapes += [jax.ShapeDtypeStruct((WD,), F32)] * m
    shapes += [jax.ShapeDtypeStruct((2, WD), F32), jax.ShapeDtypeStruct((ROW,), F32)]
    return pl.pallas_call(
        hand_out_kernel,
        out_shape=shapes,
        in_specs=[pl.BlockSpec(memory_space=pl.ANY)] * n,
        out_specs=[pl.BlockSpec(memory_space=pl.ANY)] * len(shapes),
        scratch_shapes=[pltpu.VMEM(a.shape, a.dtype) for a in arrays]
        + [pltpu.VMEM((32, WD), F32)]
        + [pltpu.SemaphoreType.DMA((n,)), pltpu.SemaphoreType.DMA((n + m + 2,))],
        compiler_params=pltpu.CompilerParams(vmem_limit_bytes=64 << 20),
    )(*arrays)


def shards_fused(
    fields,
    patch_weight,
    variable_embed,
    query_vector,
    key_weight,
    value_weight,
    merge_weight,
    merge_bias,
    position_table,
    lead_weight,
    lead_bias,
    first_gain,
    first_shift,
    joint_weight,
    joint_bias,
    output_weight,
    output_bias,
    second_gain,
    second_shift,
    expand_weight,
    expand_bias,
    reduce_weight,
    reduce_bias,
    segment_ids,
    live_rows,
    lead_steps,
    cotangent,
):
    pack = jnp.concatenate(
        [
            query_vector,
            merge_bias,
            lead_weight,
            lead_bias,
            first_gain,
            first_shift,
            output_bias,
            second_gain,
            second_shift,
            reduce_bias,
            jnp.zeros((2 * WD,), BF16),
            expand_bias,
            jnp.zeros((12 * 128,), BF16),
        ]
    ).reshape(16, 128)
    whole = fused(
        (
            fields.T,
            patch_weight.T,
            variable_embed.T,
            key_weight,
            value_weight,
            pack,
            joint_bias,
            segment_ids.reshape(1, ROW),
            live_rows.reshape(1, ROW),
            lead_steps,
            cotangent,
            position_table,
            joint_weight,
            expand_weight,
            merge_weight,
            output_weight,
            reduce_weight,
        )
    )
    (
        activations,
        field_grad,
        g_patch,
        g_embed,
        g_key,
        g_value,
        g_merge,
        g_position,
        g_joint,
        g_output,
        g_expand,
        g_reduce,
        g_query,
        g_merge_b,
        g_lead,
        g_lead_b,
        g_first_gain,
        g_first_shift,
        g_output_b,
        g_second_gain,
        g_second_shift,
        g_reduce_b,
        g_joint_b,
        g_expand_b,
    ) = hand_out(whole)
    return (
        activations,
        field_grad.T,
        g_patch.T,
        g_embed.T,
        g_query,
        g_key,
        g_value,
        g_merge,
        g_merge_b,
        g_position,
        g_lead,
        g_lead_b,
        g_first_gain,
        g_first_shift,
        g_joint,
        g_joint_b,
        g_output,
        g_output_b,
        g_second_gain,
        g_second_shift,
        g_expand,
        g_expand_b,
        g_reduce,
        g_reduce_b,
    )


def solution(mesh):
    by_row = P(ROWS, None)
    by_column = P(None, ROWS)
    vector = P(ROWS)
    in_specs = (
        by_row,
        by_column,
        by_column,
        vector,
        by_row,
        by_row,
        by_row,
        vector,
        P("seq", "grp"),
        vector,
        vector,
        vector,
        vector,
        by_row,
        by_column,
        by_row,
        vector,
        vector,
        vector,
        by_row,
        vector,
        by_row,
        vector,
        vector,
        vector,
        P("grp", None),
        by_row,
    )
    out_specs = (
        by_row,
        by_row,
        by_column,
        by_column,
        vector,
        by_row,
        by_row,
        by_row,
        vector,
        P("seq", "grp"),
        vector,
        vector,
        vector,
        vector,
        by_row,
        by_column,
        by_row,
        vector,
        vector,
        vector,
        by_row,
        vector,
        by_row,
        vector,
    )
    G, S = mesh.shape["grp"], mesh.shape["seq"]

    def body(*args):
        rows_here, weight_rows = args[0].shape[0], args[5].shape[0]
        if (G, S, rows_here, weight_rows) == (TEAM, LINE, ROW, WD):
            return shards_fused(*args)
        return shards(G, S, *args)

    return jax.shard_map(body, mesh=mesh, in_specs=in_specs, out_specs=out_specs, check_vma=False)
```

```python
import types

import jax
import jax.numpy as jnp
from jax import lax
from jax.experimental import pallas as pl
from jax.experimental.pallas import tpu as pltpu
from jax.sharding import PartitionSpec as P

D = 1024
HEADS = 16
FF = 4096
VARS = 48
PIX = 4
HDIM = 64
VP = 192
KP = 256

EPSILON = 1e-05
SCALE = 0.125
LEAD_UNIT = 0.06
MASKED = -1e30

MESH = pl.DeviceIdType.MESH
ROWS = ("grp", "seq")
F32 = jnp.float32
BF16 = jnp.bfloat16


def f32(x):
    return x.astype(F32)


def low(x):
    return x.astype(BF16)


def dot(a, b, ca, cb):
    return lax.dot_general(a, b, (((ca,), (cb,)), ((), ())), preferred_element_type=F32)


def low_sums(x):
    return dot(jnp.ones((8, x.shape[0]), BF16), x, 1, 0)[0]


def exchange(axis, parts):
    return [
        lax.all_gather(a, axis, axis=0, tiled=False)
        if mode == "all"
        else lax.all_to_all(a, axis, 0, 0, tiled=False)
        for a, mode in parts
    ]


def norm_parts(x):
    center = x - jnp.mean(x, axis=-1, keepdims=True)
    spread = jnp.mean(center * center, axis=-1, keepdims=True)
    inverse = lax.rsqrt(spread + EPSILON)
    return center * inverse, inverse


def norm_back(hat, inverse, gain, grad):
    f = grad * gain
    return inverse * (
        f
        - jnp.mean(f, axis=-1, keepdims=True)
        - hat * jnp.mean(f * hat, axis=-1, keepdims=True)
    )


def pack(pieces):
    flat = jnp.concatenate([f32(p).reshape(-1) for p in pieces])
    short = -flat.shape[0] % 1024
    return jnp.pad(flat, (0, short)).reshape(-1, 128)


def unpack(table, sizes):
    flat = table.reshape(table.shape[:-2] + (-1,))
    out, at = [], 0
    for size in sizes:
        out.append(flat[..., at : at + size])
        at += size
    return out


def softmax_parts(q, k, allowed):
    scores = jnp.einsum("hqc,hkc->hqk", q, k, preferred_element_type=F32) * SCALE
    masked = jnp.where(allowed[None], scores, MASKED)
    top = jnp.max(masked, axis=-1, keepdims=True)
    terms = jnp.where(allowed[None], jnp.exp(masked - top), 0.0)
    total = jnp.sum(terms, axis=-1, keepdims=True)
    return terms * (1.0 / total)


def attend(q, k, v, allowed):
    weights = softmax_parts(q, k, allowed)
    return jnp.einsum("hqk,hkc->hqc", low(weights), v, preferred_element_type=F32)


def attend_back(q, k, v, allowed, grad, attended):
    weights = softmax_parts(q, k, allowed)
    offset = jnp.sum(f32(grad) * attended, axis=-1)
    pushed = jnp.einsum("hqc,hkc->hqk", grad, v, preferred_element_type=F32)
    slopes = low(weights * (pushed - offset[..., None])) * BF16(SCALE)
    grad_q = jnp.einsum("hqk,hkc->hqc", slopes, k, preferred_element_type=F32)
    grad_k = jnp.einsum("hqk,hqc->hkc", slopes, q, preferred_element_type=F32)
    grad_v = jnp.einsum("hqk,hqc->hkc", low(weights), grad, preferred_element_type=F32)
    return grad_q, grad_k, grad_v


def heads_first(x):
    return x.transpose(1, 0, 2)


def heads_last(x):
    return x.transpose(1, 0, 2)


def allowed_pairs(query_codes, key_codes):
    return ((query_codes[:, None] >> 1) == (key_codes[None, :] >> 1)) & (
        (key_codes[None, :] & 1) == 1
    )


def shards(
    G,
    S,
    fields,
    patch_weight,
    variable_embed,
    query_vector,
    key_weight,
    value_weight,
    merge_weight,
    merge_bias,
    position_table,
    lead_weight,
    lead_bias,
    first_gain,
    first_shift,
    joint_weight,
    joint_bias,
    output_weight,
    output_bias,
    second_gain,
    second_shift,
    expand_weight,
    expand_bias,
    reduce_weight,
    reduce_bias,
    segment_ids,
    live_rows,
    lead_steps,
    cotangent,
):
    R = fields.shape[0]
    dn = value_weight.shape[0]
    fn = reduce_weight.shape[0]
    RG = G * R
    HL = HEADS // G
    CL = HL * HDIM
    FL = FF // G
    pairs = G * HL
    direct = pairs % S == 0 and HL % max(pairs // S, 1) == 0

    def swap(axis, *parts):
        return exchange(axis, parts)

    def gather_rows(w):
        return lax.all_gather(w, "seq", axis=0, tiled=True)

    merge_s = gather_rows(merge_weight)
    output_s = gather_rows(output_weight)

    table = jnp.concatenate(
        [patch_weight, variable_embed, jnp.zeros((KP - VP - VARS, dn), BF16)], axis=0
    )
    value_part = low(dot(value_weight, table, 0, 1)).reshape(G, CL, KP)
    key_part = low(dot(key_weight, table, 0, 1)).reshape(G, CL, KP)
    both = jnp.concatenate([value_part, key_part], axis=1)
    codes_own = segment_ids * 2 + live_rows
    vectors_own = [
        query_vector,
        merge_bias,
        lead_weight,
        lead_bias,
        first_gain,
        first_shift,
        output_bias,
        second_gain,
        second_shift,
        reduce_bias,
    ]
    small_own = pack([codes_own] + vectors_own)
    widen = (jnp.arange(VP)[:, None] == jnp.arange(KP)[None, :]).astype(BF16)
    column = jnp.arange(KP)
    field_own = low(dot(fields, widen, 1, 0) + ((column >= VP) & (column < VP + VARS)))
    joint_own = joint_weight.reshape(dn, 3, G, CL).transpose(2, 0, 1, 3).reshape(G, dn, 3 * CL)
    expand_own = expand_weight.reshape(dn, G, FL).transpose(1, 0, 2)
    both, joint_in, expand_in, field_in, position_in, small_in, cot_in = swap(
        "grp",
        (both, "each"),
        (joint_own, "each"),
        (expand_own, "each"),
        (field_own, "all"),
        (position_table, "all"),
        (small_own, "all"),
        (cotangent, "all"),
    )
    joint_s = (
        lax.all_gather(joint_in, "seq", axis=0, tiled=False)
        .transpose(1, 0, 2, 3)
        .reshape(D, 3 * CL)
    )
    expand_s = (
        lax.all_gather(expand_in, "seq", axis=0, tiled=False).transpose(1, 0, 2, 3).reshape(D, FL)
    )
    reduce_s = gather_rows(reduce_weight)
    field_rows = field_in.reshape(RG, KP)
    field_wide = dot(field_rows, (column[:, None] == column[None, :]).astype(BF16), 1, 0)
    cot_rows = cot_in.reshape(RG, D)
    position_rows = position_in.transpose(1, 0, 2).reshape(R, D)
    both = low(jnp.sum(f32(both), axis=0)).reshape(2, S, dn, KP).transpose(1, 0, 2, 3)
    small_rows = small_in.shape[0] * small_in.shape[1]
    slim = pack([joint_bias, expand_bias])
    both, small_all, slim_all = swap(
        "seq",
        (both.reshape(S, 2 * dn, KP), "each"),
        (small_in.reshape(small_rows, 128), "all"),
        (slim, "all"),
    )
    both = jnp.sum(f32(both), axis=0).reshape(2, dn, KP)
    value_own, key_own = both[0], both[1]
    probe_part = jnp.sum(key_own * f32(query_vector)[:, None], axis=0) * SCALE
    value_table, probe_parts = swap(
        "seq",
        (low(value_own), "all"),
        (jnp.broadcast_to(probe_part[None], (8, KP)), "all"),
    )
    value_table = value_table.reshape(CL, KP)
    probe_table = jnp.sum(probe_parts[:, 0].reshape(HL, S // HL, KP), axis=1)

    small_all = small_all.reshape(S, G, -1, 128)
    pieces = unpack(small_all, [R] + [dn] * len(vectors_own))
    codes = pieces[0].astype(jnp.int32)
    (
        full_query,
        full_merge_bias,
        full_lead,
        full_lead_bias,
        full_first_gain,
        full_first_shift,
        full_output_bias,
        full_second_gain,
        full_second_shift,
        full_reduce_bias,
    ) = [p.transpose(1, 0, 2).reshape(D) for p in pieces[1:]]
    joint_shift, expand_shift = unpack(slim_all, [2 * dn, fn])
    joint_shift = joint_shift.reshape(S, 2, dn).transpose(1, 0, 2).reshape(2, CL)
    expand_shift = expand_shift.reshape(FL)

    picked = jnp.where(
        segment_ids[:, None] == jnp.arange(lead_steps.shape[1])[None, :], lead_steps, 0
    )
    lead_rows = LEAD_UNIT * jnp.sum(picked, axis=1).astype(F32)

    owner = jnp.concatenate(
        [jnp.arange(VP) // PIX, jnp.arange(VARS), jnp.full((KP - VP - VARS,), VARS)]
    )
    select = (owner[:, None] == jnp.arange(VARS)[None, :]).astype(BF16)
    maps = probe_table[:, :, None] * f32(select)[None]
    maps_high = low(maps)
    maps_low = low(maps - f32(maps_high))
    scores = jnp.einsum("rk,hkv->hrv", field_rows, maps_high, preferred_element_type=F32)
    scores = scores + jnp.einsum("rk,hkv->hrv", field_rows, maps_low, preferred_element_type=F32)
    chosen = jax.nn.softmax(scores, axis=-1)
    spread = jnp.einsum("hrv,kv->hrk", low(chosen), select, preferred_element_type=F32)
    mixed = low(spread * field_wide[None])
    value_heads = value_table.reshape(HL, HDIM, KP)
    head_low = low(
        jnp.einsum("hrk,hck->rhc", mixed, value_heads, preferred_element_type=F32).reshape(RG, CL)
    )
    merged = low(dot(head_low, merge_s, 1, 0)).reshape(G, R, D)
    (merged,) = swap("grp", (merged, "each"))
    start = (
        jnp.sum(f32(merged), axis=0)
        + full_merge_bias
        + f32(position_rows)
        + lead_rows[:, None] * full_lead
        + full_lead_bias
    )
    start_hat, start_inv = norm_parts(start)
    (normed,) = swap("grp", (low(start_hat * full_first_gain + full_first_shift), "all"))
    normed = normed.reshape(RG, D)
    joint = dot(normed, joint_s, 1, 0)
    shift = jnp.concatenate([joint_shift[0], jnp.zeros((CL,), F32), joint_shift[1]])
    joint = low(joint + shift)

    if direct:
        per = pairs // S
        split = HL // per
        width = per * HDIM

        def to_pairs(x, kinds):
            x = x.reshape(G, R, kinds, split, width).transpose(0, 3, 1, 2, 4)
            (x,) = swap("seq", (x.reshape(S, R, kinds * width), "each"))
            return x.reshape(S * R, kinds, per, HDIM)

        def from_pairs(x, kinds):
            (x,) = swap("seq", (x.reshape(S, R, kinds * width), "each"))
            return (
                x.reshape(G, split, R, kinds, width)
                .transpose(0, 2, 3, 1, 4)
                .reshape(RG, kinds * CL)
            )

        mine = lax.axis_index("seq") // split
        pair_codes = lax.dynamic_index_in_dim(codes, mine, axis=1, keepdims=False).reshape(S * R)
        allowed = allowed_pairs(pair_codes, pair_codes)
        qkv = to_pairs(joint, 3)
        q, k, v = [heads_first(qkv[:, i]) for i in range(3)]
        attended = attend(q, k, v, allowed)
        attended_low = from_pairs(heads_last(low(attended)), 1)
    else:
        heads = joint.reshape(G, R, 3, HL, HDIM).transpose(0, 2, 3, 1, 4)
        everyone = lax.all_gather(heads[:, 1:], "seq", axis=3, tiled=True)
        all_codes = codes.transpose(1, 0, 2).reshape(G, S * R)
        my_codes = lax.dynamic_index_in_dim(codes, lax.axis_index("seq"), 0, keepdims=False)

        def forward_group(item):
            q, kv, query_codes, key_codes = item
            return attend(q, kv[0], kv[1], allowed_pairs(query_codes, key_codes))

        attended = lax.map(forward_group, (heads[:, 0], everyone, my_codes, all_codes))
        attended_low = low(attended).transpose(0, 2, 1, 3).reshape(RG, CL)

    branch = low(dot(attended_low, output_s, 1, 0)).reshape(G, R, D)
    (branch,) = swap("grp", (branch, "each"))
    middle = start + jnp.sum(f32(branch), axis=0) + full_output_bias
    middle_hat, middle_inv = norm_parts(middle)
    (second,) = swap("grp", (low(middle_hat * full_second_gain + full_second_shift), "all"))
    second = second.reshape(RG, D)
    hidden = dot(second, expand_s, 1, 0) + expand_shift
    inner = 0.7978845608028654 * (hidden + 0.044715 * hidden * hidden * hidden)
    bend = jnp.tanh(inner)
    active = low(0.5 * hidden * (1.0 + bend))
    slope = 0.5 * (1.0 + bend) + 0.5 * hidden * (1.0 - bend * bend) * 0.7978845608028654 * (
        1.0 + 3.0 * 0.044715 * hidden * hidden
    )
    reduced = low(dot(active, reduce_s, 1, 0)).reshape(G, R, D)

    grad_active = dot(cot_rows, reduce_s, 1, 1)
    grad_hidden = low(grad_active * slope)
    grad_second = low(dot(grad_hidden, expand_s, 1, 1)).reshape(G, R, D)
    grad_second, reduced = swap("grp", (grad_second, "each"), (reduced, "each"))
    activations = middle + jnp.sum(f32(reduced), axis=0) + full_reduce_bias
    grad_second = jnp.sum(f32(grad_second), axis=0)
    grad_top = f32(cotangent)
    grad_middle = grad_top + norm_back(middle_hat, middle_inv, full_second_gain, grad_second)
    grad_branch = low(grad_middle)

    def scatter_rows(w):
        return lax.psum_scatter(w, "seq", scatter_dimension=0, tiled=True)

    def scatter_mixed(w):
        cols = w.shape[1]
        w = w.reshape(G, S, dn, cols).transpose(1, 0, 2, 3).reshape(S, G * dn * cols // 1024, 1024)
        w = lax.psum_scatter(w, "seq", scatter_dimension=0, tiled=False)
        return w.reshape(G, dn, cols)

    grad_reduce_weight = f32(scatter_rows(low(dot(active, cot_rows, 0, 0))))
    grad_expand_mixed = scatter_mixed(low(dot(second, grad_hidden, 0, 0)))
    grad_expand_bias = low_sums(grad_hidden)

    (grad_branch_rows,) = swap("grp", (grad_branch, "all"))
    grad_branch_rows = grad_branch_rows.reshape(RG, D)
    grad_attended = low(dot(grad_branch_rows, output_s, 1, 1))
    grad_output_weight = f32(scatter_rows(low(dot(attended_low, grad_branch_rows, 0, 0))))
    if direct:
        pushed = heads_first(to_pairs(grad_attended, 1)[:, 0])
        grad_q, grad_k, grad_v = attend_back(q, k, v, allowed, pushed, attended)
        grads = [heads_last(low(x)) for x in (grad_q, grad_k, grad_v)]
        grad_joint = from_pairs(jnp.stack(grads, axis=1), 3)
    else:
        grad_heads = grad_attended.reshape(G, R, HL, HDIM).transpose(0, 2, 1, 3)

        def backward_group(item):
            q, kv, query_codes, key_codes, grad, done = item
            grad_q, grad_k, grad_v = attend_back(
                q, kv[0], kv[1], allowed_pairs(query_codes, key_codes), grad, done
            )
            return grad_q, jnp.stack([grad_k, grad_v], axis=0)

        grad_q, grad_kv = lax.map(
            backward_group,
            (heads[:, 0], everyone, my_codes, all_codes, grad_heads, attended),
        )
        grad_kv = lax.psum_scatter(grad_kv, "seq", scatter_dimension=3, tiled=True)
        grad_joint = low(jnp.concatenate([grad_q[:, None], grad_kv], axis=1))
        grad_joint = grad_joint.transpose(0, 3, 1, 2, 4).reshape(RG, 3 * CL)
    grad_normed = low(dot(grad_joint, joint_s, 1, 1)).reshape(G, R, D)
    (grad_normed,) = swap("grp", (grad_normed, "each"))
    grad_normed = jnp.sum(f32(grad_normed), axis=0)
    grad_joint_mixed = scatter_mixed(low(dot(normed, grad_joint, 0, 0)))
    joint_sums = low_sums(grad_joint)
    grad_start = grad_middle + norm_back(start_hat, start_inv, full_first_gain, grad_normed)
    grad_merged = low(grad_start)

    grad_merged_rows, grad_joint_in, grad_expand_in = swap(
        "grp", (grad_merged, "all"), (grad_joint_mixed, "each"), (grad_expand_mixed, "each")
    )
    grad_joint_weight = f32(
        grad_joint_in.reshape(G, dn, 3, CL).transpose(1, 2, 0, 3).reshape(dn, 3 * D)
    )
    grad_expand_weight = f32(grad_expand_in.transpose(1, 0, 2).reshape(dn, FF))
    grad_merged_rows = grad_merged_rows.reshape(RG, D)
    grad_head = low(dot(grad_merged_rows, merge_s, 1, 1))
    grad_merge_weight = f32(scatter_rows(low(dot(head_low, grad_merged_rows, 0, 0))))
    grad_heads_low = grad_head.reshape(RG, HL, HDIM)
    value_back = jnp.einsum(
        "rhc,hck->hrk", grad_heads_low, value_heads, preferred_element_type=F32
    )
    weighed = value_back * field_wide[None]
    weighed_high = low(weighed)
    weighed_low = low(weighed - f32(weighed_high))
    grad_chosen = jnp.einsum("hrk,kv->hrv", weighed_high, select, preferred_element_type=F32)
    grad_chosen = grad_chosen + jnp.einsum(
        "hrk,kv->hrv", weighed_low, select, preferred_element_type=F32
    )
    grad_scores = low(
        chosen * (grad_chosen - jnp.sum(chosen * grad_chosen, axis=-1, keepdims=True))
    )
    score_spread = jnp.einsum("hrv,kv->hrk", grad_scores, select, preferred_element_type=F32)
    field_part = jnp.sum(spread * value_back + score_spread * probe_table[:, None, :], axis=0)
    field_part = field_part.reshape(G, R, KP)
    score_sums = jnp.sum(score_spread * field_wide[None], axis=1)
    head_sums = jnp.einsum(
        "rhc,hrk->hck", grad_heads_low, mixed, preferred_element_type=F32
    ).reshape(S, dn, KP)

    column_sums = jnp.stack(
        [
            low_sums(grad_merged),
            jnp.sum(lead_rows[:, None] * grad_start, axis=0),
            jnp.sum(grad_start, axis=0),
            jnp.sum(grad_normed * start_hat, axis=0),
            jnp.sum(grad_normed, axis=0),
            low_sums(grad_branch),
            jnp.sum(grad_second * middle_hat, axis=0),
            jnp.sum(grad_second, axis=0),
            jnp.sum(grad_top, axis=0),
        ]
    )
    kinds = column_sums.shape[0]
    column_sums = jnp.pad(column_sums, ((0, -kinds % 16), (0, 0)))
    column_sums = column_sums.reshape(-1, G, CL).transpose(1, 0, 2)
    position_blocks = grad_merged.reshape(R, G, CL).transpose(1, 0, 2)
    column_sums, position_blocks, field_part = swap(
        "grp", (column_sums, "each"), (position_blocks, "each"), (field_part, "each")
    )
    grad_position_table = jnp.sum(f32(position_blocks), axis=0)
    field_grad = jnp.sum(field_part, axis=0)[:, :VP]
    column_sums = jnp.sum(column_sums, axis=0)
    team_sums = jnp.concatenate(
        [
            column_sums[:kinds].reshape(kinds, S, dn).transpose(1, 0, 2).reshape(S, kinds * dn),
            joint_sums[:CL].reshape(S, dn),
            joint_sums[2 * CL :].reshape(S, dn),
            grad_expand_bias.reshape(S, fn),
        ],
        axis=1,
    )
    wide = team_sums.shape[1]
    team_sums = jnp.pad(team_sums, ((0, 0), (0, -wide % 1024))).reshape(S, -1, 128)
    score_sums = jnp.pad(score_sums, ((0, -HL % 8), (0, 0)))
    team_sums, head_sums, score_sums = swap(
        "seq", (team_sums, "each"), (low(head_sums), "each"), (score_sums, "all")
    )
    team_sums = jnp.sum(team_sums, axis=0).reshape(-1)[:wide]
    own_sums = team_sums[: kinds * dn].reshape(kinds, dn)
    grad_joint_bias = team_sums[kinds * dn : (kinds + 2) * dn].reshape(2, dn)
    grad_expand_bias = team_sums[(kinds + 2) * dn :]
    (
        grad_merge_bias,
        grad_lead_weight,
        grad_lead_bias,
        grad_first_gain,
        grad_first_shift,
        grad_output_bias,
        grad_second_gain,
        grad_second_shift,
        grad_reduce_bias,
    ) = [own_sums[i] for i in range(kinds)]
    head_sums = jnp.sum(f32(head_sums), axis=0)
    score_sums = jnp.sum(score_sums, axis=0)
    my_head = lax.axis_index("seq") * dn // HDIM
    my_scores = lax.dynamic_index_in_dim(score_sums, my_head, axis=0, keepdims=False)
    grad_query_vector = jnp.sum(key_own * my_scores[None], axis=1) * SCALE
    (head_all,) = swap("seq", (low(head_sums), "all"))
    head_all, score_all = swap(
        "grp", (head_all.reshape(S * dn, KP), "all"), (score_sums, "all")
    )
    head_all = head_all.reshape(D, KP)
    score_all = score_all[:, :HL].reshape(HEADS, KP)
    grad_value_weight = dot(table, head_all, 0, 1)
    probe_own = low(
        jnp.sum((f32(key_weight) * full_query).reshape(dn, HEADS, HDIM), axis=-1) * SCALE
    )
    grad_table = dot(head_all, value_weight, 0, 1)
    grad_table = grad_table + jnp.einsum("hk,dh->kd", score_all, f32(probe_own))
    grad_probe = jnp.einsum("kd,hk->dh", f32(table), score_all)
    grad_key_weight = (
        grad_probe[:, :, None] * full_query.reshape(HEADS, HDIM)[None] * SCALE
    ).reshape(dn, D)
    grad_patch_weight = grad_table[:VP]
    grad_variable_embed = grad_table[VP : VP + VARS]
    return (
        activations,
        field_grad,
        grad_patch_weight,
        grad_variable_embed,
        grad_query_vector,
        grad_key_weight,
        grad_value_weight,
        grad_merge_weight,
        grad_merge_bias,
        grad_position_table,
        grad_lead_weight,
        grad_lead_bias,
        grad_first_gain,
        grad_first_shift,
        grad_joint_weight,
        grad_joint_bias,
        grad_output_weight,
        grad_output_bias,
        grad_second_gain,
        grad_second_shift,
        grad_expand_weight,
        grad_expand_bias,
        grad_reduce_weight,
        grad_reduce_bias,
    )


TEAM = 4
LINE = 8
ROW = 128
TALL = TEAM * ROW
GROUP = LINE * ROW
WD = D // (TEAM * LINE)
QC = D // TEAM
TEAM_HEADS = HEADS // TEAM
PACKED = 4
VECTORS = 12
QUERY, MERGE_BIAS, LEAD_WEIGHT, LEAD_BIAS, FIRST_GAIN, FIRST_SHIFT = range(6)
OUTPUT_BIAS, SECOND_GAIN, SECOND_SHIFT, REDUCE_BIAS = range(6, 10)
SUM_ROWS = 16

INPUTS = dict(
    fields=pltpu.VMEM,
    patch=pltpu.VMEM,
    embed=pltpu.VMEM,
    key_w=pltpu.VMEM,
    value_w=pltpu.VMEM,
    pack=pltpu.VMEM,
    joint_b=pltpu.VMEM,
    segments=pltpu.VMEM,
    live=pltpu.VMEM,
    steps=pltpu.SMEM,
    cot=pl.ANY,
    position=pl.ANY,
    joint_w=pl.ANY,
    expand_w=pl.ANY,
    merge_w=pl.ANY,
    output_w=pl.ANY,
    reduce_w=pl.ANY,
)

OUTPUTS = dict(
    activations=((ROW, D), F32),
    field_grad=((VP, ROW), F32),
    g_patch=((WD, VP), F32),
    g_embed=((WD, VARS), F32),
    g_key=((WD, D), F32),
    g_value=((WD, D), F32),
    g_merge=((WD, D), F32),
    g_position=((ROW, QC), F32),
    g_joint=((WD, 3 * D), F32),
    g_output=((WD, D), F32),
    g_expand=((WD, FF), F32),
    g_reduce=((ROW, D), F32),
    small=((32, 128), F32),
)

SCRATCH = dict(
    head_all=((TEAM, LINE, WD, KP), BF16),
    score_all=((TEAM, 8, KP), F32),
    score_rows=((16, KP), F32),
    key_own=((WD, KP), F32),
    sums=((SUM_ROWS, QC), F32),
    pe=((WD, KP), BF16),
    field_all=((TEAM, ROW, KP), BF16),
    pos=((ROW, D), BF16),
    cot_all=((TEAM, ROW, D), BF16),
    pack_rows=((16, 128), F32),
    pack_all=((LINE, TEAM, 16, 128), BF16),
    vecs=((16, D), F32),
    shift_e=((8, D), F32),
    seg_q=((16, GROUP), BF16),
    seg_k=((16, GROUP), BF16),
    merge_s=((LINE, WD, D), BF16),
    output_s=((LINE, WD, D), BF16),
    reduce_s=((LINE, ROW, D), BF16),
    joint_s=((TEAM, LINE, WD, 3 * QC), BF16),
    expand_s=((TEAM, LINE, WD, D), BF16),
    e2_send=((2, LINE, WD, KP), BF16),
    e2_recv=((LINE, 2, WD, KP), BF16),
    pv=((LINE, WD, KP), BF16),
    at=((LINE, 8, KP), F32),
    probe=((8, KP), F32),
    select=((KP, 128), BF16),
    select_t=((128, KP), BF16),
    chosen=((TEAM_HEADS, TALL, 128), F32),
    head_low=((TALL, QC), BF16),
    start=((ROW, D), F32),
    start_hat=((ROW, D), F32),
    start_inv=((ROW, 128), F32),
    middle=((ROW, D), F32),
    middle_hat=((ROW, D), F32),
    middle_inv=((ROW, 128), F32),
    grad_mid=((ROW, D), F32),
    normed_all=((TEAM, ROW, D), BF16),
    second_all=((TEAM, ROW, D), BF16),
    gb_all=((TEAM, ROW, D), BF16),
    gm_all=((TEAM, ROW, D), BF16),
    pair_send=((LINE, 3, ROW, 128), BF16),
    qkv=((3, GROUP, 128), BF16),
    p_low=((2, GROUP, GROUP), BF16),
    att_f=((GROUP, 128), F32),
    att_low=((GROUP, 128), BF16),
    att_all=((TEAM, ROW, QC), BF16),
    g_send=((TEAM, 2, ROW, 128), BF16),
    go=((GROUP, 128), BF16),
    dq=((GROUP, 128), F32),
    d_all=((TEAM, 3, ROW, QC), BF16),
    active_all=((TEAM, ROW, D), BF16),
    gh_all=((TEAM, ROW, D), BF16),
    own_a=((ROW, D), F32),
    own_b=((ROW, D), F32),
    far_a=((ROW, D), F32),
    far_b=((ROW, D), F32),
    far_d=((ROW, D), F32),
    gw_merge=((LINE, WD, D), BF16),
    gw_output=((LINE, WD, D), BF16),
    gw_reduce=((LINE, ROW, D), BF16),
    gw_joint=((TEAM, LINE, WD, 3 * QC), BF16),
    gw_expand=((TEAM, LINE, WD, D), BF16),
    yr_merge=((4, WD, D), BF16),
    yr_output=((4, WD, D), BF16),
    yr_reduce=((4, ROW // 2, D), BF16),
    yr_half=((1, ROW // 2, D), BF16),
    zr_half=((6, ROW // 2, D), BF16),
    za_half=((4, ROW // 2, D), BF16),
    yr_joint=((4, TEAM, WD, 3 * QC), BF16),
    yr_expand=((4, TEAM, WD, D), BF16),
    zr_merge=((3, WD, D), BF16),
    za_merge=((2, WD, D), BF16),
    zr_output=((3, WD, D), BF16),
    za_output=((2, WD, D), BF16),
    zr_reduce=((3, ROW // 2, D), BF16),
    za_reduce=((2, ROW // 2, D), BF16),
    zr_joint=((3, TEAM, WD, 3 * QC), BF16),
    za_joint=((2, TEAM, WD, 3 * QC), BF16),
    zr_expand=((3, TEAM, WD, D), BF16),
    za_expand=((2, TEAM, WD, D), BF16),
    xs_joint=((TEAM, WD, 3 * QC), BF16),
    xs_expand=((TEAM, WD, D), BF16),
    xr_joint=((TEAM, WD, 3 * QC), BF16),
    xr_expand=((TEAM, WD, D), BF16),
    csum=((16, D), F32),
    crecv=((TEAM, 16, QC), F32),
    tsum=((LINE, SUM_ROWS, QC), F32),
    f_own=((TEAM, ROW, KP), F32),
    f_recv=((3, ROW, KP), F32),
    t_send=((LINE, WD, KP), BF16),
    t_recv=((LINE, WD, KP), BF16),
    q_all=((LINE, 8, KP), F32),
)

TEAM_SUMS = dict(
    both=(2 * QC, KP),
    merge=(ROW, D),
    branch=(ROW, D),
    second=(ROW, D),
    reduced=(ROW, D),
    normed=(ROW, D),
)


def team_sum_buffers(shape):
    near = ((2,) + shape, BF16)
    one = (shape, BF16)
    return (near, near, one, one)


SEMAPHORES = 252


def nn(a, b):
    return dot(a, b, 1, 0)


def nt(a, b):
    return dot(a, b, 1, 1)


def tn(a, b):
    return dot(a, b, 0, 0)


def lanes(at, size):
    return pl.ds(pl.multiple_of(at, 128), size)


def rows(at, size):
    return pl.ds(pl.multiple_of(at, size), size)


def fused_kernel(*refs):
    n_in, n_out = len(INPUTS), len(OUTPUTS)
    results = types.SimpleNamespace(**dict(zip(OUTPUTS, refs[n_in : n_in + n_out])))
    names = list(INPUTS) + list(SCRATCH) + list(OUTPUTS)
    rest = refs[:n_in] + refs[n_in + n_out :]
    ref = types.SimpleNamespace(**dict(zip(names, rest)))
    rest = rest[len(names) :]
    send, recv = rest[-2:]
    sums = dict(zip(TEAM_SUMS, [rest[4 * i : 4 * i + 4] for i in range(len(TEAM_SUMS))]))
    sums = types.SimpleNamespace(**sums)
    g = lax.axis_index("grp")
    s = lax.axis_index("seq")
    sib = g + 1 - 2 * lax.rem(g, 2)
    far = lax.rem(g + 2, TEAM)
    diag = lax.rem(sib + 2, TEAM)
    z = s // 2
    y = s - 2 * z
    beside = s + 1 - 2 * y
    mine = lax.rem(3 * z, TEAM)
    is_middle = (z == 1) | (z == 2)
    is_end = (z == 0) | (z == 3)
    partner = s + 2 - 4 * lax.rem(z, 2)
    facing = lax.rem(s + 6 - 4 * z + LINE, LINE)
    near_places = [4 * (z // 2) + y + 2 * i for i in range(2)]
    far_places = [4 * (1 - z // 2) + y + 2 * i for i in range(2)]

    def to_team(j):
        return (j, s)

    def to_line(j):
        return (g, j)

    used = [0]
    begun = []

    def reserve(count):
        at = used[0]
        used[0] += count
        assert used[0] <= SEMAPHORES
        return at

    def remote(src, dst, device, at):
        return pltpu.make_async_remote_copy(
            src_ref=src,
            dst_ref=dst,
            send_sem=send.at[at],
            recv_sem=recv.at[at],
            device_id=device,
            device_id_type=MESH,
        )

    def push(src, dst, device):
        copy = remote(src, dst, device, reserve(1))
        copy.start()
        begun.append(copy)
        return copy

    barrier = pltpu.get_barrier_semaphore()
    for step in range(1, TEAM):
        pl.semaphore_signal(
            barrier, inc=1, device_id=to_team(lax.rem(g + step, TEAM)), device_id_type=MESH
        )
    for step in range(1, LINE):
        pl.semaphore_signal(
            barrier, inc=1, device_id=to_line(lax.rem(s + step, LINE)), device_id_type=MESH
        )

    class Together:
        def __init__(self, bulk, waits_itself=False):
            self.bulk, self.at = bulk, reserve(1)
            if not waits_itself:
                begun_together.append(self)

        def push(self, src, dst, device):
            remote(src, dst, device, self.at).start()

        def wait_recv(self):
            remote(self.bulk, self.bulk, to_line(beside), self.at).wait_recv()

        def wait_send(self):
            remote(self.bulk, self.bulk, to_line(beside), self.at).wait_send()

    begun_together = []

    def spread(buf):
        half = buf.shape[1] // 2
        across = []
        for h in range(2):
            part = buf.at[g, pl.ds(h * half, half)]
            across.append(push(part, part, to_team(far)))
        return push(buf.at[g], buf.at[g], to_team(sib)), across

    def spread_on(buf, across):
        half = buf.shape[1] // 2
        handed = Together(buf.at[far])
        for h in range(2):
            across[h].wait_recv()
            part = buf.at[far, pl.ds(h * half, half)]
            handed.push(part, part, to_team(sib))
        return [handed]

    def wait_all(copies):
        for copy in copies:
            copy.wait_recv()

    class TeamSum:
        def __init__(self, buffers):
            self.ps, self.r, self.t, self.x = buffers
            self.near_copies = [None, None]

        def near(self, slot, value=None):
            if value is not None:
                self.ps[slot] = low(value)
            self.near_copies[slot] = push(self.ps.at[slot], self.r.at[slot], to_team(sib))

        def across(self, value):
            self.near_copies[1].wait_recv()
            half = self.t.shape[0] // 2
            self.far_copies = [Together(self.x)]
            for h in range(2):
                part = pl.ds(h * half, half)
                self.t[part] = low(value(part) + f32(self.r[1, part]))
                self.far_copies[0].push(self.t.at[part], self.x.at[part], to_team(far))

        def total(self, own):
            self.near_copies[0].wait_recv()
            wait_all(self.far_copies)
            return own + f32(self.r[0]) + f32(self.x[...])

    deposits = []

    def deposit(src, dst):
        copy = pltpu.make_async_copy(src, dst, recv.at[reserve(1)])
        copy.start()
        deposits.append(copy)

    def to_whole_line(src, dst, bulk):
        group = Together(bulk)
        for step in range(1, LINE):
            place = lax.rem(s + step, LINE)
            group.push(src(place), dst, to_line(place))
        return [group]

    def share_line(buf):
        return to_whole_line(lambda place: buf.at[s], buf.at[s], buf.at[pl.ds(0, LINE - 1)])

    def to_whole_team(src, dst, bulk):
        group = Together(bulk)
        for j in (far, diag, sib):
            group.push(src(j), dst, to_team(j))
        return [group]

    def mean(x):
        return jnp.sum(x, axis=-1, keepdims=True) * (1.0 / D)

    class Gather:
        def __init__(self, slot):
            self.slot = slot
            self.at = reserve(9)

        def send(self, place, device, i, shard=None):
            part = self.slot(place)
            remote(part if shard is None else shard, part, device, self.at + i).start()

        def come(self, i):
            part = self.slot(s)
            remote(part, part, to_line(beside), self.at + i).wait_recv()

        def stage1(self, shard=None):
            self.send(s, to_line(partner), 0, shard)
            self.send(s, to_line(beside), 1, shard)

        def stage2(self, hold=False):
            self.come(0)

            @pl.when(is_middle)
            def _():
                for i in range(2):
                    self.send(near_places[i], to_line(facing), 2 + i)

            if not hold:
                self.hand_on()

        def hand_on(self):
            self.send(partner, to_line(beside), 4)

        def stage3(self):
            @pl.when(is_middle)
            def _():
                for i in range(2):
                    self.come(2 + i)
                    self.send(far_places[i], to_line(partner), 5 + i)
                    self.send(far_places[i], to_line(beside), 7 + i)

        def stage4(self):
            @pl.when(is_end)
            def _():
                for i in range(2):
                    self.come(5 + i)
                    self.send(far_places[i], to_line(beside), 7 + i)

        def finish(self):
            for i in (1, 4, 7, 8):
                self.come(i)

        def sent(self):
            part = self.slot(s)

            def gone(i):
                remote(part, part, to_line(beside), self.at + i).wait_send()

            for i in (0, 1, 4, 7, 8):
                gone(i)

            @pl.when(is_middle)
            def _():
                for i in (2, 3, 5, 6):
                    gone(i)

    class PairExchange:
        def __init__(self, bulk):
            self.group, self.own = Together(bulk, waits_itself=True), reserve(1)

        def send(self, src, dst, there):
            @pl.when(there != s)
            def _():
                self.group.push(src, dst, to_line(there))

            @pl.when(there == s)
            def _():
                pltpu.make_async_copy(src, dst, recv.at[self.own]).start()

        def wait(self, src, dst):
            pltpu.make_async_copy(src, dst, recv.at[self.own]).wait()
            self.group.wait_recv()
            self.group.wait_send()

    pe = ref.pe
    pe[:, 0:VP] = ref.patch[...]
    pe[:, VP : VP + VARS] = ref.embed[...]
    pe[:, VP + VARS :] = jnp.zeros((WD, KP - VP - VARS), BF16)
    field_all, cot_all, pack_all = ref.field_all, ref.cot_all, ref.pack_all
    field_all[g, :, 0:VP] = ref.fields[...].T
    lane = lax.broadcasted_iota(jnp.int32, (ROW, KP - VP), 1)
    field_all[g, :, VP:] = (lane < VARS).astype(BF16)
    pack_rows = ref.pack_rows
    pack_rows[...] = f32(ref.pack[...])
    for i in range(2):
        pack_rows[2:3, 64 + i * WD : 64 + (i + 1) * WD] = f32(ref.joint_b[...])[i : i + 1]
    pack_rows[4:5] = ref.segments[...].astype(F32)
    pack_rows[5:6] = ref.live[...].astype(F32)
    pack_all[s, g] = low(pack_rows[...])
    pl.semaphore_wait(barrier, TEAM - 1 + LINE - 1)

    both = TeamSum(sums.both)

    def table_product(weight, j):
        return tn(weight[:, lanes(j * QC, QC)], pe[...])

    for slot, j in ((1, diag), (0, sib)):
        both.ps[slot, 0:QC] = low(table_product(ref.value_w, j))
        both.ps[slot, QC:] = low(table_product(ref.key_w, j))
        both.near(slot)
    field_copies = spread(field_all)
    far_parts = [table_product(ref.value_w, far), table_product(ref.key_w, far)]
    both.across(lambda part: far_parts[0] if part.start == 0 else far_parts[1])
    own_parts = [table_product(ref.value_w, g), table_product(ref.key_w, g)]
    pack_here = pack_all.at[s, g]
    pack_copies = to_whole_team(lambda j: pack_here, pack_here, pack_all.at[0, pl.ds(0, 3)])

    def whole(buf):
        return lambda i: buf.at[i]

    def inner(buf):
        return lambda i: buf.at[:, i]

    def some_rows(buf, at, size):
        return lambda i: buf.at[i, pl.ds(at, size)]

    def some_lanes(buf, at, size):
        return lambda i: buf.at[:, i, :, pl.ds(at, size)]

    half_rows, half_lanes = ROW // 2, D // 2
    gather_merge = Gather(whole(ref.merge_s))
    gather_output = Gather(whole(ref.output_s))
    gather_reduce = [Gather(some_rows(ref.reduce_s, i * half_rows, half_rows)) for i in range(2)]
    gather_joint = [Gather(some_lanes(ref.joint_s, i * QC, QC)) for i in range(3)]
    gather_expand = [Gather(some_lanes(ref.expand_s, i * half_lanes, half_lanes)) for i in range(2)]
    local = []

    def keep(src, dst):
        copy = pltpu.make_async_copy(src, dst, recv.at[reserve(1)])
        copy.start()
        local.append(copy)

    keep(ref.merge_w, ref.merge_s.at[s])
    keep(ref.output_w, ref.output_s.at[s])
    keep(ref.reduce_w, ref.reduce_s.at[s])
    keep(ref.cot, cot_all.at[g])
    gather_merge.stage1(ref.merge_w)
    for i in range(2):
        gather_reduce[i].stage1(ref.reduce_w.at[pl.ds(i * half_rows, half_rows)])

    joint_copies = [Together(ref.joint_s.at[pl.ds(0, 3), 0])]
    for j in (far, diag, sib):
        for kind in range(3):
            joint_copies[0].push(
                ref.joint_w.at[:, lanes(kind * D + j * QC, QC)],
                ref.joint_s.at[g, s, :, pl.ds(kind * QC, QC)],
                to_team(j),
            )
    for kind in range(3):
        keep(
            ref.joint_w.at[:, lanes(kind * D + g * QC, QC)],
            ref.joint_s.at[g, s, :, pl.ds(kind * QC, QC)],
        )
    expand_copies = to_whole_team(
        lambda j: ref.expand_w.at[:, lanes(j * D, D)],
        ref.expand_s.at[g, s],
        ref.expand_s.at[pl.ds(0, 3), 0],
    )
    keep(ref.expand_w.at[:, lanes(g * D, D)], ref.expand_s.at[g, s])
    keep(ref.position, ref.pos.at[:, lanes(g * QC, QC)])
    position_copies = to_whole_team(
        lambda j: ref.position, ref.pos.at[:, lanes(g * QC, QC)], ref.pos.at[:, pl.ds(0, 3 * QC)]
    )

    for copy in local:
        copy.wait()
    gather_merge.stage2()

    both.near_copies[0].wait_recv()
    wait_all(both.far_copies)
    for part in range(2):
        block = pl.ds(part * QC, QC)
        total = own_parts[part] + f32(both.r[0, block]) + f32(both.x[block])
        ref.e2_send[part] = low(total).reshape(LINE, WD, KP)
    e2_send, e2_recv = ref.e2_send, ref.e2_recv
    e2_copies = to_whole_line(
        lambda place: e2_send.at[:, place], e2_recv.at[s], e2_recv.at[pl.ds(0, LINE - 1)]
    )
    e2_recv[s] = e2_send[:, s]
    wait_all(joint_copies)
    for gather in gather_joint:
        gather.stage1()
    gather_merge.stage3()

    wait_all(e2_copies)
    table_own = jnp.sum(f32(e2_recv[...]), axis=0)
    key_own = table_own[1]
    ref.key_own[...] = key_own
    query = f32(pack_all[s, g])[0:1, 0:WD]
    key_high = low(key_own)
    key_rest = low(key_own - f32(key_high))
    query_rows = low(jnp.broadcast_to(query, (16, WD)))
    probe_part = (nn(query_rows, key_high) + nn(query_rows, key_rest)) * SCALE
    pv, at = ref.pv, ref.at
    pv[s] = low(table_own[0])
    at[s] = probe_part[0:8]
    pv_copies = share_line(pv)
    at_copies = to_whole_line(
        lambda place: at.at[s, pl.ds(0, 1)],
        at.at[s, pl.ds(0, 1)],
        at.at[pl.ds(0, LINE - 1), pl.ds(0, 1)],
    )
    for gather in gather_joint:
        gather.stage2()
    wait_all(pv_copies)
    wait_all(at_copies)
    gather_merge.stage4()
    wait_all(pack_copies)
    pack_line = share_line(pack_all)
    wait_all(expand_copies)
    for gather in gather_expand:
        gather.stage1()

    probe = ref.probe
    for h in range(TEAM_HEADS):
        probe[h : h + 1] = at[2 * h, 0:1] + at[2 * h + 1, 0:1]
    probe[TEAM_HEADS:] = jnp.zeros((8 - TEAM_HEADS, KP), F32)

    def owner_of(k):
        return jnp.where(k < VP, k // PIX, jnp.where(k < VP + VARS, k - VP, VARS + 64))

    select, select_t = ref.select, ref.select_t
    select[...] = (
        owner_of(lax.broadcasted_iota(jnp.int32, (KP, 128), 0))
        == lax.broadcasted_iota(jnp.int32, (KP, 128), 1)
    ).astype(BF16)
    select_t[...] = (
        owner_of(lax.broadcasted_iota(jnp.int32, (128, KP), 1))
        == lax.broadcasted_iota(jnp.int32, (128, KP), 0)
    ).astype(BF16)
    valid = lax.broadcasted_iota(jnp.int32, (1, 128), 1) < VARS
    head_of_lane = lax.broadcasted_iota(jnp.int32, (1, QC), 1) // HDIM

    field_handed = spread_on(field_all, field_copies[1])
    field_copies[0].wait_recv()
    wait_all(field_handed)

    def tall(buf):
        return buf[...].reshape(TALL, -1)

    def split_dot(x, b):
        high = low(x)
        return nn(high, b) + nn(low(x - f32(high)), b)

    chosen, head_low = ref.chosen, ref.head_low

    def choose(h):
        field = f32(tall(field_all))
        scores = split_dot(field * probe[h : h + 1], select[...])
        scores = jnp.where(valid, scores, MASKED)
        terms = jnp.exp(scores - jnp.max(scores, axis=-1, keepdims=True))
        weights = terms * (1.0 / jnp.sum(terms, axis=-1, keepdims=True))
        chosen[h] = weights
        mix = low(nn(low(weights), select_t[...]) * field)
        table_value = pv[2 * h : 2 * h + 2].reshape(HDIM, KP)
        head_low[:, h * HDIM : (h + 1) * HDIM] = low(nt(mix, table_value))

    for h in range(TEAM_HEADS):
        choose(h)

    merge_s, output_s = ref.merge_s, ref.output_s
    gather_merge.finish()
    merge = TeamSum(sums.merge)

    def row_weight(buf):
        return buf[...].reshape(-1, D)

    def two(buf, i, j):
        return jnp.concatenate([buf[i], buf[j]], axis=0)

    def merge_part(j):
        return nn(head_low[rows(j * ROW, ROW)], row_weight(merge_s))

    merge.near(1, merge_part(diag))
    ref.far_a[...] = merge_part(far)
    merge.across(lambda part: ref.far_a[part])
    merge.near(0, merge_part(sib))
    ref.own_a[...] = merge_part(g)

    wait_all(pack_line)
    vecs, shift_e = ref.vecs, ref.shift_e
    lane_piece = lax.broadcasted_iota(jnp.int32, (LINE, 1, QC), 2) // WD
    piece = lax.broadcasted_iota(jnp.int32, (LINE, 1, QC), 0)
    for q in range(PACKED):
        place = (
            lax.broadcasted_iota(jnp.int32, (128, QC), 1) % WD + q * WD
            == lax.broadcasted_iota(jnp.int32, (128, QC), 0)
        ).astype(BF16)
        for j in range(TEAM):
            spreadout = nn(pack_all[:, j].reshape(LINE * 16, 128), place)
            spreadout = jnp.where(lane_piece == piece, spreadout.reshape(LINE, 16, QC), 0.0)
            spreadout = jnp.sum(spreadout, axis=0)
            vecs[4 * q : 4 * q + 4, j * QC : (j + 1) * QC] = spreadout[0:4]

    def vector(i):
        at_row = 4 * (i % PACKED) + i // PACKED
        return vecs[at_row : at_row + 1, :]

    joint_shift = [
        vecs[4 * (i % PACKED) + i // PACKED, lanes(g * QC, QC)].reshape(1, QC) for i in (10, 11)
    ]
    seg_q, seg_k = ref.seg_q, ref.seg_k
    sub = lax.broadcasted_iota(jnp.int32, (16, 128), 0).astype(F32)
    for j in range(LINE):
        part = f32(pack_all[j, g])
        shift_e[:, j * 128 : (j + 1) * 128] = jnp.broadcast_to(part[3:4], (8, 128))
        part = f32(pack_all[j, mine])
        same = jnp.where(sub == part[4:5], 1.0, 0.0)
        seg_q[:, j * 128 : (j + 1) * 128] = low(same)
        seg_k[:, j * 128 : (j + 1) * 128] = low(same * part[5:6])
    own_seg = ref.segments[...].astype(F32)
    steps = ref.steps
    lead_lanes = jnp.zeros((1, 128), F32)
    for i in range(steps.shape[1]):
        lead_lanes = jnp.where(own_seg == i, LEAD_UNIT * steps[0, i].astype(F32), lead_lanes)
    lead = jnp.broadcast_to(lead_lanes, (ROW, 128)).T[:, 0:1]
    wait_all(position_copies)
    for gather in gather_joint:
        gather.stage3()
    gather_output.stage1(ref.output_w)
    for gather in gather_reduce:
        gather.stage2(hold=True)

    start_ref = ref.start
    start_ref[...] = (
        merge.total(ref.own_a[...])
        + vector(MERGE_BIAS)
        + f32(ref.pos[...])
        + lead * vector(LEAD_WEIGHT)
        + vector(LEAD_BIAS)
    )

    def norm(x, hat_ref, inv_ref, gain, shift):
        center = x - mean(x)
        inverse = lax.rsqrt(mean(center * center) + EPSILON)
        hat = center * inverse
        hat_ref[...] = hat
        inv_ref[...] = jnp.broadcast_to(inverse, (ROW, 128))
        return low(hat * gain + shift)

    def norm_back_ref(grad, hat_ref, inv_ref, gain):
        f = grad * gain
        hat = hat_ref[...]
        return inv_ref[:, 0:1] * (f - mean(f) - hat * mean(f * hat))

    normed_all = ref.normed_all
    normed_all[g] = norm(
        start_ref[...],
        ref.start_hat,
        ref.start_inv,
        vector(FIRST_GAIN),
        vector(FIRST_SHIFT),
    )
    normed_copies = spread(normed_all)
    joint_s, pair_send, qkv = ref.joint_s, ref.pair_send, ref.qkv
    for gather in gather_joint:
        gather.stage4()
    e6 = [PairExchange(qkv.at[kind, pl.ds(0, 7 * ROW), :]) for kind in range(3)]

    def pair_place(j, t):
        return 2 * lax.rem(3 * j, TEAM) + t

    line_rows = rows(s * ROW, ROW)

    def joint_rows(i, j):
        block = two(normed_all, i, j)
        for kind in range(3):
            if i is g:
                gather_joint[kind].finish()
            weight = joint_s[:, :, :, kind * QC : (kind + 1) * QC].reshape(D, QC)
            part = nn(block, weight)
            if kind != 1:
                part = part + joint_shift[kind // 2]
            part = low(part)
            for n, group in enumerate((i, j)):
                for t in range(2):
                    place = pair_place(group, t)
                    pair_send[place, kind] = part[n * ROW : (n + 1) * ROW, t * 128 : (t + 1) * 128]
                    e6[kind].send(pair_send.at[place, kind], qkv.at[kind, line_rows, :], place)

    normed_copies[0].wait_recv()
    joint_rows(g, sib)
    normed_handed = spread_on(normed_all, normed_copies[1])
    wait_all(normed_handed)
    joint_rows(far, diag)
    gather_output.stage2()
    gather_expand[0].stage2()
    for gather in gather_reduce:
        gather.hand_on()
        gather.stage3()
    for kind in range(3):
        e6[kind].wait(pair_send.at[0, kind], qkv.at[kind, line_rows, :])
    gather_output.stage3()
    gather_expand[1].stage2()
    cot_copies = spread(cot_all)

    half_of_lane = lax.broadcasted_iota(jnp.int32, (1, 128), 1) // HDIM
    p_low, att_f, att_low, att_all = ref.p_low, ref.att_f, ref.att_low, ref.att_all
    e7 = PairExchange(att_low.at[pl.ds(0, 7 * ROW)])
    pair_lanes = lanes(y * 128, 128)

    def attend_rows(b, carry):
        here = rows(b * 256, 256)
        queries = f32(qkv[0, here, :]) * SCALE
        keys, values = qkv[1], qkv[2]
        allowed = tn(seg_q[:, lanes(b * 256, 256)], seg_k[...]) > 0.5
        outs = []
        for t in range(2):
            scores = nt(low(jnp.where(half_of_lane == t, queries, 0.0)), keys)
            scores = jnp.where(allowed, scores, MASKED)
            terms = jnp.exp(scores - jnp.max(scores, axis=-1, keepdims=True))
            weights = low(terms * (1.0 / jnp.sum(terms, axis=-1, keepdims=True)))
            p_low[t, here, :] = weights
            outs.append(nn(weights, values))
        out = jnp.where(half_of_lane == 0, outs[0], outs[1])
        att_f[here] = out
        att_low[here] = low(out)
        for t in range(2):
            there = 2 * b + t
            e7.send(att_low.at[rows(there * ROW, ROW)], att_all.at[mine, :, pair_lanes], there)

        return carry

    lax.fori_loop(0, GROUP // 256, attend_rows, 0, unroll=2)
    gather_output.stage4()
    for gather in gather_reduce:
        gather.stage4()
    for gather in gather_expand:
        gather.stage3()
    gather_output.finish()
    e7.wait(att_low.at[pl.ds(0, ROW)], att_all.at[mine, :, pair_lanes])

    branch = TeamSum(sums.branch)

    def branch_part(j):
        return nn(att_all[j], row_weight(output_s))

    branch.near(1, branch_part(diag))
    ref.far_a[...] = branch_part(far)
    branch.across(lambda part: ref.far_a[part])
    branch.near(0, branch_part(sib))
    ref.own_a[...] = branch_part(g)
    cot_handed = spread_on(cot_all, cot_copies[1])
    gather_expand[0].stage4()
    middle_ref = ref.middle
    middle_ref[...] = branch.total(ref.own_a[...]) + start_ref[...] + vector(OUTPUT_BIAS)

    class LineSum:
        def __init__(self, four, slot, yr, zr, za):
            self.four = four
            self.slot, self.yr, self.zr, self.za = slot, yr, zr, za
            self.at = reserve(6)

        def send(self, src, dst, device, i):
            remote(src, dst, device, self.at + i).start()

        def come(self, i):
            part = self.zr(0)
            remote(part, part, to_line(beside), self.at + i).wait_recv()

        def along_y(self):
            self.y_copies = Together(self.four)
            for i in range(4):
                self.y_copies.push(self.slot(2 * i + 1 - y), self.yr(i), to_line(beside))

        def add(self, place, came):
            block = self.slot(place)
            block[...] = low(f32(block[...]) + f32(came[...]))
            return block

        def sum_y(self):
            self.y_copies.wait_recv()

            def add(i, carry):
                self.add(2 * i + y, self.yr(i))
                return carry

            lax.fori_loop(0, 4, add, 0)

        def stage1(self):
            @pl.when(is_end)
            def _():
                for i, place in enumerate(far_places + [partner]):
                    self.send(self.slot(place), self.zr(i), to_line(partner), i)

        def stage2(self):
            @pl.when(is_middle)
            def _():
                for i, place in enumerate(far_places):
                    self.come(i)
                    block = self.add(place, self.zr(i))
                    self.send(block, self.za(i), to_line(facing), 3 + i)

        def stage3(self):
            @pl.when(is_middle)
            def _():
                for i in range(2):
                    self.come(3 + i)
                block = self.add(partner, self.za(1 - lax.rem(z, 2)))
                self.send(block, self.zr(0), to_line(partner), 5)

        def total(self, out):
            own = f32(self.slot(s)[...])

            @pl.when(is_middle)
            def _():
                self.come(2)
                total = own + f32(self.zr(2)[...]) + f32(self.za(lax.rem(z, 2))[...])
                out[...] = total.astype(out.dtype)

            @pl.when(is_end)
            def _():
                self.come(5)
                out[...] = (own + f32(self.zr(0)[...])).astype(out.dtype)

        def sent(self):
            part = self.zr(0)

            def gone(i):
                remote(part, part, to_line(beside), self.at + i).wait_send()

            @pl.when(is_middle)
            def _():
                for i in (3, 4, 5):
                    gone(i)

            @pl.when(is_end)
            def _():
                for i in range(3):
                    gone(i)

    class LineSumZ:
        def __init__(self, slot, zr, za, yr):
            self.slot, self.zr, self.za, self.yr = slot, zr, za, yr
            self.at = reserve(13)

        def both_y(self, place):
            return [place - y, place - y + 1]

        def send(self, src, dst, device, i):
            remote(src, dst, device, self.at + i).start()

        def come(self, i):
            part = self.zr(0)
            remote(part, part, to_line(beside), self.at + i).wait_recv()

        def add(self, place, came):
            block = self.slot(place)
            block[...] = low(f32(block[...]) + f32(came[...]))
            return block

        def stage1(self):
            @pl.when(is_end)
            def _():
                for i, place in enumerate(
                    self.both_y(far_places[0]) + self.both_y(far_places[1]) + self.both_y(partner)
                ):
                    self.send(self.slot(place), self.zr(i), to_line(partner), i)

        def stage2(self):
            @pl.when(is_middle)
            def _():
                for i, place in enumerate(self.both_y(far_places[0]) + self.both_y(far_places[1])):
                    self.come(i)
                    block = self.add(place, self.zr(i))
                    self.send(block, self.za(i), to_line(facing), 6 + i)

        def stage3(self):
            @pl.when(is_middle)
            def _():
                for i in range(4):
                    self.come(6 + i)
                for i, place in enumerate(self.both_y(partner)):
                    block = self.add(place, self.za(2 * (1 - lax.rem(z, 2)) + i))
                    self.send(block, self.zr(i), to_line(partner), 10 + i)
                for i, place in enumerate(self.both_y(s)):
                    self.come(4 + i)
                    self.add(place, self.zr(4 + i))
                    self.add(place, self.za(2 * lax.rem(z, 2) + i))

        def along_y(self):
            @pl.when(is_end)
            def _():
                for i, place in enumerate(self.both_y(s)):
                    self.come(10 + i)
                    self.add(place, self.zr(i))

            self.send(self.slot(beside), self.yr(0), to_line(beside), 12)

        def total(self, out):
            self.come(12)
            out[...] = f32(self.slot(s)[...]) + f32(self.yr(0)[...])

        def sent(self):
            part = self.zr(0)

            def gone(i):
                remote(part, part, to_line(beside), self.at + i).wait_send()

            gone(12)

            @pl.when(is_middle)
            def _():
                for i in (6, 7, 8, 9, 10, 11):
                    gone(i)

            @pl.when(is_end)
            def _():
                for i in range(6):
                    gone(i)

    def line_sum_of(gw, others, at=None, size=None):
        four = others[0]
        if at is None:
            return LineSum(four, whole(gw), *[whole(buf) for buf in others])
        if len(gw.shape) == 3:
            return LineSum(four, some_rows(gw, at, size), *[whole(buf) for buf in others])

        def part(buf):
            return lambda i: buf.at[i, :, :, pl.ds(at, size)]

        four = four.at[:, :, :, pl.ds(at, size)]
        return LineSum(four, some_lanes(gw, at, size), *[part(buf) for buf in others])

    output_sum = line_sum_of(ref.gw_output, [ref.yr_output, ref.zr_output, ref.za_output])
    merge_sum = line_sum_of(ref.gw_merge, [ref.yr_merge, ref.zr_merge, ref.za_merge])
    reduce_y = line_sum_of(
        ref.gw_reduce, [ref.yr_reduce, ref.zr_reduce, ref.za_reduce], 0, half_rows
    )
    reduce_z = LineSumZ(
        some_rows(ref.gw_reduce, half_rows, half_rows),
        whole(ref.zr_half),
        whole(ref.za_half),
        whole(ref.yr_half),
    )
    reduce_sums = [reduce_y, reduce_z]
    expand_sums = [
        line_sum_of(
            ref.gw_expand,
            [ref.yr_expand, ref.zr_expand, ref.za_expand],
            i * half_lanes,
            half_lanes,
        )
        for i in range(2)
    ]
    joint_sums = [
        line_sum_of(ref.gw_joint, [ref.yr_joint, ref.zr_joint, ref.za_joint], i * QC, QC)
        for i in range(3)
    ]

    second_all = ref.second_all
    second_all[g] = norm(
        middle_ref[...],
        ref.middle_hat,
        ref.middle_inv,
        vector(SECOND_GAIN),
        vector(SECOND_SHIFT),
    )
    second_copies = spread(second_all)
    for gather in [gather_expand[0]] + gather_reduce:
        gather.finish()
    cot_copies[0].wait_recv()
    wait_all(cot_handed)
    expand_s, reduce_s = ref.expand_s, ref.reduce_s
    active_all, gh_all = ref.active_all, ref.gh_all
    root = 0.7978845608028654

    def feed(j, k, acc_a, acc_b, half):
        def tile(i, carry):
            here = lanes(i * 256, 256)
            up = expand_s[:, :, :, here].reshape(D, 256)
            down = reduce_s[pl.ds(2 * i, 2)].reshape(256, D)
            hidden = nn(two(second_all, j, k), up) + shift_e[0:1, here]
            square = hidden * hidden
            bend = jnp.tanh(root * hidden * (1.0 + 0.044715 * square))
            active = low(0.5 * hidden * (1.0 + bend))
            slope = 0.5 * (1.0 + bend) + (0.5 * root) * hidden * (1.0 - bend * bend) * (
                1.0 + (3.0 * 0.044715) * square
            )
            grad = low(nt(two(cot_all, j, k), down) * slope)
            for n, block in enumerate((j, k)):
                active_all[block, :, here] = active[n * ROW : (n + 1) * ROW]
                gh_all[block, :, here] = grad[n * ROW : (n + 1) * ROW]
            for part, acc in ((nt(grad, up), acc_a), (nn(active, down), acc_b)):
                for n in range(2):
                    rows_of = part[n * ROW : (n + 1) * ROW]

                    @pl.when(i == 0)
                    def _():
                        acc[n][...] = rows_of

                    @pl.when(i > 0)
                    def _():
                        acc[n][...] += rows_of

            return carry

        lax.fori_loop(2 * half, 2 * half + 2, tile, 0, unroll=True)

    gw_expand = ref.gw_expand

    def expand_blocks(first, last, half):
        def block(i, carry):
            lhs = second_all[:, :, lanes(i * QC, QC)].reshape(TALL, QC)
            rhs = gh_all[:, :, half * half_lanes : (half + 1) * half_lanes].reshape(TALL, half_lanes)
            part = low(tn(lhs, rhs)).reshape(LINE, WD, half_lanes)
            gw_expand[i, :, :, half * half_lanes : (half + 1) * half_lanes] = part
            return carry

        lax.fori_loop(first, last, block, 0)

    second = TeamSum(sums.second)
    reduced = TeamSum(sums.reduced)
    own_a, own_b, far_a, far_b = ref.own_a, ref.own_b, ref.far_a, ref.far_b
    spare_a, spare_b = ref.grad_mid, ref.activations
    far_c, far_d = ref.g_reduce, ref.far_d
    near_blocks = (g, sib, (own_a, spare_a), (own_b, spare_b))
    far_blocks = (far, diag, (far_a, far_c), (far_b, far_d))
    second_copies[0].wait_recv()
    feed(*near_blocks, 0)
    second_handed = spread_on(second_all, second_copies[1])
    gather_expand[1].stage4()
    wait_all(second_handed)
    feed(*far_blocks, 0)
    expand_blocks(0, TEAM, 0)
    expand_sums[0].along_y()
    gather_expand[1].finish()
    feed(*near_blocks, 1)
    second.near(0, spare_a[...])
    reduced.ps[0] = low(spare_b[...])
    feed(*far_blocks, 1)
    second.near(1, far_c[...])
    reduced.ps[1] = low(far_d[...])
    second.across(lambda part: far_a[part])
    reduced.near(0)
    reduced.near(1)

    gw_reduce = ref.gw_reduce

    def reduce_block(j):
        lhs = active_all[:, :, lanes(j * ROW, ROW)].reshape(TALL, ROW)
        gw_reduce[j] = low(tn(lhs, tall(cot_all)))

    def reduce_beside(i, carry):
        reduce_block(2 * i + 1 - y)
        return carry

    def reduce_here(i, carry):
        reduce_block(2 * i + y)
        return carry

    lax.fori_loop(0, 4, reduce_beside, 0)
    reduce_y.along_y()
    lax.fori_loop(0, 4, reduce_here, 0)
    reduce_z.stage1()

    csum = ref.csum

    def note(i, value):
        csum[i : i + 1] = jnp.sum(value, axis=0, keepdims=True)

    grad_second = second.total(own_a[...])
    grad_mid = ref.grad_mid
    note(6, grad_second * ref.middle_hat[...])
    note(7, grad_second)
    grad_top = f32(cot_all[g])
    note(8, grad_top)
    grad_mid[...] = grad_top + norm_back_ref(
        grad_second, ref.middle_hat, ref.middle_inv, vector(SECOND_GAIN)
    )
    gb_all = ref.gb_all
    gb_all[g] = low(grad_mid[...])
    gb_copies = spread(gb_all)
    note(5, f32(gb_all[g]))
    g_send, go = ref.g_send, ref.go
    e12 = PairExchange(go.at[pl.ds(0, 7 * ROW)])

    def attended_back(i, j):
        part = low(nt(two(gb_all, i, j), row_weight(output_s)))
        for n, group in enumerate((i, j)):
            for t in range(2):
                g_send[group, t] = part[n * ROW : (n + 1) * ROW, t * 128 : (t + 1) * 128]
                e12.send(g_send.at[group, t], go.at[line_rows, :], pair_place(group, t))

    gb_copies[0].wait_recv()
    attended_back(g, sib)
    expand_blocks(0, 2, 1)
    gb_handed = spread_on(gb_all, gb_copies[1])
    wait_all(gb_handed)
    attended_back(far, diag)
    reduced.across(lambda part: far_b[part])
    expand_blocks(2, TEAM, 1)
    expand_sums[1].along_y()
    reduce_y.sum_y()
    reduce_y.stage1()
    gw_output = ref.gw_output
    gw_output[...] = low(tn(tall(att_all), tall(gb_all))).reshape(LINE, WD, D)
    e12.wait(g_send.at[0, 0], go.at[line_rows, :])
    output_sum.along_y()

    dq, d_all = ref.dq, ref.d_all
    dq[...] = jnp.zeros_like(dq)
    e13 = PairExchange(qkv.at[pl.ds(0, 2), pl.ds(0, 7 * ROW), :])
    products = f32(go[...]) * att_f[...]
    offsets = [
        jnp.sum(jnp.where(half_of_lane == t, products, 0.0), axis=-1, keepdims=True)
        for t in range(2)
    ]
    att_f[...] = jnp.where(half_of_lane == 0, offsets[0], offsets[1])
    pair_d = d_all.at[mine, pl.ds(1, 2), :, pair_lanes]

    def attend_back_keys(b, carry):
        here = rows(b * 256, 256)
        keys, values = qkv[1, here, :], qkv[2, here, :]
        queries, grad = f32(qkv[0]), f32(go[...])
        outs, grad_keys, grad_values = [], 0.0, 0.0
        for t in range(2):
            grad_t = low(jnp.where(half_of_lane == t, grad, 0.0))
            query_t = low(jnp.where(half_of_lane == t, queries, 0.0))
            weights = p_low[t, :, lanes(b * 256, 256)]
            offset = att_f[:, t * HDIM : t * HDIM + 1]
            slopes = low(low(f32(weights) * (nt(grad_t, values) - offset)) * SCALE)
            outs.append(nn(slopes, keys))
            grad_keys += tn(slopes, query_t)
            grad_values += tn(weights, grad_t)
        dq[...] += jnp.where(half_of_lane == 0, outs[0], outs[1])
        pair_send[pl.ds(2 * b, 2), 1] = low(grad_keys).reshape(2, ROW, 128)
        pair_send[pl.ds(2 * b, 2), 2] = low(grad_values).reshape(2, ROW, 128)
        for t in range(2):
            there = 2 * b + t
            e13.send(pair_send.at[there, pl.ds(1, 2)], pair_d, there)

        return carry

    lax.fori_loop(0, 2, attend_back_keys, 0, unroll=True)
    lax.fori_loop(2, GROUP // 256, attend_back_keys, 0, unroll=True)
    pair_send[:, 0] = low(dq[...]).reshape(LINE, ROW, 128)
    d_dst = d_all.at[mine, 0, :, pair_lanes]
    d_copies = to_whole_line(
        lambda place: pair_send.at[place, 0], d_dst, att_low.at[pl.ds(0, 7 * ROW)]
    )
    d_here = pltpu.make_async_copy(pair_send.at[s, 0], d_dst, recv.at[reserve(1)])
    d_here.start()
    d_here.wait()
    wait_all(d_copies)
    e13.wait(pair_send.at[0, pl.ds(1, 2)], pair_d)
    normed = TeamSum(sums.normed)

    def joint_back(j):
        total = None
        for kind in range(3):
            weight = joint_s[:, :, :, kind * QC : (kind + 1) * QC].reshape(D, QC)
            part = nt(d_all[j, kind], weight)
            total = part if total is None else total + part
        return total

    normed.near(1, joint_back(diag))
    far_a[...] = joint_back(far)
    normed.across(lambda part: far_a[part])
    for part in expand_sums:
        part.sum_y()
        part.stage1()
    reduce_z.stage2()
    normed.near(0, joint_back(sib))
    own_a[...] = joint_back(g)
    gw_joint = ref.gw_joint
    tsum = ref.tsum
    for kind in range(3):
        block = d_all[:, kind].reshape(TALL, QC)
        for i in range(TEAM):
            lhs = normed_all[:, :, i * QC : (i + 1) * QC].reshape(TALL, QC)
            part = low(tn(lhs, block)).reshape(LINE, WD, QC)
            gw_joint[i, :, :, kind * QC : (kind + 1) * QC] = part
        if kind != 1:
            row = 9 + kind // 2
            tsum[s, row : row + 1] = jnp.sum(f32(block), axis=0, keepdims=True)
    for part in joint_sums:
        part.along_y()
    hidden_sums = jnp.sum(f32(tall(gh_all)), axis=0, keepdims=True)
    for i in range(4):
        tsum[s, 11 + i : 12 + i] = hidden_sums[:, i * QC : (i + 1) * QC]
    tsum[s, 15:16] = jnp.zeros((1, QC), F32)

    grad_normed = normed.total(own_a[...])
    note(3, grad_normed * ref.start_hat[...])
    note(4, grad_normed)
    grad_start = grad_mid[...] + norm_back_ref(
        grad_normed, ref.start_hat, ref.start_inv, vector(FIRST_GAIN)
    )
    gm_all = ref.gm_all
    gm_all[g] = low(grad_start)
    gm_copies = spread(gm_all)
    note(0, f32(gm_all[g]))
    note(1, lead * grad_start)
    note(2, grad_start)
    csum[9:16] = jnp.zeros((7, D), F32)
    crecv = ref.crecv
    crecv[g] = csum[:, lanes(g * QC, QC)]
    c_copies = to_whole_team(
        lambda j: csum.at[:, lanes(j * QC, QC)], crecv.at[g], crecv.at[pl.ds(0, 3)]
    )
    ref.activations[...] = (
        reduced.total(own_b[...]) + middle_ref[...] + vector(REDUCE_BIAS)
    )
    deposit(ref.activations, results.activations)
    reduce_y.stage2()
    expand_sums[0].stage2()
    joint_sums[0].sum_y()
    joint_sums[0].stage1()
    gm_handed = spread_on(gm_all, gm_copies[1])
    gm_copies[0].wait_recv()
    wait_all(gm_handed)

    gw_merge = ref.gw_merge
    f_own = ref.f_own
    t_send = ref.t_send
    q_all = ref.q_all
    grad_heads = low(nt(tall(gm_all), row_weight(merge_s)))
    head_grad = ref.att_all
    head_grad[...] = grad_heads.reshape(TEAM, ROW, QC)
    q_all[s] = jnp.zeros((8, KP), F32)

    def choose_back(h):
        field = f32(tall(field_all))
        grad_h = low(jnp.where(head_of_lane == h, f32(tall(head_grad)), 0.0))
        value_back = nn(grad_h, pv[...].reshape(QC, KP))
        grad_chosen = split_dot(value_back * field, select[...])
        weights = chosen[h]
        shifted = grad_chosen - jnp.sum(weights * grad_chosen, axis=-1, keepdims=True)
        score_spread = nn(low(weights * shifted), select_t[...])
        spread_weights = nn(low(weights), select_t[...])
        pair = tall(head_grad)[:, (h // 2) * 128 : (h // 2 + 1) * 128]
        part = tn(pair, low(spread_weights * field))
        at_row = (h % 2) * HDIM
        t_send[2 * h : 2 * h + 2] = low(part[at_row : at_row + HDIM]).reshape(2, WD, KP)
        field_part = spread_weights * value_back + score_spread * probe[h : h + 1]
        field_part = field_part.reshape(TEAM, ROW, KP)
        if h == 0:
            f_own[...] = field_part
        else:
            f_own[...] += field_part
        q_all[s, h : h + 1] = jnp.sum(score_spread * field, axis=0, keepdims=True)

    for h in range(TEAM_HEADS):
        choose_back(h)
        if h == 0:
            reduce_z.stage3()
            joint_sums[1].sum_y()
            joint_sums[1].stage1()
        if h == 2:
            output_sum.sum_y()
            output_sum.stage1()
            expand_sums[1].stage2()
            reduce_y.stage3()
    t_recv = ref.t_recv
    t_copies = to_whole_line(
        lambda place: t_send.at[place], t_recv.at[s], t_recv.at[pl.ds(0, LINE - 1)]
    )
    t_recv[s] = t_send[s]
    q_copies = share_line(q_all)
    gw_merge[...] = low(tn(head_low[...], tall(gm_all))).reshape(LINE, WD, D)
    merge_sum.along_y()
    reduce_z.along_y()
    expand_sums[0].stage3()
    f_recv = ref.f_recv
    f_copies = Together(f_recv)
    for step in range(1, TEAM):
        j = lax.rem(g + step, TEAM)
        f_copies.push(f_own.at[j], f_recv.at[step - 1], to_team(j))
    position = jnp.zeros((ROW, QC), F32)
    for j in range(TEAM):
        position += f32(gm_all[j, :, lanes(g * QC, QC)])
    ref.g_position[...] = position
    deposit(ref.g_position, results.g_position)
    wait_all(c_copies)
    tsum[s, 0:9] = jnp.sum(crecv[...], axis=0)[0:9]

    joint_sums[0].stage2()
    joint_sums[2].sum_y()
    joint_sums[2].stage1()
    joint_sums[1].stage2()
    expand_sums[1].stage3()
    output_sum.stage2()
    joint_sums[2].stage2()
    merge_sum.sum_y()
    merge_sum.stage1()
    wait_all(t_copies)
    head_all, score_all = ref.head_all, ref.score_all
    head_all[g, s] = low(jnp.sum(f32(t_recv[...]), axis=0))
    h_here = head_all.at[g, s]
    h_copies = to_whole_line(lambda place: h_here, h_here, head_all.at[0, pl.ds(0, LINE - 1)])
    joint_sums[0].stage3()
    joint_sums[1].stage3()
    output_sum.stage3()
    merge_sum.stage2()

    xs_joint, xs_expand = ref.xs_joint, ref.xs_expand
    xr_joint, xr_expand = ref.xr_joint, ref.xr_expand
    x_copies = []

    def to_owners(line_sum, xs, xr, at, size):
        here = pl.ds(at, size)
        line_sum.total(xs.at[:, :, here])
        x_copies.extend(
            to_whole_team(
                lambda j: xs.at[j, :, here], xr.at[g, :, here], xr.at[pl.ds(0, 3), :, here]
            )
        )
        xr[g, :, here] = xs[g, :, here]

    to_owners(expand_sums[0], xs_expand, xr_expand, 0, half_lanes)
    joint_sums[2].stage3()
    to_owners(joint_sums[0], xs_joint, xr_joint, 0, QC)
    wait_all(h_copies)
    h_spread = spread(head_all)
    s_copies = share_line(tsum)
    merge_sum.stage3()
    wait_all(q_copies)
    score_all[g] = jnp.sum(q_all[...], axis=0)
    score_here = score_all.at[g]
    score_copies = to_whole_team(lambda j: score_here, score_here, score_all.at[pl.ds(0, 3)])
    to_owners(expand_sums[1], xs_expand, xr_expand, half_lanes, half_lanes)
    to_owners(joint_sums[1], xs_joint, xr_joint, QC, QC)
    h_handed = spread_on(head_all, h_spread[1])
    to_owners(joint_sums[2], xs_joint, xr_joint, 2 * QC, QC)
    for i in range(2):
        reduce_sums[i].total(ref.g_reduce.at[pl.ds(i * half_rows, half_rows)])
    deposit(ref.g_reduce, results.g_reduce)
    output_sum.total(ref.g_output)
    deposit(ref.g_output, results.g_output)
    f_copies.wait_recv()
    ref.field_grad[...] = (f_own[g] + f_recv[0] + f_recv[1] + f_recv[2]).T[0:VP]
    deposit(ref.field_grad, results.field_grad)
    wait_all(s_copies)
    ref.sums[...] = jnp.sum(tsum[...], axis=0)
    merge_sum.total(ref.g_merge)
    deposit(ref.g_merge, results.g_merge)
    wait_all(x_copies)
    for j in range(TEAM):
        ref.g_expand[:, j * D : (j + 1) * D] = f32(xr_expand[j])
        for kind in range(3):
            at_lane = kind * D + j * QC
            ref.g_joint[:, at_lane : at_lane + QC] = f32(
                xr_joint[j, :, kind * QC : (kind + 1) * QC]
            )
    deposit(ref.g_expand, results.g_expand)
    deposit(ref.g_joint, results.g_joint)
    wait_all(score_copies)
    score_rows = ref.score_rows
    for j in range(TEAM):
        score_rows[TEAM_HEADS * j : TEAM_HEADS * (j + 1)] = score_all[j, 0:TEAM_HEADS]

    def exact(a, b, ca, cb):
        return lax.dot_general(
            a,
            b,
            (((ca,), (cb,)), ((), ())),
            precision=lax.Precision.HIGHEST,
            preferred_element_type=F32,
        )

    scores = score_rows[...]
    query_row = vector(QUERY)
    head_of = lax.broadcasted_iota(jnp.int32, (16, D), 1) // HDIM
    head_rows = (head_of == lax.broadcasted_iota(jnp.int32, (16, D), 0)).astype(F32)
    probe_own = f32(
        low(exact(f32(ref.key_w[...]) * query_row, head_rows, 1, 1) * SCALE)
    )
    grad_probe = exact(f32(pe[...]), scores, 1, 1)
    ref.g_key[...] = exact(grad_probe, head_rows, 1, 0) * (query_row * SCALE)
    deposit(ref.g_key, results.g_key)
    small = ref.small
    picks = (
        lax.broadcasted_iota(jnp.int32, (QC, 128), 0)
        == lax.broadcasted_iota(jnp.int32, (QC, 128), 1) + s * WD
    ) & (lax.broadcasted_iota(jnp.int32, (QC, 128), 1) < WD)
    small[16:24] = jnp.zeros((8, 128), F32)
    small[0:SUM_ROWS] = exact(ref.sums[...], picks.astype(F32), 1, 0)
    hidden_row = jnp.zeros((1, QC), F32)
    score_row = jnp.zeros((1, KP), F32)
    own_scores = score_all[g]
    for i in range(4):
        hidden_row = jnp.where(s // 2 == i, ref.sums[11 + i : 12 + i], hidden_row)
        score_row = jnp.where(s // 2 == i, own_scores[i : i + 1], score_row)
    hidden_row = jnp.where(s % 2 == 0, hidden_row[:, 0:128], hidden_row[:, 128:256])
    query_grad = exact(jnp.broadcast_to(score_row, (8, KP)), ref.key_own[...], 1, 1) * SCALE
    small[24:32] = jnp.zeros((8, 128), F32)
    small[24:25] = hidden_row
    small[25:26, 0:WD] = query_grad[0:1]
    deposit(small, results.small)
    h_spread[0].wait_recv()
    wait_all(h_handed)
    heads = head_all[...].reshape(D, KP)
    ref.g_value[...] = nt(pe[...], heads)
    deposit(ref.g_value, results.g_value)
    grad_table = nn(ref.value_w[...], heads) + exact(probe_own, scores, 1, 0)
    ref.g_patch[...] = grad_table[:, 0:VP]
    ref.g_embed[...] = grad_table[:, VP : VP + VARS]
    deposit(ref.g_patch, results.g_patch)
    deposit(ref.g_embed, results.g_embed)
    for copy in begun + begun_together:
        copy.wait_send()
    for gather in [gather_merge, gather_output] + gather_reduce + gather_joint + gather_expand:
        gather.sent()
    for line_sum in [output_sum, merge_sum] + reduce_sums + joint_sums + expand_sums:
        line_sum.sent()
    for copy in deposits:
        copy.wait()


def fused(operands):
    scratch = list(SCRATCH.values()) + list(OUTPUTS.values())
    for shape in TEAM_SUMS.values():
        scratch += team_sum_buffers(shape)
    return pl.pallas_call(
        fused_kernel,
        out_shape=[jax.ShapeDtypeStruct(*shape) for shape in OUTPUTS.values()],
        in_specs=[pl.BlockSpec(memory_space=space) for space in INPUTS.values()],
        out_specs=[pl.BlockSpec(memory_space=pl.ANY)] * len(OUTPUTS),
        scratch_shapes=[pltpu.VMEM(*shape) for shape in scratch]
        + [pltpu.SemaphoreType.DMA((SEMAPHORES,))] * 2,
        compiler_params=pltpu.CompilerParams(
            collective_id=1, has_side_effects=True, vmem_limit_bytes=64 << 20
        ),
    )(*operands)


VECTOR_ROWS = (25, 0, 1, 2, 3, 4, 5, 6, 7, 8)


def hand_out_kernel(*refs):
    n, m = len(OUTPUTS), len(VECTOR_ROWS)
    arrays = refs[:n]
    results = refs[n : 2 * n - 1]
    vectors = refs[2 * n - 1 : 2 * n - 1 + m]
    joint, hidden = refs[2 * n - 1 + m : 2 * n + 1 + m]
    held = refs[2 * n + 1 + m : 3 * n + 1 + m]
    narrow, both, came, left = refs[3 * n + 1 + m :]
    fetches = [pltpu.make_async_copy(arrays[i], held[i], came.at[i]) for i in range(n)]
    for copy in fetches:
        copy.start()
    small = held[n - 1]
    fetches[n - 1].wait()
    narrow[...] = small[:, 0:WD]
    both[...] = small[9:11, 0:WD]
    stores = [
        pltpu.make_async_copy(narrow.at[row], vectors[i], left.at[n + i])
        for i, row in enumerate(VECTOR_ROWS)
    ]
    stores.append(pltpu.make_async_copy(both, joint, left.at[n + m]))
    stores.append(pltpu.make_async_copy(small.at[24], hidden, left.at[n + m + 1]))
    for copy in stores:
        copy.start()
    for i in range(n - 1):
        fetches[i].wait()
        copy = pltpu.make_async_copy(held[i], results[i], left.at[i])
        copy.start()
        stores.append(copy)
    for copy in stores:
        copy.wait()


def hand_out(arrays):
    n, m = len(arrays), len(VECTOR_ROWS)
    shapes = [jax.ShapeDtypeStruct(a.shape, a.dtype) for a in arrays[:-1]]
    shapes += [jax.ShapeDtypeStruct((WD,), F32)] * m
    shapes += [jax.ShapeDtypeStruct((2, WD), F32), jax.ShapeDtypeStruct((ROW,), F32)]
    return pl.pallas_call(
        hand_out_kernel,
        out_shape=shapes,
        in_specs=[pl.BlockSpec(memory_space=pl.ANY)] * n,
        out_specs=[pl.BlockSpec(memory_space=pl.ANY)] * len(shapes),
        scratch_shapes=[pltpu.VMEM(a.shape, a.dtype) for a in arrays]
        + [pltpu.VMEM((32, WD), F32), pltpu.VMEM((2, WD), F32)]
        + [pltpu.SemaphoreType.DMA((n,)), pltpu.SemaphoreType.DMA((n + m + 2,))],
        compiler_params=pltpu.CompilerParams(vmem_limit_bytes=64 << 20),
    )(*arrays)


def shards_fused(
    fields,
    patch_weight,
    variable_embed,
    query_vector,
    key_weight,
    value_weight,
    merge_weight,
    merge_bias,
    position_table,
    lead_weight,
    lead_bias,
    first_gain,
    first_shift,
    joint_weight,
    joint_bias,
    output_weight,
    output_bias,
    second_gain,
    second_shift,
    expand_weight,
    expand_bias,
    reduce_weight,
    reduce_bias,
    segment_ids,
    live_rows,
    lead_steps,
    cotangent,
):
    pack = jnp.concatenate(
        [
            query_vector,
            merge_bias,
            lead_weight,
            lead_bias,
            first_gain,
            first_shift,
            output_bias,
            second_gain,
            second_shift,
            reduce_bias,
            jnp.zeros((2 * WD,), BF16),
            expand_bias,
            jnp.zeros((12 * 128,), BF16),
        ]
    ).reshape(16, 128)
    whole = fused(
        (
            fields.T,
            patch_weight.T,
            variable_embed.T,
            key_weight,
            value_weight,
            pack,
            joint_bias,
            segment_ids.reshape(1, ROW),
            live_rows.reshape(1, ROW),
            lead_steps,
            cotangent,
            position_table,
            joint_weight,
            expand_weight,
            merge_weight,
            output_weight,
            reduce_weight,
        )
    )
    (
        activations,
        field_grad,
        g_patch,
        g_embed,
        g_key,
        g_value,
        g_merge,
        g_position,
        g_joint,
        g_output,
        g_expand,
        g_reduce,
        g_query,
        g_merge_b,
        g_lead,
        g_lead_b,
        g_first_gain,
        g_first_shift,
        g_output_b,
        g_second_gain,
        g_second_shift,
        g_reduce_b,
        g_joint_b,
        g_expand_b,
    ) = hand_out(whole)
    return (
        activations,
        field_grad.T,
        g_patch.T,
        g_embed.T,
        g_query,
        g_key,
        g_value,
        g_merge,
        g_merge_b,
        g_position,
        g_lead,
        g_lead_b,
        g_first_gain,
        g_first_shift,
        g_joint,
        g_joint_b,
        g_output,
        g_output_b,
        g_second_gain,
        g_second_shift,
        g_expand,
        g_expand_b,
        g_reduce,
        g_reduce_b,
    )


def solution(mesh):
    by_row = P(ROWS, None)
    by_column = P(None, ROWS)
    vector = P(ROWS)
    in_specs = (
        by_row,
        by_column,
        by_column,
        vector,
        by_row,
        by_row,
        by_row,
        vector,
        P("seq", "grp"),
        vector,
        vector,
        vector,
        vector,
        by_row,
        by_column,
        by_row,
        vector,
        vector,
        vector,
        by_row,
        vector,
        by_row,
        vector,
        vector,
        vector,
        P("grp", None),
        by_row,
    )
    out_specs = (
        by_row,
        by_row,
        by_column,
        by_column,
        vector,
        by_row,
        by_row,
        by_row,
        vector,
        P("seq", "grp"),
        vector,
        vector,
        vector,
        vector,
        by_row,
        by_column,
        by_row,
        vector,
        vector,
        vector,
        by_row,
        vector,
        by_row,
        vector,
    )
    G, S = mesh.shape["grp"], mesh.shape["seq"]

    def body(*args):
        rows_here, weight_rows = args[0].shape[0], args[5].shape[0]
        if (G, S, rows_here, weight_rows) == (TEAM, LINE, ROW, WD):
            return shards_fused(*args)
        return shards(G, S, *args)

    return jax.shard_map(body, mesh=mesh, in_specs=in_specs, out_specs=out_specs, check_vma=False)
```

```python
import types

import jax
import jax.numpy as jnp
from jax import lax
from jax.experimental import pallas as pl
from jax.experimental.pallas import tpu as pltpu
from jax.sharding import PartitionSpec as P

D = 1024
HEADS = 16
FF = 4096
VARS = 48
PIX = 4
HDIM = 64
VP = 192
KP = 256

EPSILON = 1e-05
SCALE = 0.125
LEAD_UNIT = 0.06
MASKED = -1e30

MESH = pl.DeviceIdType.MESH
ROWS = ("grp", "seq")
F32 = jnp.float32
BF16 = jnp.bfloat16


def f32(x):
    return x.astype(F32)


def low(x):
    return x.astype(BF16)


def dot(a, b, ca, cb):
    return lax.dot_general(a, b, (((ca,), (cb,)), ((), ())), preferred_element_type=F32)


def low_sums(x):
    return dot(jnp.ones((8, x.shape[0]), BF16), x, 1, 0)[0]


def exchange(axis, parts):
    return [
        lax.all_gather(a, axis, axis=0, tiled=False)
        if mode == "all"
        else lax.all_to_all(a, axis, 0, 0, tiled=False)
        for a, mode in parts
    ]


def norm_parts(x):
    center = x - jnp.mean(x, axis=-1, keepdims=True)
    spread = jnp.mean(center * center, axis=-1, keepdims=True)
    inverse = lax.rsqrt(spread + EPSILON)
    return center * inverse, inverse


def norm_back(hat, inverse, gain, grad):
    f = grad * gain
    return inverse * (
        f
        - jnp.mean(f, axis=-1, keepdims=True)
        - hat * jnp.mean(f * hat, axis=-1, keepdims=True)
    )


def pack(pieces):
    flat = jnp.concatenate([f32(p).reshape(-1) for p in pieces])
    short = -flat.shape[0] % 1024
    return jnp.pad(flat, (0, short)).reshape(-1, 128)


def unpack(table, sizes):
    flat = table.reshape(table.shape[:-2] + (-1,))
    out, at = [], 0
    for size in sizes:
        out.append(flat[..., at : at + size])
        at += size
    return out


def softmax_parts(q, k, allowed):
    scores = jnp.einsum("hqc,hkc->hqk", q, k, preferred_element_type=F32) * SCALE
    masked = jnp.where(allowed[None], scores, MASKED)
    top = jnp.max(masked, axis=-1, keepdims=True)
    terms = jnp.where(allowed[None], jnp.exp(masked - top), 0.0)
    total = jnp.sum(terms, axis=-1, keepdims=True)
    return terms * (1.0 / total)


def attend(q, k, v, allowed):
    weights = softmax_parts(q, k, allowed)
    return jnp.einsum("hqk,hkc->hqc", low(weights), v, preferred_element_type=F32)


def attend_back(q, k, v, allowed, grad, attended):
    weights = softmax_parts(q, k, allowed)
    offset = jnp.sum(f32(grad) * attended, axis=-1)
    pushed = jnp.einsum("hqc,hkc->hqk", grad, v, preferred_element_type=F32)
    slopes = low(weights * (pushed - offset[..., None])) * BF16(SCALE)
    grad_q = jnp.einsum("hqk,hkc->hqc", slopes, k, preferred_element_type=F32)
    grad_k = jnp.einsum("hqk,hqc->hkc", slopes, q, preferred_element_type=F32)
    grad_v = jnp.einsum("hqk,hqc->hkc", low(weights), grad, preferred_element_type=F32)
    return grad_q, grad_k, grad_v


def heads_first(x):
    return x.transpose(1, 0, 2)


def heads_last(x):
    return x.transpose(1, 0, 2)


def allowed_pairs(query_codes, key_codes):
    return ((query_codes[:, None] >> 1) == (key_codes[None, :] >> 1)) & (
        (key_codes[None, :] & 1) == 1
    )


def shards(
    G,
    S,
    fields,
    patch_weight,
    variable_embed,
    query_vector,
    key_weight,
    value_weight,
    merge_weight,
    merge_bias,
    position_table,
    lead_weight,
    lead_bias,
    first_gain,
    first_shift,
    joint_weight,
    joint_bias,
    output_weight,
    output_bias,
    second_gain,
    second_shift,
    expand_weight,
    expand_bias,
    reduce_weight,
    reduce_bias,
    segment_ids,
    live_rows,
    lead_steps,
    cotangent,
):
    R = fields.shape[0]
    dn = value_weight.shape[0]
    fn = reduce_weight.shape[0]
    RG = G * R
    HL = HEADS // G
    CL = HL * HDIM
    FL = FF // G
    pairs = G * HL
    direct = pairs % S == 0 and HL % max(pairs // S, 1) == 0

    def swap(axis, *parts):
        return exchange(axis, parts)

    def gather_rows(w):
        return lax.all_gather(w, "seq", axis=0, tiled=True)

    merge_s = gather_rows(merge_weight)
    output_s = gather_rows(output_weight)

    table = jnp.concatenate(
        [patch_weight, variable_embed, jnp.zeros((KP - VP - VARS, dn), BF16)], axis=0
    )
    value_part = low(dot(value_weight, table, 0, 1)).reshape(G, CL, KP)
    key_part = low(dot(key_weight, table, 0, 1)).reshape(G, CL, KP)
    both = jnp.concatenate([value_part, key_part], axis=1)
    codes_own = segment_ids * 2 + live_rows
    vectors_own = [
        query_vector,
        merge_bias,
        lead_weight,
        lead_bias,
        first_gain,
        first_shift,
        output_bias,
        second_gain,
        second_shift,
        reduce_bias,
    ]
    small_own = pack([codes_own] + vectors_own)
    widen = (jnp.arange(VP)[:, None] == jnp.arange(KP)[None, :]).astype(BF16)
    column = jnp.arange(KP)
    field_own = low(dot(fields, widen, 1, 0) + ((column >= VP) & (column < VP + VARS)))
    joint_own = joint_weight.reshape(dn, 3, G, CL).transpose(2, 0, 1, 3).reshape(G, dn, 3 * CL)
    expand_own = expand_weight.reshape(dn, G, FL).transpose(1, 0, 2)
    both, joint_in, expand_in, field_in, position_in, small_in, cot_in = swap(
        "grp",
        (both, "each"),
        (joint_own, "each"),
        (expand_own, "each"),
        (field_own, "all"),
        (position_table, "all"),
        (small_own, "all"),
        (cotangent, "all"),
    )
    joint_s = (
        lax.all_gather(joint_in, "seq", axis=0, tiled=False)
        .transpose(1, 0, 2, 3)
        .reshape(D, 3 * CL)
    )
    expand_s = (
        lax.all_gather(expand_in, "seq", axis=0, tiled=False).transpose(1, 0, 2, 3).reshape(D, FL)
    )
    reduce_s = gather_rows(reduce_weight)
    field_rows = field_in.reshape(RG, KP)
    field_wide = dot(field_rows, (column[:, None] == column[None, :]).astype(BF16), 1, 0)
    cot_rows = cot_in.reshape(RG, D)
    position_rows = position_in.transpose(1, 0, 2).reshape(R, D)
    both = low(jnp.sum(f32(both), axis=0)).reshape(2, S, dn, KP).transpose(1, 0, 2, 3)
    small_rows = small_in.shape[0] * small_in.shape[1]
    slim = pack([joint_bias, expand_bias])
    both, small_all, slim_all = swap(
        "seq",
        (both.reshape(S, 2 * dn, KP), "each"),
        (small_in.reshape(small_rows, 128), "all"),
        (slim, "all"),
    )
    both = jnp.sum(f32(both), axis=0).reshape(2, dn, KP)
    value_own, key_own = both[0], both[1]
    probe_part = jnp.sum(key_own * f32(query_vector)[:, None], axis=0) * SCALE
    value_table, probe_parts = swap(
        "seq",
        (low(value_own), "all"),
        (jnp.broadcast_to(probe_part[None], (8, KP)), "all"),
    )
    value_table = value_table.reshape(CL, KP)
    probe_table = jnp.sum(probe_parts[:, 0].reshape(HL, S // HL, KP), axis=1)

    small_all = small_all.reshape(S, G, -1, 128)
    pieces = unpack(small_all, [R] + [dn] * len(vectors_own))
    codes = pieces[0].astype(jnp.int32)
    (
        full_query,
        full_merge_bias,
        full_lead,
        full_lead_bias,
        full_first_gain,
        full_first_shift,
        full_output_bias,
        full_second_gain,
        full_second_shift,
        full_reduce_bias,
    ) = [p.transpose(1, 0, 2).reshape(D) for p in pieces[1:]]
    joint_shift, expand_shift = unpack(slim_all, [2 * dn, fn])
    joint_shift = joint_shift.reshape(S, 2, dn).transpose(1, 0, 2).reshape(2, CL)
    expand_shift = expand_shift.reshape(FL)

    picked = jnp.where(
        segment_ids[:, None] == jnp.arange(lead_steps.shape[1])[None, :], lead_steps, 0
    )
    lead_rows = LEAD_UNIT * jnp.sum(picked, axis=1).astype(F32)

    owner = jnp.concatenate(
        [jnp.arange(VP) // PIX, jnp.arange(VARS), jnp.full((KP - VP - VARS,), VARS)]
    )
    select = (owner[:, None] == jnp.arange(VARS)[None, :]).astype(BF16)
    maps = probe_table[:, :, None] * f32(select)[None]
    maps_high = low(maps)
    maps_low = low(maps - f32(maps_high))
    scores = jnp.einsum("rk,hkv->hrv", field_rows, maps_high, preferred_element_type=F32)
    scores = scores + jnp.einsum("rk,hkv->hrv", field_rows, maps_low, preferred_element_type=F32)
    chosen = jax.nn.softmax(scores, axis=-1)
    spread = jnp.einsum("hrv,kv->hrk", low(chosen), select, preferred_element_type=F32)
    mixed = low(spread * field_wide[None])
    value_heads = value_table.reshape(HL, HDIM, KP)
    head_low = low(
        jnp.einsum("hrk,hck->rhc", mixed, value_heads, preferred_element_type=F32).reshape(RG, CL)
    )
    merged = low(dot(head_low, merge_s, 1, 0)).reshape(G, R, D)
    (merged,) = swap("grp", (merged, "each"))
    start = (
        jnp.sum(f32(merged), axis=0)
        + full_merge_bias
        + f32(position_rows)
        + lead_rows[:, None] * full_lead
        + full_lead_bias
    )
    start_hat, start_inv = norm_parts(start)
    (normed,) = swap("grp", (low(start_hat * full_first_gain + full_first_shift), "all"))
    normed = normed.reshape(RG, D)
    joint = dot(normed, joint_s, 1, 0)
    shift = jnp.concatenate([joint_shift[0], jnp.zeros((CL,), F32), joint_shift[1]])
    joint = low(joint + shift)

    if direct:
        per = pairs // S
        split = HL // per
        width = per * HDIM

        def to_pairs(x, kinds):
            x = x.reshape(G, R, kinds, split, width).transpose(0, 3, 1, 2, 4)
            (x,) = swap("seq", (x.reshape(S, R, kinds * width), "each"))
            return x.reshape(S * R, kinds, per, HDIM)

        def from_pairs(x, kinds):
            (x,) = swap("seq", (x.reshape(S, R, kinds * width), "each"))
            return (
                x.reshape(G, split, R, kinds, width)
                .transpose(0, 2, 3, 1, 4)
                .reshape(RG, kinds * CL)
            )

        mine = lax.axis_index("seq") // split
        pair_codes = lax.dynamic_index_in_dim(codes, mine, axis=1, keepdims=False).reshape(S * R)
        allowed = allowed_pairs(pair_codes, pair_codes)
        qkv = to_pairs(joint, 3)
        q, k, v = [heads_first(qkv[:, i]) for i in range(3)]
        attended = attend(q, k, v, allowed)
        attended_low = from_pairs(heads_last(low(attended)), 1)
    else:
        heads = joint.reshape(G, R, 3, HL, HDIM).transpose(0, 2, 3, 1, 4)
        everyone = lax.all_gather(heads[:, 1:], "seq", axis=3, tiled=True)
        all_codes = codes.transpose(1, 0, 2).reshape(G, S * R)
        my_codes = lax.dynamic_index_in_dim(codes, lax.axis_index("seq"), 0, keepdims=False)

        def forward_group(item):
            q, kv, query_codes, key_codes = item
            return attend(q, kv[0], kv[1], allowed_pairs(query_codes, key_codes))

        attended = lax.map(forward_group, (heads[:, 0], everyone, my_codes, all_codes))
        attended_low = low(attended).transpose(0, 2, 1, 3).reshape(RG, CL)

    branch = low(dot(attended_low, output_s, 1, 0)).reshape(G, R, D)
    (branch,) = swap("grp", (branch, "each"))
    middle = start + jnp.sum(f32(branch), axis=0) + full_output_bias
    middle_hat, middle_inv = norm_parts(middle)
    (second,) = swap("grp", (low(middle_hat * full_second_gain + full_second_shift), "all"))
    second = second.reshape(RG, D)
    hidden = dot(second, expand_s, 1, 0) + expand_shift
    inner = 0.7978845608028654 * (hidden + 0.044715 * hidden * hidden * hidden)
    bend = jnp.tanh(inner)
    active = low(0.5 * hidden * (1.0 + bend))
    slope = 0.5 * (1.0 + bend) + 0.5 * hidden * (1.0 - bend * bend) * 0.7978845608028654 * (
        1.0 + 3.0 * 0.044715 * hidden * hidden
    )
    reduced = low(dot(active, reduce_s, 1, 0)).reshape(G, R, D)

    grad_active = dot(cot_rows, reduce_s, 1, 1)
    grad_hidden = low(grad_active * slope)
    grad_second = low(dot(grad_hidden, expand_s, 1, 1)).reshape(G, R, D)
    grad_second, reduced = swap("grp", (grad_second, "each"), (reduced, "each"))
    activations = middle + jnp.sum(f32(reduced), axis=0) + full_reduce_bias
    grad_second = jnp.sum(f32(grad_second), axis=0)
    grad_top = f32(cotangent)
    grad_middle = grad_top + norm_back(middle_hat, middle_inv, full_second_gain, grad_second)
    grad_branch = low(grad_middle)

    def scatter_rows(w):
        return lax.psum_scatter(w, "seq", scatter_dimension=0, tiled=True)

    def scatter_mixed(w):
        cols = w.shape[1]
        w = w.reshape(G, S, dn, cols).transpose(1, 0, 2, 3).reshape(S, G * dn * cols // 1024, 1024)
        w = lax.psum_scatter(w, "seq", scatter_dimension=0, tiled=False)
        return w.reshape(G, dn, cols)

    grad_reduce_weight = f32(scatter_rows(low(dot(active, cot_rows, 0, 0))))
    grad_expand_mixed = scatter_mixed(low(dot(second, grad_hidden, 0, 0)))
    grad_expand_bias = low_sums(grad_hidden)

    (grad_branch_rows,) = swap("grp", (grad_branch, "all"))
    grad_branch_rows = grad_branch_rows.reshape(RG, D)
    grad_attended = low(dot(grad_branch_rows, output_s, 1, 1))
    grad_output_weight = f32(scatter_rows(low(dot(attended_low, grad_branch_rows, 0, 0))))
    if direct:
        pushed = heads_first(to_pairs(grad_attended, 1)[:, 0])
        grad_q, grad_k, grad_v = attend_back(q, k, v, allowed, pushed, attended)
        grads = [heads_last(low(x)) for x in (grad_q, grad_k, grad_v)]
        grad_joint = from_pairs(jnp.stack(grads, axis=1), 3)
    else:
        grad_heads = grad_attended.reshape(G, R, HL, HDIM).transpose(0, 2, 1, 3)

        def backward_group(item):
            q, kv, query_codes, key_codes, grad, done = item
            grad_q, grad_k, grad_v = attend_back(
                q, kv[0], kv[1], allowed_pairs(query_codes, key_codes), grad, done
            )
            return grad_q, jnp.stack([grad_k, grad_v], axis=0)

        grad_q, grad_kv = lax.map(
            backward_group,
            (heads[:, 0], everyone, my_codes, all_codes, grad_heads, attended),
        )
        grad_kv = lax.psum_scatter(grad_kv, "seq", scatter_dimension=3, tiled=True)
        grad_joint = low(jnp.concatenate([grad_q[:, None], grad_kv], axis=1))
        grad_joint = grad_joint.transpose(0, 3, 1, 2, 4).reshape(RG, 3 * CL)
    grad_normed = low(dot(grad_joint, joint_s, 1, 1)).reshape(G, R, D)
    (grad_normed,) = swap("grp", (grad_normed, "each"))
    grad_normed = jnp.sum(f32(grad_normed), axis=0)
    grad_joint_mixed = scatter_mixed(low(dot(normed, grad_joint, 0, 0)))
    joint_sums = low_sums(grad_joint)
    grad_start = grad_middle + norm_back(start_hat, start_inv, full_first_gain, grad_normed)
    grad_merged = low(grad_start)

    grad_merged_rows, grad_joint_in, grad_expand_in = swap(
        "grp", (grad_merged, "all"), (grad_joint_mixed, "each"), (grad_expand_mixed, "each")
    )
    grad_joint_weight = f32(
        grad_joint_in.reshape(G, dn, 3, CL).transpose(1, 2, 0, 3).reshape(dn, 3 * D)
    )
    grad_expand_weight = f32(grad_expand_in.transpose(1, 0, 2).reshape(dn, FF))
    grad_merged_rows = grad_merged_rows.reshape(RG, D)
    grad_head = low(dot(grad_merged_rows, merge_s, 1, 1))
    grad_merge_weight = f32(scatter_rows(low(dot(head_low, grad_merged_rows, 0, 0))))
    grad_heads_low = grad_head.reshape(RG, HL, HDIM)
    value_back = jnp.einsum(
        "rhc,hck->hrk", grad_heads_low, value_heads, preferred_element_type=F32
    )
    weighed = value_back * field_wide[None]
    weighed_high = low(weighed)
    weighed_low = low(weighed - f32(weighed_high))
    grad_chosen = jnp.einsum("hrk,kv->hrv", weighed_high, select, preferred_element_type=F32)
    grad_chosen = grad_chosen + jnp.einsum(
        "hrk,kv->hrv", weighed_low, select, preferred_element_type=F32
    )
    grad_scores = low(
        chosen * (grad_chosen - jnp.sum(chosen * grad_chosen, axis=-1, keepdims=True))
    )
    score_spread = jnp.einsum("hrv,kv->hrk", grad_scores, select, preferred_element_type=F32)
    field_part = jnp.sum(spread * value_back + score_spread * probe_table[:, None, :], axis=0)
    field_part = field_part.reshape(G, R, KP)
    score_sums = jnp.sum(score_spread * field_wide[None], axis=1)
    head_sums = jnp.einsum(
        "rhc,hrk->hck", grad_heads_low, mixed, preferred_element_type=F32
    ).reshape(S, dn, KP)

    column_sums = jnp.stack(
        [
            low_sums(grad_merged),
            jnp.sum(lead_rows[:, None] * grad_start, axis=0),
            jnp.sum(grad_start, axis=0),
            jnp.sum(grad_normed * start_hat, axis=0),
            jnp.sum(grad_normed, axis=0),
            low_sums(grad_branch),
            jnp.sum(grad_second * middle_hat, axis=0),
            jnp.sum(grad_second, axis=0),
            jnp.sum(grad_top, axis=0),
        ]
    )
    kinds = column_sums.shape[0]
    column_sums = jnp.pad(column_sums, ((0, -kinds % 16), (0, 0)))
    column_sums = column_sums.reshape(-1, G, CL).transpose(1, 0, 2)
    position_blocks = grad_merged.reshape(R, G, CL).transpose(1, 0, 2)
    column_sums, position_blocks, field_part = swap(
        "grp", (column_sums, "each"), (position_blocks, "each"), (field_part, "each")
    )
    grad_position_table = jnp.sum(f32(position_blocks), axis=0)
    field_grad = jnp.sum(field_part, axis=0)[:, :VP]
    column_sums = jnp.sum(column_sums, axis=0)
    team_sums = jnp.concatenate(
        [
            column_sums[:kinds].reshape(kinds, S, dn).transpose(1, 0, 2).reshape(S, kinds * dn),
            joint_sums[:CL].reshape(S, dn),
            joint_sums[2 * CL :].reshape(S, dn),
            grad_expand_bias.reshape(S, fn),
        ],
        axis=1,
    )
    wide = team_sums.shape[1]
    team_sums = jnp.pad(team_sums, ((0, 0), (0, -wide % 1024))).reshape(S, -1, 128)
    score_sums = jnp.pad(score_sums, ((0, -HL % 8), (0, 0)))
    team_sums, head_sums, score_sums = swap(
        "seq", (team_sums, "each"), (low(head_sums), "each"), (score_sums, "all")
    )
    team_sums = jnp.sum(team_sums, axis=0).reshape(-1)[:wide]
    own_sums = team_sums[: kinds * dn].reshape(kinds, dn)
    grad_joint_bias = team_sums[kinds * dn : (kinds + 2) * dn].reshape(2, dn)
    grad_expand_bias = team_sums[(kinds + 2) * dn :]
    (
        grad_merge_bias,
        grad_lead_weight,
        grad_lead_bias,
        grad_first_gain,
        grad_first_shift,
        grad_output_bias,
        grad_second_gain,
        grad_second_shift,
        grad_reduce_bias,
    ) = [own_sums[i] for i in range(kinds)]
    head_sums = jnp.sum(f32(head_sums), axis=0)
    score_sums = jnp.sum(score_sums, axis=0)
    my_head = lax.axis_index("seq") * dn // HDIM
    my_scores = lax.dynamic_index_in_dim(score_sums, my_head, axis=0, keepdims=False)
    grad_query_vector = jnp.sum(key_own * my_scores[None], axis=1) * SCALE
    (head_all,) = swap("seq", (low(head_sums), "all"))
    head_all, score_all = swap(
        "grp", (head_all.reshape(S * dn, KP), "all"), (score_sums, "all")
    )
    head_all = head_all.reshape(D, KP)
    score_all = score_all[:, :HL].reshape(HEADS, KP)
    grad_value_weight = dot(table, head_all, 0, 1)
    probe_own = low(
        jnp.sum((f32(key_weight) * full_query).reshape(dn, HEADS, HDIM), axis=-1) * SCALE
    )
    grad_table = dot(head_all, value_weight, 0, 1)
    grad_table = grad_table + jnp.einsum("hk,dh->kd", score_all, f32(probe_own))
    grad_probe = jnp.einsum("kd,hk->dh", f32(table), score_all)
    grad_key_weight = (
        grad_probe[:, :, None] * full_query.reshape(HEADS, HDIM)[None] * SCALE
    ).reshape(dn, D)
    grad_patch_weight = grad_table[:VP]
    grad_variable_embed = grad_table[VP : VP + VARS]
    return (
        activations,
        field_grad,
        grad_patch_weight,
        grad_variable_embed,
        grad_query_vector,
        grad_key_weight,
        grad_value_weight,
        grad_merge_weight,
        grad_merge_bias,
        grad_position_table,
        grad_lead_weight,
        grad_lead_bias,
        grad_first_gain,
        grad_first_shift,
        grad_joint_weight,
        grad_joint_bias,
        grad_output_weight,
        grad_output_bias,
        grad_second_gain,
        grad_second_shift,
        grad_expand_weight,
        grad_expand_bias,
        grad_reduce_weight,
        grad_reduce_bias,
    )


TEAM = 4
LINE = 8
ROW = 128
TALL = TEAM * ROW
GROUP = LINE * ROW
WD = D // (TEAM * LINE)
QC = D // TEAM
TEAM_HEADS = HEADS // TEAM
PACKED = 4
VECTORS = 12
QUERY, MERGE_BIAS, LEAD_WEIGHT, LEAD_BIAS, FIRST_GAIN, FIRST_SHIFT = range(6)
OUTPUT_BIAS, SECOND_GAIN, SECOND_SHIFT, REDUCE_BIAS = range(6, 10)
SUM_ROWS = 16

INPUTS = dict(
    fields=pltpu.VMEM,
    patch=pltpu.VMEM,
    embed=pltpu.VMEM,
    key_w=pltpu.VMEM,
    value_w=pltpu.VMEM,
    pack=pltpu.VMEM,
    joint_b=pltpu.VMEM,
    segments=pltpu.VMEM,
    live=pltpu.VMEM,
    steps=pltpu.SMEM,
    cot=pl.ANY,
    position=pl.ANY,
    joint_w=pl.ANY,
    expand_w=pl.ANY,
    merge_w=pl.ANY,
    output_w=pl.ANY,
    reduce_w=pl.ANY,
)

OUTPUTS = dict(
    activations=((ROW, D), F32),
    field_grad=((VP, ROW), F32),
    g_patch=((WD, VP), F32),
    g_embed=((WD, VARS), F32),
    g_key=((WD, D), F32),
    g_value=((WD, D), F32),
    g_merge=((WD, D), F32),
    g_position=((ROW, QC), F32),
    g_joint=((WD, 3 * D), F32),
    g_output=((WD, D), F32),
    g_expand=((WD, FF), F32),
    g_reduce=((ROW, D), F32),
    small=((32, 128), F32),
)

SCRATCH = dict(
    head_all=((TEAM, LINE, WD, KP), BF16),
    score_all=((TEAM, 8, KP), F32),
    score_rows=((16, KP), F32),
    key_own=((WD, KP), F32),
    sums=((SUM_ROWS, QC), F32),
    pe=((WD, KP), BF16),
    field_all=((TEAM, ROW, KP), BF16),
    pos=((ROW, D), BF16),
    cot_all=((TEAM, ROW, D), BF16),
    pack_rows=((16, 128), F32),
    pack_all=((LINE, TEAM, 16, 128), BF16),
    vecs=((16, D), F32),
    shift_e=((8, D), F32),
    seg_q=((16, GROUP), BF16),
    seg_k=((16, GROUP), BF16),
    merge_s=((LINE, WD, D), BF16),
    output_s=((LINE, WD, D), BF16),
    reduce_s=((LINE, ROW, D), BF16),
    joint_s=((TEAM, LINE, WD, 3 * QC), BF16),
    expand_s=((TEAM, LINE, WD, D), BF16),
    e2_send=((2, LINE, WD, KP), BF16),
    e2_recv=((LINE, 2, WD, KP), BF16),
    pv=((LINE, WD, KP), BF16),
    at=((LINE, 8, KP), F32),
    probe=((8, KP), F32),
    select=((KP, 128), BF16),
    select_t=((128, KP), BF16),
    chosen=((TEAM_HEADS, TALL, 128), F32),
    head_low=((TALL, QC), BF16),
    start=((ROW, D), F32),
    start_hat=((ROW, D), F32),
    start_inv=((ROW, 128), F32),
    middle=((ROW, D), F32),
    middle_hat=((ROW, D), F32),
    middle_inv=((ROW, 128), F32),
    grad_mid=((ROW, D), F32),
    normed_all=((TEAM, ROW, D), BF16),
    second_all=((TEAM, ROW, D), BF16),
    gb_all=((TEAM, ROW, D), BF16),
    gm_all=((TEAM, ROW, D), BF16),
    pair_send=((LINE, 3, ROW, 128), BF16),
    qkv=((3, GROUP, 128), BF16),
    p_low=((2, GROUP, GROUP), BF16),
    att_f=((GROUP, 128), F32),
    att_low=((GROUP, 128), BF16),
    att_all=((TEAM, ROW, QC), BF16),
    g_send=((TEAM, 2, ROW, 128), BF16),
    go=((GROUP, 128), BF16),
    dq=((GROUP, 128), F32),
    d_all=((TEAM, 3, ROW, QC), BF16),
    active_all=((TEAM, ROW, D), BF16),
    gh_all=((TEAM, ROW, D), BF16),
    own_a=((ROW, D), F32),
    own_b=((ROW, D), F32),
    far_a=((ROW, D), F32),
    far_b=((ROW, D), F32),
    far_d=((ROW, D), F32),
    gw_merge=((LINE, WD, D), BF16),
    gw_output=((LINE, WD, D), BF16),
    gw_reduce=((LINE, ROW, D), BF16),
    gw_joint=((TEAM, LINE, WD, 3 * QC), BF16),
    gw_expand=((TEAM, LINE, WD, D), BF16),
    yr_merge=((4, WD, D), BF16),
    yr_output=((4, WD, D), BF16),
    yr_reduce=((4, ROW // 2, D), BF16),
    yr_half=((1, ROW // 2, D), BF16),
    zr_half=((6, ROW // 2, D), BF16),
    za_half=((4, ROW // 2, D), BF16),
    yr_joint=((4, TEAM, WD, 3 * QC), BF16),
    yr_expand=((4, TEAM, WD, D), BF16),
    zr_merge=((3, WD, D), BF16),
    za_merge=((2, WD, D), BF16),
    zr_output=((3, WD, D), BF16),
    za_output=((2, WD, D), BF16),
    zr_reduce=((3, ROW // 2, D), BF16),
    za_reduce=((2, ROW // 2, D), BF16),
    zr_joint=((3, TEAM, WD, 3 * QC), BF16),
    za_joint=((2, TEAM, WD, 3 * QC), BF16),
    zr_expand=((3, TEAM, WD, D), BF16),
    za_expand=((2, TEAM, WD, D), BF16),
    xs_joint=((TEAM, WD, 3 * QC), BF16),
    xs_expand=((TEAM, WD, D), BF16),
    xr_joint=((TEAM, WD, 3 * QC), BF16),
    xr_expand=((TEAM, WD, D), BF16),
    csum=((16, D), F32),
    crecv=((TEAM, 16, QC), F32),
    tsum=((LINE, SUM_ROWS, QC), F32),
    f_own=((TEAM, ROW, KP), F32),
    f_recv=((3, ROW, KP), F32),
    t_send=((LINE, WD, KP), BF16),
    t_recv=((LINE, WD, KP), BF16),
    q_all=((LINE, 8, KP), F32),
)

TEAM_SUMS = dict(
    both=(2 * QC, KP),
    merge=(ROW, D),
    branch=(ROW, D),
    second=(ROW, D),
    reduced=(ROW, D),
    normed=(ROW, D),
)


def team_sum_buffers(shape):
    near = ((2,) + shape, BF16)
    one = (shape, BF16)
    return (near, near, one, one)


SEMAPHORES = 252


def nn(a, b):
    return dot(a, b, 1, 0)


def nt(a, b):
    return dot(a, b, 1, 1)


def tn(a, b):
    return dot(a, b, 0, 0)


def lanes(at, size):
    return pl.ds(pl.multiple_of(at, 128), size)


def rows(at, size):
    return pl.ds(pl.multiple_of(at, size), size)


def fused_kernel(*refs):
    n_in, n_out = len(INPUTS), len(OUTPUTS)
    results = types.SimpleNamespace(**dict(zip(OUTPUTS, refs[n_in : n_in + n_out])))
    names = list(INPUTS) + list(SCRATCH) + list(OUTPUTS)
    rest = refs[:n_in] + refs[n_in + n_out :]
    ref = types.SimpleNamespace(**dict(zip(names, rest)))
    rest = rest[len(names) :]
    send, recv = rest[-2:]
    sums = dict(zip(TEAM_SUMS, [rest[4 * i : 4 * i + 4] for i in range(len(TEAM_SUMS))]))
    sums = types.SimpleNamespace(**sums)
    g = lax.axis_index("grp")
    s = lax.axis_index("seq")
    sib = g + 1 - 2 * lax.rem(g, 2)
    far = lax.rem(g + 2, TEAM)
    diag = lax.rem(sib + 2, TEAM)
    z = s // 2
    y = s - 2 * z
    beside = s + 1 - 2 * y
    mine = lax.rem(3 * z, TEAM)
    is_middle = (z == 1) | (z == 2)
    is_end = (z == 0) | (z == 3)
    partner = s + 2 - 4 * lax.rem(z, 2)
    facing = lax.rem(s + 6 - 4 * z + LINE, LINE)
    near_places = [4 * (z // 2) + y + 2 * i for i in range(2)]
    far_places = [4 * (1 - z // 2) + y + 2 * i for i in range(2)]

    def to_team(j):
        return (j, s)

    def to_line(j):
        return (g, j)

    used = [0]
    begun = []

    def reserve(count):
        at = used[0]
        used[0] += count
        assert used[0] <= SEMAPHORES
        return at

    def remote(src, dst, device, at):
        return pltpu.make_async_remote_copy(
            src_ref=src,
            dst_ref=dst,
            send_sem=send.at[at],
            recv_sem=recv.at[at],
            device_id=device,
            device_id_type=MESH,
        )

    def push(src, dst, device):
        copy = remote(src, dst, device, reserve(1))
        copy.start()
        begun.append(copy)
        return copy

    barrier = pltpu.get_barrier_semaphore()
    for step in range(1, TEAM):
        pl.semaphore_signal(
            barrier, inc=1, device_id=to_team(lax.rem(g + step, TEAM)), device_id_type=MESH
        )
    for step in range(1, LINE):
        pl.semaphore_signal(
            barrier, inc=1, device_id=to_line(lax.rem(s + step, LINE)), device_id_type=MESH
        )

    class Together:
        def __init__(self, bulk, waits_itself=False):
            self.bulk, self.at = bulk, reserve(1)
            if not waits_itself:
                begun_together.append(self)

        def push(self, src, dst, device):
            remote(src, dst, device, self.at).start()

        def wait_recv(self):
            remote(self.bulk, self.bulk, to_line(beside), self.at).wait_recv()

        def wait_send(self):
            remote(self.bulk, self.bulk, to_line(beside), self.at).wait_send()

    begun_together = []

    def spread(buf):
        half = buf.shape[1] // 2
        across = []
        for h in range(2):
            part = buf.at[g, pl.ds(h * half, half)]
            across.append(push(part, part, to_team(far)))
        return push(buf.at[g], buf.at[g], to_team(sib)), across

    def spread_on(buf, across):
        half = buf.shape[1] // 2
        handed = Together(buf.at[far])
        for h in range(2):
            across[h].wait_recv()
            part = buf.at[far, pl.ds(h * half, half)]
            handed.push(part, part, to_team(sib))
        return [handed]

    def wait_all(copies):
        for copy in copies:
            copy.wait_recv()

    class TeamSum:
        def __init__(self, buffers):
            self.ps, self.r, self.t, self.x = buffers
            self.near_copies = [None, None]

        def near(self, slot, value=None):
            if value is not None:
                self.ps[slot] = low(value)
            self.near_copies[slot] = push(self.ps.at[slot], self.r.at[slot], to_team(sib))

        def across(self, value):
            self.near_copies[1].wait_recv()
            half = self.t.shape[0] // 2
            self.far_copies = [Together(self.x)]
            for h in range(2):
                part = pl.ds(h * half, half)
                self.t[part] = low(value(part) + f32(self.r[1, part]))
                self.far_copies[0].push(self.t.at[part], self.x.at[part], to_team(far))

        def total(self, own):
            self.near_copies[0].wait_recv()
            wait_all(self.far_copies)
            return own + f32(self.r[0]) + f32(self.x[...])

    deposits = []

    def deposit(src, dst):
        copy = pltpu.make_async_copy(src, dst, recv.at[reserve(1)])
        copy.start()
        deposits.append(copy)

    def to_whole_line(src, dst, bulk):
        group = Together(bulk)
        for step in range(1, LINE):
            place = lax.rem(s + step, LINE)
            group.push(src(place), dst, to_line(place))
        return [group]

    def share_line(buf):
        return to_whole_line(lambda place: buf.at[s], buf.at[s], buf.at[pl.ds(0, LINE - 1)])

    def to_whole_team(src, dst, bulk):
        group = Together(bulk)
        for j in (far, diag, sib):
            group.push(src(j), dst, to_team(j))
        return [group]

    def mean(x):
        return jnp.sum(x, axis=-1, keepdims=True) * (1.0 / D)

    class Gather:
        def __init__(self, slot):
            self.slot = slot
            self.at = reserve(9)

        def send(self, place, device, i, shard=None):
            part = self.slot(place)
            remote(part if shard is None else shard, part, device, self.at + i).start()

        def come(self, i):
            part = self.slot(s)
            remote(part, part, to_line(beside), self.at + i).wait_recv()

        def stage1(self, shard=None):
            self.send(s, to_line(partner), 0, shard)
            self.send(s, to_line(beside), 1, shard)

        def stage2(self, hold=False):
            self.come(0)

            @pl.when(is_middle)
            def _():
                for i in range(2):
                    self.send(near_places[i], to_line(facing), 2 + i)

            if not hold:
                self.hand_on()

        def hand_on(self):
            self.send(partner, to_line(beside), 4)

        def stage3(self):
            @pl.when(is_middle)
            def _():
                for i in range(2):
                    self.come(2 + i)
                    self.send(far_places[i], to_line(partner), 5 + i)
                    self.send(far_places[i], to_line(beside), 7 + i)

        def stage4(self):
            @pl.when(is_end)
            def _():
                for i in range(2):
                    self.come(5 + i)
                    self.send(far_places[i], to_line(beside), 7 + i)

        def finish(self):
            for i in (1, 4, 7, 8):
                self.come(i)

        def sent(self):
            part = self.slot(s)

            def gone(i):
                remote(part, part, to_line(beside), self.at + i).wait_send()

            for i in (0, 1, 4, 7, 8):
                gone(i)

            @pl.when(is_middle)
            def _():
                for i in (2, 3, 5, 6):
                    gone(i)

    class PairExchange:
        def __init__(self, bulk):
            self.group, self.own = Together(bulk, waits_itself=True), reserve(1)

        def send(self, src, dst, there):
            @pl.when(there != s)
            def _():
                self.group.push(src, dst, to_line(there))

            @pl.when(there == s)
            def _():
                pltpu.make_async_copy(src, dst, recv.at[self.own]).start()

        def wait(self, src, dst):
            pltpu.make_async_copy(src, dst, recv.at[self.own]).wait()
            self.group.wait_recv()
            self.group.wait_send()

    pe = ref.pe
    pe[:, 0:VP] = ref.patch[...]
    pe[:, VP : VP + VARS] = ref.embed[...]
    pe[:, VP + VARS :] = jnp.zeros((WD, KP - VP - VARS), BF16)
    field_all, cot_all, pack_all = ref.field_all, ref.cot_all, ref.pack_all
    field_all[g, :, 0:VP] = ref.fields[...].T
    lane = lax.broadcasted_iota(jnp.int32, (ROW, KP - VP), 1)
    field_all[g, :, VP:] = (lane < VARS).astype(BF16)
    pack_rows = ref.pack_rows
    pack_rows[...] = f32(ref.pack[...])
    for i in range(2):
        pack_rows[2:3, 64 + i * WD : 64 + (i + 1) * WD] = f32(ref.joint_b[...])[i : i + 1]
    pack_rows[4:5] = ref.segments[...].astype(F32)
    pack_rows[5:6] = ref.live[...].astype(F32)
    pack_all[s, g] = low(pack_rows[...])
    pl.semaphore_wait(barrier, TEAM - 1 + LINE - 1)

    both = TeamSum(sums.both)

    def table_product(weight, j):
        return tn(weight[:, lanes(j * QC, QC)], pe[...])

    for slot, j in ((1, diag), (0, sib)):
        both.ps[slot, 0:QC] = low(table_product(ref.value_w, j))
        both.ps[slot, QC:] = low(table_product(ref.key_w, j))
        both.near(slot)
    field_copies = spread(field_all)
    far_parts = [table_product(ref.value_w, far), table_product(ref.key_w, far)]
    both.across(lambda part: far_parts[0] if part.start == 0 else far_parts[1])
    own_parts = [table_product(ref.value_w, g), table_product(ref.key_w, g)]
    pack_here = pack_all.at[s, g]
    pack_copies = to_whole_team(lambda j: pack_here, pack_here, pack_all.at[0, pl.ds(0, 3)])

    def whole(buf):
        return lambda i: buf.at[i]

    def inner(buf):
        return lambda i: buf.at[:, i]

    def some_rows(buf, at, size):
        return lambda i: buf.at[i, pl.ds(at, size)]

    def some_lanes(buf, at, size):
        return lambda i: buf.at[:, i, :, pl.ds(at, size)]

    half_rows, half_lanes = ROW // 2, D // 2
    gather_merge = Gather(whole(ref.merge_s))
    gather_output = Gather(whole(ref.output_s))
    gather_reduce = [Gather(some_rows(ref.reduce_s, i * half_rows, half_rows)) for i in range(2)]
    gather_joint = [Gather(some_lanes(ref.joint_s, i * QC, QC)) for i in range(3)]
    gather_expand = [Gather(some_lanes(ref.expand_s, i * half_lanes, half_lanes)) for i in range(2)]
    local = []

    def keep(src, dst):
        copy = pltpu.make_async_copy(src, dst, recv.at[reserve(1)])
        copy.start()
        local.append(copy)

    keep(ref.merge_w, ref.merge_s.at[s])
    keep(ref.output_w, ref.output_s.at[s])
    keep(ref.reduce_w, ref.reduce_s.at[s])
    keep(ref.cot, cot_all.at[g])
    gather_merge.stage1(ref.merge_w)
    for i in range(2):
        gather_reduce[i].stage1(ref.reduce_w.at[pl.ds(i * half_rows, half_rows)])

    joint_copies = [Together(ref.joint_s.at[pl.ds(0, 3), 0])]
    for j in (far, diag, sib):
        for kind in range(3):
            joint_copies[0].push(
                ref.joint_w.at[:, lanes(kind * D + j * QC, QC)],
                ref.joint_s.at[g, s, :, pl.ds(kind * QC, QC)],
                to_team(j),
            )
    for kind in range(3):
        keep(
            ref.joint_w.at[:, lanes(kind * D + g * QC, QC)],
            ref.joint_s.at[g, s, :, pl.ds(kind * QC, QC)],
        )
    expand_copies = to_whole_team(
        lambda j: ref.expand_w.at[:, lanes(j * D, D)],
        ref.expand_s.at[g, s],
        ref.expand_s.at[pl.ds(0, 3), 0],
    )
    keep(ref.expand_w.at[:, lanes(g * D, D)], ref.expand_s.at[g, s])
    keep(ref.position, ref.pos.at[:, lanes(g * QC, QC)])
    position_copies = to_whole_team(
        lambda j: ref.position, ref.pos.at[:, lanes(g * QC, QC)], ref.pos.at[:, pl.ds(0, 3 * QC)]
    )

    for copy in local:
        copy.wait()
    gather_merge.stage2()

    both.near_copies[0].wait_recv()
    wait_all(both.far_copies)
    for part in range(2):
        block = pl.ds(part * QC, QC)
        total = own_parts[part] + f32(both.r[0, block]) + f32(both.x[block])
        ref.e2_send[part] = low(total).reshape(LINE, WD, KP)
    e2_send, e2_recv = ref.e2_send, ref.e2_recv
    e2_copies = to_whole_line(
        lambda place: e2_send.at[:, place], e2_recv.at[s], e2_recv.at[pl.ds(0, LINE - 1)]
    )
    e2_recv[s] = e2_send[:, s]
    wait_all(joint_copies)
    for gather in gather_joint:
        gather.stage1()
    gather_merge.stage3()

    wait_all(e2_copies)
    table_own = jnp.sum(f32(e2_recv[...]), axis=0)
    key_own = table_own[1]
    ref.key_own[...] = key_own
    query = f32(pack_all[s, g])[0:1, 0:WD]
    key_high = low(key_own)
    key_rest = low(key_own - f32(key_high))
    query_rows = low(jnp.broadcast_to(query, (16, WD)))
    probe_part = (nn(query_rows, key_high) + nn(query_rows, key_rest)) * SCALE
    pv, at = ref.pv, ref.at
    pv[s] = low(table_own[0])
    at[s] = probe_part[0:8]
    pv_copies = share_line(pv)
    at_copies = to_whole_line(
        lambda place: at.at[s, pl.ds(0, 1)],
        at.at[s, pl.ds(0, 1)],
        at.at[pl.ds(0, LINE - 1), pl.ds(0, 1)],
    )
    for gather in gather_joint:
        gather.stage2()
    wait_all(pv_copies)
    wait_all(at_copies)
    gather_merge.stage4()
    wait_all(pack_copies)
    pack_line = share_line(pack_all)
    wait_all(expand_copies)
    for gather in gather_expand:
        gather.stage1()

    probe = ref.probe
    for h in range(TEAM_HEADS):
        probe[h : h + 1] = at[2 * h, 0:1] + at[2 * h + 1, 0:1]
    probe[TEAM_HEADS:] = jnp.zeros((8 - TEAM_HEADS, KP), F32)

    def owner_of(k):
        return jnp.where(k < VP, k // PIX, jnp.where(k < VP + VARS, k - VP, VARS + 64))

    select, select_t = ref.select, ref.select_t
    select[...] = (
        owner_of(lax.broadcasted_iota(jnp.int32, (KP, 128), 0))
        == lax.broadcasted_iota(jnp.int32, (KP, 128), 1)
    ).astype(BF16)
    select_t[...] = (
        owner_of(lax.broadcasted_iota(jnp.int32, (128, KP), 1))
        == lax.broadcasted_iota(jnp.int32, (128, KP), 0)
    ).astype(BF16)
    valid = lax.broadcasted_iota(jnp.int32, (1, 128), 1) < VARS
    head_of_lane = lax.broadcasted_iota(jnp.int32, (1, QC), 1) // HDIM

    field_handed = spread_on(field_all, field_copies[1])
    field_copies[0].wait_recv()
    wait_all(field_handed)

    def tall(buf):
        return buf[...].reshape(TALL, -1)

    def split_dot(x, b):
        high = low(x)
        return nn(high, b) + nn(low(x - f32(high)), b)

    chosen, head_low = ref.chosen, ref.head_low

    def choose(h):
        field = f32(tall(field_all))
        scores = split_dot(field * probe[h : h + 1], select[...])
        scores = jnp.where(valid, scores, MASKED)
        terms = jnp.exp(scores - jnp.max(scores, axis=-1, keepdims=True))
        weights = terms * (1.0 / jnp.sum(terms, axis=-1, keepdims=True))
        chosen[h] = weights
        mix = low(nn(low(weights), select_t[...]) * field)
        table_value = pv[2 * h : 2 * h + 2].reshape(HDIM, KP)
        head_low[:, h * HDIM : (h + 1) * HDIM] = low(nt(mix, table_value))

    for h in range(TEAM_HEADS):
        choose(h)

    merge_s, output_s = ref.merge_s, ref.output_s
    gather_merge.finish()
    merge = TeamSum(sums.merge)

    def row_weight(buf):
        return buf[...].reshape(-1, D)

    def two(buf, i, j):
        return jnp.concatenate([buf[i], buf[j]], axis=0)

    def merge_part(j):
        return nn(head_low[rows(j * ROW, ROW)], row_weight(merge_s))

    merge.near(1, merge_part(diag))
    ref.far_a[...] = merge_part(far)
    merge.across(lambda part: ref.far_a[part])
    merge.near(0, merge_part(sib))
    ref.own_a[...] = merge_part(g)

    wait_all(pack_line)
    vecs, shift_e = ref.vecs, ref.shift_e
    lane_piece = lax.broadcasted_iota(jnp.int32, (LINE, 1, QC), 2) // WD
    piece = lax.broadcasted_iota(jnp.int32, (LINE, 1, QC), 0)
    for q in range(PACKED):
        place = (
            lax.broadcasted_iota(jnp.int32, (128, QC), 1) % WD + q * WD
            == lax.broadcasted_iota(jnp.int32, (128, QC), 0)
        ).astype(BF16)
        for j in range(TEAM):
            spreadout = nn(pack_all[:, j].reshape(LINE * 16, 128), place)
            spreadout = jnp.where(lane_piece == piece, spreadout.reshape(LINE, 16, QC), 0.0)
            spreadout = jnp.sum(spreadout, axis=0)
            vecs[4 * q : 4 * q + 4, j * QC : (j + 1) * QC] = spreadout[0:4]

    def vector(i):
        at_row = 4 * (i % PACKED) + i // PACKED
        return vecs[at_row : at_row + 1, :]

    joint_shift = [
        vecs[4 * (i % PACKED) + i // PACKED, lanes(g * QC, QC)].reshape(1, QC) for i in (10, 11)
    ]
    seg_q, seg_k = ref.seg_q, ref.seg_k
    sub = lax.broadcasted_iota(jnp.int32, (16, 128), 0).astype(F32)
    for j in range(LINE):
        part = f32(pack_all[j, g])
        shift_e[:, j * 128 : (j + 1) * 128] = jnp.broadcast_to(part[3:4], (8, 128))
        part = f32(pack_all[j, mine])
        same = jnp.where(sub == part[4:5], 1.0, 0.0)
        seg_q[:, j * 128 : (j + 1) * 128] = low(same)
        seg_k[:, j * 128 : (j + 1) * 128] = low(same * part[5:6])
    own_seg = ref.segments[...].astype(F32)
    steps = ref.steps
    lead_lanes = jnp.zeros((1, 128), F32)
    for i in range(steps.shape[1]):
        lead_lanes = jnp.where(own_seg == i, LEAD_UNIT * steps[0, i].astype(F32), lead_lanes)
    lead = jnp.broadcast_to(lead_lanes, (ROW, 128)).T[:, 0:1]
    wait_all(position_copies)
    for gather in gather_joint:
        gather.stage3()
    gather_output.stage1(ref.output_w)
    for gather in gather_reduce:
        gather.stage2(hold=True)

    start_ref = ref.start
    start_ref[...] = (
        merge.total(ref.own_a[...])
        + vector(MERGE_BIAS)
        + f32(ref.pos[...])
        + lead * vector(LEAD_WEIGHT)
        + vector(LEAD_BIAS)
    )

    def norm(x, hat_ref, inv_ref, gain, shift):
        center = x - mean(x)
        inverse = lax.rsqrt(mean(center * center) + EPSILON)
        hat = center * inverse
        hat_ref[...] = hat
        inv_ref[...] = jnp.broadcast_to(inverse, (ROW, 128))
        return low(hat * gain + shift)

    def norm_back_ref(grad, hat_ref, inv_ref, gain):
        f = grad * gain
        hat = hat_ref[...]
        return inv_ref[:, 0:1] * (f - mean(f) - hat * mean(f * hat))

    normed_all = ref.normed_all
    normed_all[g] = norm(
        start_ref[...],
        ref.start_hat,
        ref.start_inv,
        vector(FIRST_GAIN),
        vector(FIRST_SHIFT),
    )
    normed_copies = spread(normed_all)
    joint_s, pair_send, qkv = ref.joint_s, ref.pair_send, ref.qkv
    for gather in gather_joint:
        gather.stage4()
    e6 = [PairExchange(qkv.at[kind, pl.ds(0, 7 * ROW), :]) for kind in range(3)]

    def pair_place(j, t):
        return 2 * lax.rem(3 * j, TEAM) + t

    line_rows = rows(s * ROW, ROW)

    def joint_rows(i, j):
        block = two(normed_all, i, j)
        for kind in range(3):
            if i is g:
                gather_joint[kind].finish()
            weight = joint_s[:, :, :, kind * QC : (kind + 1) * QC].reshape(D, QC)
            part = nn(block, weight)
            if kind != 1:
                part = part + joint_shift[kind // 2]
            part = low(part)
            for n, group in enumerate((i, j)):
                for t in range(2):
                    place = pair_place(group, t)
                    pair_send[place, kind] = part[n * ROW : (n + 1) * ROW, t * 128 : (t + 1) * 128]
                    e6[kind].send(pair_send.at[place, kind], qkv.at[kind, line_rows, :], place)

    normed_copies[0].wait_recv()
    joint_rows(g, sib)
    normed_handed = spread_on(normed_all, normed_copies[1])
    wait_all(normed_handed)
    joint_rows(far, diag)
    gather_output.stage2()
    gather_expand[0].stage2()
    for gather in gather_reduce:
        gather.hand_on()
        gather.stage3()
    for kind in range(3):
        e6[kind].wait(pair_send.at[0, kind], qkv.at[kind, line_rows, :])
    gather_output.stage3()
    gather_expand[1].stage2()
    cot_copies = spread(cot_all)

    half_of_lane = lax.broadcasted_iota(jnp.int32, (1, 128), 1) // HDIM
    p_low, att_f, att_low, att_all = ref.p_low, ref.att_f, ref.att_low, ref.att_all
    e7 = PairExchange(att_low.at[pl.ds(0, 7 * ROW)])
    pair_lanes = lanes(y * 128, 128)

    def attend_rows(b, carry):
        here = rows(b * 256, 256)
        queries = f32(qkv[0, here, :]) * SCALE
        keys, values = qkv[1], qkv[2]
        allowed = tn(seg_q[:, lanes(b * 256, 256)], seg_k[...]) > 0.5
        outs = []
        for t in range(2):
            scores = nt(low(jnp.where(half_of_lane == t, queries, 0.0)), keys)
            scores = jnp.where(allowed, scores, MASKED)
            terms = jnp.exp(scores - jnp.max(scores, axis=-1, keepdims=True))
            weights = low(terms * (1.0 / jnp.sum(terms, axis=-1, keepdims=True)))
            p_low[t, here, :] = weights
            outs.append(nn(weights, values))
        out = jnp.where(half_of_lane == 0, outs[0], outs[1])
        att_f[here] = out
        att_low[here] = low(out)
        for t in range(2):
            there = 2 * b + t
            e7.send(att_low.at[rows(there * ROW, ROW)], att_all.at[mine, :, pair_lanes], there)

        return carry

    lax.fori_loop(0, GROUP // 256, attend_rows, 0)
    gather_output.stage4()
    for gather in gather_reduce:
        gather.stage4()
    for gather in gather_expand:
        gather.stage3()
    gather_output.finish()
    e7.wait(att_low.at[pl.ds(0, ROW)], att_all.at[mine, :, pair_lanes])

    branch = TeamSum(sums.branch)

    def branch_part(j):
        return nn(att_all[j], row_weight(output_s))

    branch.near(1, branch_part(diag))
    ref.far_a[...] = branch_part(far)
    branch.across(lambda part: ref.far_a[part])
    branch.near(0, branch_part(sib))
    ref.own_a[...] = branch_part(g)
    cot_handed = spread_on(cot_all, cot_copies[1])
    gather_expand[0].stage4()
    middle_ref = ref.middle
    middle_ref[...] = branch.total(ref.own_a[...]) + start_ref[...] + vector(OUTPUT_BIAS)

    class LineSum:
        def __init__(self, four, slot, yr, zr, za):
            self.four = four
            self.slot, self.yr, self.zr, self.za = slot, yr, zr, za
            self.at = reserve(6)

        def send(self, src, dst, device, i):
            remote(src, dst, device, self.at + i).start()

        def come(self, i):
            part = self.zr(0)
            remote(part, part, to_line(beside), self.at + i).wait_recv()

        def along_y(self):
            self.y_copies = Together(self.four)
            for i in range(4):
                self.y_copies.push(self.slot(2 * i + 1 - y), self.yr(i), to_line(beside))

        def add(self, place, came):
            block = self.slot(place)
            block[...] = low(f32(block[...]) + f32(came[...]))
            return block

        def sum_y(self):
            self.y_copies.wait_recv()

            def add(i, carry):
                self.add(2 * i + y, self.yr(i))
                return carry

            lax.fori_loop(0, 4, add, 0)

        def stage1(self):
            @pl.when(is_end)
            def _():
                for i, place in enumerate(far_places + [partner]):
                    self.send(self.slot(place), self.zr(i), to_line(partner), i)

        def stage2(self):
            @pl.when(is_middle)
            def _():
                for i, place in enumerate(far_places):
                    self.come(i)
                    block = self.add(place, self.zr(i))
                    self.send(block, self.za(i), to_line(facing), 3 + i)

        def stage3(self):
            @pl.when(is_middle)
            def _():
                for i in range(2):
                    self.come(3 + i)
                block = self.add(partner, self.za(1 - lax.rem(z, 2)))
                self.send(block, self.zr(0), to_line(partner), 5)

        def total(self, out):
            own = f32(self.slot(s)[...])

            @pl.when(is_middle)
            def _():
                self.come(2)
                total = own + f32(self.zr(2)[...]) + f32(self.za(lax.rem(z, 2))[...])
                out[...] = total.astype(out.dtype)

            @pl.when(is_end)
            def _():
                self.come(5)
                out[...] = (own + f32(self.zr(0)[...])).astype(out.dtype)

        def sent(self):
            part = self.zr(0)

            def gone(i):
                remote(part, part, to_line(beside), self.at + i).wait_send()

            @pl.when(is_middle)
            def _():
                for i in (3, 4, 5):
                    gone(i)

            @pl.when(is_end)
            def _():
                for i in range(3):
                    gone(i)

    class LineSumZ:
        def __init__(self, slot, zr, za, yr):
            self.slot, self.zr, self.za, self.yr = slot, zr, za, yr
            self.at = reserve(13)

        def both_y(self, place):
            return [place - y, place - y + 1]

        def send(self, src, dst, device, i):
            remote(src, dst, device, self.at + i).start()

        def come(self, i):
            part = self.zr(0)
            remote(part, part, to_line(beside), self.at + i).wait_recv()

        def add(self, place, came):
            block = self.slot(place)
            block[...] = low(f32(block[...]) + f32(came[...]))
            return block

        def stage1(self):
            @pl.when(is_end)
            def _():
                for i, place in enumerate(
                    self.both_y(far_places[0]) + self.both_y(far_places[1]) + self.both_y(partner)
                ):
                    self.send(self.slot(place), self.zr(i), to_line(partner), i)

        def stage2(self):
            @pl.when(is_middle)
            def _():
                for i, place in enumerate(self.both_y(far_places[0]) + self.both_y(far_places[1])):
                    self.come(i)
                    block = self.add(place, self.zr(i))
                    self.send(block, self.za(i), to_line(facing), 6 + i)

        def stage3(self):
            @pl.when(is_middle)
            def _():
                for i in range(4):
                    self.come(6 + i)
                for i, place in enumerate(self.both_y(partner)):
                    block = self.add(place, self.za(2 * (1 - lax.rem(z, 2)) + i))
                    self.send(block, self.zr(i), to_line(partner), 10 + i)
                for i, place in enumerate(self.both_y(s)):
                    self.come(4 + i)
                    self.add(place, self.zr(4 + i))
                    self.add(place, self.za(2 * lax.rem(z, 2) + i))

        def along_y(self):
            @pl.when(is_end)
            def _():
                for i, place in enumerate(self.both_y(s)):
                    self.come(10 + i)
                    self.add(place, self.zr(i))

            self.send(self.slot(beside), self.yr(0), to_line(beside), 12)

        def total(self, out):
            self.come(12)
            out[...] = f32(self.slot(s)[...]) + f32(self.yr(0)[...])

        def sent(self):
            part = self.zr(0)

            def gone(i):
                remote(part, part, to_line(beside), self.at + i).wait_send()

            gone(12)

            @pl.when(is_middle)
            def _():
                for i in (6, 7, 8, 9, 10, 11):
                    gone(i)

            @pl.when(is_end)
            def _():
                for i in range(6):
                    gone(i)

    def line_sum_of(gw, others, at=None, size=None):
        four = others[0]
        if at is None:
            return LineSum(four, whole(gw), *[whole(buf) for buf in others])
        if len(gw.shape) == 3:
            return LineSum(four, some_rows(gw, at, size), *[whole(buf) for buf in others])

        def part(buf):
            return lambda i: buf.at[i, :, :, pl.ds(at, size)]

        four = four.at[:, :, :, pl.ds(at, size)]
        return LineSum(four, some_lanes(gw, at, size), *[part(buf) for buf in others])

    output_sum = line_sum_of(ref.gw_output, [ref.yr_output, ref.zr_output, ref.za_output])
    merge_sum = line_sum_of(ref.gw_merge, [ref.yr_merge, ref.zr_merge, ref.za_merge])
    reduce_y = line_sum_of(
        ref.gw_reduce, [ref.yr_reduce, ref.zr_reduce, ref.za_reduce], 0, half_rows
    )
    reduce_z = LineSumZ(
        some_rows(ref.gw_reduce, half_rows, half_rows),
        whole(ref.zr_half),
        whole(ref.za_half),
        whole(ref.yr_half),
    )
    reduce_sums = [reduce_y, reduce_z]
    expand_sums = [
        line_sum_of(
            ref.gw_expand,
            [ref.yr_expand, ref.zr_expand, ref.za_expand],
            i * half_lanes,
            half_lanes,
        )
        for i in range(2)
    ]
    joint_sums = [
        line_sum_of(ref.gw_joint, [ref.yr_joint, ref.zr_joint, ref.za_joint], i * QC, QC)
        for i in range(3)
    ]

    second_all = ref.second_all
    second_all[g] = norm(
        middle_ref[...],
        ref.middle_hat,
        ref.middle_inv,
        vector(SECOND_GAIN),
        vector(SECOND_SHIFT),
    )
    second_copies = spread(second_all)
    for gather in [gather_expand[0]] + gather_reduce:
        gather.finish()
    cot_copies[0].wait_recv()
    wait_all(cot_handed)
    expand_s, reduce_s = ref.expand_s, ref.reduce_s
    active_all, gh_all = ref.active_all, ref.gh_all
    root = 0.7978845608028654

    def feed(j, k, acc_a, acc_b, half):
        def tile(i, carry):
            here = lanes(i * 256, 256)
            up = expand_s[:, :, :, here].reshape(D, 256)
            down = reduce_s[pl.ds(2 * i, 2)].reshape(256, D)
            hidden = nn(two(second_all, j, k), up) + shift_e[0:1, here]
            square = hidden * hidden
            bend = jnp.tanh(root * hidden * (1.0 + 0.044715 * square))
            active = low(0.5 * hidden * (1.0 + bend))
            slope = 0.5 * (1.0 + bend) + (0.5 * root) * hidden * (1.0 - bend * bend) * (
                1.0 + (3.0 * 0.044715) * square
            )
            grad = low(nt(two(cot_all, j, k), down) * slope)
            for n, block in enumerate((j, k)):
                active_all[block, :, here] = active[n * ROW : (n + 1) * ROW]
                gh_all[block, :, here] = grad[n * ROW : (n + 1) * ROW]
            for part, acc in ((nt(grad, up), acc_a), (nn(active, down), acc_b)):
                for n in range(2):
                    rows_of = part[n * ROW : (n + 1) * ROW]

                    @pl.when(i == 0)
                    def _():
                        acc[n][...] = rows_of

                    @pl.when(i > 0)
                    def _():
                        acc[n][...] += rows_of

            return carry

        lax.fori_loop(2 * half, 2 * half + 2, tile, 0)

    gw_expand = ref.gw_expand

    def expand_blocks(first, last, half):
        def block(i, carry):
            lhs = second_all[:, :, lanes(i * QC, QC)].reshape(TALL, QC)
            rhs = gh_all[:, :, half * half_lanes : (half + 1) * half_lanes].reshape(TALL, half_lanes)
            part = low(tn(lhs, rhs)).reshape(LINE, WD, half_lanes)
            gw_expand[i, :, :, half * half_lanes : (half + 1) * half_lanes] = part
            return carry

        lax.fori_loop(first, last, block, 0)

    second = TeamSum(sums.second)
    reduced = TeamSum(sums.reduced)
    own_a, own_b, far_a, far_b = ref.own_a, ref.own_b, ref.far_a, ref.far_b
    spare_a, spare_b = ref.grad_mid, ref.activations
    far_c, far_d = ref.g_reduce, ref.far_d
    near_blocks = (g, sib, (own_a, spare_a), (own_b, spare_b))
    far_blocks = (far, diag, (far_a, far_c), (far_b, far_d))
    second_copies[0].wait_recv()
    feed(*near_blocks, 0)
    second_handed = spread_on(second_all, second_copies[1])
    gather_expand[1].stage4()
    wait_all(second_handed)
    feed(*far_blocks, 0)
    expand_blocks(0, TEAM, 0)
    expand_sums[0].along_y()
    gather_expand[1].finish()
    feed(*near_blocks, 1)
    second.near(0, spare_a[...])
    reduced.ps[0] = low(spare_b[...])
    feed(*far_blocks, 1)
    second.near(1, far_c[...])
    reduced.ps[1] = low(far_d[...])
    second.across(lambda part: far_a[part])
    reduced.near(0)
    reduced.near(1)

    gw_reduce = ref.gw_reduce

    def reduce_block(j):
        lhs = active_all[:, :, lanes(j * ROW, ROW)].reshape(TALL, ROW)
        gw_reduce[j] = low(tn(lhs, tall(cot_all)))

    def reduce_beside(i, carry):
        reduce_block(2 * i + 1 - y)
        return carry

    def reduce_here(i, carry):
        reduce_block(2 * i + y)
        return carry

    lax.fori_loop(0, 4, reduce_beside, 0)
    reduce_y.along_y()
    lax.fori_loop(0, 4, reduce_here, 0)
    reduce_z.stage1()

    csum = ref.csum

    def note(i, value):
        csum[i : i + 1] = jnp.sum(value, axis=0, keepdims=True)

    grad_second = second.total(own_a[...])
    grad_mid = ref.grad_mid
    note(6, grad_second * ref.middle_hat[...])
    note(7, grad_second)
    grad_top = f32(cot_all[g])
    note(8, grad_top)
    grad_mid[...] = grad_top + norm_back_ref(
        grad_second, ref.middle_hat, ref.middle_inv, vector(SECOND_GAIN)
    )
    gb_all = ref.gb_all
    gb_all[g] = low(grad_mid[...])
    gb_copies = spread(gb_all)
    note(5, f32(gb_all[g]))
    g_send, go = ref.g_send, ref.go
    e12 = PairExchange(go.at[pl.ds(0, 7 * ROW)])

    def attended_back(i, j):
        part = low(nt(two(gb_all, i, j), row_weight(output_s)))
        for n, group in enumerate((i, j)):
            for t in range(2):
                g_send[group, t] = part[n * ROW : (n + 1) * ROW, t * 128 : (t + 1) * 128]
                e12.send(g_send.at[group, t], go.at[line_rows, :], pair_place(group, t))

    gb_copies[0].wait_recv()
    attended_back(g, sib)
    expand_blocks(0, 2, 1)
    gb_handed = spread_on(gb_all, gb_copies[1])
    wait_all(gb_handed)
    attended_back(far, diag)
    reduced.across(lambda part: far_b[part])
    expand_blocks(2, TEAM, 1)
    expand_sums[1].along_y()
    reduce_y.sum_y()
    reduce_y.stage1()
    gw_output = ref.gw_output
    gw_output[...] = low(tn(tall(att_all), tall(gb_all))).reshape(LINE, WD, D)
    e12.wait(g_send.at[0, 0], go.at[line_rows, :])
    output_sum.along_y()

    dq, d_all = ref.dq, ref.d_all
    dq[...] = jnp.zeros_like(dq)
    e13 = PairExchange(qkv.at[pl.ds(0, 2), pl.ds(0, 7 * ROW), :])
    products = f32(go[...]) * att_f[...]
    offsets = [
        jnp.sum(jnp.where(half_of_lane == t, products, 0.0), axis=-1, keepdims=True)
        for t in range(2)
    ]
    att_f[...] = jnp.where(half_of_lane == 0, offsets[0], offsets[1])
    pair_d = d_all.at[mine, pl.ds(1, 2), :, pair_lanes]

    def attend_back_keys(b, carry):
        here = rows(b * 256, 256)
        keys, values = qkv[1, here, :], qkv[2, here, :]
        queries, grad = f32(qkv[0]), f32(go[...])
        outs, grad_keys, grad_values = [], 0.0, 0.0
        for t in range(2):
            grad_t = low(jnp.where(half_of_lane == t, grad, 0.0))
            query_t = low(jnp.where(half_of_lane == t, queries, 0.0))
            weights = p_low[t, :, lanes(b * 256, 256)]
            offset = att_f[:, t * HDIM : t * HDIM + 1]
            slopes = low(low(f32(weights) * (nt(grad_t, values) - offset)) * SCALE)
            outs.append(nn(slopes, keys))
            grad_keys += tn(slopes, query_t)
            grad_values += tn(weights, grad_t)
        dq[...] += jnp.where(half_of_lane == 0, outs[0], outs[1])
        pair_send[pl.ds(2 * b, 2), 1] = low(grad_keys).reshape(2, ROW, 128)
        pair_send[pl.ds(2 * b, 2), 2] = low(grad_values).reshape(2, ROW, 128)
        for t in range(2):
            there = 2 * b + t
            e13.send(pair_send.at[there, pl.ds(1, 2)], pair_d, there)

        return carry

    lax.fori_loop(0, 2, attend_back_keys, 0)
    lax.fori_loop(2, GROUP // 256, attend_back_keys, 0)
    pair_send[:, 0] = low(dq[...]).reshape(LINE, ROW, 128)
    d_dst = d_all.at[mine, 0, :, pair_lanes]
    d_copies = to_whole_line(
        lambda place: pair_send.at[place, 0], d_dst, att_low.at[pl.ds(0, 7 * ROW)]
    )
    d_here = pltpu.make_async_copy(pair_send.at[s, 0], d_dst, recv.at[reserve(1)])
    d_here.start()
    d_here.wait()
    wait_all(d_copies)
    e13.wait(pair_send.at[0, pl.ds(1, 2)], pair_d)
    normed = TeamSum(sums.normed)

    def joint_back(j):
        total = None
        for kind in range(3):
            weight = joint_s[:, :, :, kind * QC : (kind + 1) * QC].reshape(D, QC)
            part = nt(d_all[j, kind], weight)
            total = part if total is None else total + part
        return total

    normed.near(1, joint_back(diag))
    far_a[...] = joint_back(far)
    normed.across(lambda part: far_a[part])
    for part in expand_sums:
        part.sum_y()
        part.stage1()
    reduce_z.stage2()
    normed.near(0, joint_back(sib))
    own_a[...] = joint_back(g)
    gw_joint = ref.gw_joint
    tsum = ref.tsum
    for kind in range(3):
        block = d_all[:, kind].reshape(TALL, QC)
        for i in range(TEAM):
            lhs = normed_all[:, :, i * QC : (i + 1) * QC].reshape(TALL, QC)
            part = low(tn(lhs, block)).reshape(LINE, WD, QC)
            gw_joint[i, :, :, kind * QC : (kind + 1) * QC] = part
        if kind != 1:
            row = 9 + kind // 2
            tsum[s, row : row + 1] = jnp.sum(f32(block), axis=0, keepdims=True)
    for part in joint_sums:
        part.along_y()
    hidden_sums = jnp.sum(f32(tall(gh_all)), axis=0, keepdims=True)
    for i in range(4):
        tsum[s, 11 + i : 12 + i] = hidden_sums[:, i * QC : (i + 1) * QC]
    tsum[s, 15:16] = jnp.zeros((1, QC), F32)

    grad_normed = normed.total(own_a[...])
    note(3, grad_normed * ref.start_hat[...])
    note(4, grad_normed)
    grad_start = grad_mid[...] + norm_back_ref(
        grad_normed, ref.start_hat, ref.start_inv, vector(FIRST_GAIN)
    )
    gm_all = ref.gm_all
    gm_all[g] = low(grad_start)
    gm_copies = spread(gm_all)
    note(0, f32(gm_all[g]))
    note(1, lead * grad_start)
    note(2, grad_start)
    csum[9:16] = jnp.zeros((7, D), F32)
    crecv = ref.crecv
    crecv[g] = csum[:, lanes(g * QC, QC)]
    c_copies = to_whole_team(
        lambda j: csum.at[:, lanes(j * QC, QC)], crecv.at[g], crecv.at[pl.ds(0, 3)]
    )
    ref.activations[...] = (
        reduced.total(own_b[...]) + middle_ref[...] + vector(REDUCE_BIAS)
    )
    deposit(ref.activations, results.activations)
    reduce_y.stage2()
    expand_sums[0].stage2()
    joint_sums[0].sum_y()
    joint_sums[0].stage1()
    gm_handed = spread_on(gm_all, gm_copies[1])
    gm_copies[0].wait_recv()
    wait_all(gm_handed)

    gw_merge = ref.gw_merge
    f_own = ref.f_own
    t_send = ref.t_send
    q_all = ref.q_all
    grad_heads = low(nt(tall(gm_all), row_weight(merge_s)))
    head_grad = ref.att_all
    head_grad[...] = grad_heads.reshape(TEAM, ROW, QC)
    q_all[s] = jnp.zeros((8, KP), F32)

    def choose_back(h):
        field = f32(tall(field_all))
        grad_h = low(jnp.where(head_of_lane == h, f32(tall(head_grad)), 0.0))
        value_back = nn(grad_h, pv[...].reshape(QC, KP))
        grad_chosen = split_dot(value_back * field, select[...])
        weights = chosen[h]
        shifted = grad_chosen - jnp.sum(weights * grad_chosen, axis=-1, keepdims=True)
        score_spread = nn(low(weights * shifted), select_t[...])
        spread_weights = nn(low(weights), select_t[...])
        pair = tall(head_grad)[:, (h // 2) * 128 : (h // 2 + 1) * 128]
        part = tn(pair, low(spread_weights * field))
        at_row = (h % 2) * HDIM
        t_send[2 * h : 2 * h + 2] = low(part[at_row : at_row + HDIM]).reshape(2, WD, KP)
        field_part = spread_weights * value_back + score_spread * probe[h : h + 1]
        field_part = field_part.reshape(TEAM, ROW, KP)
        if h == 0:
            f_own[...] = field_part
        else:
            f_own[...] += field_part
        q_all[s, h : h + 1] = jnp.sum(score_spread * field, axis=0, keepdims=True)

    for h in range(TEAM_HEADS):
        choose_back(h)
        if h == 0:
            reduce_z.stage3()
            joint_sums[1].sum_y()
            joint_sums[1].stage1()
        if h == 2:
            output_sum.sum_y()
            output_sum.stage1()
            expand_sums[1].stage2()
            reduce_y.stage3()
    t_recv = ref.t_recv
    t_copies = to_whole_line(
        lambda place: t_send.at[place], t_recv.at[s], t_recv.at[pl.ds(0, LINE - 1)]
    )
    t_recv[s] = t_send[s]
    q_copies = share_line(q_all)
    gw_merge[...] = low(tn(head_low[...], tall(gm_all))).reshape(LINE, WD, D)
    merge_sum.along_y()
    reduce_z.along_y()
    expand_sums[0].stage3()
    f_recv = ref.f_recv
    f_copies = Together(f_recv)
    for step in range(1, TEAM):
        j = lax.rem(g + step, TEAM)
        f_copies.push(f_own.at[j], f_recv.at[step - 1], to_team(j))
    position = jnp.zeros((ROW, QC), F32)
    for j in range(TEAM):
        position += f32(gm_all[j, :, lanes(g * QC, QC)])
    ref.g_position[...] = position
    deposit(ref.g_position, results.g_position)
    wait_all(c_copies)
    tsum[s, 0:9] = jnp.sum(crecv[...], axis=0)[0:9]

    joint_sums[0].stage2()
    joint_sums[2].sum_y()
    joint_sums[2].stage1()
    joint_sums[1].stage2()
    expand_sums[1].stage3()
    output_sum.stage2()
    joint_sums[2].stage2()
    merge_sum.sum_y()
    merge_sum.stage1()
    wait_all(t_copies)
    head_all, score_all = ref.head_all, ref.score_all
    head_all[g, s] = low(jnp.sum(f32(t_recv[...]), axis=0))
    h_here = head_all.at[g, s]
    h_copies = to_whole_line(lambda place: h_here, h_here, head_all.at[0, pl.ds(0, LINE - 1)])
    joint_sums[0].stage3()
    joint_sums[1].stage3()
    output_sum.stage3()
    merge_sum.stage2()

    xs_joint, xs_expand = ref.xs_joint, ref.xs_expand
    xr_joint, xr_expand = ref.xr_joint, ref.xr_expand
    x_copies = []

    def to_owners(line_sum, xs, xr, at, size):
        here = pl.ds(at, size)
        line_sum.total(xs.at[:, :, here])
        x_copies.extend(
            to_whole_team(
                lambda j: xs.at[j, :, here], xr.at[g, :, here], xr.at[pl.ds(0, 3), :, here]
            )
        )
        xr[g, :, here] = xs[g, :, here]

    to_owners(expand_sums[0], xs_expand, xr_expand, 0, half_lanes)
    joint_sums[2].stage3()
    to_owners(joint_sums[0], xs_joint, xr_joint, 0, QC)
    wait_all(h_copies)
    h_spread = spread(head_all)
    s_copies = share_line(tsum)
    merge_sum.stage3()
    wait_all(q_copies)
    score_all[g] = jnp.sum(q_all[...], axis=0)
    score_here = score_all.at[g]
    score_copies = to_whole_team(lambda j: score_here, score_here, score_all.at[pl.ds(0, 3)])
    to_owners(expand_sums[1], xs_expand, xr_expand, half_lanes, half_lanes)
    to_owners(joint_sums[1], xs_joint, xr_joint, QC, QC)
    h_handed = spread_on(head_all, h_spread[1])
    to_owners(joint_sums[2], xs_joint, xr_joint, 2 * QC, QC)
    for i in range(2):
        reduce_sums[i].total(ref.g_reduce.at[pl.ds(i * half_rows, half_rows)])
    deposit(ref.g_reduce, results.g_reduce)
    output_sum.total(ref.g_output)
    deposit(ref.g_output, results.g_output)
    f_copies.wait_recv()
    ref.field_grad[...] = (f_own[g] + f_recv[0] + f_recv[1] + f_recv[2]).T[0:VP]
    deposit(ref.field_grad, results.field_grad)
    wait_all(s_copies)
    ref.sums[...] = jnp.sum(tsum[...], axis=0)
    merge_sum.total(ref.g_merge)
    deposit(ref.g_merge, results.g_merge)
    wait_all(x_copies)
    for j in range(TEAM):
        ref.g_expand[:, j * D : (j + 1) * D] = f32(xr_expand[j])
        for kind in range(3):
            at_lane = kind * D + j * QC
            ref.g_joint[:, at_lane : at_lane + QC] = f32(
                xr_joint[j, :, kind * QC : (kind + 1) * QC]
            )
    deposit(ref.g_expand, results.g_expand)
    deposit(ref.g_joint, results.g_joint)
    wait_all(score_copies)
    score_rows = ref.score_rows
    for j in range(TEAM):
        score_rows[TEAM_HEADS * j : TEAM_HEADS * (j + 1)] = score_all[j, 0:TEAM_HEADS]

    def exact(a, b, ca, cb):
        return lax.dot_general(
            a,
            b,
            (((ca,), (cb,)), ((), ())),
            precision=lax.Precision.HIGHEST,
            preferred_element_type=F32,
        )

    scores = score_rows[...]
    query_row = vector(QUERY)
    head_of = lax.broadcasted_iota(jnp.int32, (16, D), 1) // HDIM
    head_rows = (head_of == lax.broadcasted_iota(jnp.int32, (16, D), 0)).astype(F32)
    probe_own = f32(
        low(exact(f32(ref.key_w[...]) * query_row, head_rows, 1, 1) * SCALE)
    )
    grad_probe = exact(f32(pe[...]), scores, 1, 1)
    ref.g_key[...] = exact(grad_probe, head_rows, 1, 0) * (query_row * SCALE)
    deposit(ref.g_key, results.g_key)
    small = ref.small
    picks = (
        lax.broadcasted_iota(jnp.int32, (QC, 128), 0)
        == lax.broadcasted_iota(jnp.int32, (QC, 128), 1) + s * WD
    ) & (lax.broadcasted_iota(jnp.int32, (QC, 128), 1) < WD)
    small[16:24] = jnp.zeros((8, 128), F32)
    small[0:SUM_ROWS] = exact(ref.sums[...], picks.astype(F32), 1, 0)
    hidden_row = jnp.zeros((1, QC), F32)
    score_row = jnp.zeros((1, KP), F32)
    own_scores = score_all[g]
    for i in range(4):
        hidden_row = jnp.where(s // 2 == i, ref.sums[11 + i : 12 + i], hidden_row)
        score_row = jnp.where(s // 2 == i, own_scores[i : i + 1], score_row)
    hidden_row = jnp.where(s % 2 == 0, hidden_row[:, 0:128], hidden_row[:, 128:256])
    query_grad = exact(jnp.broadcast_to(score_row, (8, KP)), ref.key_own[...], 1, 1) * SCALE
    small[24:32] = jnp.zeros((8, 128), F32)
    small[24:25] = hidden_row
    small[25:26, 0:WD] = query_grad[0:1]
    deposit(small, results.small)
    h_spread[0].wait_recv()
    wait_all(h_handed)
    heads = head_all[...].reshape(D, KP)
    ref.g_value[...] = nt(pe[...], heads)
    deposit(ref.g_value, results.g_value)
    grad_table = nn(ref.value_w[...], heads) + exact(probe_own, scores, 1, 0)
    ref.g_patch[...] = grad_table[:, 0:VP]
    ref.g_embed[...] = grad_table[:, VP : VP + VARS]
    deposit(ref.g_patch, results.g_patch)
    deposit(ref.g_embed, results.g_embed)
    for copy in begun + begun_together:
        copy.wait_send()
    for gather in [gather_merge, gather_output] + gather_reduce + gather_joint + gather_expand:
        gather.sent()
    for line_sum in [output_sum, merge_sum] + reduce_sums + joint_sums + expand_sums:
        line_sum.sent()
    for copy in deposits:
        copy.wait()


def fused(operands):
    scratch = list(SCRATCH.values()) + list(OUTPUTS.values())
    for shape in TEAM_SUMS.values():
        scratch += team_sum_buffers(shape)
    return pl.pallas_call(
        fused_kernel,
        out_shape=[jax.ShapeDtypeStruct(*shape) for shape in OUTPUTS.values()],
        in_specs=[pl.BlockSpec(memory_space=space) for space in INPUTS.values()],
        out_specs=[pl.BlockSpec(memory_space=pl.ANY)] * len(OUTPUTS),
        scratch_shapes=[pltpu.VMEM(*shape) for shape in scratch]
        + [pltpu.SemaphoreType.DMA((SEMAPHORES,))] * 2,
        compiler_params=pltpu.CompilerParams(
            collective_id=1, has_side_effects=True, vmem_limit_bytes=64 << 20
        ),
    )(*operands)


VECTOR_ROWS = (25, 0, 1, 2, 3, 4, 5, 6, 7, 8)


def hand_out_kernel(*refs):
    n, m = len(OUTPUTS), len(VECTOR_ROWS)
    arrays = refs[:n]
    results = refs[n : 2 * n - 1]
    vectors = refs[2 * n - 1 : 2 * n - 1 + m]
    joint, hidden = refs[2 * n - 1 + m : 2 * n + 1 + m]
    held = refs[2 * n + 1 + m : 3 * n + 1 + m]
    narrow, both, came, left = refs[3 * n + 1 + m :]
    fetches = [pltpu.make_async_copy(arrays[i], held[i], came.at[i]) for i in range(n)]
    for copy in fetches:
        copy.start()
    small = held[n - 1]
    fetches[n - 1].wait()
    narrow[...] = small[:, 0:WD]
    both[...] = small[9:11, 0:WD]
    stores = [
        pltpu.make_async_copy(narrow.at[row], vectors[i], left.at[n + i])
        for i, row in enumerate(VECTOR_ROWS)
    ]
    stores.append(pltpu.make_async_copy(both, joint, left.at[n + m]))
    stores.append(pltpu.make_async_copy(small.at[24], hidden, left.at[n + m + 1]))
    for copy in stores:
        copy.start()
    for i in range(n - 1):
        fetches[i].wait()
        copy = pltpu.make_async_copy(held[i], results[i], left.at[i])
        copy.start()
        stores.append(copy)
    for copy in stores:
        copy.wait()


def hand_out(arrays):
    n, m = len(arrays), len(VECTOR_ROWS)
    shapes = [jax.ShapeDtypeStruct(a.shape, a.dtype) for a in arrays[:-1]]
    shapes += [jax.ShapeDtypeStruct((WD,), F32)] * m
    shapes += [jax.ShapeDtypeStruct((2, WD), F32), jax.ShapeDtypeStruct((ROW,), F32)]
    return pl.pallas_call(
        hand_out_kernel,
        out_shape=shapes,
        in_specs=[pl.BlockSpec(memory_space=pl.ANY)] * n,
        out_specs=[pl.BlockSpec(memory_space=pl.ANY)] * len(shapes),
        scratch_shapes=[pltpu.VMEM(a.shape, a.dtype) for a in arrays]
        + [pltpu.VMEM((32, WD), F32), pltpu.VMEM((2, WD), F32)]
        + [pltpu.SemaphoreType.DMA((n,)), pltpu.SemaphoreType.DMA((n + m + 2,))],
        compiler_params=pltpu.CompilerParams(vmem_limit_bytes=64 << 20),
    )(*arrays)


def shards_fused(
    fields,
    patch_weight,
    variable_embed,
    query_vector,
    key_weight,
    value_weight,
    merge_weight,
    merge_bias,
    position_table,
    lead_weight,
    lead_bias,
    first_gain,
    first_shift,
    joint_weight,
    joint_bias,
    output_weight,
    output_bias,
    second_gain,
    second_shift,
    expand_weight,
    expand_bias,
    reduce_weight,
    reduce_bias,
    segment_ids,
    live_rows,
    lead_steps,
    cotangent,
):
    pack = jnp.concatenate(
        [
            query_vector,
            merge_bias,
            lead_weight,
            lead_bias,
            first_gain,
            first_shift,
            output_bias,
            second_gain,
            second_shift,
            reduce_bias,
            jnp.zeros((2 * WD,), BF16),
            expand_bias,
            jnp.zeros((12 * 128,), BF16),
        ]
    ).reshape(16, 128)
    whole = fused(
        (
            fields.T,
            patch_weight.T,
            variable_embed.T,
            key_weight,
            value_weight,
            pack,
            joint_bias,
            segment_ids.reshape(1, ROW),
            live_rows.reshape(1, ROW),
            lead_steps,
            cotangent,
            position_table,
            joint_weight,
            expand_weight,
            merge_weight,
            output_weight,
            reduce_weight,
        )
    )
    (
        activations,
        field_grad,
        g_patch,
        g_embed,
        g_key,
        g_value,
        g_merge,
        g_position,
        g_joint,
        g_output,
        g_expand,
        g_reduce,
        g_query,
        g_merge_b,
        g_lead,
        g_lead_b,
        g_first_gain,
        g_first_shift,
        g_output_b,
        g_second_gain,
        g_second_shift,
        g_reduce_b,
        g_joint_b,
        g_expand_b,
    ) = hand_out(whole)
    return (
        activations,
        field_grad.T,
        g_patch.T,
        g_embed.T,
        g_query,
        g_key,
        g_value,
        g_merge,
        g_merge_b,
        g_position,
        g_lead,
        g_lead_b,
        g_first_gain,
        g_first_shift,
        g_joint,
        g_joint_b,
        g_output,
        g_output_b,
        g_second_gain,
        g_second_shift,
        g_expand,
        g_expand_b,
        g_reduce,
        g_reduce_b,
    )


def solution(mesh):
    by_row = P(ROWS, None)
    by_column = P(None, ROWS)
    vector = P(ROWS)
    in_specs = (
        by_row,
        by_column,
        by_column,
        vector,
        by_row,
        by_row,
        by_row,
        vector,
        P("seq", "grp"),
        vector,
        vector,
        vector,
        vector,
        by_row,
        by_column,
        by_row,
        vector,
        vector,
        vector,
        by_row,
        vector,
        by_row,
        vector,
        vector,
        vector,
        P("grp", None),
        by_row,
    )
    out_specs = (
        by_row,
        by_row,
        by_column,
        by_column,
        vector,
        by_row,
        by_row,
        by_row,
        vector,
        P("seq", "grp"),
        vector,
        vector,
        vector,
        vector,
        by_row,
        by_column,
        by_row,
        vector,
        vector,
        vector,
        by_row,
        vector,
        by_row,
        vector,
    )
    G, S = mesh.shape["grp"], mesh.shape["seq"]

    def body(*args):
        rows_here, weight_rows = args[0].shape[0], args[5].shape[0]
        if (G, S, rows_here, weight_rows) == (TEAM, LINE, ROW, WD):
            return shards_fused(*args)
        return shards(G, S, *args)

    return jax.shard_map(body, mesh=mesh, in_specs=in_specs, out_specs=out_specs, check_vma=False)
```

```python
import types

import jax
import jax.numpy as jnp
from jax import lax
from jax.experimental import pallas as pl
from jax.experimental.pallas import tpu as pltpu
from jax.sharding import PartitionSpec as P

D = 1024
HEADS = 16
FF = 4096
VARS = 48
PIX = 4
HDIM = 64
VP = 192
KP = 256

EPSILON = 1e-05
SCALE = 0.125
LEAD_UNIT = 0.06
MASKED = -1e30

MESH = pl.DeviceIdType.MESH
ROWS = ("grp", "seq")
F32 = jnp.float32
BF16 = jnp.bfloat16


def f32(x):
    return x.astype(F32)


def low(x):
    return x.astype(BF16)


def dot(a, b, ca, cb):
    return lax.dot_general(a, b, (((ca,), (cb,)), ((), ())), preferred_element_type=F32)


def low_sums(x):
    return dot(jnp.ones((8, x.shape[0]), BF16), x, 1, 0)[0]


def exchange(axis, parts):
    return [
        lax.all_gather(a, axis, axis=0, tiled=False)
        if mode == "all"
        else lax.all_to_all(a, axis, 0, 0, tiled=False)
        for a, mode in parts
    ]


def norm_parts(x):
    center = x - jnp.mean(x, axis=-1, keepdims=True)
    spread = jnp.mean(center * center, axis=-1, keepdims=True)
    inverse = lax.rsqrt(spread + EPSILON)
    return center * inverse, inverse


def norm_back(hat, inverse, gain, grad):
    f = grad * gain
    return inverse * (
        f
        - jnp.mean(f, axis=-1, keepdims=True)
        - hat * jnp.mean(f * hat, axis=-1, keepdims=True)
    )


def pack(pieces):
    flat = jnp.concatenate([f32(p).reshape(-1) for p in pieces])
    short = -flat.shape[0] % 1024
    return jnp.pad(flat, (0, short)).reshape(-1, 128)


def unpack(table, sizes):
    flat = table.reshape(table.shape[:-2] + (-1,))
    out, at = [], 0
    for size in sizes:
        out.append(flat[..., at : at + size])
        at += size
    return out


def softmax_parts(q, k, allowed):
    scores = jnp.einsum("hqc,hkc->hqk", q, k, preferred_element_type=F32) * SCALE
    masked = jnp.where(allowed[None], scores, MASKED)
    top = jnp.max(masked, axis=-1, keepdims=True)
    terms = jnp.where(allowed[None], jnp.exp(masked - top), 0.0)
    total = jnp.sum(terms, axis=-1, keepdims=True)
    return terms * (1.0 / total)


def attend(q, k, v, allowed):
    weights = softmax_parts(q, k, allowed)
    return jnp.einsum("hqk,hkc->hqc", low(weights), v, preferred_element_type=F32)


def attend_back(q, k, v, allowed, grad, attended):
    weights = softmax_parts(q, k, allowed)
    offset = jnp.sum(f32(grad) * attended, axis=-1)
    pushed = jnp.einsum("hqc,hkc->hqk", grad, v, preferred_element_type=F32)
    slopes = low(weights * (pushed - offset[..., None])) * BF16(SCALE)
    grad_q = jnp.einsum("hqk,hkc->hqc", slopes, k, preferred_element_type=F32)
    grad_k = jnp.einsum("hqk,hqc->hkc", slopes, q, preferred_element_type=F32)
    grad_v = jnp.einsum("hqk,hqc->hkc", low(weights), grad, preferred_element_type=F32)
    return grad_q, grad_k, grad_v


def heads_first(x):
    return x.transpose(1, 0, 2)


def heads_last(x):
    return x.transpose(1, 0, 2)


def allowed_pairs(query_codes, key_codes):
    return ((query_codes[:, None] >> 1) == (key_codes[None, :] >> 1)) & (
        (key_codes[None, :] & 1) == 1
    )


def shards(
    G,
    S,
    fields,
    patch_weight,
    variable_embed,
    query_vector,
    key_weight,
    value_weight,
    merge_weight,
    merge_bias,
    position_table,
    lead_weight,
    lead_bias,
    first_gain,
    first_shift,
    joint_weight,
    joint_bias,
    output_weight,
    output_bias,
    second_gain,
    second_shift,
    expand_weight,
    expand_bias,
    reduce_weight,
    reduce_bias,
    segment_ids,
    live_rows,
    lead_steps,
    cotangent,
):
    R = fields.shape[0]
    dn = value_weight.shape[0]
    fn = reduce_weight.shape[0]
    RG = G * R
    HL = HEADS // G
    CL = HL * HDIM
    FL = FF // G
    pairs = G * HL
    direct = pairs % S == 0 and HL % max(pairs // S, 1) == 0

    def swap(axis, *parts):
        return exchange(axis, parts)

    def gather_rows(w):
        return lax.all_gather(w, "seq", axis=0, tiled=True)

    merge_s = gather_rows(merge_weight)
    output_s = gather_rows(output_weight)

    table = jnp.concatenate(
        [patch_weight, variable_embed, jnp.zeros((KP - VP - VARS, dn), BF16)], axis=0
    )
    value_part = low(dot(value_weight, table, 0, 1)).reshape(G, CL, KP)
    key_part = low(dot(key_weight, table, 0, 1)).reshape(G, CL, KP)
    both = jnp.concatenate([value_part, key_part], axis=1)
    codes_own = segment_ids * 2 + live_rows
    vectors_own = [
        query_vector,
        merge_bias,
        lead_weight,
        lead_bias,
        first_gain,
        first_shift,
        output_bias,
        second_gain,
        second_shift,
        reduce_bias,
    ]
    small_own = pack([codes_own] + vectors_own)
    widen = (jnp.arange(VP)[:, None] == jnp.arange(KP)[None, :]).astype(BF16)
    column = jnp.arange(KP)
    field_own = low(dot(fields, widen, 1, 0) + ((column >= VP) & (column < VP + VARS)))
    joint_own = joint_weight.reshape(dn, 3, G, CL).transpose(2, 0, 1, 3).reshape(G, dn, 3 * CL)
    expand_own = expand_weight.reshape(dn, G, FL).transpose(1, 0, 2)
    both, joint_in, expand_in, field_in, position_in, small_in, cot_in = swap(
        "grp",
        (both, "each"),
        (joint_own, "each"),
        (expand_own, "each"),
        (field_own, "all"),
        (position_table, "all"),
        (small_own, "all"),
        (cotangent, "all"),
    )
    joint_s = (
        lax.all_gather(joint_in, "seq", axis=0, tiled=False)
        .transpose(1, 0, 2, 3)
        .reshape(D, 3 * CL)
    )
    expand_s = (
        lax.all_gather(expand_in, "seq", axis=0, tiled=False).transpose(1, 0, 2, 3).reshape(D, FL)
    )
    reduce_s = gather_rows(reduce_weight)
    field_rows = field_in.reshape(RG, KP)
    field_wide = dot(field_rows, (column[:, None] == column[None, :]).astype(BF16), 1, 0)
    cot_rows = cot_in.reshape(RG, D)
    position_rows = position_in.transpose(1, 0, 2).reshape(R, D)
    both = low(jnp.sum(f32(both), axis=0)).reshape(2, S, dn, KP).transpose(1, 0, 2, 3)
    small_rows = small_in.shape[0] * small_in.shape[1]
    slim = pack([joint_bias, expand_bias])
    both, small_all, slim_all = swap(
        "seq",
        (both.reshape(S, 2 * dn, KP), "each"),
        (small_in.reshape(small_rows, 128), "all"),
        (slim, "all"),
    )
    both = jnp.sum(f32(both), axis=0).reshape(2, dn, KP)
    value_own, key_own = both[0], both[1]
    probe_part = jnp.sum(key_own * f32(query_vector)[:, None], axis=0) * SCALE
    value_table, probe_parts = swap(
        "seq",
        (low(value_own), "all"),
        (jnp.broadcast_to(probe_part[None], (8, KP)), "all"),
    )
    value_table = value_table.reshape(CL, KP)
    probe_table = jnp.sum(probe_parts[:, 0].reshape(HL, S // HL, KP), axis=1)

    small_all = small_all.reshape(S, G, -1, 128)
    pieces = unpack(small_all, [R] + [dn] * len(vectors_own))
    codes = pieces[0].astype(jnp.int32)
    (
        full_query,
        full_merge_bias,
        full_lead,
        full_lead_bias,
        full_first_gain,
        full_first_shift,
        full_output_bias,
        full_second_gain,
        full_second_shift,
        full_reduce_bias,
    ) = [p.transpose(1, 0, 2).reshape(D) for p in pieces[1:]]
    joint_shift, expand_shift = unpack(slim_all, [2 * dn, fn])
    joint_shift = joint_shift.reshape(S, 2, dn).transpose(1, 0, 2).reshape(2, CL)
    expand_shift = expand_shift.reshape(FL)

    picked = jnp.where(
        segment_ids[:, None] == jnp.arange(lead_steps.shape[1])[None, :], lead_steps, 0
    )
    lead_rows = LEAD_UNIT * jnp.sum(picked, axis=1).astype(F32)

    owner = jnp.concatenate(
        [jnp.arange(VP) // PIX, jnp.arange(VARS), jnp.full((KP - VP - VARS,), VARS)]
    )
    select = (owner[:, None] == jnp.arange(VARS)[None, :]).astype(BF16)
    maps = probe_table[:, :, None] * f32(select)[None]
    maps_high = low(maps)
    maps_low = low(maps - f32(maps_high))
    scores = jnp.einsum("rk,hkv->hrv", field_rows, maps_high, preferred_element_type=F32)
    scores = scores + jnp.einsum("rk,hkv->hrv", field_rows, maps_low, preferred_element_type=F32)
    chosen = jax.nn.softmax(scores, axis=-1)
    spread = jnp.einsum("hrv,kv->hrk", low(chosen), select, preferred_element_type=F32)
    mixed = low(spread * field_wide[None])
    value_heads = value_table.reshape(HL, HDIM, KP)
    head_low = low(
        jnp.einsum("hrk,hck->rhc", mixed, value_heads, preferred_element_type=F32).reshape(RG, CL)
    )
    merged = low(dot(head_low, merge_s, 1, 0)).reshape(G, R, D)
    (merged,) = swap("grp", (merged, "each"))
    start = (
        jnp.sum(f32(merged), axis=0)
        + full_merge_bias
        + f32(position_rows)
        + lead_rows[:, None] * full_lead
        + full_lead_bias
    )
    start_hat, start_inv = norm_parts(start)
    (normed,) = swap("grp", (low(start_hat * full_first_gain + full_first_shift), "all"))
    normed = normed.reshape(RG, D)
    joint = dot(normed, joint_s, 1, 0)
    shift = jnp.concatenate([joint_shift[0], jnp.zeros((CL,), F32), joint_shift[1]])
    joint = low(joint + shift)

    if direct:
        per = pairs // S
        split = HL // per
        width = per * HDIM

        def to_pairs(x, kinds):
            x = x.reshape(G, R, kinds, split, width).transpose(0, 3, 1, 2, 4)
            (x,) = swap("seq", (x.reshape(S, R, kinds * width), "each"))
            return x.reshape(S * R, kinds, per, HDIM)

        def from_pairs(x, kinds):
            (x,) = swap("seq", (x.reshape(S, R, kinds * width), "each"))
            return (
                x.reshape(G, split, R, kinds, width)
                .transpose(0, 2, 3, 1, 4)
                .reshape(RG, kinds * CL)
            )

        mine = lax.axis_index("seq") // split
        pair_codes = lax.dynamic_index_in_dim(codes, mine, axis=1, keepdims=False).reshape(S * R)
        allowed = allowed_pairs(pair_codes, pair_codes)
        qkv = to_pairs(joint, 3)
        q, k, v = [heads_first(qkv[:, i]) for i in range(3)]
        attended = attend(q, k, v, allowed)
        attended_low = from_pairs(heads_last(low(attended)), 1)
    else:
        heads = joint.reshape(G, R, 3, HL, HDIM).transpose(0, 2, 3, 1, 4)
        everyone = lax.all_gather(heads[:, 1:], "seq", axis=3, tiled=True)
        all_codes = codes.transpose(1, 0, 2).reshape(G, S * R)
        my_codes = lax.dynamic_index_in_dim(codes, lax.axis_index("seq"), 0, keepdims=False)

        def forward_group(item):
            q, kv, query_codes, key_codes = item
            return attend(q, kv[0], kv[1], allowed_pairs(query_codes, key_codes))

        attended = lax.map(forward_group, (heads[:, 0], everyone, my_codes, all_codes))
        attended_low = low(attended).transpose(0, 2, 1, 3).reshape(RG, CL)

    branch = low(dot(attended_low, output_s, 1, 0)).reshape(G, R, D)
    (branch,) = swap("grp", (branch, "each"))
    middle = start + jnp.sum(f32(branch), axis=0) + full_output_bias
    middle_hat, middle_inv = norm_parts(middle)
    (second,) = swap("grp", (low(middle_hat * full_second_gain + full_second_shift), "all"))
    second = second.reshape(RG, D)
    hidden = dot(second, expand_s, 1, 0) + expand_shift
    inner = 0.7978845608028654 * (hidden + 0.044715 * hidden * hidden * hidden)
    bend = jnp.tanh(inner)
    active = low(0.5 * hidden * (1.0 + bend))
    slope = 0.5 * (1.0 + bend) + 0.5 * hidden * (1.0 - bend * bend) * 0.7978845608028654 * (
        1.0 + 3.0 * 0.044715 * hidden * hidden
    )
    reduced = low(dot(active, reduce_s, 1, 0)).reshape(G, R, D)

    grad_active = dot(cot_rows, reduce_s, 1, 1)
    grad_hidden = low(grad_active * slope)
    grad_second = low(dot(grad_hidden, expand_s, 1, 1)).reshape(G, R, D)
    grad_second, reduced = swap("grp", (grad_second, "each"), (reduced, "each"))
    activations = middle + jnp.sum(f32(reduced), axis=0) + full_reduce_bias
    grad_second = jnp.sum(f32(grad_second), axis=0)
    grad_top = f32(cotangent)
    grad_middle = grad_top + norm_back(middle_hat, middle_inv, full_second_gain, grad_second)
    grad_branch = low(grad_middle)

    def scatter_rows(w):
        return lax.psum_scatter(w, "seq", scatter_dimension=0, tiled=True)

    def scatter_mixed(w):
        cols = w.shape[1]
        w = w.reshape(G, S, dn, cols).transpose(1, 0, 2, 3).reshape(S, G * dn * cols // 1024, 1024)
        w = lax.psum_scatter(w, "seq", scatter_dimension=0, tiled=False)
        return w.reshape(G, dn, cols)

    grad_reduce_weight = f32(scatter_rows(low(dot(active, cot_rows, 0, 0))))
    grad_expand_mixed = scatter_mixed(low(dot(second, grad_hidden, 0, 0)))
    grad_expand_bias = low_sums(grad_hidden)

    (grad_branch_rows,) = swap("grp", (grad_branch, "all"))
    grad_branch_rows = grad_branch_rows.reshape(RG, D)
    grad_attended = low(dot(grad_branch_rows, output_s, 1, 1))
    grad_output_weight = f32(scatter_rows(low(dot(attended_low, grad_branch_rows, 0, 0))))
    if direct:
        pushed = heads_first(to_pairs(grad_attended, 1)[:, 0])
        grad_q, grad_k, grad_v = attend_back(q, k, v, allowed, pushed, attended)
        grads = [heads_last(low(x)) for x in (grad_q, grad_k, grad_v)]
        grad_joint = from_pairs(jnp.stack(grads, axis=1), 3)
    else:
        grad_heads = grad_attended.reshape(G, R, HL, HDIM).transpose(0, 2, 1, 3)

        def backward_group(item):
            q, kv, query_codes, key_codes, grad, done = item
            grad_q, grad_k, grad_v = attend_back(
                q, kv[0], kv[1], allowed_pairs(query_codes, key_codes), grad, done
            )
            return grad_q, jnp.stack([grad_k, grad_v], axis=0)

        grad_q, grad_kv = lax.map(
            backward_group,
            (heads[:, 0], everyone, my_codes, all_codes, grad_heads, attended),
        )
        grad_kv = lax.psum_scatter(grad_kv, "seq", scatter_dimension=3, tiled=True)
        grad_joint = low(jnp.concatenate([grad_q[:, None], grad_kv], axis=1))
        grad_joint = grad_joint.transpose(0, 3, 1, 2, 4).reshape(RG, 3 * CL)
    grad_normed = low(dot(grad_joint, joint_s, 1, 1)).reshape(G, R, D)
    (grad_normed,) = swap("grp", (grad_normed, "each"))
    grad_normed = jnp.sum(f32(grad_normed), axis=0)
    grad_joint_mixed = scatter_mixed(low(dot(normed, grad_joint, 0, 0)))
    joint_sums = low_sums(grad_joint)
    grad_start = grad_middle + norm_back(start_hat, start_inv, full_first_gain, grad_normed)
    grad_merged = low(grad_start)

    grad_merged_rows, grad_joint_in, grad_expand_in = swap(
        "grp", (grad_merged, "all"), (grad_joint_mixed, "each"), (grad_expand_mixed, "each")
    )
    grad_joint_weight = f32(
        grad_joint_in.reshape(G, dn, 3, CL).transpose(1, 2, 0, 3).reshape(dn, 3 * D)
    )
    grad_expand_weight = f32(grad_expand_in.transpose(1, 0, 2).reshape(dn, FF))
    grad_merged_rows = grad_merged_rows.reshape(RG, D)
    grad_head = low(dot(grad_merged_rows, merge_s, 1, 1))
    grad_merge_weight = f32(scatter_rows(low(dot(head_low, grad_merged_rows, 0, 0))))
    grad_heads_low = grad_head.reshape(RG, HL, HDIM)
    value_back = jnp.einsum(
        "rhc,hck->hrk", grad_heads_low, value_heads, preferred_element_type=F32
    )
    weighed = value_back * field_wide[None]
    weighed_high = low(weighed)
    weighed_low = low(weighed - f32(weighed_high))
    grad_chosen = jnp.einsum("hrk,kv->hrv", weighed_high, select, preferred_element_type=F32)
    grad_chosen = grad_chosen + jnp.einsum(
        "hrk,kv->hrv", weighed_low, select, preferred_element_type=F32
    )
    grad_scores = low(
        chosen * (grad_chosen - jnp.sum(chosen * grad_chosen, axis=-1, keepdims=True))
    )
    score_spread = jnp.einsum("hrv,kv->hrk", grad_scores, select, preferred_element_type=F32)
    field_part = jnp.sum(spread * value_back + score_spread * probe_table[:, None, :], axis=0)
    field_part = field_part.reshape(G, R, KP)
    score_sums = jnp.sum(score_spread * field_wide[None], axis=1)
    head_sums = jnp.einsum(
        "rhc,hrk->hck", grad_heads_low, mixed, preferred_element_type=F32
    ).reshape(S, dn, KP)

    column_sums = jnp.stack(
        [
            low_sums(grad_merged),
            jnp.sum(lead_rows[:, None] * grad_start, axis=0),
            jnp.sum(grad_start, axis=0),
            jnp.sum(grad_normed * start_hat, axis=0),
            jnp.sum(grad_normed, axis=0),
            low_sums(grad_branch),
            jnp.sum(grad_second * middle_hat, axis=0),
            jnp.sum(grad_second, axis=0),
            jnp.sum(grad_top, axis=0),
        ]
    )
    kinds = column_sums.shape[0]
    column_sums = jnp.pad(column_sums, ((0, -kinds % 16), (0, 0)))
    column_sums = column_sums.reshape(-1, G, CL).transpose(1, 0, 2)
    position_blocks = grad_merged.reshape(R, G, CL).transpose(1, 0, 2)
    column_sums, position_blocks, field_part = swap(
        "grp", (column_sums, "each"), (position_blocks, "each"), (field_part, "each")
    )
    grad_position_table = jnp.sum(f32(position_blocks), axis=0)
    field_grad = jnp.sum(field_part, axis=0)[:, :VP]
    column_sums = jnp.sum(column_sums, axis=0)
    team_sums = jnp.concatenate(
        [
            column_sums[:kinds].reshape(kinds, S, dn).transpose(1, 0, 2).reshape(S, kinds * dn),
            joint_sums[:CL].reshape(S, dn),
            joint_sums[2 * CL :].reshape(S, dn),
            grad_expand_bias.reshape(S, fn),
        ],
        axis=1,
    )
    wide = team_sums.shape[1]
    team_sums = jnp.pad(team_sums, ((0, 0), (0, -wide % 1024))).reshape(S, -1, 128)
    score_sums = jnp.pad(score_sums, ((0, -HL % 8), (0, 0)))
    team_sums, head_sums, score_sums = swap(
        "seq", (team_sums, "each"), (low(head_sums), "each"), (score_sums, "all")
    )
    team_sums = jnp.sum(team_sums, axis=0).reshape(-1)[:wide]
    own_sums = team_sums[: kinds * dn].reshape(kinds, dn)
    grad_joint_bias = team_sums[kinds * dn : (kinds + 2) * dn].reshape(2, dn)
    grad_expand_bias = team_sums[(kinds + 2) * dn :]
    (
        grad_merge_bias,
        grad_lead_weight,
        grad_lead_bias,
        grad_first_gain,
        grad_first_shift,
        grad_output_bias,
        grad_second_gain,
        grad_second_shift,
        grad_reduce_bias,
    ) = [own_sums[i] for i in range(kinds)]
    head_sums = jnp.sum(f32(head_sums), axis=0)
    score_sums = jnp.sum(score_sums, axis=0)
    my_head = lax.axis_index("seq") * dn // HDIM
    my_scores = lax.dynamic_index_in_dim(score_sums, my_head, axis=0, keepdims=False)
    grad_query_vector = jnp.sum(key_own * my_scores[None], axis=1) * SCALE
    (head_all,) = swap("seq", (low(head_sums), "all"))
    head_all, score_all = swap(
        "grp", (head_all.reshape(S * dn, KP), "all"), (score_sums, "all")
    )
    head_all = head_all.reshape(D, KP)
    score_all = score_all[:, :HL].reshape(HEADS, KP)
    grad_value_weight = dot(table, head_all, 0, 1)
    probe_own = low(
        jnp.sum((f32(key_weight) * full_query).reshape(dn, HEADS, HDIM), axis=-1) * SCALE
    )
    grad_table = dot(head_all, value_weight, 0, 1)
    grad_table = grad_table + jnp.einsum("hk,dh->kd", score_all, f32(probe_own))
    grad_probe = jnp.einsum("kd,hk->dh", f32(table), score_all)
    grad_key_weight = (
        grad_probe[:, :, None] * full_query.reshape(HEADS, HDIM)[None] * SCALE
    ).reshape(dn, D)
    grad_patch_weight = grad_table[:VP]
    grad_variable_embed = grad_table[VP : VP + VARS]
    return (
        activations,
        field_grad,
        grad_patch_weight,
        grad_variable_embed,
        grad_query_vector,
        grad_key_weight,
        grad_value_weight,
        grad_merge_weight,
        grad_merge_bias,
        grad_position_table,
        grad_lead_weight,
        grad_lead_bias,
        grad_first_gain,
        grad_first_shift,
        grad_joint_weight,
        grad_joint_bias,
        grad_output_weight,
        grad_output_bias,
        grad_second_gain,
        grad_second_shift,
        grad_expand_weight,
        grad_expand_bias,
        grad_reduce_weight,
        grad_reduce_bias,
    )


TEAM = 4
LINE = 8
ROW = 128
TALL = TEAM * ROW
GROUP = LINE * ROW
WD = D // (TEAM * LINE)
QC = D // TEAM
TEAM_HEADS = HEADS // TEAM
PACKED = 4
VECTORS = 12
QUERY, MERGE_BIAS, LEAD_WEIGHT, LEAD_BIAS, FIRST_GAIN, FIRST_SHIFT = range(6)
OUTPUT_BIAS, SECOND_GAIN, SECOND_SHIFT, REDUCE_BIAS = range(6, 10)
SUM_ROWS = 16

INPUTS = dict(
    fields=pltpu.VMEM,
    patch=pltpu.VMEM,
    embed=pltpu.VMEM,
    key_w=pltpu.VMEM,
    value_w=pltpu.VMEM,
    pack=pltpu.VMEM,
    joint_b=pltpu.VMEM,
    segments=pltpu.VMEM,
    live=pltpu.VMEM,
    steps=pltpu.SMEM,
    cot=pl.ANY,
    position=pl.ANY,
    joint_w=pl.ANY,
    expand_w=pl.ANY,
    merge_w=pl.ANY,
    output_w=pl.ANY,
    reduce_w=pl.ANY,
)

OUTPUTS = dict(
    activations=((ROW, D), F32),
    field_grad=((VP, ROW), F32),
    g_patch=((WD, VP), F32),
    g_embed=((WD, VARS), F32),
    g_key=((WD, D), F32),
    g_value=((WD, D), F32),
    g_merge=((WD, D), F32),
    g_position=((ROW, QC), F32),
    g_joint=((WD, 3 * D), F32),
    g_output=((WD, D), F32),
    g_expand=((WD, FF), F32),
    g_reduce=((ROW, D), F32),
    small=((32, 128), F32),
)

SCRATCH = dict(
    head_all=((TEAM, LINE, WD, KP), BF16),
    score_all=((TEAM, 8, KP), F32),
    score_rows=((16, KP), F32),
    key_own=((WD, KP), F32),
    sums=((SUM_ROWS, QC), F32),
    pe=((WD, KP), BF16),
    field_all=((TEAM, ROW, KP), BF16),
    pos=((ROW, D), BF16),
    cot_all=((TEAM, ROW, D), BF16),
    pack_rows=((16, 128), F32),
    pack_all=((LINE, TEAM, 16, 128), BF16),
    vecs=((16, D), F32),
    shift_e=((8, D), F32),
    seg_q=((16, GROUP), BF16),
    seg_k=((16, GROUP), BF16),
    merge_s=((LINE, WD, D), BF16),
    output_s=((LINE, WD, D), BF16),
    reduce_s=((LINE, ROW, D), BF16),
    joint_s=((TEAM, LINE, WD, 3 * QC), BF16),
    expand_s=((TEAM, LINE, WD, D), BF16),
    e2_send=((2, LINE, WD, KP), BF16),
    e2_recv=((LINE, 2, WD, KP), BF16),
    pv=((LINE, WD, KP), BF16),
    at=((LINE, 8, KP), F32),
    probe=((8, KP), F32),
    select=((KP, 128), BF16),
    select_t=((128, KP), BF16),
    chosen=((TEAM_HEADS, TALL, 128), F32),
    head_low=((TALL, QC), BF16),
    start=((ROW, D), F32),
    start_hat=((ROW, D), F32),
    start_inv=((ROW, 128), F32),
    middle=((ROW, D), F32),
    middle_hat=((ROW, D), F32),
    middle_inv=((ROW, 128), F32),
    grad_mid=((ROW, D), F32),
    normed_all=((TEAM, ROW, D), BF16),
    second_all=((TEAM, ROW, D), BF16),
    gb_all=((TEAM, ROW, D), BF16),
    gm_all=((TEAM, ROW, D), BF16),
    pair_send=((LINE, 3, ROW, 128), BF16),
    qkv=((3, GROUP, 128), BF16),
    p_low=((2, GROUP, GROUP), BF16),
    att_f=((GROUP, 128), F32),
    att_low=((GROUP, 128), BF16),
    att_all=((TEAM, ROW, QC), BF16),
    g_send=((TEAM, 2, ROW, 128), BF16),
    go=((GROUP, 128), BF16),
    dq=((GROUP, 128), F32),
    d_all=((TEAM, 3, ROW, QC), BF16),
    active_all=((TEAM, ROW, D), BF16),
    gh_all=((TEAM, ROW, D), BF16),
    own_a=((ROW, D), F32),
    own_b=((ROW, D), F32),
    far_a=((ROW, D), F32),
    far_b=((ROW, D), F32),
    far_d=((ROW, D), F32),
    gw_merge=((LINE, WD, D), BF16),
    gw_output=((LINE, WD, D), BF16),
    gw_reduce=((LINE, ROW, D), BF16),
    gw_joint=((TEAM, LINE, WD, 3 * QC), BF16),
    gw_expand=((TEAM, LINE, WD, D), BF16),
    yr_merge=((4, WD, D), BF16),
    yr_output=((4, WD, D), BF16),
    yr_reduce=((4, ROW // 2, D), BF16),
    yr_half=((1, ROW // 2, D), BF16),
    zr_half=((6, ROW // 2, D), BF16),
    za_half=((4, ROW // 2, D), BF16),
    yr_joint=((4, TEAM, WD, 3 * QC), BF16),
    yr_expand=((4, TEAM, WD, D), BF16),
    zr_merge=((3, WD, D), BF16),
    za_merge=((2, WD, D), BF16),
    zr_output=((3, WD, D), BF16),
    za_output=((2, WD, D), BF16),
    zr_reduce=((3, ROW // 2, D), BF16),
    za_reduce=((2, ROW // 2, D), BF16),
    zr_joint=((3, TEAM, WD, 3 * QC), BF16),
    za_joint=((2, TEAM, WD, 3 * QC), BF16),
    zr_expand=((3, TEAM, WD, D), BF16),
    za_expand=((2, TEAM, WD, D), BF16),
    xs_joint=((TEAM, WD, 3 * QC), BF16),
    xs_expand=((TEAM, WD, D), BF16),
    xr_joint=((TEAM, WD, 3 * QC), BF16),
    xr_expand=((TEAM, WD, D), BF16),
    csum=((16, D), F32),
    crecv=((TEAM, 16, QC), F32),
    tsum=((LINE, SUM_ROWS, QC), F32),
    f_own=((TEAM, ROW, KP), F32),
    f_recv=((3, ROW, KP), F32),
    t_send=((LINE, WD, KP), BF16),
    t_recv=((LINE, WD, KP), BF16),
    q_all=((LINE, 8, KP), F32),
)

TEAM_SUMS = dict(
    both=(2 * QC, KP),
    merge=(ROW, D),
    branch=(ROW, D),
    second=(ROW, D),
    reduced=(ROW, D),
    normed=(ROW, D),
)


def team_sum_buffers(shape):
    near = ((2,) + shape, BF16)
    one = (shape, BF16)
    return (near, near, one, one)


SEMAPHORES = 223
HERE = 29


def nn(a, b):
    return dot(a, b, 1, 0)


def nt(a, b):
    return dot(a, b, 1, 1)


def tn(a, b):
    return dot(a, b, 0, 0)


def lanes(at, size):
    return pl.ds(pl.multiple_of(at, 128), size)


def rows(at, size):
    return pl.ds(pl.multiple_of(at, size), size)


def fused_kernel(*refs):
    n_in, n_out = len(INPUTS), len(OUTPUTS)
    results = types.SimpleNamespace(**dict(zip(OUTPUTS, refs[n_in : n_in + n_out])))
    names = list(INPUTS) + list(SCRATCH) + list(OUTPUTS)
    rest = refs[:n_in] + refs[n_in + n_out :]
    ref = types.SimpleNamespace(**dict(zip(names, rest)))
    rest = rest[len(names) :]
    send, recv, here_sems = rest[-3:]
    sums = dict(zip(TEAM_SUMS, [rest[4 * i : 4 * i + 4] for i in range(len(TEAM_SUMS))]))
    sums = types.SimpleNamespace(**sums)
    g = lax.axis_index("grp")
    s = lax.axis_index("seq")
    sib = g + 1 - 2 * lax.rem(g, 2)
    far = lax.rem(g + 2, TEAM)
    diag = lax.rem(sib + 2, TEAM)
    z = s // 2
    y = s - 2 * z
    beside = s + 1 - 2 * y
    mine = lax.rem(3 * z, TEAM)
    is_middle = (z == 1) | (z == 2)
    is_end = (z == 0) | (z == 3)
    partner = s + 2 - 4 * lax.rem(z, 2)
    facing = lax.rem(s + 6 - 4 * z + LINE, LINE)
    near_places = [4 * (z // 2) + y + 2 * i for i in range(2)]
    far_places = [4 * (1 - z // 2) + y + 2 * i for i in range(2)]

    def to_team(j):
        return (j, s)

    def to_line(j):
        return (g, j)

    used = [0]
    begun = []

    def reserve(count):
        at = used[0]
        used[0] += count
        assert used[0] <= SEMAPHORES
        return at

    used_here = [0]

    def reserve_here():
        used_here[0] += 1
        assert used_here[0] <= HERE
        return used_here[0] - 1

    def remote(src, dst, device, at):
        return pltpu.make_async_remote_copy(
            src_ref=src,
            dst_ref=dst,
            send_sem=send.at[at],
            recv_sem=recv.at[at],
            device_id=device,
            device_id_type=MESH,
        )

    def push(src, dst, device):
        copy = remote(src, dst, device, reserve(1))
        copy.start()
        begun.append(copy)
        return copy

    barrier = pltpu.get_barrier_semaphore()
    for step in range(1, TEAM):
        pl.semaphore_signal(
            barrier, inc=1, device_id=to_team(lax.rem(g + step, TEAM)), device_id_type=MESH
        )
    for step in range(1, LINE):
        pl.semaphore_signal(
            barrier, inc=1, device_id=to_line(lax.rem(s + step, LINE)), device_id_type=MESH
        )

    class Together:
        def __init__(self, bulk, waits_itself=False):
            self.bulk, self.at = bulk, reserve(1)
            if not waits_itself:
                begun_together.append(self)

        def push(self, src, dst, device):
            remote(src, dst, device, self.at).start()

        def wait_recv(self):
            remote(self.bulk, self.bulk, to_line(beside), self.at).wait_recv()

        def wait_send(self):
            remote(self.bulk, self.bulk, to_line(beside), self.at).wait_send()

    begun_together = []

    def spread(buf):
        half = buf.shape[1] // 2
        across = []
        for h in range(2):
            part = buf.at[g, pl.ds(h * half, half)]
            across.append(push(part, part, to_team(far)))
        return push(buf.at[g], buf.at[g], to_team(sib)), across

    def spread_on(buf, across):
        half = buf.shape[1] // 2
        handed = Together(buf.at[far])
        for h in range(2):
            across[h].wait_recv()
            part = buf.at[far, pl.ds(h * half, half)]
            handed.push(part, part, to_team(sib))
        return [handed]

    def wait_all(copies):
        for copy in copies:
            copy.wait_recv()

    class TeamSum:
        def __init__(self, buffers):
            self.ps, self.r, self.t, self.x = buffers
            self.near_copies = [None, None]

        def near(self, slot, value=None):
            if value is not None:
                self.ps[slot] = low(value)
            self.near_copies[slot] = push(self.ps.at[slot], self.r.at[slot], to_team(sib))

        def across(self, value):
            self.near_copies[1].wait_recv()
            half = self.t.shape[0] // 2
            self.far_copies = [Together(self.x)]
            for h in range(2):
                part = pl.ds(h * half, half)
                self.t[part] = low(value(part) + f32(self.r[1, part]))
                self.far_copies[0].push(self.t.at[part], self.x.at[part], to_team(far))

        def total(self, own):
            self.near_copies[0].wait_recv()
            wait_all(self.far_copies)
            return own + f32(self.r[0]) + f32(self.x[...])

    deposits = []

    def deposit(src, dst):
        copy = pltpu.make_async_copy(src, dst, here_sems.at[reserve_here()])
        copy.start()
        deposits.append(copy)

    def to_whole_line(src, dst, bulk):
        group = Together(bulk)
        for step in range(1, LINE):
            place = lax.rem(s + step, LINE)
            group.push(src(place), dst, to_line(place))
        return [group]

    def share_line(buf):
        return to_whole_line(lambda place: buf.at[s], buf.at[s], buf.at[pl.ds(0, LINE - 1)])

    def to_whole_team(src, dst, bulk):
        group = Together(bulk)
        for j in (far, diag, sib):
            group.push(src(j), dst, to_team(j))
        return [group]

    def mean(x):
        return jnp.sum(x, axis=-1, keepdims=True) * (1.0 / D)

    class Gather:
        def __init__(self, slot):
            self.slot = slot
            self.at = reserve(9)

        def send(self, place, device, i, shard=None):
            part = self.slot(place)
            remote(part if shard is None else shard, part, device, self.at + i).start()

        def come(self, i):
            part = self.slot(s)
            remote(part, part, to_line(beside), self.at + i).wait_recv()

        def stage1(self, shard=None):
            self.send(s, to_line(partner), 0, shard)
            self.send(s, to_line(beside), 1, shard)

        def stage2(self, hold=False):
            self.come(0)

            @pl.when(is_middle)
            def _():
                for i in range(2):
                    self.send(near_places[i], to_line(facing), 2 + i)

            if not hold:
                self.hand_on()

        def hand_on(self):
            self.send(partner, to_line(beside), 4)

        def stage3(self):
            @pl.when(is_middle)
            def _():
                for i in range(2):
                    self.come(2 + i)
                    self.send(far_places[i], to_line(partner), 5 + i)
                    self.send(far_places[i], to_line(beside), 7 + i)

        def stage4(self):
            @pl.when(is_end)
            def _():
                for i in range(2):
                    self.come(5 + i)
                    self.send(far_places[i], to_line(beside), 7 + i)

        def finish(self):
            for i in (1, 4, 7, 8):
                self.come(i)

        def sent(self):
            part = self.slot(s)

            def gone(i):
                remote(part, part, to_line(beside), self.at + i).wait_send()

            for i in (0, 1, 4, 7, 8):
                gone(i)

            @pl.when(is_middle)
            def _():
                for i in (2, 3, 5, 6):
                    gone(i)

    class PairExchange:
        def __init__(self, bulk):
            self.group, self.own = Together(bulk, waits_itself=True), reserve_here()

        def send(self, src, dst, there):
            @pl.when(there != s)
            def _():
                self.group.push(src, dst, to_line(there))

            @pl.when(there == s)
            def _():
                pltpu.make_async_copy(src, dst, here_sems.at[self.own]).start()

        def wait(self, src, dst):
            pltpu.make_async_copy(src, dst, here_sems.at[self.own]).wait()
            self.group.wait_recv()
            self.group.wait_send()

    pe = ref.pe
    pe[:, 0:VP] = ref.patch[...]
    pe[:, VP : VP + VARS] = ref.embed[...]
    pe[:, VP + VARS :] = jnp.zeros((WD, KP - VP - VARS), BF16)
    field_all, cot_all, pack_all = ref.field_all, ref.cot_all, ref.pack_all
    field_all[g, :, 0:VP] = ref.fields[...].T
    lane = lax.broadcasted_iota(jnp.int32, (ROW, KP - VP), 1)
    field_all[g, :, VP:] = (lane < VARS).astype(BF16)
    pack_rows = ref.pack_rows
    pack_rows[...] = f32(ref.pack[...])
    for i in range(2):
        pack_rows[2:3, 64 + i * WD : 64 + (i + 1) * WD] = f32(ref.joint_b[...])[i : i + 1]
    pack_rows[4:5] = ref.segments[...].astype(F32)
    pack_rows[5:6] = ref.live[...].astype(F32)
    pack_all[s, g] = low(pack_rows[...])
    pl.semaphore_wait(barrier, TEAM - 1 + LINE - 1)

    both = TeamSum(sums.both)

    def table_product(weight, j):
        return tn(weight[:, lanes(j * QC, QC)], pe[...])

    for slot, j in ((1, diag), (0, sib)):
        both.ps[slot, 0:QC] = low(table_product(ref.value_w, j))
        both.ps[slot, QC:] = low(table_product(ref.key_w, j))
        both.near(slot)
    field_copies = spread(field_all)
    far_parts = [table_product(ref.value_w, far), table_product(ref.key_w, far)]
    both.across(lambda part: far_parts[0] if part.start == 0 else far_parts[1])
    own_parts = [table_product(ref.value_w, g), table_product(ref.key_w, g)]
    pack_here = pack_all.at[s, g]
    pack_copies = to_whole_team(lambda j: pack_here, pack_here, pack_all.at[0, pl.ds(0, 3)])

    def whole(buf):
        return lambda i: buf.at[i]

    def inner(buf):
        return lambda i: buf.at[:, i]

    def some_rows(buf, at, size):
        return lambda i: buf.at[i, pl.ds(at, size)]

    def some_lanes(buf, at, size):
        return lambda i: buf.at[:, i, :, pl.ds(at, size)]

    half_rows, half_lanes = ROW // 2, D // 2
    gather_merge = Gather(whole(ref.merge_s))
    gather_output = Gather(whole(ref.output_s))
    gather_reduce = [Gather(some_rows(ref.reduce_s, i * half_rows, half_rows)) for i in range(2)]
    gather_joint = [Gather(some_lanes(ref.joint_s, i * QC, QC)) for i in range(3)]
    gather_expand = [Gather(some_lanes(ref.expand_s, i * half_lanes, half_lanes)) for i in range(2)]
    local = []

    def keep(src, dst):
        copy = pltpu.make_async_copy(src, dst, here_sems.at[reserve_here()])
        copy.start()
        local.append(copy)

    keep(ref.merge_w, ref.merge_s.at[s])
    keep(ref.output_w, ref.output_s.at[s])
    keep(ref.reduce_w, ref.reduce_s.at[s])
    keep(ref.cot, cot_all.at[g])
    gather_merge.stage1(ref.merge_w)
    for i in range(2):
        gather_reduce[i].stage1(ref.reduce_w.at[pl.ds(i * half_rows, half_rows)])

    joint_copies = [Together(ref.joint_s.at[pl.ds(0, 3), 0])]
    for j in (far, diag, sib):
        for kind in range(3):
            joint_copies[0].push(
                ref.joint_w.at[:, lanes(kind * D + j * QC, QC)],
                ref.joint_s.at[g, s, :, pl.ds(kind * QC, QC)],
                to_team(j),
            )
    for kind in range(3):
        keep(
            ref.joint_w.at[:, lanes(kind * D + g * QC, QC)],
            ref.joint_s.at[g, s, :, pl.ds(kind * QC, QC)],
        )
    expand_copies = to_whole_team(
        lambda j: ref.expand_w.at[:, lanes(j * D, D)],
        ref.expand_s.at[g, s],
        ref.expand_s.at[pl.ds(0, 3), 0],
    )
    keep(ref.expand_w.at[:, lanes(g * D, D)], ref.expand_s.at[g, s])
    keep(ref.position, ref.pos.at[:, lanes(g * QC, QC)])
    position_copies = to_whole_team(
        lambda j: ref.position, ref.pos.at[:, lanes(g * QC, QC)], ref.pos.at[:, pl.ds(0, 3 * QC)]
    )

    for copy in local:
        copy.wait()
    gather_merge.stage2()

    both.near_copies[0].wait_recv()
    wait_all(both.far_copies)
    for part in range(2):
        block = pl.ds(part * QC, QC)
        total = own_parts[part] + f32(both.r[0, block]) + f32(both.x[block])
        ref.e2_send[part] = low(total).reshape(LINE, WD, KP)
    e2_send, e2_recv = ref.e2_send, ref.e2_recv
    e2_copies = to_whole_line(
        lambda place: e2_send.at[:, place], e2_recv.at[s], e2_recv.at[pl.ds(0, LINE - 1)]
    )
    e2_recv[s] = e2_send[:, s]
    wait_all(joint_copies)
    for gather in gather_joint:
        gather.stage1()
    gather_merge.stage3()

    wait_all(e2_copies)
    table_own = jnp.sum(f32(e2_recv[...]), axis=0)
    key_own = table_own[1]
    ref.key_own[...] = key_own
    query = f32(pack_all[s, g])[0:1, 0:WD]
    key_high = low(key_own)
    key_rest = low(key_own - f32(key_high))
    query_rows = low(jnp.broadcast_to(query, (16, WD)))
    probe_part = (nn(query_rows, key_high) + nn(query_rows, key_rest)) * SCALE
    pv, at = ref.pv, ref.at
    pv[s] = low(table_own[0])
    at[s] = probe_part[0:8]
    pv_copies = share_line(pv)
    at_copies = to_whole_line(
        lambda place: at.at[s, pl.ds(0, 1)],
        at.at[s, pl.ds(0, 1)],
        at.at[pl.ds(0, LINE - 1), pl.ds(0, 1)],
    )
    for gather in gather_joint:
        gather.stage2()
    wait_all(pv_copies)
    wait_all(at_copies)
    gather_merge.stage4()
    wait_all(pack_copies)
    pack_line = share_line(pack_all)
    wait_all(expand_copies)
    for gather in gather_expand:
        gather.stage1()

    probe = ref.probe
    for h in range(TEAM_HEADS):
        probe[h : h + 1] = at[2 * h, 0:1] + at[2 * h + 1, 0:1]
    probe[TEAM_HEADS:] = jnp.zeros((8 - TEAM_HEADS, KP), F32)

    def owner_of(k):
        return jnp.where(k < VP, k // PIX, jnp.where(k < VP + VARS, k - VP, VARS + 64))

    select, select_t = ref.select, ref.select_t
    select[...] = (
        owner_of(lax.broadcasted_iota(jnp.int32, (KP, 128), 0))
        == lax.broadcasted_iota(jnp.int32, (KP, 128), 1)
    ).astype(BF16)
    select_t[...] = (
        owner_of(lax.broadcasted_iota(jnp.int32, (128, KP), 1))
        == lax.broadcasted_iota(jnp.int32, (128, KP), 0)
    ).astype(BF16)
    valid = lax.broadcasted_iota(jnp.int32, (1, 128), 1) < VARS
    head_of_lane = lax.broadcasted_iota(jnp.int32, (1, QC), 1) // HDIM

    field_handed = spread_on(field_all, field_copies[1])
    field_copies[0].wait_recv()
    wait_all(field_handed)

    def tall(buf):
        return buf[...].reshape(TALL, -1)

    def split_dot(x, b):
        high = low(x)
        return nn(high, b) + nn(low(x - f32(high)), b)

    chosen, head_low = ref.chosen, ref.head_low

    def choose(h):
        field = f32(tall(field_all))
        scores = split_dot(field * probe[h : h + 1], select[...])
        scores = jnp.where(valid, scores, MASKED)
        terms = jnp.exp(scores - jnp.max(scores, axis=-1, keepdims=True))
        weights = terms * (1.0 / jnp.sum(terms, axis=-1, keepdims=True))
        chosen[h] = weights
        mix = low(nn(low(weights), select_t[...]) * field)
        table_value = pv[2 * h : 2 * h + 2].reshape(HDIM, KP)
        head_low[:, h * HDIM : (h + 1) * HDIM] = low(nt(mix, table_value))

    for h in range(TEAM_HEADS):
        choose(h)

    merge_s, output_s = ref.merge_s, ref.output_s
    gather_merge.finish()
    merge = TeamSum(sums.merge)

    def row_weight(buf):
        return buf[...].reshape(-1, D)

    def two(buf, i, j):
        return jnp.concatenate([buf[i], buf[j]], axis=0)

    def merge_part(j):
        return nn(head_low[rows(j * ROW, ROW)], row_weight(merge_s))

    merge.near(1, merge_part(diag))
    ref.far_a[...] = merge_part(far)
    merge.across(lambda part: ref.far_a[part])
    merge.near(0, merge_part(sib))
    ref.own_a[...] = merge_part(g)

    wait_all(pack_line)
    vecs, shift_e = ref.vecs, ref.shift_e
    lane_piece = lax.broadcasted_iota(jnp.int32, (LINE, 1, QC), 2) // WD
    piece = lax.broadcasted_iota(jnp.int32, (LINE, 1, QC), 0)
    for q in range(PACKED):
        place = (
            lax.broadcasted_iota(jnp.int32, (128, QC), 1) % WD + q * WD
            == lax.broadcasted_iota(jnp.int32, (128, QC), 0)
        ).astype(BF16)
        for j in range(TEAM):
            spreadout = nn(pack_all[:, j].reshape(LINE * 16, 128), place)
            spreadout = jnp.where(lane_piece == piece, spreadout.reshape(LINE, 16, QC), 0.0)
            spreadout = jnp.sum(spreadout, axis=0)
            vecs[4 * q : 4 * q + 4, j * QC : (j + 1) * QC] = spreadout[0:4]

    def vector(i):
        at_row = 4 * (i % PACKED) + i // PACKED
        return vecs[at_row : at_row + 1, :]

    joint_shift = [
        vecs[4 * (i % PACKED) + i // PACKED, lanes(g * QC, QC)].reshape(1, QC) for i in (10, 11)
    ]
    seg_q, seg_k = ref.seg_q, ref.seg_k
    sub = lax.broadcasted_iota(jnp.int32, (16, 128), 0).astype(F32)
    for j in range(LINE):
        part = f32(pack_all[j, g])
        shift_e[:, j * 128 : (j + 1) * 128] = jnp.broadcast_to(part[3:4], (8, 128))
        part = f32(pack_all[j, mine])
        same = jnp.where(sub == part[4:5], 1.0, 0.0)
        seg_q[:, j * 128 : (j + 1) * 128] = low(same)
        seg_k[:, j * 128 : (j + 1) * 128] = low(same * part[5:6])
    own_seg = ref.segments[...].astype(F32)
    steps = ref.steps
    lead_lanes = jnp.zeros((1, 128), F32)
    for i in range(steps.shape[1]):
        lead_lanes = jnp.where(own_seg == i, LEAD_UNIT * steps[0, i].astype(F32), lead_lanes)
    lead = jnp.broadcast_to(lead_lanes, (ROW, 128)).T[:, 0:1]
    wait_all(position_copies)
    for gather in gather_joint:
        gather.stage3()
    gather_output.stage1(ref.output_w)
    for gather in gather_reduce:
        gather.stage2(hold=True)

    start_ref = ref.start
    start_ref[...] = (
        merge.total(ref.own_a[...])
        + vector(MERGE_BIAS)
        + f32(ref.pos[...])
        + lead * vector(LEAD_WEIGHT)
        + vector(LEAD_BIAS)
    )

    def norm(x, hat_ref, inv_ref, gain, shift):
        center = x - mean(x)
        inverse = lax.rsqrt(mean(center * center) + EPSILON)
        hat = center * inverse
        hat_ref[...] = hat
        inv_ref[...] = jnp.broadcast_to(inverse, (ROW, 128))
        return low(hat * gain + shift)

    def norm_back_ref(grad, hat_ref, inv_ref, gain):
        f = grad * gain
        hat = hat_ref[...]
        return inv_ref[:, 0:1] * (f - mean(f) - hat * mean(f * hat))

    normed_all = ref.normed_all
    normed_all[g] = norm(
        start_ref[...],
        ref.start_hat,
        ref.start_inv,
        vector(FIRST_GAIN),
        vector(FIRST_SHIFT),
    )
    normed_copies = spread(normed_all)
    joint_s, pair_send, qkv = ref.joint_s, ref.pair_send, ref.qkv
    for gather in gather_joint:
        gather.stage4()
    e6 = [PairExchange(qkv.at[kind, pl.ds(0, 7 * ROW), :]) for kind in range(3)]

    def pair_place(j, t):
        return 2 * lax.rem(3 * j, TEAM) + t

    line_rows = rows(s * ROW, ROW)

    def joint_rows(i, j):
        block = two(normed_all, i, j)
        for kind in range(3):
            if i is g:
                gather_joint[kind].finish()
            weight = joint_s[:, :, :, kind * QC : (kind + 1) * QC].reshape(D, QC)
            part = nn(block, weight)
            if kind != 1:
                part = part + joint_shift[kind // 2]
            part = low(part)
            for n, group in enumerate((i, j)):
                for t in range(2):
                    place = pair_place(group, t)
                    pair_send[place, kind] = part[n * ROW : (n + 1) * ROW, t * 128 : (t + 1) * 128]
                    e6[kind].send(pair_send.at[place, kind], qkv.at[kind, line_rows, :], place)

    normed_copies[0].wait_recv()
    joint_rows(g, sib)
    normed_handed = spread_on(normed_all, normed_copies[1])
    wait_all(normed_handed)
    joint_rows(far, diag)
    gather_output.stage2()
    gather_expand[0].stage2()
    for gather in gather_reduce:
        gather.hand_on()
        gather.stage3()
    for kind in range(3):
        e6[kind].wait(pair_send.at[0, kind], qkv.at[kind, line_rows, :])
    gather_output.stage3()
    gather_expand[1].stage2()
    cot_copies = spread(cot_all)

    half_of_lane = lax.broadcasted_iota(jnp.int32, (1, 128), 1) // HDIM
    p_low, att_f, att_low, att_all = ref.p_low, ref.att_f, ref.att_low, ref.att_all
    e7 = PairExchange(att_low.at[pl.ds(0, 7 * ROW)])
    pair_lanes = lanes(y * 128, 128)

    def attend_rows(b, carry):
        here = rows(b * 256, 256)
        queries = f32(qkv[0, here, :]) * SCALE
        keys, values = qkv[1], qkv[2]
        allowed = tn(seg_q[:, lanes(b * 256, 256)], seg_k[...]) > 0.5
        outs = []
        for t in range(2):
            scores = nt(low(jnp.where(half_of_lane == t, queries, 0.0)), keys)
            scores = jnp.where(allowed, scores, MASKED)
            terms = jnp.exp(scores - jnp.max(scores, axis=-1, keepdims=True))
            weights = low(terms * (1.0 / jnp.sum(terms, axis=-1, keepdims=True)))
            p_low[t, here, :] = weights
            outs.append(nn(weights, values))
        out = jnp.where(half_of_lane == 0, outs[0], outs[1])
        att_f[here] = out
        att_low[here] = low(out)
        for t in range(2):
            there = 2 * b + t
            e7.send(att_low.at[rows(there * ROW, ROW)], att_all.at[mine, :, pair_lanes], there)

        return carry

    lax.fori_loop(0, GROUP // 256, attend_rows, 0)
    gather_output.stage4()
    for gather in gather_reduce:
        gather.stage4()
    for gather in gather_expand:
        gather.stage3()
    gather_output.finish()
    e7.wait(att_low.at[pl.ds(0, ROW)], att_all.at[mine, :, pair_lanes])

    branch = TeamSum(sums.branch)

    def branch_part(j):
        return nn(att_all[j], row_weight(output_s))

    branch.near(1, branch_part(diag))
    ref.far_a[...] = branch_part(far)
    branch.across(lambda part: ref.far_a[part])
    branch.near(0, branch_part(sib))
    ref.own_a[...] = branch_part(g)
    cot_handed = spread_on(cot_all, cot_copies[1])
    gather_expand[0].stage4()
    middle_ref = ref.middle
    middle_ref[...] = branch.total(ref.own_a[...]) + start_ref[...] + vector(OUTPUT_BIAS)

    class LineSum:
        def __init__(self, four, slot, yr, zr, za):
            self.four = four
            self.slot, self.yr, self.zr, self.za = slot, yr, zr, za
            self.at = reserve(6)

        def send(self, src, dst, device, i):
            remote(src, dst, device, self.at + i).start()

        def come(self, i):
            part = self.zr(0)
            remote(part, part, to_line(beside), self.at + i).wait_recv()

        def along_y(self):
            self.y_copies = Together(self.four)
            for i in range(4):
                self.y_copies.push(self.slot(2 * i + 1 - y), self.yr(i), to_line(beside))

        def add(self, place, came):
            block = self.slot(place)
            block[...] = low(f32(block[...]) + f32(came[...]))
            return block

        def sum_y(self):
            self.y_copies.wait_recv()

            def add(i, carry):
                self.add(2 * i + y, self.yr(i))
                return carry

            lax.fori_loop(0, 4, add, 0)

        def stage1(self):
            @pl.when(is_end)
            def _():
                for i, place in enumerate(far_places + [partner]):
                    self.send(self.slot(place), self.zr(i), to_line(partner), i)

        def stage2(self):
            @pl.when(is_middle)
            def _():
                for i, place in enumerate(far_places):
                    self.come(i)
                    block = self.add(place, self.zr(i))
                    self.send(block, self.za(i), to_line(facing), 3 + i)

        def stage3(self):
            @pl.when(is_middle)
            def _():
                for i in range(2):
                    self.come(3 + i)
                block = self.add(partner, self.za(1 - lax.rem(z, 2)))
                self.send(block, self.zr(0), to_line(partner), 5)

        def total(self, out):
            own = f32(self.slot(s)[...])

            @pl.when(is_middle)
            def _():
                self.come(2)
                total = own + f32(self.zr(2)[...]) + f32(self.za(lax.rem(z, 2))[...])
                out[...] = total.astype(out.dtype)

            @pl.when(is_end)
            def _():
                self.come(5)
                out[...] = (own + f32(self.zr(0)[...])).astype(out.dtype)

        def sent(self):
            part = self.zr(0)

            def gone(i):
                remote(part, part, to_line(beside), self.at + i).wait_send()

            @pl.when(is_middle)
            def _():
                for i in (3, 4, 5):
                    gone(i)

            @pl.when(is_end)
            def _():
                for i in range(3):
                    gone(i)

    class LineSumZ:
        def __init__(self, slot, zr, za, yr):
            self.slot, self.zr, self.za, self.yr = slot, zr, za, yr
            self.at = reserve(13)

        def both_y(self, place):
            return [place - y, place - y + 1]

        def send(self, src, dst, device, i):
            remote(src, dst, device, self.at + i).start()

        def come(self, i):
            part = self.zr(0)
            remote(part, part, to_line(beside), self.at + i).wait_recv()

        def add(self, place, came):
            block = self.slot(place)
            block[...] = low(f32(block[...]) + f32(came[...]))
            return block

        def stage1(self):
            @pl.when(is_end)
            def _():
                for i, place in enumerate(
                    self.both_y(far_places[0]) + self.both_y(far_places[1]) + self.both_y(partner)
                ):
                    self.send(self.slot(place), self.zr(i), to_line(partner), i)

        def stage2(self):
            @pl.when(is_middle)
            def _():
                for i, place in enumerate(self.both_y(far_places[0]) + self.both_y(far_places[1])):
                    self.come(i)
                    block = self.add(place, self.zr(i))
                    self.send(block, self.za(i), to_line(facing), 6 + i)

        def stage3(self):
            @pl.when(is_middle)
            def _():
                for i in range(4):
                    self.come(6 + i)
                for i, place in enumerate(self.both_y(partner)):
                    block = self.add(place, self.za(2 * (1 - lax.rem(z, 2)) + i))
                    self.send(block, self.zr(i), to_line(partner), 10 + i)
                for i, place in enumerate(self.both_y(s)):
                    self.come(4 + i)
                    self.add(place, self.zr(4 + i))
                    self.add(place, self.za(2 * lax.rem(z, 2) + i))

        def along_y(self):
            @pl.when(is_end)
            def _():
                for i, place in enumerate(self.both_y(s)):
                    self.come(10 + i)
                    self.add(place, self.zr(i))

            self.send(self.slot(beside), self.yr(0), to_line(beside), 12)

        def total(self, out):
            self.come(12)
            out[...] = f32(self.slot(s)[...]) + f32(self.yr(0)[...])

        def sent(self):
            part = self.zr(0)

            def gone(i):
                remote(part, part, to_line(beside), self.at + i).wait_send()

            gone(12)

            @pl.when(is_middle)
            def _():
                for i in (6, 7, 8, 9, 10, 11):
                    gone(i)

            @pl.when(is_end)
            def _():
                for i in range(6):
                    gone(i)

    def line_sum_of(gw, others, at=None, size=None):
        four = others[0]
        if at is None:
            return LineSum(four, whole(gw), *[whole(buf) for buf in others])
        if len(gw.shape) == 3:
            return LineSum(four, some_rows(gw, at, size), *[whole(buf) for buf in others])

        def part(buf):
            return lambda i: buf.at[i, :, :, pl.ds(at, size)]

        four = four.at[:, :, :, pl.ds(at, size)]
        return LineSum(four, some_lanes(gw, at, size), *[part(buf) for buf in others])

    output_sum = line_sum_of(ref.gw_output, [ref.yr_output, ref.zr_output, ref.za_output])
    merge_sum = line_sum_of(ref.gw_merge, [ref.yr_merge, ref.zr_merge, ref.za_merge])
    reduce_y = line_sum_of(
        ref.gw_reduce, [ref.yr_reduce, ref.zr_reduce, ref.za_reduce], 0, half_rows
    )
    reduce_z = LineSumZ(
        some_rows(ref.gw_reduce, half_rows, half_rows),
        whole(ref.zr_half),
        whole(ref.za_half),
        whole(ref.yr_half),
    )
    reduce_sums = [reduce_y, reduce_z]
    expand_sums = [
        line_sum_of(
            ref.gw_expand,
            [ref.yr_expand, ref.zr_expand, ref.za_expand],
            i * half_lanes,
            half_lanes,
        )
        for i in range(2)
    ]
    joint_sums = [
        line_sum_of(ref.gw_joint, [ref.yr_joint, ref.zr_joint, ref.za_joint], i * QC, QC)
        for i in range(3)
    ]

    second_all = ref.second_all
    second_all[g] = norm(
        middle_ref[...],
        ref.middle_hat,
        ref.middle_inv,
        vector(SECOND_GAIN),
        vector(SECOND_SHIFT),
    )
    second_copies = spread(second_all)
    for gather in [gather_expand[0]] + gather_reduce:
        gather.finish()
    cot_copies[0].wait_recv()
    wait_all(cot_handed)
    expand_s, reduce_s = ref.expand_s, ref.reduce_s
    active_all, gh_all = ref.active_all, ref.gh_all
    root = 0.7978845608028654

    def feed(j, k, acc_a, acc_b, half):
        def tile(i, carry):
            here = lanes(i * 256, 256)
            up = expand_s[:, :, :, here].reshape(D, 256)
            down = reduce_s[pl.ds(2 * i, 2)].reshape(256, D)
            hidden = nn(two(second_all, j, k), up) + shift_e[0:1, here]
            square = hidden * hidden
            bend = jnp.tanh(root * hidden * (1.0 + 0.044715 * square))
            active = low(0.5 * hidden * (1.0 + bend))
            slope = 0.5 * (1.0 + bend) + (0.5 * root) * hidden * (1.0 - bend * bend) * (
                1.0 + (3.0 * 0.044715) * square
            )
            grad = low(nt(two(cot_all, j, k), down) * slope)
            for n, block in enumerate((j, k)):
                active_all[block, :, here] = active[n * ROW : (n + 1) * ROW]
                gh_all[block, :, here] = grad[n * ROW : (n + 1) * ROW]
            for part, acc in ((nt(grad, up), acc_a), (nn(active, down), acc_b)):
                for n in range(2):
                    rows_of = part[n * ROW : (n + 1) * ROW]

                    @pl.when(i == 0)
                    def _():
                        acc[n][...] = rows_of

                    @pl.when(i > 0)
                    def _():
                        acc[n][...] += rows_of

            return carry

        lax.fori_loop(2 * half, 2 * half + 2, tile, 0)

    gw_expand = ref.gw_expand

    def expand_blocks(first, last, half):
        def block(i, carry):
            lhs = second_all[:, :, lanes(i * QC, QC)].reshape(TALL, QC)
            rhs = gh_all[:, :, half * half_lanes : (half + 1) * half_lanes].reshape(TALL, half_lanes)
            part = low(tn(lhs, rhs)).reshape(LINE, WD, half_lanes)
            gw_expand[i, :, :, half * half_lanes : (half + 1) * half_lanes] = part
            return carry

        lax.fori_loop(first, last, block, 0)

    second = TeamSum(sums.second)
    reduced = TeamSum(sums.reduced)
    own_a, own_b, far_a, far_b = ref.own_a, ref.own_b, ref.far_a, ref.far_b
    spare_a, spare_b = ref.grad_mid, ref.activations
    far_c, far_d = ref.g_reduce, ref.far_d
    near_blocks = (g, sib, (own_a, spare_a), (own_b, spare_b))
    far_blocks = (far, diag, (far_a, far_c), (far_b, far_d))
    second_copies[0].wait_recv()
    feed(*near_blocks, 0)
    second_handed = spread_on(second_all, second_copies[1])
    gather_expand[1].stage4()
    wait_all(second_handed)
    feed(*far_blocks, 0)
    expand_blocks(0, TEAM, 0)
    expand_sums[0].along_y()
    gather_expand[1].finish()
    feed(*near_blocks, 1)
    second.near(0, spare_a[...])
    reduced.ps[0] = low(spare_b[...])
    feed(*far_blocks, 1)
    second.near(1, far_c[...])
    reduced.ps[1] = low(far_d[...])
    second.across(lambda part: far_a[part])
    reduced.near(0)
    reduced.near(1)

    gw_reduce = ref.gw_reduce

    def reduce_block(j):
        lhs = active_all[:, :, lanes(j * ROW, ROW)].reshape(TALL, ROW)
        gw_reduce[j] = low(tn(lhs, tall(cot_all)))

    def reduce_beside(i, carry):
        reduce_block(2 * i + 1 - y)
        return carry

    def reduce_here(i, carry):
        reduce_block(2 * i + y)
        return carry

    lax.fori_loop(0, 4, reduce_beside, 0)
    reduce_y.along_y()
    lax.fori_loop(0, 4, reduce_here, 0)
    reduce_z.stage1()

    csum = ref.csum

    def note(i, value):
        csum[i : i + 1] = jnp.sum(value, axis=0, keepdims=True)

    grad_second = second.total(own_a[...])
    grad_mid = ref.grad_mid
    note(6, grad_second * ref.middle_hat[...])
    note(7, grad_second)
    grad_top = f32(cot_all[g])
    note(8, grad_top)
    grad_mid[...] = grad_top + norm_back_ref(
        grad_second, ref.middle_hat, ref.middle_inv, vector(SECOND_GAIN)
    )
    gb_all = ref.gb_all
    gb_all[g] = low(grad_mid[...])
    gb_copies = spread(gb_all)
    note(5, f32(gb_all[g]))
    g_send, go = ref.g_send, ref.go
    e12 = PairExchange(go.at[pl.ds(0, 7 * ROW)])

    def attended_back(i, j):
        part = low(nt(two(gb_all, i, j), row_weight(output_s)))
        for n, group in enumerate((i, j)):
            for t in range(2):
                g_send[group, t] = part[n * ROW : (n + 1) * ROW, t * 128 : (t + 1) * 128]
                e12.send(g_send.at[group, t], go.at[line_rows, :], pair_place(group, t))

    gb_copies[0].wait_recv()
    attended_back(g, sib)
    expand_blocks(0, 2, 1)
    gb_handed = spread_on(gb_all, gb_copies[1])
    wait_all(gb_handed)
    attended_back(far, diag)
    reduced.across(lambda part: far_b[part])
    expand_blocks(2, TEAM, 1)
    expand_sums[1].along_y()
    reduce_y.sum_y()
    reduce_y.stage1()
    gw_output = ref.gw_output
    gw_output[...] = low(tn(tall(att_all), tall(gb_all))).reshape(LINE, WD, D)
    e12.wait(g_send.at[0, 0], go.at[line_rows, :])
    output_sum.along_y()

    dq, d_all = ref.dq, ref.d_all
    dq[...] = jnp.zeros_like(dq)
    e13 = PairExchange(qkv.at[pl.ds(0, 2), pl.ds(0, 7 * ROW), :])
    products = f32(go[...]) * att_f[...]
    offsets = [
        jnp.sum(jnp.where(half_of_lane == t, products, 0.0), axis=-1, keepdims=True)
        for t in range(2)
    ]
    att_f[...] = jnp.where(half_of_lane == 0, offsets[0], offsets[1])
    pair_d = d_all.at[mine, pl.ds(1, 2), :, pair_lanes]

    def attend_back_keys(b, carry):
        here = rows(b * 256, 256)
        keys, values = qkv[1, here, :], qkv[2, here, :]
        queries, grad = f32(qkv[0]), f32(go[...])
        outs, grad_keys, grad_values = [], 0.0, 0.0
        for t in range(2):
            grad_t = low(jnp.where(half_of_lane == t, grad, 0.0))
            query_t = low(jnp.where(half_of_lane == t, queries, 0.0))
            weights = p_low[t, :, lanes(b * 256, 256)]
            offset = att_f[:, t * HDIM : t * HDIM + 1]
            slopes = low(low(f32(weights) * (nt(grad_t, values) - offset)) * SCALE)
            outs.append(nn(slopes, keys))
            grad_keys += tn(slopes, query_t)
            grad_values += tn(weights, grad_t)
        dq[...] += jnp.where(half_of_lane == 0, outs[0], outs[1])
        pair_send[pl.ds(2 * b, 2), 1] = low(grad_keys).reshape(2, ROW, 128)
        pair_send[pl.ds(2 * b, 2), 2] = low(grad_values).reshape(2, ROW, 128)
        for t in range(2):
            there = 2 * b + t
            e13.send(pair_send.at[there, pl.ds(1, 2)], pair_d, there)

        return carry

    lax.fori_loop(0, 2, attend_back_keys, 0)
    lax.fori_loop(2, GROUP // 256, attend_back_keys, 0)
    pair_send[:, 0] = low(dq[...]).reshape(LINE, ROW, 128)
    d_dst = d_all.at[mine, 0, :, pair_lanes]
    d_copies = to_whole_line(
        lambda place: pair_send.at[place, 0], d_dst, att_low.at[pl.ds(0, 7 * ROW)]
    )
    d_here = pltpu.make_async_copy(pair_send.at[s, 0], d_dst, here_sems.at[reserve_here()])
    d_here.start()
    d_here.wait()
    wait_all(d_copies)
    e13.wait(pair_send.at[0, pl.ds(1, 2)], pair_d)
    normed = TeamSum(sums.normed)

    def joint_back(j):
        total = None
        for kind in range(3):
            weight = joint_s[:, :, :, kind * QC : (kind + 1) * QC].reshape(D, QC)
            part = nt(d_all[j, kind], weight)
            total = part if total is None else total + part
        return total

    normed.near(1, joint_back(diag))
    far_a[...] = joint_back(far)
    normed.across(lambda part: far_a[part])
    for part in expand_sums:
        part.sum_y()
        part.stage1()
    reduce_z.stage2()
    normed.near(0, joint_back(sib))
    own_a[...] = joint_back(g)
    gw_joint = ref.gw_joint
    tsum = ref.tsum
    for kind in range(3):
        block = d_all[:, kind].reshape(TALL, QC)
        for i in range(TEAM):
            lhs = normed_all[:, :, i * QC : (i + 1) * QC].reshape(TALL, QC)
            part = low(tn(lhs, block)).reshape(LINE, WD, QC)
            gw_joint[i, :, :, kind * QC : (kind + 1) * QC] = part
        if kind != 1:
            row = 9 + kind // 2
            tsum[s, row : row + 1] = jnp.sum(f32(block), axis=0, keepdims=True)
    for part in joint_sums:
        part.along_y()
    hidden_sums = jnp.sum(f32(tall(gh_all)), axis=0, keepdims=True)
    for i in range(4):
        tsum[s, 11 + i : 12 + i] = hidden_sums[:, i * QC : (i + 1) * QC]
    tsum[s, 15:16] = jnp.zeros((1, QC), F32)

    grad_normed = normed.total(own_a[...])
    note(3, grad_normed * ref.start_hat[...])
    note(4, grad_normed)
    grad_start = grad_mid[...] + norm_back_ref(
        grad_normed, ref.start_hat, ref.start_inv, vector(FIRST_GAIN)
    )
    gm_all = ref.gm_all
    gm_all[g] = low(grad_start)
    gm_copies = spread(gm_all)
    note(0, f32(gm_all[g]))
    note(1, lead * grad_start)
    note(2, grad_start)
    csum[9:16] = jnp.zeros((7, D), F32)
    crecv = ref.crecv
    crecv[g] = csum[:, lanes(g * QC, QC)]
    c_copies = to_whole_team(
        lambda j: csum.at[:, lanes(j * QC, QC)], crecv.at[g], crecv.at[pl.ds(0, 3)]
    )
    ref.activations[...] = (
        reduced.total(own_b[...]) + middle_ref[...] + vector(REDUCE_BIAS)
    )
    deposit(ref.activations, results.activations)
    reduce_y.stage2()
    expand_sums[0].stage2()
    joint_sums[0].sum_y()
    joint_sums[0].stage1()
    gm_handed = spread_on(gm_all, gm_copies[1])
    gm_copies[0].wait_recv()
    wait_all(gm_handed)

    gw_merge = ref.gw_merge
    f_own = ref.f_own
    t_send = ref.t_send
    q_all = ref.q_all
    grad_heads = low(nt(tall(gm_all), row_weight(merge_s)))
    head_grad = ref.att_all
    head_grad[...] = grad_heads.reshape(TEAM, ROW, QC)
    q_all[s] = jnp.zeros((8, KP), F32)

    def choose_back(h):
        field = f32(tall(field_all))
        grad_h = low(jnp.where(head_of_lane == h, f32(tall(head_grad)), 0.0))
        value_back = nn(grad_h, pv[...].reshape(QC, KP))
        grad_chosen = split_dot(value_back * field, select[...])
        weights = chosen[h]
        shifted = grad_chosen - jnp.sum(weights * grad_chosen, axis=-1, keepdims=True)
        score_spread = nn(low(weights * shifted), select_t[...])
        spread_weights = nn(low(weights), select_t[...])
        pair = tall(head_grad)[:, (h // 2) * 128 : (h // 2 + 1) * 128]
        part = tn(pair, low(spread_weights * field))
        at_row = (h % 2) * HDIM
        t_send[2 * h : 2 * h + 2] = low(part[at_row : at_row + HDIM]).reshape(2, WD, KP)
        field_part = spread_weights * value_back + score_spread * probe[h : h + 1]
        field_part = field_part.reshape(TEAM, ROW, KP)
        if h == 0:
            f_own[...] = field_part
        else:
            f_own[...] += field_part
        q_all[s, h : h + 1] = jnp.sum(score_spread * field, axis=0, keepdims=True)

    for h in range(TEAM_HEADS):
        choose_back(h)
        if h == 0:
            reduce_z.stage3()
            joint_sums[1].sum_y()
            joint_sums[1].stage1()
        if h == 2:
            output_sum.sum_y()
            output_sum.stage1()
            expand_sums[1].stage2()
            reduce_y.stage3()
    t_recv = ref.t_recv
    t_copies = to_whole_line(
        lambda place: t_send.at[place], t_recv.at[s], t_recv.at[pl.ds(0, LINE - 1)]
    )
    t_recv[s] = t_send[s]
    q_copies = share_line(q_all)
    gw_merge[...] = low(tn(head_low[...], tall(gm_all))).reshape(LINE, WD, D)
    merge_sum.along_y()
    reduce_z.along_y()
    expand_sums[0].stage3()
    f_recv = ref.f_recv
    f_copies = Together(f_recv)
    for step in range(1, TEAM):
        j = lax.rem(g + step, TEAM)
        f_copies.push(f_own.at[j], f_recv.at[step - 1], to_team(j))
    position = jnp.zeros((ROW, QC), F32)
    for j in range(TEAM):
        position += f32(gm_all[j, :, lanes(g * QC, QC)])
    ref.g_position[...] = position
    deposit(ref.g_position, results.g_position)
    wait_all(c_copies)
    tsum[s, 0:9] = jnp.sum(crecv[...], axis=0)[0:9]

    joint_sums[0].stage2()
    joint_sums[2].sum_y()
    joint_sums[2].stage1()
    joint_sums[1].stage2()
    expand_sums[1].stage3()
    output_sum.stage2()
    joint_sums[2].stage2()
    merge_sum.sum_y()
    merge_sum.stage1()
    wait_all(t_copies)
    head_all, score_all = ref.head_all, ref.score_all
    head_all[g, s] = low(jnp.sum(f32(t_recv[...]), axis=0))
    h_here = head_all.at[g, s]
    h_copies = to_whole_line(lambda place: h_here, h_here, head_all.at[0, pl.ds(0, LINE - 1)])
    joint_sums[0].stage3()
    joint_sums[1].stage3()
    output_sum.stage3()
    merge_sum.stage2()

    xs_joint, xs_expand = ref.xs_joint, ref.xs_expand
    xr_joint, xr_expand = ref.xr_joint, ref.xr_expand
    x_copies = []

    def to_owners(line_sum, xs, xr, at, size):
        here = pl.ds(at, size)
        line_sum.total(xs.at[:, :, here])
        x_copies.extend(
            to_whole_team(
                lambda j: xs.at[j, :, here], xr.at[g, :, here], xr.at[pl.ds(0, 3), :, here]
            )
        )
        xr[g, :, here] = xs[g, :, here]

    to_owners(expand_sums[0], xs_expand, xr_expand, 0, half_lanes)
    joint_sums[2].stage3()
    to_owners(joint_sums[0], xs_joint, xr_joint, 0, QC)
    wait_all(h_copies)
    h_spread = spread(head_all)
    s_copies = share_line(tsum)
    merge_sum.stage3()
    wait_all(q_copies)
    score_all[g] = jnp.sum(q_all[...], axis=0)
    score_here = score_all.at[g]
    score_copies = to_whole_team(lambda j: score_here, score_here, score_all.at[pl.ds(0, 3)])
    to_owners(expand_sums[1], xs_expand, xr_expand, half_lanes, half_lanes)
    to_owners(joint_sums[1], xs_joint, xr_joint, QC, QC)
    h_handed = spread_on(head_all, h_spread[1])
    to_owners(joint_sums[2], xs_joint, xr_joint, 2 * QC, QC)
    for i in range(2):
        reduce_sums[i].total(ref.g_reduce.at[pl.ds(i * half_rows, half_rows)])
    deposit(ref.g_reduce, results.g_reduce)
    output_sum.total(ref.g_output)
    deposit(ref.g_output, results.g_output)
    f_copies.wait_recv()
    ref.field_grad[...] = (f_own[g] + f_recv[0] + f_recv[1] + f_recv[2]).T[0:VP]
    deposit(ref.field_grad, results.field_grad)
    wait_all(s_copies)
    ref.sums[...] = jnp.sum(tsum[...], axis=0)
    merge_sum.total(ref.g_merge)
    deposit(ref.g_merge, results.g_merge)
    wait_all(x_copies)
    for j in range(TEAM):
        ref.g_expand[:, j * D : (j + 1) * D] = f32(xr_expand[j])
        for kind in range(3):
            at_lane = kind * D + j * QC
            ref.g_joint[:, at_lane : at_lane + QC] = f32(
                xr_joint[j, :, kind * QC : (kind + 1) * QC]
            )
    deposit(ref.g_expand, results.g_expand)
    deposit(ref.g_joint, results.g_joint)
    wait_all(score_copies)
    score_rows = ref.score_rows
    for j in range(TEAM):
        score_rows[TEAM_HEADS * j : TEAM_HEADS * (j + 1)] = score_all[j, 0:TEAM_HEADS]

    def exact(a, b, ca, cb):
        return lax.dot_general(
            a,
            b,
            (((ca,), (cb,)), ((), ())),
            precision=lax.Precision.HIGHEST,
            preferred_element_type=F32,
        )

    scores = score_rows[...]
    query_row = vector(QUERY)
    head_of = lax.broadcasted_iota(jnp.int32, (16, D), 1) // HDIM
    head_rows = (head_of == lax.broadcasted_iota(jnp.int32, (16, D), 0)).astype(F32)
    probe_own = f32(
        low(exact(f32(ref.key_w[...]) * query_row, head_rows, 1, 1) * SCALE)
    )
    grad_probe = exact(f32(pe[...]), scores, 1, 1)
    ref.g_key[...] = exact(grad_probe, head_rows, 1, 0) * (query_row * SCALE)
    deposit(ref.g_key, results.g_key)
    small = ref.small
    picks = (
        lax.broadcasted_iota(jnp.int32, (QC, 128), 0)
        == lax.broadcasted_iota(jnp.int32, (QC, 128), 1) + s * WD
    ) & (lax.broadcasted_iota(jnp.int32, (QC, 128), 1) < WD)
    small[16:24] = jnp.zeros((8, 128), F32)
    small[0:SUM_ROWS] = exact(ref.sums[...], picks.astype(F32), 1, 0)
    hidden_row = jnp.zeros((1, QC), F32)
    score_row = jnp.zeros((1, KP), F32)
    own_scores = score_all[g]
    for i in range(4):
        hidden_row = jnp.where(s // 2 == i, ref.sums[11 + i : 12 + i], hidden_row)
        score_row = jnp.where(s // 2 == i, own_scores[i : i + 1], score_row)
    hidden_row = jnp.where(s % 2 == 0, hidden_row[:, 0:128], hidden_row[:, 128:256])
    query_grad = exact(jnp.broadcast_to(score_row, (8, KP)), ref.key_own[...], 1, 1) * SCALE
    small[24:32] = jnp.zeros((8, 128), F32)
    small[24:25] = hidden_row
    small[25:26, 0:WD] = query_grad[0:1]
    deposit(small, results.small)
    h_spread[0].wait_recv()
    wait_all(h_handed)
    heads = head_all[...].reshape(D, KP)
    ref.g_value[...] = nt(pe[...], heads)
    deposit(ref.g_value, results.g_value)
    grad_table = nn(ref.value_w[...], heads) + exact(probe_own, scores, 1, 0)
    ref.g_patch[...] = grad_table[:, 0:VP]
    ref.g_embed[...] = grad_table[:, VP : VP + VARS]
    deposit(ref.g_patch, results.g_patch)
    deposit(ref.g_embed, results.g_embed)
    for copy in begun + begun_together:
        copy.wait_send()
    for gather in [gather_merge, gather_output] + gather_reduce + gather_joint + gather_expand:
        gather.sent()
    for line_sum in [output_sum, merge_sum] + reduce_sums + joint_sums + expand_sums:
        line_sum.sent()
    for copy in deposits:
        copy.wait()


def fused(operands):
    scratch = list(SCRATCH.values()) + list(OUTPUTS.values())
    for shape in TEAM_SUMS.values():
        scratch += team_sum_buffers(shape)
    return pl.pallas_call(
        fused_kernel,
        out_shape=[jax.ShapeDtypeStruct(*shape) for shape in OUTPUTS.values()],
        in_specs=[pl.BlockSpec(memory_space=space) for space in INPUTS.values()],
        out_specs=[pl.BlockSpec(memory_space=pl.ANY)] * len(OUTPUTS),
        scratch_shapes=[pltpu.VMEM(*shape) for shape in scratch]
        + [pltpu.SemaphoreType.DMA((SEMAPHORES,))] * 2
        + [pltpu.SemaphoreType.DMA((HERE,))],
        compiler_params=pltpu.CompilerParams(
            collective_id=1, has_side_effects=True, vmem_limit_bytes=64 << 20
        ),
    )(*operands)


VECTOR_ROWS = (25, 0, 1, 2, 3, 4, 5, 6, 7, 8)


def hand_out_kernel(*refs):
    n, m = len(OUTPUTS), len(VECTOR_ROWS)
    arrays = refs[:n]
    results = refs[n : 2 * n - 1]
    vectors = refs[2 * n - 1 : 2 * n - 1 + m]
    joint, hidden = refs[2 * n - 1 + m : 2 * n + 1 + m]
    held = refs[2 * n + 1 + m : 3 * n + 1 + m]
    narrow, both, came, left = refs[3 * n + 1 + m :]
    fetches = [pltpu.make_async_copy(arrays[i], held[i], came.at[i]) for i in range(n)]
    for copy in fetches:
        copy.start()
    stores = []
    for i in range(n - 1):
        fetches[i].wait()
        stores.append(pltpu.make_async_copy(held[i], results[i], left.at[i]))
        stores[-1].start()
    small = held[n - 1]
    fetches[n - 1].wait()
    narrow[...] = small[:, 0:WD]
    both[...] = small[9:11, 0:WD]
    last = [
        pltpu.make_async_copy(narrow.at[row], vectors[i], left.at[n + i])
        for i, row in enumerate(VECTOR_ROWS)
    ]
    last.append(pltpu.make_async_copy(both, joint, left.at[n + m]))
    last.append(pltpu.make_async_copy(small.at[24], hidden, left.at[n + m + 1]))
    for copy in last:
        copy.start()
    stores += last
    for copy in stores:
        copy.wait()


def hand_out(arrays):
    n, m = len(arrays), len(VECTOR_ROWS)
    shapes = [jax.ShapeDtypeStruct(a.shape, a.dtype) for a in arrays[:-1]]
    shapes += [jax.ShapeDtypeStruct((WD,), F32)] * m
    shapes += [jax.ShapeDtypeStruct((2, WD), F32), jax.ShapeDtypeStruct((ROW,), F32)]
    return pl.pallas_call(
        hand_out_kernel,
        out_shape=shapes,
        in_specs=[pl.BlockSpec(memory_space=pl.ANY)] * n,
        out_specs=[pl.BlockSpec(memory_space=pl.ANY)] * len(shapes),
        scratch_shapes=[pltpu.VMEM(a.shape, a.dtype) for a in arrays]
        + [pltpu.VMEM((32, WD), F32), pltpu.VMEM((2, WD), F32)]
        + [pltpu.SemaphoreType.DMA((n,)), pltpu.SemaphoreType.DMA((n + m + 2,))],
        compiler_params=pltpu.CompilerParams(vmem_limit_bytes=64 << 20),
    )(*arrays)


def shards_fused(
    fields,
    patch_weight,
    variable_embed,
    query_vector,
    key_weight,
    value_weight,
    merge_weight,
    merge_bias,
    position_table,
    lead_weight,
    lead_bias,
    first_gain,
    first_shift,
    joint_weight,
    joint_bias,
    output_weight,
    output_bias,
    second_gain,
    second_shift,
    expand_weight,
    expand_bias,
    reduce_weight,
    reduce_bias,
    segment_ids,
    live_rows,
    lead_steps,
    cotangent,
):
    pack = jnp.concatenate(
        [
            query_vector,
            merge_bias,
            lead_weight,
            lead_bias,
            first_gain,
            first_shift,
            output_bias,
            second_gain,
            second_shift,
            reduce_bias,
            jnp.zeros((2 * WD,), BF16),
            expand_bias,
            jnp.zeros((12 * 128,), BF16),
        ]
    ).reshape(16, 128)
    whole = fused(
        (
            fields.T,
            patch_weight.T,
            variable_embed.T,
            key_weight,
            value_weight,
            pack,
            joint_bias,
            segment_ids.reshape(1, ROW),
            live_rows.reshape(1, ROW),
            lead_steps,
            cotangent,
            position_table,
            joint_weight,
            expand_weight,
            merge_weight,
            output_weight,
            reduce_weight,
        )
    )
    (
        activations,
        field_grad,
        g_patch,
        g_embed,
        g_key,
        g_value,
        g_merge,
        g_position,
        g_joint,
        g_output,
        g_expand,
        g_reduce,
        g_query,
        g_merge_b,
        g_lead,
        g_lead_b,
        g_first_gain,
        g_first_shift,
        g_output_b,
        g_second_gain,
        g_second_shift,
        g_reduce_b,
        g_joint_b,
        g_expand_b,
    ) = hand_out(whole)
    return (
        activations,
        field_grad.T,
        g_patch.T,
        g_embed.T,
        g_query,
        g_key,
        g_value,
        g_merge,
        g_merge_b,
        g_position,
        g_lead,
        g_lead_b,
        g_first_gain,
        g_first_shift,
        g_joint,
        g_joint_b,
        g_output,
        g_output_b,
        g_second_gain,
        g_second_shift,
        g_expand,
        g_expand_b,
        g_reduce,
        g_reduce_b,
    )


def solution(mesh):
    by_row = P(ROWS, None)
    by_column = P(None, ROWS)
    vector = P(ROWS)
    in_specs = (
        by_row,
        by_column,
        by_column,
        vector,
        by_row,
        by_row,
        by_row,
        vector,
        P("seq", "grp"),
        vector,
        vector,
        vector,
        vector,
        by_row,
        by_column,
        by_row,
        vector,
        vector,
        vector,
        by_row,
        vector,
        by_row,
        vector,
        vector,
        vector,
        P("grp", None),
        by_row,
    )
    out_specs = (
        by_row,
        by_row,
        by_column,
        by_column,
        vector,
        by_row,
        by_row,
        by_row,
        vector,
        P("seq", "grp"),
        vector,
        vector,
        vector,
        vector,
        by_row,
        by_column,
        by_row,
        vector,
        vector,
        vector,
        by_row,
        vector,
        by_row,
        vector,
    )
    G, S = mesh.shape["grp"], mesh.shape["seq"]

    def body(*args):
        rows_here, weight_rows = args[0].shape[0], args[5].shape[0]
        if (G, S, rows_here, weight_rows) == (TEAM, LINE, ROW, WD):
            return shards_fused(*args)
        return shards(G, S, *args)

    return jax.shard_map(body, mesh=mesh, in_specs=in_specs, out_specs=out_specs, check_vma=False)
```
